32 devices in a mesh: ctx: 4 (over y, x), tp: 8 (over z, core).
Axes of the slice: x: 2, y: 2, z: 4, core: 2. Of those that a mesh axis runs over, the one named last changes fastest.
Arguments:
- query_gate: bfloat16 [2048, 8192], P('ctx', 'tp'), may hold values from -6 to 6
- key_gate: bfloat16 [2048, 8192], P('ctx', 'tp'), may hold values from -6 to 6
- value_input: bfloat16 [2048, 8192], P('ctx', 'tp'), may hold values from -6 to 6
- filter_taps: float32 [2048, 512], P('ctx', 'tp'), may hold values from -6 to 6
- out_weight: bfloat16 [8192, 8192], P('tp'), may hold values from -0.09375 to 0.09375
- out_grad: bfloat16 [2048, 8192], P('ctx', 'tp'), may hold values from -6 to 6
Outputs:
- projected: bfloat16 [2048, 8192], P('ctx', 'tp')
- grad_query: bfloat16 [2048, 8192], P('ctx', 'tp')
- grad_key: bfloat16 [2048, 8192], P('ctx', 'tp')
- grad_value: bfloat16 [2048, 8192], P('ctx', 'tp')
- grad_filter: float32 [2048, 512], P('ctx', 'tp')
The draws below stay inside these ranges and needn't reach their ends.
All inputs are finite; a program needn't handle non-finite values.
Results may differ from the reference program's by a relative error of at most 0.027.
Values may be sent and summed in bfloat16 or wider, within the bound.
No kernel may reach another device: no remote copies, remote signals or barrier semaphores. Data moves between devices by JAX's collectives and lax.ppermute only.
A program may use at most 192 MiB of HBM per device.

```python
import math
import jax
import jax.numpy as jnp
from jax import lax

D = 8192
GROUP = 16
SEQ = 2048
GROUPS = 512
N_TP = 8


def raised(values, rng, source, target, shards_of, factor):
    owner, partner = [(jnp.arange(values.shape[axis_at]) // (values.shape[axis_at] // shards_of)).reshape([-1 if axis == axis_at else 1 for axis in range(values.ndim)]) for axis_at in (source, target)]
    chosen = jax.random.permutation(rng, shards_of)[partner]
    strong = (owner == chosen) | (owner == (partner + shards_of // 2) % shards_of)
    return jnp.where(strong, factor * values, values)


def steps_of(stream_key, extent, split, low, largest):
    def one(axis_at, shards_of):
        steps = jax.random.uniform(jax.random.fold_in(jax.random.fold_in(stream_key, 6), axis_at), (shards_of,), jnp.float32, low / len(split), largest / len(split))
        return jnp.repeat(jnp.exp(steps), extent[axis_at] // shards_of).reshape((-1,) + (1,) * (len(extent) - axis_at - 1))

    loudness = one(*split[0])
    for cut in split[1:]:
        loudness = loudness * one(*cut)
    return loudness


def bell_draw(rng, dims, width, most, pieces=(), kind=jnp.bfloat16):
    level = steps_of(rng, dims, pieces, -0.22, 0.18) if pieces else 1.0
    result = jax.random.normal(rng, dims, jnp.float32) * width * level
    return jnp.minimum(jnp.maximum(result, -most), most).astype(kind)


def bell_draw_with(key, dims, spread, most, split, heavy, dtype=jnp.bfloat16):
    array = spread * jax.random.normal(key, dims, jnp.float32)
    if split:
        array = array * steps_of(key, dims, split, -0.22, 0.18)
    return jnp.clip(raised(array, jax.random.fold_in(key, 3), *heavy), -most, most).astype(dtype)


def setup_inputs(seed: int = 0) -> dict:
    key_list = jax.random.split(jax.random.key(seed), 7)
    return {
        "query_gate": bell_draw(key_list[0], (SEQ, D), 1.0, 6.0, ((0, 4), (1, 8))),
        "key_gate": bell_draw(key_list[1], (SEQ, D), 1.0, 6.0, ((0, 4), (1, 8))),
        "value_input": bell_draw(key_list[2], (SEQ, D), 1.0, 6.0, ((0, 4), (1, 8))),
        "filter_taps": bell_draw(key_list[3], (SEQ, GROUPS), 1.0, 6.0, ((0, 4), (1, 8)), jnp.float32),
        "out_weight": bell_draw_with(key_list[4], (D, D), D ** -0.5, 0.09375, ((0, 8),), (0, 1, 8, 2.0)),
        "out_grad": bell_draw(key_list[5], (SEQ, D), 1.0, 6.0, ((0, 4), (1, 8))),
    }


def reference(query_gate, key_gate, value_input, filter_taps, out_weight, out_grad):
    seq_len, model_width = query_gate.shape
    tap_scale = 1.0 / math.sqrt(seq_len)
    fft_len = 2 * seq_len
    product_in = (key_gate.astype(jnp.float32) * value_input.astype(jnp.float32)).astype(jnp.bfloat16)
    tap_rows = filter_taps * tap_scale
    tap_spec = jnp.repeat(jnp.fft.rfft(tap_rows, n=fft_len, axis=0), GROUP, axis=1)
    input_spec = jnp.fft.rfft(product_in.astype(jnp.float32), n=fft_len, axis=0)
    convolved = jnp.fft.irfft(input_spec * tap_spec, n=fft_len, axis=0)[:seq_len]
    gated_out = (query_gate.astype(jnp.float32) * convolved).astype(jnp.bfloat16)
    block_width = model_width // N_TP
    projected = jnp.zeros((seq_len, model_width), jnp.float32)
    for block_no in range(N_TP):
        block_begin = block_no * block_width
        block_end = block_begin + block_width
        block_sum = jnp.dot(gated_out[:, block_begin:block_end], out_weight[block_begin:block_end], preferred_element_type=jnp.float32).astype(jnp.bfloat16)
        block_sum = lax.optimization_barrier(block_sum)
        projected = projected + block_sum.astype(jnp.float32)
    projected = projected.astype(jnp.bfloat16)
    dgated = jnp.dot(out_grad, out_weight.T, preferred_element_type=jnp.float32).astype(jnp.bfloat16)
    grad_query = (dgated.astype(jnp.float32) * convolved).astype(jnp.bfloat16)
    conv_grad = (dgated.astype(jnp.float32) * query_gate.astype(jnp.float32)).astype(jnp.bfloat16)
    grad_spec = jnp.fft.rfft(conv_grad.astype(jnp.float32), n=fft_len, axis=0)
    input_grad = jnp.fft.irfft(jnp.conj(tap_spec) * grad_spec, n=fft_len, axis=0)[:seq_len]
    grad_key = (input_grad * value_input.astype(jnp.float32)).astype(jnp.bfloat16)
    grad_value = (input_grad * key_gate.astype(jnp.float32)).astype(jnp.bfloat16)
    cross_spec = (grad_spec * jnp.conj(input_spec)).reshape(grad_spec.shape[0], model_width // GROUP, GROUP).sum(axis=2)
    grad_filter = jnp.fft.irfft(cross_spec, n=fft_len, axis=0)[:seq_len] * tap_scale
    return (projected, grad_query, grad_key, grad_value, grad_filter)
```

```python
import functools
import math
import jax
import jax.numpy as jnp
from jax import lax
from jax.experimental import pallas as pl
from jax.experimental.pallas import tpu as pltpu
from jax.sharding import PartitionSpec as P

BLOCK = 128
NT = (((1,), (1,)), ((), ()))


def lag_matrix(row, length):
    lanes = lax.broadcasted_iota(jnp.int32, (BLOCK, length), 1)
    rows = lax.broadcasted_iota(jnp.int32, (BLOCK, length), 0)
    spread = pltpu.roll(
        jnp.broadcast_to(row, (BLOCK, length)), 0, axis=1, stride=1, stride_axis=0
    )
    return jnp.where(lanes >= rows, spread, 0.0).astype(jnp.bfloat16)


def stacked(ref, start, rows, members, width):
    pieces = []
    for member in range(members):
        part = ref[member, pl.ds(start, rows), :]
        for at in range(0, width, BLOCK):
            pieces.append(part[:, at : at + BLOCK])
    return jnp.concatenate(pieces, axis=0)


def spread_out(ref, start, rows, value, members, width):
    per_member = width // BLOCK
    for member in range(members):
        base = member * per_member * rows
        parts = [value[base + i * rows : base + (i + 1) * rows] for i in range(per_member)]
        ref[member, pl.ds(start, rows), :] = jnp.concatenate(parts, axis=1)


def forward_kernel(members, per_group, pos_ref, *refs):
    inputs, taps = refs[:members], refs[members : 2 * members]
    outputs = refs[2 * members : 3 * members]
    tap_scr, in_scr, out_scr = refs[3 * members :]
    position = pos_ref[0]
    width, channels = inputs[0].shape
    groups = taps[0].shape[0]
    length = members * width
    blocks = length // BLOCK
    for step in range(members):
        at = position ^ step
        in_scr[at] = inputs[step][...].T
        tap_scr[:, pl.ds(pl.multiple_of(at * width, width), width)] = taps[step][...]

    def one_group(group, carry):
        start = pl.multiple_of(group * per_group, per_group)
        lags = lag_matrix(tap_scr[pl.ds(group, 1), :], length)
        data = stacked(in_scr, start, per_group, members, width)
        total = [jnp.zeros((per_group, BLOCK), jnp.float32) for _ in range(blocks)]
        for offset in range(0, blocks, 2):
            rows = (blocks - offset) * per_group
            result = jnp.dot(
                data[:rows],
                lags[:, offset * BLOCK : (offset + 2) * BLOCK],
                preferred_element_type=jnp.float32,
            )
            for side in range(2):
                for source in range(blocks - offset - side):
                    total[source + offset + side] += result[
                        source * per_group : (source + 1) * per_group,
                        side * BLOCK : (side + 1) * BLOCK,
                    ]
        value = jnp.concatenate(total, axis=0).astype(jnp.bfloat16)
        spread_out(out_scr, start, per_group, value, members, width)
        return carry

    lax.fori_loop(0, groups, one_group, 0)
    for step in range(members):
        outputs[step][...] = out_scr[position ^ step].T


def backward_kernel(members, per_group, scale, pos_ref, *refs):
    inputs, cotangents, taps = (
        refs[:members],
        refs[members : 2 * members],
        refs[2 * members : 3 * members],
    )
    outputs = refs[3 * members : 4 * members]
    tap_grads = refs[4 * members : 5 * members]
    tap_scr, in_scr, cot_scr, out_scr, grad_scr, pad_scr = refs[5 * members :]
    position = pos_ref[0]
    width, channels = inputs[0].shape
    groups = taps[0].shape[0]
    length = members * width
    blocks = length // BLOCK
    depth = blocks * per_group
    for step in range(members):
        at = position ^ step
        in_scr[at] = inputs[step][...].T
        cot_scr[at] = cotangents[step][...].T
        tap_scr[:, pl.ds(pl.multiple_of(at * width, width), width)] = taps[step][...]
    pad_scr[...] = jnp.zeros_like(pad_scr)
    rows_of = lax.broadcasted_iota(jnp.int32, (BLOCK, BLOCK), 0)
    lanes_of = lax.broadcasted_iota(jnp.int32, (BLOCK, BLOCK), 1)
    mirror = (rows_of + lanes_of == BLOCK - 1).astype(jnp.bfloat16)

    def one_group(group, carry):
        start = pl.multiple_of(group * per_group, per_group)
        lags = lag_matrix(tap_scr[pl.ds(group, 1), :], length)
        data = stacked(in_scr, start, per_group, members, width)
        cot = stacked(cot_scr, start, per_group, members, width)
        pad_scr[:depth, :BLOCK] = cot
        pad_scr[: depth - per_group, BLOCK:] = cot[per_group:]
        flipped = lax.dot_general(
            mirror, data, NT, preferred_element_type=jnp.float32
        ).astype(jnp.bfloat16)
        total = jnp.zeros((depth, BLOCK), jnp.float32)
        products = []
        for offset in range(0, blocks, 2):
            rows = depth - offset * per_group
            pair = pad_scr[offset * per_group : offset * per_group + depth, :]
            result = lax.dot_general(
                pair[:rows],
                lags[:, offset * BLOCK : (offset + 2) * BLOCK],
                NT,
                preferred_element_type=jnp.float32,
            )
            if rows < depth:
                result = jnp.concatenate(
                    [result, jnp.zeros((depth - rows, BLOCK), jnp.float32)], axis=0
                )
            total = total + result
            products.append(jnp.dot(flipped, pair, preferred_element_type=jnp.float32))
        spread_out(
            out_scr, start, per_group, total.astype(jnp.bfloat16), members, width
        )
        product = jnp.concatenate(products, axis=1)
        lanes = lax.broadcasted_iota(jnp.int32, (BLOCK, length), 1)
        back = BLOCK - 1 - lax.broadcasted_iota(jnp.int32, (BLOCK, length), 0)
        product = jnp.where(lanes >= back, product, 0.0)
        product = pltpu.roll(
            product, length - (BLOCK - 1), axis=1, stride=1, stride_axis=0
        )
        grad_scr[pl.ds(group, 1), :] = jnp.sum(product, axis=0, keepdims=True) * scale
        return carry

    lax.fori_loop(0, groups, one_group, 0)
    for step in range(members):
        at = position ^ step
        outputs[step][...] = out_scr[at].T
        tap_grads[step][...] = grad_scr[:, pl.ds(pl.multiple_of(at * width, width), width)]


VMEM = pl.BlockSpec(memory_space=pltpu.VMEM)
SMEM = pl.BlockSpec(memory_space=pltpu.SMEM)


def convolve(position, inputs, taps, per_group):
    members = len(inputs)
    width, channels = inputs[0].shape
    groups = taps[0].shape[0]
    length = members * width
    flops = 4 * length * length * channels
    return pl.pallas_call(
        functools.partial(forward_kernel, members, per_group),
        out_shape=[jax.ShapeDtypeStruct((width, channels), jnp.bfloat16)] * members,
        in_specs=[SMEM] + [VMEM] * (2 * members),
        out_specs=[VMEM] * members,
        scratch_shapes=[
            pltpu.VMEM((groups, length), jnp.float32),
            pltpu.VMEM((members, channels, width), jnp.bfloat16),
            pltpu.VMEM((members, channels, width), jnp.bfloat16),
        ],
        compiler_params=pltpu.CompilerParams(vmem_limit_bytes=32 * 2**20),
        cost_estimate=pl.CostEstimate(
            flops=flops, bytes_accessed=4 * length * channels, transcendentals=0
        ),
        name="causal_conv",
    )(position, *inputs, *taps)


def correlate(position, inputs, cotangents, taps, per_group, scale):
    members = len(inputs)
    width, channels = inputs[0].shape
    groups = taps[0].shape[0]
    length = members * width
    flops = 8 * length * length * channels
    results = pl.pallas_call(
        functools.partial(backward_kernel, members, per_group, scale),
        out_shape=[jax.ShapeDtypeStruct((width, channels), jnp.bfloat16)] * members
        + [jax.ShapeDtypeStruct((groups, width), jnp.float32)] * members,
        in_specs=[SMEM] + [VMEM] * (3 * members),
        out_specs=[VMEM] * (2 * members),
        scratch_shapes=[
            pltpu.VMEM((groups, length), jnp.float32),
            pltpu.VMEM((members, channels, width), jnp.bfloat16),
            pltpu.VMEM((members, channels, width), jnp.bfloat16),
            pltpu.VMEM((members, channels, width), jnp.bfloat16),
            pltpu.VMEM((groups, length), jnp.float32),
            pltpu.VMEM((2 * length // BLOCK * per_group, 2 * BLOCK), jnp.bfloat16),
        ],
        compiler_params=pltpu.CompilerParams(vmem_limit_bytes=32 * 2**20),
        cost_estimate=pl.CostEstimate(
            flops=flops, bytes_accessed=6 * length * channels, transcendentals=0
        ),
        name="causal_conv_grads",
    )(position, *inputs, *cotangents, *taps)
    return results[:members], results[members:]


def swapped(array, axis, step):
    size = lax.axis_size(axis)
    return lax.ppermute(array, axis, [(i, i ^ step) for i in range(size)])


def traded(pieces, axis):
    return [pieces[0]] + [swapped(pieces[step], axis, step) for step in range(1, len(pieces))]


def cut(array, position, members, axis):
    width = array.shape[axis] // members
    return [
        lax.dynamic_slice_in_dim(array, (position ^ step) * width, width, axis)
        for step in range(members)
    ]


def joined(pieces, position, axis):
    members = len(pieces)
    width = pieces[0].shape[axis]
    shape = list(pieces[0].shape)
    shape[axis] = members * width
    whole = jnp.zeros(shape, pieces[0].dtype)
    for step in range(members):
        whole = lax.dynamic_update_slice_in_dim(
            whole, pieces[step], (position ^ step) * width, axis
        )
    return whole


def wide(array):
    return array.astype(jnp.float32)


def local(query_gate, key_gate, value_input, filter_taps, out_weight, out_grad):
    length, channels = query_gate.shape
    groups = filter_taps.shape[1]
    per_group = channels // groups
    members = lax.axis_size("ctx")
    position = lax.axis_index("ctx")
    at = position.reshape((1,)).astype(jnp.int32)
    tap_scale = 1.0 / math.sqrt(length * members)

    all_cotangents = lax.all_gather(out_grad, "tp", axis=1, tiled=True)
    tap_rows = (filter_taps * tap_scale).astype(jnp.bfloat16).T
    tap_parts = [wide(p) for p in traded(cut(tap_rows, position, members, 0), "ctx")]
    product_in = (wide(key_gate) * wide(value_input)).astype(jnp.bfloat16)
    input_parts = traded(cut(product_in, position, members, 1), "ctx")
    conv_parts = traded(convolve(at, input_parts, tap_parts, per_group), "ctx")
    convolved = joined(conv_parts, position, 1)
    gated_out = (wide(query_gate) * wide(convolved)).astype(jnp.bfloat16)
    partial_value = jnp.dot(gated_out, out_weight, preferred_element_type=jnp.float32)
    projected = lax.psum_scatter(
        partial_value.astype(jnp.bfloat16), "tp", scatter_dimension=1, tiled=True
    )
    dgated = jnp.einsum(
        "tk,ck->tc", all_cotangents, out_weight, preferred_element_type=jnp.float32
    ).astype(jnp.bfloat16)
    grad_query = (wide(dgated) * wide(convolved)).astype(jnp.bfloat16)
    conv_grad = (wide(dgated) * wide(query_gate)).astype(jnp.bfloat16)
    grad_parts = traded(cut(conv_grad, position, members, 1), "ctx")
    back_parts, filter_parts = correlate(
        at, input_parts, grad_parts, tap_parts, per_group, tap_scale
    )
    input_grad = wide(joined(traded(back_parts, "ctx"), position, 1))
    grad_filter = joined(traded(filter_parts, "ctx"), position, 0).T
    grad_key = (input_grad * wide(value_input)).astype(jnp.bfloat16)
    grad_value = (input_grad * wide(key_gate)).astype(jnp.bfloat16)
    return (projected, grad_query, grad_key, grad_value, grad_filter)


def solution(mesh):
    both = P("ctx", "tp")
    return jax.shard_map(
        local,
        mesh=mesh,
        in_specs=(both, both, both, both, P("tp", None), both),
        out_specs=(both,) * 5,
        check_vma=False,
    )
```

```python
import functools
import math
import jax
import jax.numpy as jnp
from jax import lax
from jax.experimental import pallas as pl
from jax.experimental.pallas import tpu as pltpu
from jax.sharding import PartitionSpec as P

BLOCK = 128
NT = (((1,), (1,)), ((), ()))


def lag_matrix(row, length):
    lanes = lax.broadcasted_iota(jnp.int32, (BLOCK, length), 1)
    rows = lax.broadcasted_iota(jnp.int32, (BLOCK, length), 0)
    spread = pltpu.roll(
        jnp.broadcast_to(row, (BLOCK, length)), 0, axis=1, stride=1, stride_axis=0
    )
    return jnp.where(lanes >= rows, spread, 0.0).astype(jnp.bfloat16)


def stacked(ref, start, rows, members, width):
    pieces = []
    for member in range(members):
        part = ref[member, pl.ds(start, rows), :]
        for at in range(0, width, BLOCK):
            pieces.append(part[:, at : at + BLOCK])
    return jnp.concatenate(pieces, axis=0)


def spread_out(ref, start, rows, value, members, width):
    per_member = width // BLOCK
    for member in range(members):
        base = member * per_member * rows
        parts = [value[base + i * rows : base + (i + 1) * rows] for i in range(per_member)]
        ref[member, pl.ds(start, rows), :] = jnp.concatenate(parts, axis=1)


def forward_kernel(members, per_group, pos_ref, *refs):
    inputs, taps = refs[:members], refs[members : 2 * members]
    outputs = refs[2 * members : 3 * members]
    tap_scr, in_scr, out_scr = refs[3 * members :]
    position = pos_ref[0]
    width, channels = inputs[0].shape
    groups = taps[0].shape[0]
    length = members * width
    blocks = length // BLOCK
    for step in range(members):
        at = position ^ step
        in_scr[at] = inputs[step][...].T
        tap_scr[:, pl.ds(pl.multiple_of(at * width, width), width)] = taps[step][...]

    def one_group(group, carry):
        start = pl.multiple_of(group * per_group, per_group)
        lags = lag_matrix(tap_scr[pl.ds(group, 1), :], length)
        data = stacked(in_scr, start, per_group, members, width)
        total = [jnp.zeros((per_group, BLOCK), jnp.float32) for _ in range(blocks)]
        for offset in range(0, blocks, 2):
            rows = (blocks - offset) * per_group
            result = jnp.dot(
                data[:rows],
                lags[:, offset * BLOCK : (offset + 2) * BLOCK],
                preferred_element_type=jnp.float32,
            )
            for side in range(2):
                for source in range(blocks - offset - side):
                    total[source + offset + side] += result[
                        source * per_group : (source + 1) * per_group,
                        side * BLOCK : (side + 1) * BLOCK,
                    ]
        value = jnp.concatenate(total, axis=0).astype(jnp.bfloat16)
        spread_out(out_scr, start, per_group, value, members, width)
        return carry

    lax.fori_loop(0, groups, one_group, 0)
    for step in range(members):
        outputs[step][...] = out_scr[position ^ step].T


def backward_kernel(members, per_group, scale, pos_ref, *refs):
    inputs, cotangents, taps = (
        refs[:members],
        refs[members : 2 * members],
        refs[2 * members : 3 * members],
    )
    outputs = refs[3 * members : 4 * members]
    tap_grads = refs[4 * members : 5 * members]
    tap_scr, in_scr, cot_scr, out_scr, grad_scr, pad_scr = refs[5 * members :]
    position = pos_ref[0]
    width, channels = inputs[0].shape
    groups = taps[0].shape[0]
    length = members * width
    blocks = length // BLOCK
    depth = blocks * per_group
    for step in range(members):
        at = position ^ step
        in_scr[at] = inputs[step][...].T
        cot_scr[at] = cotangents[step][...].T
        tap_scr[:, pl.ds(pl.multiple_of(at * width, width), width)] = taps[step][...]
    pad_scr[...] = jnp.zeros_like(pad_scr)
    rows_of = lax.broadcasted_iota(jnp.int32, (BLOCK, BLOCK), 0)
    lanes_of = lax.broadcasted_iota(jnp.int32, (BLOCK, BLOCK), 1)
    mirror = (rows_of + lanes_of == BLOCK - 1).astype(jnp.bfloat16)

    def one_group(group, carry):
        start = pl.multiple_of(group * per_group, per_group)
        lags = lag_matrix(tap_scr[pl.ds(group, 1), :], length)
        data = stacked(in_scr, start, per_group, members, width)
        cot = stacked(cot_scr, start, per_group, members, width)
        pad_scr[:depth, :BLOCK] = cot
        pad_scr[: depth - per_group, BLOCK:] = cot[per_group:]
        flipped = lax.dot_general(
            mirror, data, NT, preferred_element_type=jnp.float32
        ).astype(jnp.bfloat16)
        total = jnp.zeros((depth, BLOCK), jnp.float32)
        products = []
        for offset in range(0, blocks, 2):
            rows = depth - offset * per_group
            pair = pad_scr[offset * per_group : offset * per_group + depth, :]
            result = lax.dot_general(
                pair[:rows],
                lags[:, offset * BLOCK : (offset + 2) * BLOCK],
                NT,
                preferred_element_type=jnp.float32,
            )
            if rows < depth:
                result = jnp.concatenate(
                    [result, jnp.zeros((depth - rows, BLOCK), jnp.float32)], axis=0
                )
            total = total + result
            products.append(jnp.dot(flipped, pair, preferred_element_type=jnp.float32))
        spread_out(
            out_scr, start, per_group, total.astype(jnp.bfloat16), members, width
        )
        product = jnp.concatenate(products, axis=1)
        lanes = lax.broadcasted_iota(jnp.int32, (BLOCK, length), 1)
        back = BLOCK - 1 - lax.broadcasted_iota(jnp.int32, (BLOCK, length), 0)
        product = jnp.where(lanes >= back, product, 0.0)
        product = pltpu.roll(
            product, length - (BLOCK - 1), axis=1, stride=1, stride_axis=0
        )
        grad_scr[pl.ds(group, 1), :] = jnp.sum(product, axis=0, keepdims=True) * scale
        return carry

    lax.fori_loop(0, groups, one_group, 0)
    for step in range(members):
        at = position ^ step
        outputs[step][...] = out_scr[at].T
        tap_grads[step][...] = grad_scr[:, pl.ds(pl.multiple_of(at * width, width), width)]


VMEM = pl.BlockSpec(memory_space=pltpu.VMEM)
SMEM = pl.BlockSpec(memory_space=pltpu.SMEM)


def convolve(position, inputs, taps, per_group):
    members = len(inputs)
    width, channels = inputs[0].shape
    groups = taps[0].shape[0]
    length = members * width
    flops = 4 * length * length * channels
    return pl.pallas_call(
        functools.partial(forward_kernel, members, per_group),
        out_shape=[jax.ShapeDtypeStruct((width, channels), jnp.bfloat16)] * members,
        in_specs=[SMEM] + [VMEM] * (2 * members),
        out_specs=[VMEM] * members,
        scratch_shapes=[
            pltpu.VMEM((groups, length), jnp.float32),
            pltpu.VMEM((members, channels, width), jnp.bfloat16),
            pltpu.VMEM((members, channels, width), jnp.bfloat16),
        ],
        compiler_params=pltpu.CompilerParams(vmem_limit_bytes=32 * 2**20),
        cost_estimate=pl.CostEstimate(
            flops=flops, bytes_accessed=4 * length * channels, transcendentals=0
        ),
        name="causal_conv",
    )(position, *inputs, *taps)


def correlate(position, inputs, cotangents, taps, per_group, scale):
    members = len(inputs)
    width, channels = inputs[0].shape
    groups = taps[0].shape[0]
    length = members * width
    flops = 8 * length * length * channels
    results = pl.pallas_call(
        functools.partial(backward_kernel, members, per_group, scale),
        out_shape=[jax.ShapeDtypeStruct((width, channels), jnp.bfloat16)] * members
        + [jax.ShapeDtypeStruct((groups, width), jnp.float32)] * members,
        in_specs=[SMEM] + [VMEM] * (3 * members),
        out_specs=[VMEM] * (2 * members),
        scratch_shapes=[
            pltpu.VMEM((groups, length), jnp.float32),
            pltpu.VMEM((members, channels, width), jnp.bfloat16),
            pltpu.VMEM((members, channels, width), jnp.bfloat16),
            pltpu.VMEM((members, channels, width), jnp.bfloat16),
            pltpu.VMEM((groups, length), jnp.float32),
            pltpu.VMEM((2 * length // BLOCK * per_group, 2 * BLOCK), jnp.bfloat16),
        ],
        compiler_params=pltpu.CompilerParams(vmem_limit_bytes=32 * 2**20),
        cost_estimate=pl.CostEstimate(
            flops=flops, bytes_accessed=6 * length * channels, transcendentals=0
        ),
        name="causal_conv_grads",
    )(position, *inputs, *cotangents, *taps)
    return results[:members], results[members:]


def swapped(array, axis, step):
    size = lax.axis_size(axis)
    return lax.ppermute(array, axis, [(i, i ^ step) for i in range(size)])


def traded(pieces, axis):
    return [pieces[0]] + [swapped(pieces[step], axis, step) for step in range(1, len(pieces))]


def cut(array, position, members, axis):
    width = array.shape[axis] // members
    return [
        lax.dynamic_slice_in_dim(array, (position ^ step) * width, width, axis)
        for step in range(members)
    ]


def joined(pieces, position, axis):
    members = len(pieces)
    width = pieces[0].shape[axis]
    shape = list(pieces[0].shape)
    shape[axis] = members * width
    whole = jnp.zeros(shape, pieces[0].dtype)
    for step in range(members):
        whole = lax.dynamic_update_slice_in_dim(
            whole, pieces[step], (position ^ step) * width, axis
        )
    return whole


def wide(array):
    return array.astype(jnp.float32)


def hop(array, pairs):
    return lax.ppermute(
        array, "tp", [(2 * i + core, 2 * j + core) for i, j in pairs for core in range(2)]
    )


INWARD = ((0, 1), (3, 2))
ACROSS = ((1, 2), (2, 1))
OUTWARD = ((1, 0), (2, 3))


def of_chip(chip, table):
    return jnp.asarray(table, jnp.int32)[chip]


def columns(array, block, width):
    return lax.dynamic_slice_in_dim(array, block * width, width, 1)


def gathered_product(block, out_weight):
    place = lax.axis_index("tp")
    chip, core = place // 2, place % 2
    width = block.shape[1]
    middle = (chip == 1) | (chip == 2)
    to_middle = hop(block, INWARD)
    swap_middle = hop(block, ACROSS)
    to_end = hop(block, OUTWARD)
    far_middle = hop(to_middle, ACROSS)
    far_end = hop(swap_middle, OUTWARD)
    last_end = hop(far_middle, OUTWARD)
    arrivals = (
        (block, (0, 1, 2, 3)),
        (jnp.where(middle, to_middle, to_end), (1, 0, 3, 2)),
        (jnp.where(middle, swap_middle, far_end), (2, 2, 1, 1)),
        (jnp.where(middle, far_middle, last_end), (3, 3, 0, 0)),
    )
    total = jnp.zeros((block.shape[0], out_weight.shape[0]), jnp.float32)
    for array, table in arrivals:
        source = 2 * of_chip(chip, table)
        other = swapped(array, "tp", 1)
        for part, at in ((array, source + core), (other, source + 1 - core)):
            total = total + jnp.einsum(
                "tk,ck->tc",
                part,
                columns(out_weight, at, width),
                preferred_element_type=jnp.float32,
            )
    return total


def scattered_product(data, out_weight, width):
    place = lax.axis_index("tp")
    chip, core = place // 2, place % 2

    def share(table):
        source = 2 * of_chip(chip, table)
        given = jnp.dot(
            data,
            columns(out_weight, source + 1 - core, width),
            preferred_element_type=jnp.float32,
        ).astype(jnp.bfloat16)
        kept = jnp.dot(
            data, columns(out_weight, source + core, width), preferred_element_type=jnp.float32
        )
        return kept + wide(swapped(given, "tp", 1))

    def short(array):
        return array.astype(jnp.bfloat16)

    first = share((3, 3, 0, 0))
    one = hop(short(first), INWARD)
    second = share((2, 2, 1, 1))
    two_a = hop(short(first + wide(one)), ACROSS)
    two_b = hop(short(second), INWARD)
    third = share((1, 0, 3, 2))
    three_a = hop(short(third + wide(two_a)), OUTWARD)
    three_b = hop(short(second + wide(two_b)), ACROSS)
    three_c = hop(short(third), INWARD)
    own = share((0, 1, 2, 3))
    return short(own + wide(three_a) + wide(three_b) + wide(three_c))


def local(query_gate, key_gate, value_input, filter_taps, out_weight, out_grad):
    length, channels = query_gate.shape
    groups = filter_taps.shape[1]
    per_group = channels // groups
    members = lax.axis_size("ctx")
    position = lax.axis_index("ctx")
    at = position.reshape((1,)).astype(jnp.int32)
    tap_scale = 1.0 / math.sqrt(length * members)

    in_line = lax.axis_size("tp") == 8
    if in_line:
        dgated = gathered_product(out_grad, out_weight).astype(jnp.bfloat16)
    else:
        dgated = jnp.einsum(
            "tk,ck->tc",
            lax.all_gather(out_grad, "tp", axis=1, tiled=True),
            out_weight,
            preferred_element_type=jnp.float32,
        ).astype(jnp.bfloat16)
    tap_rows = (filter_taps * tap_scale).astype(jnp.bfloat16).T
    tap_parts = [wide(p) for p in traded(cut(tap_rows, position, members, 0), "ctx")]
    product_in = (wide(key_gate) * wide(value_input)).astype(jnp.bfloat16)
    input_parts = traded(cut(product_in, position, members, 1), "ctx")
    conv_parts = traded(convolve(at, input_parts, tap_parts, per_group), "ctx")
    convolved = joined(conv_parts, position, 1)
    gated_out = (wide(query_gate) * wide(convolved)).astype(jnp.bfloat16)
    if in_line:
        projected = scattered_product(gated_out, out_weight, channels)
    else:
        partial_value = jnp.dot(gated_out, out_weight, preferred_element_type=jnp.float32)
        projected = lax.psum_scatter(
            partial_value.astype(jnp.bfloat16), "tp", scatter_dimension=1, tiled=True
        )
    grad_query = (wide(dgated) * wide(convolved)).astype(jnp.bfloat16)
    conv_grad = (wide(dgated) * wide(query_gate)).astype(jnp.bfloat16)
    grad_parts = traded(cut(conv_grad, position, members, 1), "ctx")
    back_parts, filter_parts = correlate(
        at, input_parts, grad_parts, tap_parts, per_group, tap_scale
    )
    input_grad = wide(joined(traded(back_parts, "ctx"), position, 1))
    grad_filter = joined(traded(filter_parts, "ctx"), position, 0).T
    grad_key = (input_grad * wide(value_input)).astype(jnp.bfloat16)
    grad_value = (input_grad * wide(key_gate)).astype(jnp.bfloat16)
    return (projected, grad_query, grad_key, grad_value, grad_filter)


def solution(mesh):
    both = P("ctx", "tp")
    return jax.shard_map(
        local,
        mesh=mesh,
        in_specs=(both, both, both, both, P("tp", None), both),
        out_specs=(both,) * 5,
        check_vma=False,
    )
```

```python
import functools
import math
import jax
import jax.numpy as jnp
from jax import lax
from jax.experimental import pallas as pl
from jax.experimental.pallas import tpu as pltpu
from jax.sharding import PartitionSpec as P

BLOCK = 128
NT = (((1,), (1,)), ((), ()))
COST = pl.CostEstimate(flops=2**20, bytes_accessed=2**12, transcendentals=0)


def lag_matrix(row, length):
    lanes = lax.broadcasted_iota(jnp.int32, (BLOCK, length), 1)
    rows = lax.broadcasted_iota(jnp.int32, (BLOCK, length), 0)
    spread = pltpu.roll(
        jnp.broadcast_to(row, (BLOCK, length)), 0, axis=1, stride=1, stride_axis=0
    )
    return jnp.where(lanes >= rows, spread, 0.0).astype(jnp.bfloat16)


def stacked(ref, start, rows, members, width):
    pieces = []
    for member in range(members):
        part = ref[member, pl.ds(start, rows), :]
        for at in range(0, width, BLOCK):
            pieces.append(part[:, at : at + BLOCK])
    return jnp.concatenate(pieces, axis=0)


def spread_out(ref, start, rows, value, members, width):
    per_member = width // BLOCK
    for member in range(members):
        base = member * per_member * rows
        parts = [value[base + i * rows : base + (i + 1) * rows] for i in range(per_member)]
        ref[member, pl.ds(start, rows), :] = jnp.concatenate(parts, axis=1)


def forward_kernel(members, per_group, pos_ref, *refs):
    inputs, taps = refs[:members], refs[members : 2 * members]
    outputs = refs[2 * members : 3 * members]
    tap_scr, in_scr, out_scr = refs[3 * members :]
    position = pos_ref[0]
    width, channels = inputs[0].shape
    groups = taps[0].shape[0]
    length = members * width
    blocks = length // BLOCK
    for step in range(members):
        at = position ^ step
        in_scr[at] = inputs[step][...].T
        tap_scr[:, pl.ds(pl.multiple_of(at * width, width), width)] = taps[step][...]

    def one_group(group, carry):
        start = pl.multiple_of(group * per_group, per_group)
        lags = lag_matrix(tap_scr[pl.ds(group, 1), :], length)
        data = stacked(in_scr, start, per_group, members, width)
        total = [jnp.zeros((per_group, BLOCK), jnp.float32) for _ in range(blocks)]
        for offset in range(0, blocks, 2):
            rows = (blocks - offset) * per_group
            result = jnp.dot(
                data[:rows],
                lags[:, offset * BLOCK : (offset + 2) * BLOCK],
                preferred_element_type=jnp.float32,
            )
            for side in range(2):
                for source in range(blocks - offset - side):
                    total[source + offset + side] += result[
                        source * per_group : (source + 1) * per_group,
                        side * BLOCK : (side + 1) * BLOCK,
                    ]
        value = jnp.concatenate(total, axis=0).astype(jnp.bfloat16)
        spread_out(out_scr, start, per_group, value, members, width)
        return carry

    lax.fori_loop(0, groups, one_group, 0)
    for step in range(members):
        outputs[step][...] = out_scr[position ^ step].T


def backward_kernel(members, per_group, scale, pos_ref, *refs):
    inputs, cotangents, taps = (
        refs[:members],
        refs[members : 2 * members],
        refs[2 * members : 3 * members],
    )
    outputs = refs[3 * members : 4 * members]
    tap_grads = refs[4 * members : 5 * members]
    tap_scr, in_scr, cot_scr, out_scr, grad_scr, pad_scr = refs[5 * members :]
    position = pos_ref[0]
    width, channels = inputs[0].shape
    groups = taps[0].shape[0]
    length = members * width
    blocks = length // BLOCK
    depth = blocks * per_group
    for step in range(members):
        at = position ^ step
        in_scr[at] = inputs[step][...].T
        cot_scr[at] = cotangents[step][...].T
        tap_scr[:, pl.ds(pl.multiple_of(at * width, width), width)] = taps[step][...]
    pad_scr[...] = jnp.zeros_like(pad_scr)
    rows_of = lax.broadcasted_iota(jnp.int32, (BLOCK, BLOCK), 0)
    lanes_of = lax.broadcasted_iota(jnp.int32, (BLOCK, BLOCK), 1)
    mirror = (rows_of + lanes_of == BLOCK - 1).astype(jnp.bfloat16)

    def one_group(group, carry):
        start = pl.multiple_of(group * per_group, per_group)
        lags = lag_matrix(tap_scr[pl.ds(group, 1), :], length)
        data = stacked(in_scr, start, per_group, members, width)
        cot = stacked(cot_scr, start, per_group, members, width)
        pad_scr[:depth, :BLOCK] = cot
        pad_scr[: depth - per_group, BLOCK:] = cot[per_group:]
        flipped = lax.dot_general(
            mirror, data, NT, preferred_element_type=jnp.float32
        ).astype(jnp.bfloat16)
        total = jnp.zeros((depth, BLOCK), jnp.float32)
        products = []
        for offset in range(0, blocks, 2):
            rows = depth - offset * per_group
            pair = pad_scr[offset * per_group : offset * per_group + depth, :]
            result = lax.dot_general(
                pair[:rows],
                lags[:, offset * BLOCK : (offset + 2) * BLOCK],
                NT,
                preferred_element_type=jnp.float32,
            )
            if rows < depth:
                result = jnp.concatenate(
                    [result, jnp.zeros((depth - rows, BLOCK), jnp.float32)], axis=0
                )
            total = total + result
            products.append(jnp.dot(flipped, pair, preferred_element_type=jnp.float32))
        spread_out(
            out_scr, start, per_group, total.astype(jnp.bfloat16), members, width
        )
        product = jnp.concatenate(products, axis=1)
        lanes = lax.broadcasted_iota(jnp.int32, (BLOCK, length), 1)
        back = BLOCK - 1 - lax.broadcasted_iota(jnp.int32, (BLOCK, length), 0)
        product = jnp.where(lanes >= back, product, 0.0)
        product = pltpu.roll(
            product, length - (BLOCK - 1), axis=1, stride=1, stride_axis=0
        )
        grad_scr[pl.ds(group, 1), :] = jnp.sum(product, axis=0, keepdims=True) * scale
        return carry

    lax.fori_loop(0, groups, one_group, 0)
    for step in range(members):
        at = position ^ step
        outputs[step][...] = out_scr[at].T
        tap_grads[step][...] = grad_scr[:, pl.ds(pl.multiple_of(at * width, width), width)]


VMEM = pl.BlockSpec(memory_space=pltpu.VMEM)
SMEM = pl.BlockSpec(memory_space=pltpu.SMEM)


def convolve(position, inputs, taps, per_group):
    members = len(inputs)
    width, channels = inputs[0].shape
    groups = taps[0].shape[0]
    length = members * width
    return pl.pallas_call(
        functools.partial(forward_kernel, members, per_group),
        out_shape=[jax.ShapeDtypeStruct((width, channels), jnp.bfloat16)] * members,
        in_specs=[SMEM] + [VMEM] * (2 * members),
        out_specs=[VMEM] * members,
        scratch_shapes=[
            pltpu.VMEM((groups, length), jnp.float32),
            pltpu.VMEM((members, channels, width), jnp.bfloat16),
            pltpu.VMEM((members, channels, width), jnp.bfloat16),
        ],
        compiler_params=pltpu.CompilerParams(vmem_limit_bytes=32 * 2**20),
        cost_estimate=COST,
        name="causal_conv",
    )(position, *inputs, *taps)


def correlate(position, inputs, cotangents, taps, per_group, scale):
    members = len(inputs)
    width, channels = inputs[0].shape
    groups = taps[0].shape[0]
    length = members * width
    results = pl.pallas_call(
        functools.partial(backward_kernel, members, per_group, scale),
        out_shape=[jax.ShapeDtypeStruct((width, channels), jnp.bfloat16)] * members
        + [jax.ShapeDtypeStruct((groups, width), jnp.float32)] * members,
        in_specs=[SMEM] + [VMEM] * (3 * members),
        out_specs=[VMEM] * (2 * members),
        scratch_shapes=[
            pltpu.VMEM((groups, length), jnp.float32),
            pltpu.VMEM((members, channels, width), jnp.bfloat16),
            pltpu.VMEM((members, channels, width), jnp.bfloat16),
            pltpu.VMEM((members, channels, width), jnp.bfloat16),
            pltpu.VMEM((groups, length), jnp.float32),
            pltpu.VMEM((2 * length // BLOCK * per_group, 2 * BLOCK), jnp.bfloat16),
        ],
        compiler_params=pltpu.CompilerParams(vmem_limit_bytes=32 * 2**20),
        cost_estimate=COST,
        name="causal_conv_grads",
    )(position, *inputs, *cotangents, *taps)
    return results[:members], results[members:]


def swapped(array, axis, step):
    size = lax.axis_size(axis)
    return lax.ppermute(array, axis, [(i, i ^ step) for i in range(size)])


def traded(pieces, axis):
    return [pieces[0]] + [swapped(pieces[step], axis, step) for step in range(1, len(pieces))]


def cut(array, position, members, axis):
    width = array.shape[axis] // members
    return [
        lax.dynamic_slice_in_dim(array, (position ^ step) * width, width, axis)
        for step in range(members)
    ]


def joined(pieces, position, axis):
    members = len(pieces)
    width = pieces[0].shape[axis]
    shape = list(pieces[0].shape)
    shape[axis] = members * width
    whole = jnp.zeros(shape, pieces[0].dtype)
    for step in range(members):
        whole = lax.dynamic_update_slice_in_dim(
            whole, pieces[step], (position ^ step) * width, axis
        )
    return whole


def wide(array):
    return array.astype(jnp.float32)


def hop(array, pairs):
    return lax.ppermute(
        array, "tp", [(2 * i + core, 2 * j + core) for i, j in pairs for core in range(2)]
    )


INWARD = ((0, 1), (3, 2))
ACROSS = ((1, 2), (2, 1))
OUTWARD = ((1, 0), (2, 3))


def of_chip(chip, table):
    return jnp.where(
        chip == 0, table[0], jnp.where(chip == 1, table[1], jnp.where(chip == 2, table[2], table[3]))
    )


def pass_kernel(*refs):
    del refs


def held_until(value, after):
    return pl.pallas_call(
        pass_kernel,
        out_shape=jax.ShapeDtypeStruct(value.shape, value.dtype),
        in_specs=[pl.BlockSpec(memory_space=pl.ANY)] * (1 + len(after)),
        out_specs=pl.BlockSpec(memory_space=pl.ANY),
        input_output_aliases={0: 0},
        name="held",
    )(value, *after)


def column_kernel(_, data_ref, weight_ref, *refs):
    out_ref = refs[-1]
    out_ref[...] = jnp.dot(
        data_ref[...], weight_ref[...], preferred_element_type=jnp.float32
    ).astype(jnp.bfloat16)


def column_sum_kernel(_, data_ref, weight_ref, more_ref, out_ref):
    product = jnp.dot(data_ref[...], weight_ref[...], preferred_element_type=jnp.float32)
    out_ref[...] = (product + wide(more_ref[...])).astype(jnp.bfloat16)


def column_product(data, out_weight, block, width, more=(), after=()):
    rows, depth = data.shape
    tile = min(width, 256)
    tiles = width // tile
    column = pl.BlockSpec((rows, tile), lambda i, at: (0, i))
    return pl.pallas_call(
        column_sum_kernel if more else column_kernel,
        out_shape=jax.ShapeDtypeStruct((rows, width), jnp.bfloat16),
        grid_spec=pltpu.PrefetchScalarGridSpec(
            num_scalar_prefetch=1,
            grid=(tiles,),
            in_specs=[
                pl.BlockSpec((rows, depth), lambda i, at: (0, 0)),
                pl.BlockSpec((depth, tile), lambda i, at: (0, at[0] * tiles + i)),
            ]
            + [column] * len(more)
            + [pl.BlockSpec(memory_space=pl.ANY)] * len(after),
            out_specs=column,
        ),
        compiler_params=pltpu.CompilerParams(vmem_limit_bytes=50 * 2**20),
        cost_estimate=COST,
        name="projection_block",
    )(block.reshape((1,)).astype(jnp.int32), data, out_weight, *more, *after)


def first_half_kernel(_, data_ref, weight_ref, out_ref):
    product = lax.dot_general(
        data_ref[0], weight_ref[...], NT, preferred_element_type=jnp.float32
    )

    @pl.when(pl.program_id(0) == 0)
    def _():
        out_ref[...] = product

    @pl.when(pl.program_id(0) > 0)
    def _():
        out_ref[...] += product


def second_half_kernel(
    _, data_ref, weight_ref, start_ref, conv_ref, query_ref, grad_ref, cot_ref, total
):
    product = lax.dot_general(
        data_ref[0], weight_ref[...], NT, preferred_element_type=jnp.float32
    )

    @pl.when(pl.program_id(0) == 0)
    def _():
        total[...] = start_ref[...] + product

    @pl.when(pl.program_id(0) > 0)
    def _():
        total[...] += product

    @pl.when(pl.program_id(0) == pl.num_programs(0) - 1)
    def _():
        dgated = wide(total[...].astype(jnp.bfloat16))
        grad_ref[...] = (dgated * wide(conv_ref[...])).astype(jnp.bfloat16)
        cot_ref[...] = (dgated * wide(query_ref[...])).astype(jnp.bfloat16)


def cotangent_product(parity, blocks, out_weight, rest=None):
    chips, rows, width = blocks.shape
    channels = out_weight.shape[0]
    whole = pl.BlockSpec((rows, channels), lambda i, at: (0, 0))
    array = jax.ShapeDtypeStruct((rows, channels), jnp.bfloat16)
    return pl.pallas_call(
        first_half_kernel if rest is None else second_half_kernel,
        out_shape=jax.ShapeDtypeStruct((rows, channels), jnp.float32)
        if rest is None
        else [array, array],
        grid_spec=pltpu.PrefetchScalarGridSpec(
            num_scalar_prefetch=1,
            grid=(chips,),
            in_specs=[
                pl.BlockSpec((1, rows, width), lambda i, at: (i, 0, 0)),
                pl.BlockSpec((channels, width), lambda i, at: (0, 2 * i + at[0])),
            ]
            + ([] if rest is None else [whole] * 3),
            out_specs=whole if rest is None else [whole, whole],
            scratch_shapes=[]
            if rest is None
            else [pltpu.VMEM((rows, channels), jnp.float32)],
        ),
        compiler_params=pltpu.CompilerParams(vmem_limit_bytes=50 * 2**20),
        cost_estimate=COST,
        name="cotangent_half",
    )(
        parity.reshape((1,)).astype(jnp.int32),
        blocks,
        out_weight,
        *(() if rest is None else rest),
    )


def scattered_product(data, out_weight, width):
    place = lax.axis_index("tp")
    chip, core = place // 2, place % 2

    def given(table, after=()):
        source = 2 * of_chip(chip, table)
        return column_product(data, out_weight, source + 1 - core, width, after=after)

    def kept(table, other):
        source = 2 * of_chip(chip, table)
        more = (swapped(other, "tp", 1),)
        return column_product(data, out_weight, source + core, width, more)

    def added(*arrays):
        return sum(wide(array) for array in arrays).astype(jnp.bfloat16)

    tables = ((3, 3, 0, 0), (2, 2, 1, 1), (1, 0, 3, 2), (0, 1, 2, 3))
    for_first, for_second = given(tables[0]), given(tables[1])
    first, second = kept(tables[0], for_first), kept(tables[1], for_second)
    third = kept(tables[2], given(tables[2], (first,)))
    own = kept(tables[3], given(tables[3], (first,)))
    one = hop(first, INWARD)
    two_b = hop(second, INWARD)
    two_a = hop(added(first, one), ACROSS)

    def rest(after):
        three_b = hop(added(second, held_until(two_b, after)), ACROSS)
        three_a = hop(added(third, held_until(two_a, after)), OUTWARD + INWARD)
        return added(own, three_a, three_b)

    return rest, (one, second, third, own)


def local(query_gate, key_gate, value_input, filter_taps, out_weight, out_grad):
    length, channels = query_gate.shape
    groups = filter_taps.shape[1]
    per_group = channels // groups
    members = lax.axis_size("ctx")
    position = lax.axis_index("ctx")
    at = position.reshape((1,)).astype(jnp.int32)
    tap_scale = 1.0 / math.sqrt(length * members)

    place = lax.axis_index("tp")
    devices = lax.axis_size("tp")
    core = place % 2
    lines = [list(range(parity, devices, 2)) for parity in range(2)]
    cotangents = lax.all_gather(out_grad, "tp", axis_index_groups=lines)
    tap_rows = (filter_taps * tap_scale).astype(jnp.bfloat16).T
    tap_parts = [wide(p) for p in traded(cut(tap_rows, position, members, 0), "ctx")]
    product_in = (wide(key_gate) * wide(value_input)).astype(jnp.bfloat16)
    input_parts = traded(cut(product_in, position, members, 1), "ctx")
    conv_parts = traded(convolve(at, input_parts, tap_parts, per_group), "ctx")
    convolved = joined(conv_parts, position, 1)
    gated_out = (wide(query_gate) * wide(convolved)).astype(jnp.bfloat16)
    if devices == 8:
        finish, after = scattered_product(gated_out, out_weight, channels)
    else:
        partial_value = jnp.dot(gated_out, out_weight, preferred_element_type=jnp.float32)
        projected = lax.psum_scatter(
            partial_value.astype(jnp.bfloat16), "tp", scatter_dimension=1, tiled=True
        )
        after = (gated_out,)
    cotangents = held_until(cotangents, after)
    half = cotangent_product(core, cotangents, out_weight)
    grad_query, conv_grad = cotangent_product(
        1 - core,
        swapped(cotangents, "tp", 1),
        out_weight,
        rest=(half, convolved, query_gate),
    )
    if devices == 8:
        projected = finish((conv_grad,))
    grad_parts = traded(cut(conv_grad, position, members, 1), "ctx")
    back_parts, filter_parts = correlate(
        at, input_parts, grad_parts, tap_parts, per_group, tap_scale
    )
    input_grad = wide(joined(traded(back_parts, "ctx"), position, 1))
    grad_filter = joined(traded(filter_parts, "ctx"), position, 0).T
    grad_key = (input_grad * wide(value_input)).astype(jnp.bfloat16)
    grad_value = (input_grad * wide(key_gate)).astype(jnp.bfloat16)
    return (projected, grad_query, grad_key, grad_value, grad_filter)


def solution(mesh):
    both = P("ctx", "tp")
    return jax.shard_map(
        local,
        mesh=mesh,
        in_specs=(both, both, both, both, P("tp", None), both),
        out_specs=(both,) * 5,
        check_vma=False,
    )
```

```python
import functools
import math
import jax
import jax.numpy as jnp
from jax import lax
from jax.experimental import pallas as pl
from jax.experimental.pallas import tpu as pltpu
from jax.sharding import PartitionSpec as P

BLOCK = 128
NT = (((1,), (1,)), ((), ()))
COST = pl.CostEstimate(flops=2**20, bytes_accessed=2**12, transcendentals=0)


def lag_matrix(row, length):
    lanes = lax.broadcasted_iota(jnp.int32, (BLOCK, length), 1)
    rows = lax.broadcasted_iota(jnp.int32, (BLOCK, length), 0)
    spread = pltpu.roll(
        jnp.broadcast_to(row, (BLOCK, length)), 0, axis=1, stride=1, stride_axis=0
    )
    return jnp.where(lanes >= rows, spread, 0.0).astype(jnp.bfloat16)


def stacked(ref, start, rows, members, width):
    pieces = []
    for member in range(members):
        part = ref[member, pl.ds(start, rows), :]
        for at in range(0, width, BLOCK):
            pieces.append(part[:, at : at + BLOCK])
    return jnp.concatenate(pieces, axis=0)


def spread_out(ref, start, rows, value, members, width):
    per_member = width // BLOCK
    for member in range(members):
        base = member * per_member * rows
        parts = [value[base + i * rows : base + (i + 1) * rows] for i in range(per_member)]
        ref[member, pl.ds(start, rows), :] = jnp.concatenate(parts, axis=1)


def padded(groups):
    return -(-groups // 16) * 16


def load_taps(tap_scr, packed, at, width):
    groups, channels = tap_scr.shape[0], packed.shape[1]
    rows = padded(groups)
    parts = [
        packed[width + chunk * rows : width + (chunk + 1) * rows, :].astype(jnp.float32)
        for chunk in range(width // channels)
    ]
    start = pl.multiple_of(at * width, width)
    tap_scr[:, pl.ds(start, width)] = jnp.concatenate(parts, axis=1)[:groups]


def forward_kernel(members, per_group, width, pos_ref, *refs):
    inputs, outputs = refs[:members], refs[-members - 3 : -3]
    tap_scr, in_scr, out_scr = refs[-3:]
    position = pos_ref[0]
    channels = inputs[0].shape[1]
    groups = channels // per_group
    length = members * width
    blocks = length // BLOCK
    for step in range(members):
        at = position ^ step
        in_scr[at] = inputs[step][:width].T
        load_taps(tap_scr, inputs[step], at, width)

    def one_group(group, carry):
        start = pl.multiple_of(group * per_group, per_group)
        lags = lag_matrix(tap_scr[pl.ds(group, 1), :], length)
        data = stacked(in_scr, start, per_group, members, width)
        total = [jnp.zeros((per_group, BLOCK), jnp.float32) for _ in range(blocks)]
        for offset in range(0, blocks, 2):
            rows = (blocks - offset) * per_group
            result = jnp.dot(
                data[:rows],
                lags[:, offset * BLOCK : (offset + 2) * BLOCK],
                preferred_element_type=jnp.float32,
            )
            for side in range(2):
                for source in range(blocks - offset - side):
                    total[source + offset + side] += result[
                        source * per_group : (source + 1) * per_group,
                        side * BLOCK : (side + 1) * BLOCK,
                    ]
        value = jnp.concatenate(total, axis=0).astype(jnp.bfloat16)
        spread_out(out_scr, start, per_group, value, members, width)
        return carry

    lax.fori_loop(0, groups, one_group, 0)
    for step in range(members):
        outputs[step][...] = out_scr[position ^ step].T


def backward_kernel(members, per_group, scale, width, pos_ref, *refs):
    inputs, cotangents = refs[:members], refs[members : 2 * members]
    outputs = refs[-members - 6 : -6]
    tap_scr, in_scr, cot_scr, out_scr, grad_scr, pad_scr = refs[-6:]
    position = pos_ref[0]
    channels = inputs[0].shape[1]
    groups = channels // per_group
    length = members * width
    blocks = length // BLOCK
    depth = blocks * per_group
    for step in range(members):
        at = position ^ step
        in_scr[at] = inputs[step][:width].T
        cot_scr[at] = cotangents[step][...].T
        load_taps(tap_scr, inputs[step], at, width)
    pad_scr[...] = jnp.zeros_like(pad_scr)
    rows_of = lax.broadcasted_iota(jnp.int32, (BLOCK, BLOCK), 0)
    lanes_of = lax.broadcasted_iota(jnp.int32, (BLOCK, BLOCK), 1)
    mirror = (rows_of + lanes_of == BLOCK - 1).astype(jnp.bfloat16)

    def one_group(group, carry):
        start = pl.multiple_of(group * per_group, per_group)
        lags = lag_matrix(tap_scr[pl.ds(group, 1), :], length)
        data = stacked(in_scr, start, per_group, members, width)
        cot = stacked(cot_scr, start, per_group, members, width)
        pad_scr[:depth, :BLOCK] = cot
        pad_scr[: depth - per_group, BLOCK:] = cot[per_group:]
        flipped = lax.dot_general(
            mirror, data, NT, preferred_element_type=jnp.float32
        ).astype(jnp.bfloat16)
        total = jnp.zeros((depth, BLOCK), jnp.float32)
        products = []
        for offset in range(0, blocks, 2):
            rows = depth - offset * per_group
            pair = pad_scr[offset * per_group : offset * per_group + depth, :]
            result = lax.dot_general(
                pair[:rows],
                lags[:, offset * BLOCK : (offset + 2) * BLOCK],
                NT,
                preferred_element_type=jnp.float32,
            )
            if rows < depth:
                result = jnp.concatenate(
                    [result, jnp.zeros((depth - rows, BLOCK), jnp.float32)], axis=0
                )
            total = total + result
            products.append(jnp.dot(flipped, pair, preferred_element_type=jnp.float32))
        spread_out(
            out_scr, start, per_group, total.astype(jnp.bfloat16), members, width
        )
        product = jnp.concatenate(products, axis=1)
        lanes = lax.broadcasted_iota(jnp.int32, (BLOCK, length), 1)
        back = BLOCK - 1 - lax.broadcasted_iota(jnp.int32, (BLOCK, length), 0)
        product = jnp.where(lanes >= back, product, 0.0)
        product = pltpu.roll(
            product, length - (BLOCK - 1), axis=1, stride=1, stride_axis=0
        )
        grad_scr[pl.ds(group, 1), :] = jnp.sum(product, axis=0, keepdims=True) * scale
        return carry

    lax.fori_loop(0, groups, one_group, 0)
    for step in range(members):
        at = position ^ step
        outputs[step][:width] = out_scr[at].T
        rows = padded(groups)
        whole = grad_scr[:, pl.ds(pl.multiple_of(at * width, width), width)].astype(jnp.bfloat16)
        if rows > groups:
            blank = jnp.zeros((rows - groups, width), jnp.bfloat16)
            whole = jnp.concatenate([whole, blank], axis=0)
        for chunk in range(width // channels):
            outputs[step][width + chunk * rows : width + (chunk + 1) * rows, :] = whole[
                :, chunk * channels : (chunk + 1) * channels
            ]


VMEM = pl.BlockSpec(memory_space=pltpu.VMEM)
ANYWHERE = pl.BlockSpec(memory_space=pl.ANY)
SMEM = pl.BlockSpec(memory_space=pltpu.SMEM)


def convolve(position, inputs, width, per_group, after=()):
    members = len(inputs)
    channels = inputs[0].shape[1]
    length = members * width
    return pl.pallas_call(
        functools.partial(forward_kernel, members, per_group, width),
        out_shape=[jax.ShapeDtypeStruct((width, channels), jnp.bfloat16)] * members,
        in_specs=[SMEM] + [VMEM] * members + [ANYWHERE] * len(after),
        out_specs=[VMEM] * members,
        scratch_shapes=[
            pltpu.VMEM((channels // per_group, length), jnp.float32),
            pltpu.VMEM((members, channels, width), jnp.bfloat16),
            pltpu.VMEM((members, channels, width), jnp.bfloat16),
        ],
        compiler_params=pltpu.CompilerParams(vmem_limit_bytes=24 * 2**20),
        cost_estimate=COST,
        name="causal_conv",
    )(position, *inputs, *after)


def correlate(position, inputs, cotangents, per_group, scale, after=()):
    members = len(inputs)
    width, channels = cotangents[0].shape
    length = members * width
    groups = channels // per_group
    return pl.pallas_call(
        functools.partial(backward_kernel, members, per_group, scale, width),
        out_shape=[jax.ShapeDtypeStruct(inputs[0].shape, jnp.bfloat16)] * members,
        in_specs=[SMEM] + [VMEM] * (2 * members) + [ANYWHERE] * len(after),
        out_specs=[VMEM] * members,
        scratch_shapes=[
            pltpu.VMEM((groups, length), jnp.float32),
            pltpu.VMEM((members, channels, width), jnp.bfloat16),
            pltpu.VMEM((members, channels, width), jnp.bfloat16),
            pltpu.VMEM((members, channels, width), jnp.bfloat16),
            pltpu.VMEM((groups, length), jnp.float32),
            pltpu.VMEM((2 * length // BLOCK * per_group, 2 * BLOCK), jnp.bfloat16),
        ],
        compiler_params=pltpu.CompilerParams(vmem_limit_bytes=24 * 2**20),
        cost_estimate=COST,
        name="causal_conv_grads",
    )(position, *inputs, *cotangents, *after)


def prepare_kernel(members, scale, pos_ref, key_ref, value_ref, taps_ref, *refs):
    outputs = refs
    position = pos_ref[0]
    width, channels = key_ref.shape
    share = channels // members
    groups = taps_ref.shape[0] // members
    for step in range(members):
        at = position ^ step
        columns = pl.ds(pl.multiple_of(at * share, share), share)
        product = key_ref[:, columns].astype(jnp.float32) * value_ref[:, columns].astype(
            jnp.float32
        )
        outputs[step][:width] = product.astype(jnp.bfloat16)
        taps = taps_ref[pl.ds(pl.multiple_of(at * groups, groups), groups), :]
        taps = (taps * scale).astype(jnp.bfloat16)
        for chunk in range(width // share):
            outputs[step][width + chunk * groups : width + (chunk + 1) * groups, :] = taps[
                :, chunk * share : (chunk + 1) * share
            ]


def prepare(position, key_gate, value_input, filter_taps, members, scale):
    width, channels = key_gate.shape
    share = channels // members
    rows = width + filter_taps.size // members // share
    return pl.pallas_call(
        functools.partial(prepare_kernel, members, scale),
        out_shape=[jax.ShapeDtypeStruct((rows, share), jnp.bfloat16)] * members,
        in_specs=[SMEM] + [VMEM] * 3,
        out_specs=[VMEM] * members,
        compiler_params=pltpu.CompilerParams(vmem_limit_bytes=24 * 2**20),
        cost_estimate=COST,
        name="gated_input",
    )(position, key_gate, value_input, filter_taps.T)


def finish_kernel(members, pos_ref, *refs):
    parts = refs[:members]
    key_ref, value_ref, key_out, value_out, taps_out = refs[members:]
    position = pos_ref[0]
    width, channels = key_ref.shape
    share = channels // members
    groups = taps_out.shape[0] // members
    for step in range(members):
        at = position ^ step
        columns = pl.ds(pl.multiple_of(at * share, share), share)
        grad = parts[step][:width].astype(jnp.float32)
        key_out[:, columns] = (grad * value_ref[:, columns].astype(jnp.float32)).astype(
            jnp.bfloat16
        )
        value_out[:, columns] = (grad * key_ref[:, columns].astype(jnp.float32)).astype(
            jnp.bfloat16
        )
        taps = [
            parts[step][width + chunk * groups : width + (chunk + 1) * groups, :]
            for chunk in range(width // share)
        ]
        taps_out[pl.ds(pl.multiple_of(at * groups, groups), groups), :] = jnp.concatenate(
            taps, axis=1
        ).astype(jnp.float32)


def finished(position, parts, key_gate, value_input, groups):
    members = len(parts)
    width, channels = key_gate.shape
    array = jax.ShapeDtypeStruct((width, channels), jnp.bfloat16)
    grad_key, grad_value, taps = pl.pallas_call(
        functools.partial(finish_kernel, members),
        out_shape=[array, array, jax.ShapeDtypeStruct((groups, width), jnp.float32)],
        in_specs=[SMEM] + [VMEM] * (members + 2),
        out_specs=[VMEM] * 3,
        compiler_params=pltpu.CompilerParams(vmem_limit_bytes=24 * 2**20),
        cost_estimate=COST,
        name="input_gradients",
    )(position, *parts, key_gate, value_input)
    return grad_key, grad_value, taps.T


def swapped(array, axis, step):
    size = lax.axis_size(axis)
    return lax.ppermute(array, axis, [(i, i ^ step) for i in range(size)])


def traded(pieces, axis):
    return [pieces[0]] + [swapped(pieces[step], axis, step) for step in range(1, len(pieces))]


def cut(array, position, members, axis):
    width = array.shape[axis] // members
    return [
        lax.dynamic_slice_in_dim(array, (position ^ step) * width, width, axis)
        for step in range(members)
    ]


def joined(pieces, position, axis):
    members = len(pieces)
    width = pieces[0].shape[axis]
    shape = list(pieces[0].shape)
    shape[axis] = members * width
    whole = jnp.zeros(shape, pieces[0].dtype)
    for step in range(members):
        whole = lax.dynamic_update_slice_in_dim(
            whole, pieces[step], (position ^ step) * width, axis
        )
    return whole


def wide(array):
    return array.astype(jnp.float32)


def hop(array, pairs):
    return lax.ppermute(
        array, "tp", [(2 * i + core, 2 * j + core) for i, j in pairs for core in range(2)]
    )


INWARD = ((0, 1), (3, 2))
ACROSS = ((1, 2), (2, 1))
OUTWARD = ((1, 0), (2, 3))


def of_chip(chip, table):
    return jnp.where(
        chip == 0, table[0], jnp.where(chip == 1, table[1], jnp.where(chip == 2, table[2], table[3]))
    )


def pass_kernel(*refs):
    del refs


def in_hbm(array):
    return pltpu.with_memory_space_constraint(array, pltpu.HBM)


def held_until(values, after):
    return pl.pallas_call(
        pass_kernel,
        out_shape=[jax.ShapeDtypeStruct(value.shape, value.dtype) for value in values],
        in_specs=[ANYWHERE] * (len(values) + len(after)),
        out_specs=[ANYWHERE] * len(values),
        input_output_aliases={number: number for number in range(len(values))},
        cost_estimate=COST,
        name="held",
    )(*values, *after)


def given_kernel(_, data_ref, weight_ref, *refs):
    refs[-1][0] = jnp.dot(
        data_ref[...], weight_ref[...], preferred_element_type=jnp.float32
    ).astype(jnp.bfloat16)


def kept_kernel(tiles, count, _, data_ref, weight_ref, more_ref, *refs):
    product = jnp.dot(data_ref[...], weight_ref[...], preferred_element_type=jnp.float32)
    result = (product + wide(more_ref[0])).astype(jnp.bfloat16)
    for number, out_ref in enumerate(refs[-count:]):

        @pl.when(pl.program_id(0) // tiles == number)
        def _(out_ref=out_ref):
            out_ref[...] = result


def column_products(data, out_weight, blocks, width, more=None, after=()):
    rows, depth = data.shape
    tile = min(width, 512)
    tiles = width // tile
    count = len(blocks)
    stack = pl.BlockSpec((1, rows, tile), lambda i, at: (i // tiles, 0, i % tiles))
    array = jax.ShapeDtypeStruct((rows, width), jnp.bfloat16)

    def column(number):
        return pl.BlockSpec(
            (rows, tile), lambda i, at: (0, jnp.clip(i - number * tiles, 0, tiles - 1))
        )

    return pl.pallas_call(
        given_kernel if more is None else functools.partial(kept_kernel, tiles, count),
        out_shape=jax.ShapeDtypeStruct((count, rows, width), jnp.bfloat16)
        if more is None
        else [array] * count,
        grid_spec=pltpu.PrefetchScalarGridSpec(
            num_scalar_prefetch=1,
            grid=(count * tiles,),
            in_specs=[
                pl.BlockSpec((rows, depth), lambda i, at: (0, 0)),
                pl.BlockSpec((depth, tile), lambda i, at: (0, at[i // tiles] * tiles + i % tiles)),
            ]
            + ([] if more is None else [stack])
            + [ANYWHERE] * len(after),
            out_specs=stack if more is None else [column(number) for number in range(count)],
        ),
        compiler_params=pltpu.CompilerParams(vmem_limit_bytes=24 * 2**20),
        cost_estimate=COST,
        name="projection_blocks",
    )(
        jnp.stack(blocks).astype(jnp.int32),
        data,
        in_hbm(out_weight),
        *(() if more is None else (more,)),
        *after,
    )


def cotangent_kernel(count, first, last, _, weight_ref, *refs):
    blocks, refs = refs[:count], refs[count:]
    step = pl.program_id(0)
    total = refs[-1]

    @pl.when(step == 0)
    def _():
        total[...] = jnp.zeros_like(total) if first else refs[0][...]

    for number, block in enumerate(blocks):

        @pl.when(step == number)
        def _(block=block):
            total[...] += lax.dot_general(
                block[...], weight_ref[...], NT, preferred_element_type=jnp.float32
            )

    if last:
        conv_ref, query_ref = refs[1:3]
        grad_ref, cot_ref = refs[-3:-1]

        @pl.when(step == count - 1)
        def _():
            dgated = wide(total[...].astype(jnp.bfloat16))
            grad_ref[...] = (dgated * wide(conv_ref[...])).astype(jnp.bfloat16)
            cot_ref[...] = (dgated * wide(query_ref[...])).astype(jnp.bfloat16)


def cotangent_products(blocks, places, out_weight, start=None, gates=(), after=()):
    rows, width = blocks[0].shape
    channels = out_weight.shape[0]
    count = len(blocks)
    whole = pl.BlockSpec((rows, channels), lambda i, at: (0, 0))
    part = pl.BlockSpec((rows, width), lambda i, at: (0, 0))
    array = jax.ShapeDtypeStruct((rows, channels), jnp.bfloat16)
    first, last = start is None, bool(gates)
    extra = (() if first else (start,)) + tuple(gates)
    return pl.pallas_call(
        functools.partial(cotangent_kernel, count, first, last),
        out_shape=[array, array] if last else jax.ShapeDtypeStruct((rows, channels), jnp.float32),
        grid_spec=pltpu.PrefetchScalarGridSpec(
            num_scalar_prefetch=1,
            grid=(count,),
            in_specs=[pl.BlockSpec((channels, width), lambda i, at: (0, at[i]))]
            + [part] * count
            + [whole] * len(extra)
            + [ANYWHERE] * len(after),
            out_specs=[whole, whole] if last else whole,
            scratch_shapes=[pltpu.VMEM((rows, channels), jnp.float32)] if last else [],
        ),
        compiler_params=pltpu.CompilerParams(vmem_limit_bytes=24 * 2**20),
        cost_estimate=COST,
        name="cotangent_blocks",
    )(jnp.stack(places).astype(jnp.int32), in_hbm(out_weight), *blocks, *extra, *after)


OWN, NEAR, MIDDLE, FAR = (0, 1, 2, 3), (1, 0, 3, 2), (2, 2, 1, 1), (3, 3, 0, 0)


def added(*arrays):
    return sum(wide(array) for array in arrays).astype(jnp.bfloat16)


def line_scatter(data, out_weight, width, before, later):
    place = lax.axis_index("tp")
    chip, core = place // 2, place % 2

    def share(tables, before, later=()):
        sources = [2 * of_chip(chip, table) for table in tables]
        given = column_products(
            data, out_weight, [at + 1 - core for at in sources], width, after=before
        )
        more = swapped(given, "tp", 1)
        return column_products(
            data, out_weight, [at + core for at in sources], width, more, after=later
        )

    (first,) = share((FAR,), before, later)
    one = hop(first, INWARD)
    second, third, own = share((MIDDLE, NEAR, OWN), (first,))
    two_b = hop(second, INWARD)
    through = added(first, one)
    two_a = hop(through, ACROSS)

    def ready(after):
        across, inward = held_until([two_a, two_b], after)
        return added(third, across), added(second, inward)

    def rest(final, onward):
        return added(own, hop(final, OUTWARD + INWARD), hop(onward, ACROSS))

    return own, through, ready, rest


def line_cotangents(block, table, out_weight, start=None, gates=(), after=()):
    place = lax.axis_index("tp")
    core = place % 2
    source = 2 * of_chip(place // 2, table)
    places = (source + core, source + 1 - core)
    parts = (block, swapped(block, "tp", 1))
    return cotangent_products(parts, places, out_weight, start, gates, after)


def packed_parts(position, key_gate, value_input, filter_taps, members, scale):
    length, channels = key_gate.shape
    share = channels // members
    product_in = (wide(key_gate) * wide(value_input)).astype(jnp.bfloat16)
    tap_rows = (filter_taps * scale).astype(jnp.bfloat16).T
    owned = filter_taps.shape[1] // members
    chunks = length // share
    packed = []
    pieces = cut(product_in, position, members, 1)
    for piece, taps in zip(pieces, cut(tap_rows, position, members, 0)):
        taps = taps.reshape(owned, chunks, share).transpose(1, 0, 2)
        taps = jnp.pad(taps, ((0, 0), (0, padded(owned) - owned), (0, 0)))
        packed.append(jnp.concatenate([piece, taps.reshape(-1, share)], axis=0))
    return packed


def unpacked_parts(position, parts, key_gate, value_input, groups):
    length, channels = key_gate.shape
    members = len(parts)
    share = channels // members
    owned = groups // members
    chunks = length // share
    input_grad = wide(joined([part[:length] for part in parts], position, 1))
    filter_parts = [
        part[length:]
        .reshape(chunks, padded(owned), share)[:, :owned]
        .transpose(1, 0, 2)
        .reshape(owned, length)
        for part in parts
    ]
    grad_filter = wide(joined(filter_parts, position, 0)).T
    grad_key = (input_grad * wide(value_input)).astype(jnp.bfloat16)
    grad_value = (input_grad * wide(key_gate)).astype(jnp.bfloat16)
    return grad_key, grad_value, grad_filter


def local(query_gate, key_gate, value_input, filter_taps, out_weight, out_grad):
    length, channels = query_gate.shape
    groups = filter_taps.shape[1]
    per_group = channels // groups
    members = lax.axis_size("ctx")
    position = lax.axis_index("ctx")
    at = position.reshape((1,)).astype(jnp.int32)
    tap_scale = 1.0 / math.sqrt(length * members)
    share = channels // members
    in_line = lax.axis_size("tp") == 8

    if in_line:
        near, cross = hop(out_grad, INWARD + OUTWARD), hop(out_grad, ACROSS)
        total = line_cotangents(out_grad, OWN, out_weight)
    in_tiles = share % 128 == 0 and groups // members % 16 == 0
    if in_tiles:
        packed = prepare(at, key_gate, value_input, filter_taps, members, tap_scale)
    else:
        packed = packed_parts(position, key_gate, value_input, filter_taps, members, tap_scale)
    input_parts = traded(packed, "ctx")
    conv_parts = convolve(at, input_parts, length, per_group, (total,) if in_line else ())
    if in_line:
        *conv_parts, near, cross = held_until([*conv_parts, near, cross], ())
    conv_parts = traded(conv_parts, "ctx")
    convolved = joined(conv_parts, position, 1)
    gated_out = (wide(query_gate) * wide(convolved)).astype(jnp.bfloat16)
    if in_line:
        far, skip = hop(near, ACROSS), hop(cross, OUTWARD)
        total = line_cotangents(near, NEAR, out_weight, total)
        own, through, ready, rest = line_scatter(
            gated_out, out_weight, channels, (total,), (far, skip)
        )
        total = line_cotangents(added(cross, skip), MIDDLE, out_weight, total)
        (last,) = held_until([hop(far, OUTWARD)], (own,))
        grad_query, conv_grad = line_cotangents(
            added(far, last), FAR, out_weight, total, (convolved, query_gate), (through,)
        )
    else:
        partial_value = jnp.dot(gated_out, out_weight, preferred_element_type=jnp.float32)
        projected = lax.psum_scatter(
            partial_value.astype(jnp.bfloat16), "tp", scatter_dimension=1, tiled=True
        )
        dgated = jnp.einsum(
            "tk,ck->tc",
            lax.all_gather(out_grad, "tp", axis=1, tiled=True),
            out_weight,
            preferred_element_type=jnp.float32,
        ).astype(jnp.bfloat16)
        grad_query = (wide(dgated) * wide(convolved)).astype(jnp.bfloat16)
        conv_grad = (wide(dgated) * wide(query_gate)).astype(jnp.bfloat16)
    grad_parts = traded(cut(conv_grad, position, members, 1), "ctx")
    arrived = ready(tuple(grad_parts[1:])) if in_line else ()
    back_parts = correlate(at, input_parts, grad_parts, per_group, tap_scale, arrived)
    if in_line:
        projected = rest(*arrived)
    back_parts = traded(back_parts, "ctx")
    unpack = finished if in_tiles else unpacked_parts
    arguments = (at if in_tiles else position, back_parts, key_gate, value_input, groups)
    grad_key, grad_value, grad_filter = unpack(*arguments)
    return (projected, grad_query, grad_key, grad_value, grad_filter)


def solution(mesh):
    both = P("ctx", "tp")
    return jax.shard_map(
        local,
        mesh=mesh,
        in_specs=(both, both, both, both, P("tp", None), both),
        out_specs=(both,) * 5,
        check_vma=False,
    )
```

```python
import functools
import math
import jax
import jax.numpy as jnp
from jax import lax
from jax.experimental import pallas as pl
from jax.experimental.pallas import tpu as pltpu
from jax.sharding import PartitionSpec as P

BLOCK = 128
NT = (((1,), (1,)), ((), ()))
COST = pl.CostEstimate(flops=2**20, bytes_accessed=2**12, transcendentals=0)


def lag_matrix(row, length):
    lanes = lax.broadcasted_iota(jnp.int32, (BLOCK, length), 1)
    rows = lax.broadcasted_iota(jnp.int32, (BLOCK, length), 0)
    spread = pltpu.roll(
        jnp.broadcast_to(row, (BLOCK, length)), 0, axis=1, stride=1, stride_axis=0
    )
    return jnp.where(lanes >= rows, spread, 0.0).astype(jnp.bfloat16)


def stacked(ref, start, rows, members, width):
    pieces = []
    for member in range(members):
        part = ref[member, pl.ds(start, rows), :]
        for at in range(0, width, BLOCK):
            pieces.append(part[:, at : at + BLOCK])
    return jnp.concatenate(pieces, axis=0)


def spread_out(ref, start, rows, value, members, width):
    per_member = width // BLOCK
    for member in range(members):
        base = member * per_member * rows
        parts = [value[base + i * rows : base + (i + 1) * rows] for i in range(per_member)]
        ref[member, pl.ds(start, rows), :] = jnp.concatenate(parts, axis=1)


def padded(groups):
    return -(-groups // 16) * 16


def load_taps(tap_scr, packed, at, width):
    groups, channels = tap_scr.shape[0], packed.shape[1]
    rows = padded(groups)
    parts = [
        packed[width + chunk * rows : width + (chunk + 1) * rows, :].astype(jnp.float32)
        for chunk in range(width // channels)
    ]
    start = pl.multiple_of(at * width, width)
    tap_scr[:, pl.ds(start, width)] = jnp.concatenate(parts, axis=1)[:groups]


def forward_kernel(members, per_group, width, pos_ref, *refs):
    inputs, outputs = refs[:members], refs[-members - 3 : -3]
    tap_scr, in_scr, out_scr = refs[-3:]
    position = pos_ref[0]
    channels = inputs[0].shape[1]
    groups = channels // per_group
    length = members * width
    blocks = length // BLOCK
    for step in range(members):
        at = position ^ step
        in_scr[at] = inputs[step][:width].T
        load_taps(tap_scr, inputs[step], at, width)

    def one_group(group, carry):
        start = pl.multiple_of(group * per_group, per_group)
        lags = lag_matrix(tap_scr[pl.ds(group, 1), :], length)
        data = stacked(in_scr, start, per_group, members, width)
        total = [jnp.zeros((per_group, BLOCK), jnp.float32) for _ in range(blocks)]
        for offset in range(0, blocks, 2):
            rows = (blocks - offset) * per_group
            result = jnp.dot(
                data[:rows],
                lags[:, offset * BLOCK : (offset + 2) * BLOCK],
                preferred_element_type=jnp.float32,
            )
            for side in range(2):
                for source in range(blocks - offset - side):
                    total[source + offset + side] += result[
                        source * per_group : (source + 1) * per_group,
                        side * BLOCK : (side + 1) * BLOCK,
                    ]
        value = jnp.concatenate(total, axis=0).astype(jnp.bfloat16)
        spread_out(out_scr, start, per_group, value, members, width)
        return carry

    lax.fori_loop(0, groups, one_group, 0)
    for step in range(members):
        outputs[step][...] = out_scr[position ^ step].T


def backward_kernel(members, per_group, scale, width, pos_ref, *refs):
    inputs, cotangents = refs[:members], refs[members : 2 * members]
    outputs = refs[-members - 6 : -6]
    tap_scr, in_scr, cot_scr, out_scr, grad_scr, pad_scr = refs[-6:]
    position = pos_ref[0]
    channels = inputs[0].shape[1]
    groups = channels // per_group
    length = members * width
    blocks = length // BLOCK
    depth = blocks * per_group
    for step in range(members):
        at = position ^ step
        in_scr[at] = inputs[step][:width].T
        cot_scr[at] = cotangents[step][...].T
        load_taps(tap_scr, inputs[step], at, width)
    pad_scr[...] = jnp.zeros_like(pad_scr)
    rows_of = lax.broadcasted_iota(jnp.int32, (BLOCK, BLOCK), 0)
    lanes_of = lax.broadcasted_iota(jnp.int32, (BLOCK, BLOCK), 1)
    mirror = (rows_of + lanes_of == BLOCK - 1).astype(jnp.bfloat16)

    def one_group(group, carry):
        start = pl.multiple_of(group * per_group, per_group)
        lags = lag_matrix(tap_scr[pl.ds(group, 1), :], length)
        data = stacked(in_scr, start, per_group, members, width)
        cot = stacked(cot_scr, start, per_group, members, width)
        pad_scr[:depth, :BLOCK] = cot
        pad_scr[: depth - per_group, BLOCK:] = cot[per_group:]
        flipped = lax.dot_general(
            mirror, data, NT, preferred_element_type=jnp.float32
        ).astype(jnp.bfloat16)
        total = jnp.zeros((depth, BLOCK), jnp.float32)
        products = []
        for offset in range(0, blocks, 2):
            rows = depth - offset * per_group
            pair = pad_scr[offset * per_group : offset * per_group + depth, :]
            result = lax.dot_general(
                pair[:rows],
                lags[:, offset * BLOCK : (offset + 2) * BLOCK],
                NT,
                preferred_element_type=jnp.float32,
            )
            if rows < depth:
                result = jnp.concatenate(
                    [result, jnp.zeros((depth - rows, BLOCK), jnp.float32)], axis=0
                )
            total = total + result
            products.append(jnp.dot(flipped, pair, preferred_element_type=jnp.float32))
        spread_out(
            out_scr, start, per_group, total.astype(jnp.bfloat16), members, width
        )
        product = jnp.concatenate(products, axis=1)
        lanes = lax.broadcasted_iota(jnp.int32, (BLOCK, length), 1)
        back = BLOCK - 1 - lax.broadcasted_iota(jnp.int32, (BLOCK, length), 0)
        product = jnp.where(lanes >= back, product, 0.0)
        product = pltpu.roll(
            product, length - (BLOCK - 1), axis=1, stride=1, stride_axis=0
        )
        grad_scr[pl.ds(group, 1), :] = jnp.sum(product, axis=0, keepdims=True) * scale
        return carry

    lax.fori_loop(0, groups, one_group, 0)
    for step in range(members):
        at = position ^ step
        outputs[step][:width] = out_scr[at].T
        rows = padded(groups)
        whole = grad_scr[:, pl.ds(pl.multiple_of(at * width, width), width)].astype(jnp.bfloat16)
        if rows > groups:
            blank = jnp.zeros((rows - groups, width), jnp.bfloat16)
            whole = jnp.concatenate([whole, blank], axis=0)
        for chunk in range(width // channels):
            outputs[step][width + chunk * rows : width + (chunk + 1) * rows, :] = whole[
                :, chunk * channels : (chunk + 1) * channels
            ]


VMEM = pl.BlockSpec(memory_space=pltpu.VMEM)
ANYWHERE = pl.BlockSpec(memory_space=pl.ANY)
SMEM = pl.BlockSpec(memory_space=pltpu.SMEM)


def convolve(position, inputs, width, per_group, after=()):
    members = len(inputs)
    channels = inputs[0].shape[1]
    length = members * width
    return pl.pallas_call(
        functools.partial(forward_kernel, members, per_group, width),
        out_shape=[jax.ShapeDtypeStruct((width, channels), jnp.bfloat16)] * members,
        in_specs=[SMEM] + [VMEM] * members + [ANYWHERE] * len(after),
        out_specs=[VMEM] * members,
        scratch_shapes=[
            pltpu.VMEM((channels // per_group, length), jnp.float32),
            pltpu.VMEM((members, channels, width), jnp.bfloat16),
            pltpu.VMEM((members, channels, width), jnp.bfloat16),
        ],
        compiler_params=pltpu.CompilerParams(vmem_limit_bytes=24 * 2**20),
        cost_estimate=COST,
        name="causal_conv",
    )(position, *inputs, *after)


def correlate(position, inputs, cotangents, per_group, scale, after=()):
    members = len(inputs)
    width, channels = cotangents[0].shape
    length = members * width
    groups = channels // per_group
    return pl.pallas_call(
        functools.partial(backward_kernel, members, per_group, scale, width),
        out_shape=[jax.ShapeDtypeStruct(inputs[0].shape, jnp.bfloat16)] * members,
        in_specs=[SMEM] + [VMEM] * (2 * members) + [ANYWHERE] * len(after),
        out_specs=[VMEM] * members,
        scratch_shapes=[
            pltpu.VMEM((groups, length), jnp.float32),
            pltpu.VMEM((members, channels, width), jnp.bfloat16),
            pltpu.VMEM((members, channels, width), jnp.bfloat16),
            pltpu.VMEM((members, channels, width), jnp.bfloat16),
            pltpu.VMEM((groups, length), jnp.float32),
            pltpu.VMEM((2 * length // BLOCK * per_group, 2 * BLOCK), jnp.bfloat16),
        ],
        compiler_params=pltpu.CompilerParams(vmem_limit_bytes=24 * 2**20),
        cost_estimate=COST,
        name="causal_conv_grads",
    )(position, *inputs, *cotangents, *after)


def in_hbm(array):
    return pltpu.with_memory_space_constraint(array, pltpu.HBM)


def prepare_kernel(members, scale, pos_ref, key_ref, value_ref, taps_ref, *outputs):
    position = pos_ref[0]
    step_no = pl.program_id(0)
    rows, channels = key_ref.shape
    share = channels // members
    groups = taps_ref.shape[0] // members
    total_width = taps_ref.shape[1]
    for step in range(members):
        at = position ^ step
        columns = pl.ds(pl.multiple_of(at * share, share), share)
        product = key_ref[:, columns].astype(jnp.float32) * value_ref[:, columns].astype(
            jnp.float32
        )
        here = pl.ds(pl.multiple_of(step_no * rows, rows), rows)
        outputs[step][here, :] = product.astype(jnp.bfloat16)

    @pl.when(step_no == 0)
    def _():
        for step in range(members):
            at = position ^ step
            taps = taps_ref[pl.ds(pl.multiple_of(at * groups, groups), groups), :]
            taps = (taps * scale).astype(jnp.bfloat16)
            for chunk in range(total_width // share):
                start = total_width + chunk * groups
                outputs[step][start : start + groups, :] = taps[
                    :, chunk * share : (chunk + 1) * share
                ]


def prepare(position, key_gate, value_input, filter_taps, members, scale):
    width, channels = key_gate.shape
    share = channels // members
    rows = width + filter_taps.size // members // share
    tile = width // 4
    part = pl.BlockSpec((tile, channels), lambda i: (i, 0))
    return pl.pallas_call(
        functools.partial(prepare_kernel, members, scale),
        out_shape=[jax.ShapeDtypeStruct((rows, share), jnp.bfloat16)] * members,
        grid=(4,),
        in_specs=[SMEM, part, part, pl.BlockSpec(filter_taps.shape[::-1], lambda i: (0, 0))],
        out_specs=[VMEM] * members,
        compiler_params=pltpu.CompilerParams(vmem_limit_bytes=24 * 2**20),
        cost_estimate=COST,
        name="gated_input",
    )(position, in_hbm(key_gate), in_hbm(value_input), in_hbm(filter_taps.T))


def finish_kernel(members, pos_ref, *refs):
    parts = refs[:members]
    key_ref, value_ref, key_out, value_out, taps_out = refs[members:]
    position = pos_ref[0]
    width, channels = key_ref.shape
    share = channels // members
    groups = taps_out.shape[0] // members
    for step in range(members):
        at = position ^ step
        columns = pl.ds(pl.multiple_of(at * share, share), share)
        grad = parts[step][:width].astype(jnp.float32)
        key_out[:, columns] = (grad * value_ref[:, columns].astype(jnp.float32)).astype(
            jnp.bfloat16
        )
        value_out[:, columns] = (grad * key_ref[:, columns].astype(jnp.float32)).astype(
            jnp.bfloat16
        )
        taps = [
            parts[step][width + chunk * groups : width + (chunk + 1) * groups, :]
            for chunk in range(width // share)
        ]
        taps_out[pl.ds(pl.multiple_of(at * groups, groups), groups), :] = jnp.concatenate(
            taps, axis=1
        ).astype(jnp.float32)


def finished(position, parts, key_gate, value_input, groups):
    members = len(parts)
    width, channels = key_gate.shape
    array = jax.ShapeDtypeStruct((width, channels), jnp.bfloat16)
    grad_key, grad_value, taps = pl.pallas_call(
        functools.partial(finish_kernel, members),
        out_shape=[array, array, jax.ShapeDtypeStruct((groups, width), jnp.float32)],
        in_specs=[SMEM] + [VMEM] * (members + 2),
        out_specs=[VMEM] * 3,
        compiler_params=pltpu.CompilerParams(vmem_limit_bytes=24 * 2**20),
        cost_estimate=COST,
        name="input_gradients",
    )(position, *parts, key_gate, value_input)
    return grad_key, grad_value, taps.T


def swapped(array, axis, step):
    size = lax.axis_size(axis)
    return lax.ppermute(array, axis, [(i, i ^ step) for i in range(size)])


def traded(pieces, axis):
    return [pieces[0]] + [swapped(pieces[step], axis, step) for step in range(1, len(pieces))]


def cut(array, position, members, axis):
    width = array.shape[axis] // members
    return [
        lax.dynamic_slice_in_dim(array, (position ^ step) * width, width, axis)
        for step in range(members)
    ]


def joined(pieces, position, axis):
    members = len(pieces)
    width = pieces[0].shape[axis]
    shape = list(pieces[0].shape)
    shape[axis] = members * width
    whole = jnp.zeros(shape, pieces[0].dtype)
    for step in range(members):
        whole = lax.dynamic_update_slice_in_dim(
            whole, pieces[step], (position ^ step) * width, axis
        )
    return whole


def wide(array):
    return array.astype(jnp.float32)


def hop(array, pairs):
    return lax.ppermute(
        array, "tp", [(2 * i + core, 2 * j + core) for i, j in pairs for core in range(2)]
    )


INWARD = ((0, 1), (3, 2))
ACROSS = ((1, 2), (2, 1))
OUTWARD = ((1, 0), (2, 3))


def of_chip(chip, table):
    return jnp.where(
        chip == 0, table[0], jnp.where(chip == 1, table[1], jnp.where(chip == 2, table[2], table[3]))
    )


def pass_kernel(*refs):
    del refs


def held_until(values, after):
    return pl.pallas_call(
        pass_kernel,
        out_shape=[jax.ShapeDtypeStruct(value.shape, value.dtype) for value in values],
        in_specs=[ANYWHERE] * (len(values) + len(after)),
        out_specs=[ANYWHERE] * len(values),
        input_output_aliases={number: number for number in range(len(values))},
        compiler_params=pltpu.CompilerParams(vmem_limit_bytes=2**20),
        cost_estimate=COST,
        name="held",
    )(*values, *after)


def given_kernel(_, data_ref, weight_ref, *refs):
    refs[-1][0] = jnp.dot(
        data_ref[...], weight_ref[...], preferred_element_type=jnp.float32
    ).astype(jnp.bfloat16)


def kept_kernel(tiles, count, _, data_ref, weight_ref, more_ref, *refs):
    product = jnp.dot(data_ref[...], weight_ref[...], preferred_element_type=jnp.float32)
    result = (product + wide(more_ref[0])).astype(jnp.bfloat16)
    for number, out_ref in enumerate(refs[-count:]):

        @pl.when(pl.program_id(0) // tiles == number)
        def _(out_ref=out_ref):
            out_ref[...] = result


def column_products(data, out_weight, blocks, width, more=None, after=()):
    rows, depth = data.shape
    tile = min(width, 512)
    tiles = width // tile
    count = len(blocks)
    stack = pl.BlockSpec((1, rows, tile), lambda i, at: (i // tiles, 0, i % tiles))
    array = jax.ShapeDtypeStruct((rows, width), jnp.bfloat16)

    def column(number):
        return pl.BlockSpec(
            (rows, tile), lambda i, at: (0, jnp.clip(i - number * tiles, 0, tiles - 1))
        )

    return pl.pallas_call(
        given_kernel if more is None else functools.partial(kept_kernel, tiles, count),
        out_shape=jax.ShapeDtypeStruct((count, rows, width), jnp.bfloat16)
        if more is None
        else [array] * count,
        grid_spec=pltpu.PrefetchScalarGridSpec(
            num_scalar_prefetch=1,
            grid=(count * tiles,),
            in_specs=[
                pl.BlockSpec((rows, depth), lambda i, at: (0, 0)),
                pl.BlockSpec((depth, tile), lambda i, at: (0, at[i // tiles] * tiles + i % tiles)),
            ]
            + ([] if more is None else [stack])
            + [ANYWHERE] * len(after),
            out_specs=stack if more is None else [column(number) for number in range(count)],
        ),
        compiler_params=pltpu.CompilerParams(vmem_limit_bytes=24 * 2**20),
        cost_estimate=COST,
        name="projection_blocks",
    )(
        jnp.stack(blocks).astype(jnp.int32),
        data,
        in_hbm(out_weight),
        *(() if more is None else (more,)),
        *after,
    )


def cotangent_kernel(count, first, last, _, weight_ref, *refs):
    blocks, refs = refs[:count], refs[count:]
    step = pl.program_id(0)
    total = refs[-1]

    @pl.when(step == 0)
    def _():
        total[...] = jnp.zeros_like(total) if first else refs[0][...]

    for number, block in enumerate(blocks):

        @pl.when(step == number)
        def _(block=block):
            total[...] += lax.dot_general(
                block[...], weight_ref[...], NT, preferred_element_type=jnp.float32
            )

    if last:
        conv_ref, query_ref = refs[1:3]
        grad_ref, cot_ref = refs[-3:-1]

        @pl.when(step == count - 1)
        def _():
            dgated = wide(total[...].astype(jnp.bfloat16))
            grad_ref[...] = (dgated * wide(conv_ref[...])).astype(jnp.bfloat16)
            cot_ref[...] = (dgated * wide(query_ref[...])).astype(jnp.bfloat16)


def cotangent_products(blocks, places, out_weight, start=None, gates=(), after=()):
    rows, width = blocks[0].shape
    channels = out_weight.shape[0]
    count = len(blocks)
    whole = pl.BlockSpec((rows, channels), lambda i, at: (0, 0))
    part = pl.BlockSpec((rows, width), lambda i, at: (0, 0))
    array = jax.ShapeDtypeStruct((rows, channels), jnp.bfloat16)
    first, last = start is None, bool(gates)
    extra = (() if first else (start,)) + tuple(gates)
    return pl.pallas_call(
        functools.partial(cotangent_kernel, count, first, last),
        out_shape=[array, array] if last else jax.ShapeDtypeStruct((rows, channels), jnp.float32),
        grid_spec=pltpu.PrefetchScalarGridSpec(
            num_scalar_prefetch=1,
            grid=(count,),
            in_specs=[pl.BlockSpec((channels, width), lambda i, at: (0, at[i]))]
            + [part] * count
            + [whole] * len(extra)
            + [ANYWHERE] * len(after),
            out_specs=[whole, whole] if last else whole,
            scratch_shapes=[pltpu.VMEM((rows, channels), jnp.float32)] if last else [],
        ),
        compiler_params=pltpu.CompilerParams(vmem_limit_bytes=24 * 2**20),
        cost_estimate=COST,
        name="cotangent_blocks",
    )(jnp.stack(places).astype(jnp.int32), in_hbm(out_weight), *blocks, *extra, *after)


OWN, NEAR, MIDDLE, FAR = (0, 1, 2, 3), (1, 0, 3, 2), (2, 2, 1, 1), (3, 3, 0, 0)


def added(*arrays):
    return sum(wide(array) for array in arrays).astype(jnp.bfloat16)


def line_scatter(data, out_weight, width, later):
    place = lax.axis_index("tp")
    chip, core = place // 2, place % 2

    def product(tables, other, more=None, after=()):
        blocks = [2 * of_chip(chip, table) + other for table in tables]
        return column_products(data, out_weight, blocks, width, more, after)

    others = (MIDDLE, NEAR, OWN)
    given = product((FAR,), 1 - core, after=later)
    given_others = product(others, 1 - core, after=(given,))
    (first,) = product((FAR,), core, swapped(given, "tp", 1), (given_others,))
    one = hop(first, INWARD)
    (given_others,) = held_until([given_others], (first,))
    second, third, own = product(others, core, swapped(given_others, "tp", 1))
    two_b = hop(second, INWARD)

    def passed(after):
        (arrived,) = held_until([one], after)
        through = added(first, arrived)
        return through, hop(through, ACROSS)

    def ready(two_a, after):
        across, inward = held_until([two_a, two_b], after)
        return added(third, across), added(second, inward)

    def rest(final, onward):
        return added(own, hop(final, OUTWARD + INWARD), hop(onward, ACROSS))

    return first, own, passed, ready, rest


def line_cotangents(blocks, tables, out_weight, start=None, gates=(), after=()):
    place = lax.axis_index("tp")
    core = place % 2
    parts, places = [], []
    for block, table in zip(blocks, tables):
        source = 2 * of_chip(place // 2, table)
        parts += [block, swapped(block, "tp", 1)]
        places += [source + core, source + 1 - core]
    return cotangent_products(parts, places, out_weight, start, gates, after)


def packed_parts(position, key_gate, value_input, filter_taps, members, scale):
    length, channels = key_gate.shape
    share = channels // members
    product_in = (wide(key_gate) * wide(value_input)).astype(jnp.bfloat16)
    tap_rows = (filter_taps * scale).astype(jnp.bfloat16).T
    owned = filter_taps.shape[1] // members
    chunks = length // share
    packed = []
    pieces = cut(product_in, position, members, 1)
    for piece, taps in zip(pieces, cut(tap_rows, position, members, 0)):
        taps = taps.reshape(owned, chunks, share).transpose(1, 0, 2)
        taps = jnp.pad(taps, ((0, 0), (0, padded(owned) - owned), (0, 0)))
        packed.append(jnp.concatenate([piece, taps.reshape(-1, share)], axis=0))
    return packed


def unpacked_parts(position, parts, key_gate, value_input, groups):
    length, channels = key_gate.shape
    members = len(parts)
    share = channels // members
    owned = groups // members
    chunks = length // share
    input_grad = wide(joined([part[:length] for part in parts], position, 1))
    filter_parts = [
        part[length:]
        .reshape(chunks, padded(owned), share)[:, :owned]
        .transpose(1, 0, 2)
        .reshape(owned, length)
        for part in parts
    ]
    grad_filter = wide(joined(filter_parts, position, 0)).T
    grad_key = (input_grad * wide(value_input)).astype(jnp.bfloat16)
    grad_value = (input_grad * wide(key_gate)).astype(jnp.bfloat16)
    return grad_key, grad_value, grad_filter


def local(query_gate, key_gate, value_input, filter_taps, out_weight, out_grad):
    length, channels = query_gate.shape
    groups = filter_taps.shape[1]
    per_group = channels // groups
    members = lax.axis_size("ctx")
    position = lax.axis_index("ctx")
    at = position.reshape((1,)).astype(jnp.int32)
    tap_scale = 1.0 / math.sqrt(length * members)
    share = channels // members
    in_line = lax.axis_size("tp") == 8

    if in_line:
        near, cross = hop(out_grad, INWARD + OUTWARD), hop(out_grad, ACROSS)
        total = line_cotangents((out_grad,), (OWN,), out_weight)
    in_tiles = share % 128 == 0 and groups // members % 16 == 0
    if in_tiles:
        packed = prepare(at, key_gate, value_input, filter_taps, members, tap_scale)
    else:
        packed = packed_parts(position, key_gate, value_input, filter_taps, members, tap_scale)
    input_parts = traded(packed, "ctx")
    conv_parts = convolve(at, input_parts, length, per_group, (total,) if in_line else ())
    if in_line:
        *conv_parts, near, cross = held_until([*conv_parts, near, cross], ())
    conv_parts = traded(conv_parts, "ctx")
    convolved = joined(conv_parts, position, 1)
    gated_out = (wide(query_gate) * wide(convolved)).astype(jnp.bfloat16)
    if in_line:
        far, skip = hop(near, ACROSS), hop(cross, OUTWARD)
        first, own, passed, ready, rest = line_scatter(
            gated_out, out_weight, channels, (far, skip)
        )
        blocks = (near, added(cross, skip))
        total = line_cotangents(blocks, (NEAR, MIDDLE), out_weight, total, after=(first,))
        through, two_a = passed((total,))
        (last,) = held_until([hop(far, OUTWARD)], (own, total))
        grad_query, conv_grad = line_cotangents(
            (added(far, last),), (FAR,), out_weight, total, (convolved, query_gate), (through,)
        )
    else:
        partial_value = jnp.dot(gated_out, out_weight, preferred_element_type=jnp.float32)
        projected = lax.psum_scatter(
            partial_value.astype(jnp.bfloat16), "tp", scatter_dimension=1, tiled=True
        )
        dgated = jnp.einsum(
            "tk,ck->tc",
            lax.all_gather(out_grad, "tp", axis=1, tiled=True),
            out_weight,
            preferred_element_type=jnp.float32,
        ).astype(jnp.bfloat16)
        grad_query = (wide(dgated) * wide(convolved)).astype(jnp.bfloat16)
        conv_grad = (wide(dgated) * wide(query_gate)).astype(jnp.bfloat16)
    grad_parts = traded(cut(conv_grad, position, members, 1), "ctx")
    arrived = ready(two_a, tuple(grad_parts[1:])) if in_line else ()
    back_parts = correlate(at, input_parts, grad_parts, per_group, tap_scale, arrived)
    if in_line:
        projected = rest(*arrived)
    back_parts = traded(back_parts, "ctx")
    unpack = finished if in_tiles else unpacked_parts
    arguments = (at if in_tiles else position, back_parts, key_gate, value_input, groups)
    grad_key, grad_value, grad_filter = unpack(*arguments)
    return (projected, grad_query, grad_key, grad_value, grad_filter)


def solution(mesh):
    both = P("ctx", "tp")
    return jax.shard_map(
        local,
        mesh=mesh,
        in_specs=(both, both, both, both, P("tp", None), both),
        out_specs=(both,) * 5,
        check_vma=False,
    )
```

```python
import functools
import math
import jax
import jax.numpy as jnp
from jax import lax
from jax.experimental import pallas as pl
from jax.experimental.pallas import tpu as pltpu
from jax.sharding import PartitionSpec as P

BLOCK = 128
POSITION = 8
NT = (((1,), (1,)), ((), ()))
COST = pl.CostEstimate(flops=2**20, bytes_accessed=2**12, transcendentals=0)


def lag_matrix(row, length):
    lanes = lax.broadcasted_iota(jnp.int32, (BLOCK, length), 1)
    rows = lax.broadcasted_iota(jnp.int32, (BLOCK, length), 0)
    spread = pltpu.roll(
        jnp.broadcast_to(row, (BLOCK, length)), 0, axis=1, stride=1, stride_axis=0
    )
    return jnp.where(lanes >= rows, spread, 0.0).astype(jnp.bfloat16)


def stacked(ref, start, rows, members, width):
    pieces = []
    for member in range(members):
        part = ref[member, pl.ds(start, rows), :]
        for at in range(0, width, BLOCK):
            pieces.append(part[:, at : at + BLOCK])
    return jnp.concatenate(pieces, axis=0)


def spread_out(ref, start, rows, value, members, width):
    per_member = width // BLOCK
    for member in range(members):
        base = member * per_member * rows
        parts = [value[base + i * rows : base + (i + 1) * rows] for i in range(per_member)]
        ref[member, pl.ds(start, rows), :] = jnp.concatenate(parts, axis=1)


def padded(groups):
    return -(-groups // 16) * 16


def load_taps(tap_scr, packed, at, width):
    groups, channels = tap_scr.shape[0], packed.shape[1]
    rows = padded(groups)
    parts = [
        packed[width + chunk * rows : width + (chunk + 1) * rows, :].astype(jnp.float32)
        for chunk in range(width // channels)
    ]
    start = pl.multiple_of(at * width, width)
    tap_scr[:, pl.ds(start, width)] = jnp.concatenate(parts, axis=1)[:groups]


def forward_kernel(members, per_group, width, plan_ref, *refs):
    inputs, outputs = refs[:members], refs[-members - 3 : -3]
    tap_scr, in_scr, out_scr = refs[-3:]
    position = plan_ref[POSITION]
    channels = inputs[0].shape[1]
    groups = channels // per_group
    length = members * width
    blocks = length // BLOCK
    for step in range(members):
        at = position ^ step
        in_scr[at] = inputs[step][:width].T
        load_taps(tap_scr, inputs[step], at, width)

    def one_group(group, carry):
        start = pl.multiple_of(group * per_group, per_group)
        lags = lag_matrix(tap_scr[pl.ds(group, 1), :], length)
        data = stacked(in_scr, start, per_group, members, width)
        total = [jnp.zeros((per_group, BLOCK), jnp.float32) for _ in range(blocks)]
        for offset in range(0, blocks, 2):
            rows = (blocks - offset) * per_group
            result = jnp.dot(
                data[:rows],
                lags[:, offset * BLOCK : (offset + 2) * BLOCK],
                preferred_element_type=jnp.float32,
            )
            for side in range(2):
                for source in range(blocks - offset - side):
                    total[source + offset + side] += result[
                        source * per_group : (source + 1) * per_group,
                        side * BLOCK : (side + 1) * BLOCK,
                    ]
        value = jnp.concatenate(total, axis=0).astype(jnp.bfloat16)
        spread_out(out_scr, start, per_group, value, members, width)
        return carry

    lax.fori_loop(0, groups, one_group, 0)
    for step in range(members):
        outputs[step][...] = out_scr[position ^ step].T


def backward_kernel(members, per_group, scale, width, plan_ref, *refs):
    inputs, cotangents = refs[:members], refs[members : 2 * members]
    outputs = refs[-members - 6 : -6]
    tap_scr, in_scr, cot_scr, out_scr, grad_scr, pad_scr = refs[-6:]
    position = plan_ref[POSITION]
    channels = inputs[0].shape[1]
    groups = channels // per_group
    length = members * width
    blocks = length // BLOCK
    depth = blocks * per_group
    for step in range(members):
        at = position ^ step
        in_scr[at] = inputs[step][:width].T
        cot_scr[at] = cotangents[step][...].T
        load_taps(tap_scr, inputs[step], at, width)
    pad_scr[...] = jnp.zeros_like(pad_scr)
    rows_of = lax.broadcasted_iota(jnp.int32, (BLOCK, BLOCK), 0)
    lanes_of = lax.broadcasted_iota(jnp.int32, (BLOCK, BLOCK), 1)
    mirror = (rows_of + lanes_of == BLOCK - 1).astype(jnp.bfloat16)

    def one_group(group, carry):
        start = pl.multiple_of(group * per_group, per_group)
        lags = lag_matrix(tap_scr[pl.ds(group, 1), :], length)
        data = stacked(in_scr, start, per_group, members, width)
        cot = stacked(cot_scr, start, per_group, members, width)
        pad_scr[:depth, :BLOCK] = cot
        pad_scr[: depth - per_group, BLOCK:] = cot[per_group:]
        flipped = lax.dot_general(
            mirror, data, NT, preferred_element_type=jnp.float32
        ).astype(jnp.bfloat16)
        total = jnp.zeros((depth, BLOCK), jnp.float32)
        products = []
        for offset in range(0, blocks, 2):
            rows = depth - offset * per_group
            pair = pad_scr[offset * per_group : offset * per_group + depth, :]
            result = lax.dot_general(
                pair[:rows],
                lags[:, offset * BLOCK : (offset + 2) * BLOCK],
                NT,
                preferred_element_type=jnp.float32,
            )
            if rows < depth:
                result = jnp.concatenate(
                    [result, jnp.zeros((depth - rows, BLOCK), jnp.float32)], axis=0
                )
            total = total + result
            products.append(jnp.dot(flipped, pair, preferred_element_type=jnp.float32))
        spread_out(
            out_scr, start, per_group, total.astype(jnp.bfloat16), members, width
        )
        product = jnp.concatenate(products, axis=1)
        lanes = lax.broadcasted_iota(jnp.int32, (BLOCK, length), 1)
        back = BLOCK - 1 - lax.broadcasted_iota(jnp.int32, (BLOCK, length), 0)
        product = jnp.where(lanes >= back, product, 0.0)
        product = pltpu.roll(
            product, length - (BLOCK - 1), axis=1, stride=1, stride_axis=0
        )
        grad_scr[pl.ds(group, 1), :] = jnp.sum(product, axis=0, keepdims=True) * scale
        return carry

    lax.fori_loop(0, groups, one_group, 0)
    for step in range(members):
        at = position ^ step
        outputs[step][:width] = out_scr[at].T
        rows = padded(groups)
        whole = grad_scr[:, pl.ds(pl.multiple_of(at * width, width), width)].astype(jnp.bfloat16)
        if rows > groups:
            blank = jnp.zeros((rows - groups, width), jnp.bfloat16)
            whole = jnp.concatenate([whole, blank], axis=0)
        for chunk in range(width // channels):
            outputs[step][width + chunk * rows : width + (chunk + 1) * rows, :] = whole[
                :, chunk * channels : (chunk + 1) * channels
            ]


VMEM = pl.BlockSpec(memory_space=pltpu.VMEM)
ANYWHERE = pl.BlockSpec(memory_space=pl.ANY)
SMEM = pl.BlockSpec(memory_space=pltpu.SMEM)


def convolve(plan, inputs, width, per_group, after=()):
    members = len(inputs)
    channels = inputs[0].shape[1]
    length = members * width
    return pl.pallas_call(
        functools.partial(forward_kernel, members, per_group, width),
        out_shape=[jax.ShapeDtypeStruct((width, channels), jnp.bfloat16)] * members,
        in_specs=[SMEM] + [VMEM] * members + [ANYWHERE] * len(after),
        out_specs=[VMEM] * members,
        scratch_shapes=[
            pltpu.VMEM((channels // per_group, length), jnp.float32),
            pltpu.VMEM((members, channels, width), jnp.bfloat16),
            pltpu.VMEM((members, channels, width), jnp.bfloat16),
        ],
        compiler_params=pltpu.CompilerParams(vmem_limit_bytes=24 * 2**20),
        cost_estimate=COST,
        name="causal_conv",
    )(plan, *inputs, *after)


def correlate(plan, inputs, cotangents, per_group, scale, after=()):
    members = len(inputs)
    width, channels = cotangents[0].shape
    length = members * width
    groups = channels // per_group
    return pl.pallas_call(
        functools.partial(backward_kernel, members, per_group, scale, width),
        out_shape=[jax.ShapeDtypeStruct(inputs[0].shape, jnp.bfloat16)] * members,
        in_specs=[SMEM] + [VMEM] * (2 * members) + [ANYWHERE] * len(after),
        out_specs=[VMEM] * members,
        scratch_shapes=[
            pltpu.VMEM((groups, length), jnp.float32),
            pltpu.VMEM((members, channels, width), jnp.bfloat16),
            pltpu.VMEM((members, channels, width), jnp.bfloat16),
            pltpu.VMEM((members, channels, width), jnp.bfloat16),
            pltpu.VMEM((groups, length), jnp.float32),
            pltpu.VMEM((2 * length // BLOCK * per_group, 2 * BLOCK), jnp.bfloat16),
        ],
        compiler_params=pltpu.CompilerParams(vmem_limit_bytes=24 * 2**20),
        cost_estimate=COST,
        name="causal_conv_grads",
    )(plan, *inputs, *cotangents, *after)


def in_hbm(array):
    return pltpu.with_memory_space_constraint(array, pltpu.HBM)


def prepare_kernel(members, scale, plan_ref, key_ref, value_ref, taps_ref, *outputs):
    position = plan_ref[POSITION]
    step_no = pl.program_id(0)
    rows, channels = key_ref.shape
    share = channels // members
    groups = taps_ref.shape[0] // members
    total_width = taps_ref.shape[1]
    for step in range(members):
        at = position ^ step
        columns = pl.ds(pl.multiple_of(at * share, share), share)
        product = key_ref[:, columns].astype(jnp.float32) * value_ref[:, columns].astype(
            jnp.float32
        )
        here = pl.ds(pl.multiple_of(step_no * rows, rows), rows)
        outputs[step][here, :] = product.astype(jnp.bfloat16)

    @pl.when(step_no == 0)
    def _():
        for step in range(members):
            at = position ^ step
            taps = taps_ref[pl.ds(pl.multiple_of(at * groups, groups), groups), :]
            taps = (taps * scale).astype(jnp.bfloat16)
            for chunk in range(total_width // share):
                start = total_width + chunk * groups
                outputs[step][start : start + groups, :] = taps[
                    :, chunk * share : (chunk + 1) * share
                ]


def prepare(plan, key_gate, value_input, filter_taps, members, scale):
    width, channels = key_gate.shape
    share = channels // members
    rows = width + filter_taps.size // members // share
    tile = width // 4
    part = pl.BlockSpec((tile, channels), lambda i: (i, 0))
    return pl.pallas_call(
        functools.partial(prepare_kernel, members, scale),
        out_shape=[jax.ShapeDtypeStruct((rows, share), jnp.bfloat16)] * members,
        grid=(4,),
        in_specs=[SMEM, part, part, pl.BlockSpec(filter_taps.shape[::-1], lambda i: (0, 0))],
        out_specs=[VMEM] * members,
        compiler_params=pltpu.CompilerParams(vmem_limit_bytes=24 * 2**20),
        cost_estimate=COST,
        name="gated_input",
    )(plan, in_hbm(key_gate), in_hbm(value_input), in_hbm(filter_taps.T))


def finish_kernel(members, plan_ref, *refs):
    parts = refs[:members]
    key_ref, value_ref, key_out, value_out, taps_out = refs[members:]
    position = plan_ref[POSITION]
    width, channels = key_ref.shape
    share = channels // members
    groups = taps_out.shape[0] // members
    for step in range(members):
        at = position ^ step
        columns = pl.ds(pl.multiple_of(at * share, share), share)
        grad = parts[step][:width].astype(jnp.float32)
        key_out[:, columns] = (grad * value_ref[:, columns].astype(jnp.float32)).astype(
            jnp.bfloat16
        )
        value_out[:, columns] = (grad * key_ref[:, columns].astype(jnp.float32)).astype(
            jnp.bfloat16
        )
        taps = [
            parts[step][width + chunk * groups : width + (chunk + 1) * groups, :]
            for chunk in range(width // share)
        ]
        taps_out[pl.ds(pl.multiple_of(at * groups, groups), groups), :] = jnp.concatenate(
            taps, axis=1
        ).astype(jnp.float32)


def finished(plan, parts, key_gate, value_input, groups):
    members = len(parts)
    width, channels = key_gate.shape
    array = jax.ShapeDtypeStruct((width, channels), jnp.bfloat16)
    grad_key, grad_value, taps = pl.pallas_call(
        functools.partial(finish_kernel, members),
        out_shape=[array, array, jax.ShapeDtypeStruct((groups, width), jnp.float32)],
        in_specs=[SMEM] + [VMEM] * (members + 2),
        out_specs=[VMEM] * 3,
        compiler_params=pltpu.CompilerParams(vmem_limit_bytes=24 * 2**20),
        cost_estimate=COST,
        name="input_gradients",
    )(plan, *parts, key_gate, value_input)
    return grad_key, grad_value, taps.T


def swapped(array, axis, step):
    size = lax.axis_size(axis)
    return lax.ppermute(array, axis, [(i, i ^ step) for i in range(size)])


def traded(pieces, axis):
    return [pieces[0]] + [swapped(pieces[step], axis, step) for step in range(1, len(pieces))]


def cut(array, position, members, axis):
    width = array.shape[axis] // members
    return [
        lax.dynamic_slice_in_dim(array, (position ^ step) * width, width, axis)
        for step in range(members)
    ]


def joined(pieces, position, axis):
    members = len(pieces)
    width = pieces[0].shape[axis]
    shape = list(pieces[0].shape)
    shape[axis] = members * width
    whole = jnp.zeros(shape, pieces[0].dtype)
    for step in range(members):
        whole = lax.dynamic_update_slice_in_dim(
            whole, pieces[step], (position ^ step) * width, axis
        )
    return whole


def wide(array):
    return array.astype(jnp.float32)


def hop(array, pairs):
    return lax.ppermute(
        array, "tp", [(2 * i + core, 2 * j + core) for i, j in pairs for core in range(2)]
    )


INWARD = ((0, 1), (3, 2))
ACROSS = ((1, 2), (2, 1))
OUTWARD = ((1, 0), (2, 3))
OWN, NEAR, MIDDLE, FAR = range(4)
CHIPS = ((0, 1, 2, 3), (1, 0, 3, 2), (2, 2, 1, 1), (3, 3, 0, 0))


def plan_kernel(who_ref, plan_ref):
    place = who_ref[1]
    chip, core = place // 2, place % 2
    for number, table in enumerate(CHIPS):
        source = jnp.where(
            chip < 2,
            jnp.where(chip == 0, table[0], table[1]),
            jnp.where(chip == 2, table[2], table[3]),
        )
        plan_ref[2 * number] = 2 * source + core
        plan_ref[2 * number + 1] = 2 * source + 1 - core
    plan_ref[POSITION] = who_ref[0]


def planned():
    who = jnp.stack([lax.axis_index("ctx"), lax.axis_index("tp")]).astype(jnp.int32)
    return pl.pallas_call(
        plan_kernel,
        out_shape=jax.ShapeDtypeStruct((POSITION + 1,), jnp.int32),
        in_specs=[SMEM],
        out_specs=SMEM,
        compiler_params=pltpu.CompilerParams(vmem_limit_bytes=2**20),
        cost_estimate=COST,
        name="plan",
    )(who)


def pass_kernel(*refs):
    del refs


def held_until(values, after):
    return pl.pallas_call(
        pass_kernel,
        out_shape=[jax.ShapeDtypeStruct(value.shape, value.dtype) for value in values],
        in_specs=[ANYWHERE] * (len(values) + len(after)),
        out_specs=[ANYWHERE] * len(values),
        input_output_aliases={number: number for number in range(len(values))},
        compiler_params=pltpu.CompilerParams(vmem_limit_bytes=2**20),
        cost_estimate=COST,
        name="held",
    )(*values, *after)


def add_kernel(*refs):
    refs[-1][...] = sum(wide(ref[...]) for ref in refs[:-1]).astype(jnp.bfloat16)


def added(*arrays):
    rows, width = arrays[0].shape
    part = pl.BlockSpec((rows // 4, width), lambda i: (i, 0))
    return pl.pallas_call(
        add_kernel,
        out_shape=jax.ShapeDtypeStruct((rows, width), jnp.bfloat16),
        grid=(4,),
        in_specs=[part] * len(arrays),
        out_specs=part,
        compiler_params=pltpu.CompilerParams(vmem_limit_bytes=8 * 2**20),
        cost_estimate=COST,
        name="added",
    )(*arrays)


def gate_kernel(members, plan_ref, *refs):
    parts = refs[:members]
    query_ref, gated_ref, conv_ref = refs[members:]
    position = plan_ref[POSITION]
    share = parts[0].shape[1]
    for step in range(members):
        columns = pl.ds(pl.multiple_of((position ^ step) * share, share), share)
        conv = parts[step][...]
        conv_ref[:, columns] = conv
        gated_ref[:, columns] = (wide(conv) * wide(query_ref[:, columns])).astype(jnp.bfloat16)


def gated(plan, parts, query_gate):
    array = jax.ShapeDtypeStruct(query_gate.shape, jnp.bfloat16)
    return pl.pallas_call(
        functools.partial(gate_kernel, len(parts)),
        out_shape=[array, array],
        in_specs=[SMEM] + [VMEM] * (len(parts) + 1),
        out_specs=[VMEM] * 2,
        compiler_params=pltpu.CompilerParams(vmem_limit_bytes=8 * 2**20),
        cost_estimate=COST,
        name="gated_output",
    )(plan, *parts, query_gate)


def product_kernel(tiles, count, extra, _, data_ref, weight_ref, *refs):
    more, outputs = refs[:extra], refs[-count:]
    product = jnp.dot(data_ref[...], weight_ref[...], preferred_element_type=jnp.float32)
    for number, out_ref in enumerate(outputs):

        @pl.when(pl.program_id(0) // tiles == number)
        def _(number=number, out_ref=out_ref):
            total = product + wide(more[number][...]) if more else product
            out_ref[...] = total.astype(jnp.bfloat16)


def column_products(plan, data, out_weight, first, count, other, more=(), after=()):
    rows, depth = data.shape
    width = data.shape[1]
    tile = min(width, 512)
    tiles = width // tile

    def column(number):
        return pl.BlockSpec(
            (rows, tile), lambda i, at: (0, jnp.clip(i - number * tiles, 0, tiles - 1))
        )

    def weights(i, at):
        return 0, at[2 * (first - i // tiles) + other] * tiles + i % tiles

    columns = [column(number) for number in range(count)]
    return pl.pallas_call(
        functools.partial(product_kernel, tiles, count, len(more)),
        out_shape=[jax.ShapeDtypeStruct((rows, width), jnp.bfloat16)] * count,
        grid_spec=pltpu.PrefetchScalarGridSpec(
            num_scalar_prefetch=1,
            grid=(count * tiles,),
            in_specs=[
                pl.BlockSpec((rows, depth), lambda i, at: (0, 0)),
                pl.BlockSpec((depth, tile), weights),
            ]
            + columns[: len(more)]
            + [ANYWHERE] * len(after),
            out_specs=columns,
        ),
        compiler_params=pltpu.CompilerParams(vmem_limit_bytes=24 * 2**20),
        cost_estimate=COST,
        name="projection_blocks",
    )(plan, data, in_hbm(out_weight), *more, *after)


def cotangent_kernel(count, begin, last, members, plan_ref, weight_ref, *refs):
    blocks, refs = refs[:count], refs[count:]
    step = pl.program_id(0)
    total = refs[-1]

    @pl.when(step == 0)
    def _():
        total[...] = jnp.zeros_like(total) if begin else refs[0][...]

    for number, block in enumerate(blocks):

        @pl.when(step == number)
        def _(block=block):
            total[...] += lax.dot_general(
                block[...], weight_ref[...], NT, preferred_element_type=jnp.float32
            )

    if last:
        conv_ref, query_ref = refs[1:3]
        grad_ref, parts = refs[-2 - members], refs[-1 - members : -1]

        @pl.when(step == count - 1)
        def _():
            dgated = wide(total[...].astype(jnp.bfloat16))
            grad_ref[...] = (dgated * wide(conv_ref[...])).astype(jnp.bfloat16)
            share = parts[0].shape[1]
            for step in range(members):
                start = pl.multiple_of((plan_ref[POSITION] ^ step) * share, share)
                columns = pl.ds(start, share)
                dgated = wide(total[:, columns].astype(jnp.bfloat16))
                parts[step][...] = (dgated * wide(query_ref[:, columns])).astype(jnp.bfloat16)


def cotangent_products(
    plan, first, blocks, out_weight, start=None, gates=(), after=(), members=0
):
    parts = [part for block in blocks for part in (block, swapped(block, "tp", 1))]
    rows, width = blocks[0].shape
    channels = out_weight.shape[0]
    count = len(parts)
    whole = pl.BlockSpec((rows, channels), lambda i, at: (0, 0))
    part = pl.BlockSpec((rows, width), lambda i, at: (0, 0))
    piece = pl.BlockSpec((rows, channels // max(members, 1)), lambda i, at: (0, 0))
    array = jax.ShapeDtypeStruct((rows, channels), jnp.bfloat16)
    cut_array = jax.ShapeDtypeStruct((rows, channels // max(members, 1)), jnp.bfloat16)
    begin, last = start is None, bool(gates)
    extra = (() if begin else (start,)) + tuple(gates)
    return pl.pallas_call(
        functools.partial(cotangent_kernel, count, begin, last, members),
        out_shape=[array] + [cut_array] * members
        if last
        else jax.ShapeDtypeStruct((rows, channels), jnp.float32),
        grid_spec=pltpu.PrefetchScalarGridSpec(
            num_scalar_prefetch=1,
            grid=(count,),
            in_specs=[pl.BlockSpec((channels, width), lambda i, at: (0, at[2 * first + i]))]
            + [part] * count
            + [whole] * len(extra)
            + [ANYWHERE] * len(after),
            out_specs=[whole] + [piece] * members if last else whole,
            scratch_shapes=[pltpu.VMEM((rows, channels), jnp.float32)] if last else [],
        ),
        compiler_params=pltpu.CompilerParams(vmem_limit_bytes=24 * 2**20),
        cost_estimate=COST,
        name="cotangent_blocks",
    )(plan, in_hbm(out_weight), *parts, *extra, *after)


def packed_parts(position, key_gate, value_input, filter_taps, members, scale):
    length, channels = key_gate.shape
    share = channels // members
    product_in = (wide(key_gate) * wide(value_input)).astype(jnp.bfloat16)
    tap_rows = (filter_taps * scale).astype(jnp.bfloat16).T
    owned = filter_taps.shape[1] // members
    chunks = length // share
    packed = []
    pieces = cut(product_in, position, members, 1)
    for piece, taps in zip(pieces, cut(tap_rows, position, members, 0)):
        taps = taps.reshape(owned, chunks, share).transpose(1, 0, 2)
        taps = jnp.pad(taps, ((0, 0), (0, padded(owned) - owned), (0, 0)))
        packed.append(jnp.concatenate([piece, taps.reshape(-1, share)], axis=0))
    return packed


def unpacked_parts(position, parts, key_gate, value_input, groups):
    length, channels = key_gate.shape
    members = len(parts)
    share = channels // members
    owned = groups // members
    chunks = length // share
    input_grad = wide(joined([part[:length] for part in parts], position, 1))
    filter_parts = [
        part[length:]
        .reshape(chunks, padded(owned), share)[:, :owned]
        .transpose(1, 0, 2)
        .reshape(owned, length)
        for part in parts
    ]
    grad_filter = wide(joined(filter_parts, position, 0)).T
    grad_key = (input_grad * wide(value_input)).astype(jnp.bfloat16)
    grad_value = (input_grad * wide(key_gate)).astype(jnp.bfloat16)
    return grad_key, grad_value, grad_filter


def in_line(
    query_gate, key_gate, value_input, filter_taps, out_weight, out_grad, members, scale
):
    length, channels = query_gate.shape
    groups = filter_taps.shape[1]
    per_group = channels // groups
    plan = planned()
    near, cross = hop(out_grad, INWARD + OUTWARD), hop(out_grad, ACROSS)
    total = cotangent_products(plan, OWN, (out_grad,), out_weight)

    packed = prepare(plan, key_gate, value_input, filter_taps, members, scale)
    input_parts = traded(packed, "ctx")
    conv_parts = convolve(plan, input_parts, length, per_group, (total,))
    *conv_parts, near, cross = held_until([*conv_parts, near, cross], ())
    far, skip = hop(near, ACROSS), hop(cross, OUTWARD)
    gated_out, convolved = gated(plan, traded(conv_parts, "ctx"), query_gate)

    def product(first, count, other, more=(), after=()):
        return column_products(plan, gated_out, out_weight, first, count, other, more, after)

    given_far, given_middle = product(FAR, 2, 1)
    far, skip = held_until([far, skip], (given_far,))
    last = hop(far, OUTWARD)
    middle_block = added(cross, skip)
    (first,) = product(FAR, 1, 0, (swapped(given_far, "tp", 1),))
    one = hop(first, INWARD)
    (second,) = product(MIDDLE, 1, 0, (swapped(given_middle, "tp", 1),), (first,))
    near, middle_block = held_until([near, middle_block], (first,))
    total = cotangent_products(plan, NEAR, (near, middle_block), out_weight, total)
    given_near, given_own = product(NEAR, 2, 1, (), (second,))
    (one,) = held_until([one], (total, given_near))
    through = added(first, one)
    two_a = hop(through, ACROSS)
    (second,) = held_until([second], (one,))
    two_b = hop(second, INWARD)

    (last,) = held_until([last], (total, given_near))
    grad_query, *grad_parts = cotangent_products(
        plan,
        FAR,
        (added(far, last),),
        out_weight,
        total,
        (convolved, query_gate),
        (through,),
        members,
    )
    received = (swapped(given_near, "tp", 1), swapped(given_own, "tp", 1))
    third, own = product(NEAR, 2, 0, received, (grad_parts[0],))
    grad_parts = traded(grad_parts, "ctx")

    two_a, two_b = held_until([two_a, two_b], tuple(grad_parts[1:]))
    third, second = added(third, two_a), added(second, two_b)
    back_parts = correlate(plan, input_parts, grad_parts, per_group, scale, (third, second))
    projected = added(own, hop(third, OUTWARD + INWARD), hop(second, ACROSS))
    back_parts = traded(back_parts, "ctx")
    return projected, grad_query, *finished(plan, back_parts, key_gate, value_input, groups)


def anywhere(
    query_gate, key_gate, value_input, filter_taps, out_weight, out_grad, members, scale
):
    length, channels = query_gate.shape
    groups = filter_taps.shape[1]
    per_group = channels // groups
    position = lax.axis_index("ctx")
    plan = jnp.full((POSITION + 1,), position, jnp.int32)
    packed = packed_parts(position, key_gate, value_input, filter_taps, members, scale)
    input_parts = traded(packed, "ctx")
    conv_parts = traded(convolve(plan, input_parts, length, per_group), "ctx")
    convolved = joined(conv_parts, position, 1)
    gated_out = (wide(query_gate) * wide(convolved)).astype(jnp.bfloat16)
    partial_value = jnp.dot(gated_out, out_weight, preferred_element_type=jnp.float32)
    projected = lax.psum_scatter(
        partial_value.astype(jnp.bfloat16), "tp", scatter_dimension=1, tiled=True
    )
    dgated = jnp.einsum(
        "tk,ck->tc",
        lax.all_gather(out_grad, "tp", axis=1, tiled=True),
        out_weight,
        preferred_element_type=jnp.float32,
    ).astype(jnp.bfloat16)
    grad_query = (wide(dgated) * wide(convolved)).astype(jnp.bfloat16)
    conv_grad = (wide(dgated) * wide(query_gate)).astype(jnp.bfloat16)
    grad_parts = traded(cut(conv_grad, position, members, 1), "ctx")
    back_parts = correlate(plan, input_parts, grad_parts, per_group, scale)
    back_parts = traded(back_parts, "ctx")
    return (
        projected,
        grad_query,
        *unpacked_parts(position, back_parts, key_gate, value_input, groups),
    )


def local(query_gate, key_gate, value_input, filter_taps, out_weight, out_grad):
    length, channels = query_gate.shape
    groups = filter_taps.shape[1]
    members = lax.axis_size("ctx")
    scale = 1.0 / math.sqrt(length * members)
    fits = channels // members % 128 == 0 and groups // members % 16 == 0
    body = in_line if lax.axis_size("tp") == 8 and fits else anywhere
    return body(
        query_gate, key_gate, value_input, filter_taps, out_weight, out_grad, members, scale
    )


def solution(mesh):
    both = P("ctx", "tp")
    return jax.shard_map(
        local,
        mesh=mesh,
        in_specs=(both, both, both, both, P("tp", None), both),
        out_specs=(both,) * 5,
        check_vma=False,
    )
```

```python
import functools
import math
import jax
import jax.numpy as jnp
from jax import lax
from jax.experimental import pallas as pl
from jax.experimental.pallas import tpu as pltpu
from jax.sharding import PartitionSpec as P

BLOCK = 128
POSITION = 8
NT = (((1,), (1,)), ((), ()))
COST = pl.CostEstimate(flops=2**20, bytes_accessed=2**12, transcendentals=0)


def lag_matrix(row, length):
    lanes = lax.broadcasted_iota(jnp.int32, (BLOCK, BLOCK), 1)
    rows = lax.broadcasted_iota(jnp.int32, (BLOCK, BLOCK), 0)
    spread = pltpu.roll(
        jnp.broadcast_to(row, (BLOCK, length)), 0, axis=1, stride=1, stride_axis=0
    )
    first = jnp.where(lanes >= rows, spread[:, :BLOCK], 0.0)
    return jnp.concatenate(
        [first.astype(jnp.bfloat16), spread[:, BLOCK:].astype(jnp.bfloat16)], axis=1
    )


def stacked(ref, start, rows, members, width):
    pieces = []
    for member in range(members):
        part = ref[member, pl.ds(start, rows), :]
        for at in range(0, width, BLOCK):
            pieces.append(part[:, at : at + BLOCK])
    return jnp.concatenate(pieces, axis=0)


def spread_out(ref, start, rows, value, members, width):
    per_member = width // BLOCK
    for member in range(members):
        base = member * per_member * rows
        parts = [value[base + i * rows : base + (i + 1) * rows] for i in range(per_member)]
        ref[member, pl.ds(start, rows), :] = jnp.concatenate(parts, axis=1)


def padded(groups):
    return -(-groups // 16) * 16


def load_taps(tap_scr, packed, at, width):
    groups, channels = tap_scr.shape[0], packed.shape[1]
    rows = padded(groups)
    parts = [
        packed[width + chunk * rows : width + (chunk + 1) * rows, :].astype(jnp.float32)
        for chunk in range(width // channels)
    ]
    start = pl.multiple_of(at * width, width)
    tap_scr[:, pl.ds(start, width)] = jnp.concatenate(parts, axis=1)[:groups]


def forward_kernel(members, per_group, width, plan_ref, *refs):
    inputs, outputs = refs[:members], refs[-members - 3 : -3]
    tap_scr, in_scr, out_scr = refs[-3:]
    position = plan_ref[POSITION]
    channels = inputs[0].shape[1]
    groups = channels // per_group
    length = members * width
    blocks = length // BLOCK
    for step in range(members):
        at = position ^ step
        in_scr[at] = inputs[step][:width].T
        load_taps(tap_scr, inputs[step], at, width)

    def one_group(group, carry):
        start = pl.multiple_of(group * per_group, per_group)
        lags = lag_matrix(tap_scr[pl.ds(group, 1), :], length)
        data = stacked(in_scr, start, per_group, members, width)
        total = [jnp.zeros((per_group, BLOCK), jnp.float32) for _ in range(blocks)]
        for offset in range(0, blocks, 2):
            rows = (blocks - offset) * per_group
            result = jnp.dot(
                data[:rows],
                lags[:, offset * BLOCK : (offset + 2) * BLOCK],
                preferred_element_type=jnp.float32,
            )
            for side in range(2):
                for source in range(blocks - offset - side):
                    total[source + offset + side] += result[
                        source * per_group : (source + 1) * per_group,
                        side * BLOCK : (side + 1) * BLOCK,
                    ]
        value = jnp.concatenate(total, axis=0).astype(jnp.bfloat16)
        spread_out(out_scr, start, per_group, value, members, width)
        return carry

    lax.fori_loop(0, groups, one_group, 0, unroll=2)
    for step in range(members):
        outputs[step][...] = out_scr[position ^ step].T


def backward_kernel(members, per_group, scale, width, plan_ref, *refs):
    inputs, cotangents = refs[:members], refs[members : 2 * members]
    outputs = refs[-members - 6 : -6]
    tap_scr, in_scr, cot_scr, out_scr, grad_scr, pad_scr = refs[-6:]
    position = plan_ref[POSITION]
    channels = inputs[0].shape[1]
    groups = channels // per_group
    length = members * width
    blocks = length // BLOCK
    depth = blocks * per_group
    for step in range(members):
        at = position ^ step
        in_scr[at] = inputs[step][:width].T
        cot_scr[at] = cotangents[step][...].T
        load_taps(tap_scr, inputs[step], at, width)
    pad_scr[...] = jnp.zeros_like(pad_scr)
    rows_of = lax.broadcasted_iota(jnp.int32, (BLOCK, BLOCK), 0)
    lanes_of = lax.broadcasted_iota(jnp.int32, (BLOCK, BLOCK), 1)
    mirror = (rows_of + lanes_of == BLOCK - 1).astype(jnp.bfloat16)

    def one_group(group, carry):
        start = pl.multiple_of(group * per_group, per_group)
        lags = lag_matrix(tap_scr[pl.ds(group, 1), :], length)
        data = stacked(in_scr, start, per_group, members, width)
        cot = stacked(cot_scr, start, per_group, members, width)
        pad_scr[:depth, :BLOCK] = cot
        pad_scr[: depth - per_group, BLOCK:] = cot[per_group:]
        flipped = lax.dot_general(
            mirror, data, NT, preferred_element_type=jnp.float32
        ).astype(jnp.bfloat16)
        total = jnp.zeros((depth, BLOCK), jnp.float32)
        products = []
        for offset in range(0, blocks, 2):
            rows = depth - offset * per_group
            pair = pad_scr[offset * per_group : offset * per_group + depth, :]
            result = lax.dot_general(
                pair[:rows],
                lags[:, offset * BLOCK : (offset + 2) * BLOCK],
                NT,
                preferred_element_type=jnp.float32,
            )
            if rows < depth:
                result = jnp.concatenate(
                    [result, jnp.zeros((depth - rows, BLOCK), jnp.float32)], axis=0
                )
            total = total + result
            products.append(jnp.dot(flipped, pair, preferred_element_type=jnp.float32))
        spread_out(
            out_scr, start, per_group, total.astype(jnp.bfloat16), members, width
        )
        kept = jnp.where(rows_of + lanes_of >= BLOCK - 1, products[0][:, :BLOCK], 0.0)
        product = jnp.concatenate([kept, products[0][:, BLOCK:], *products[1:]], axis=1)
        product = pltpu.roll(
            product, length - (BLOCK - 1), axis=1, stride=1, stride_axis=0
        )
        grad_scr[pl.ds(group, 1), :] = jnp.sum(product, axis=0, keepdims=True) * scale
        return carry

    lax.fori_loop(0, groups, one_group, 0, unroll=2)
    for step in range(members):
        at = position ^ step
        outputs[step][:width] = out_scr[at].T
        rows = padded(groups)
        whole = grad_scr[:, pl.ds(pl.multiple_of(at * width, width), width)].astype(jnp.bfloat16)
        if rows > groups:
            blank = jnp.zeros((rows - groups, width), jnp.bfloat16)
            whole = jnp.concatenate([whole, blank], axis=0)
        for chunk in range(width // channels):
            outputs[step][width + chunk * rows : width + (chunk + 1) * rows, :] = whole[
                :, chunk * channels : (chunk + 1) * channels
            ]


VMEM = pl.BlockSpec(memory_space=pltpu.VMEM)
ANYWHERE = pl.BlockSpec(memory_space=pl.ANY)
SMEM = pl.BlockSpec(memory_space=pltpu.SMEM)


def convolve(plan, inputs, width, per_group, after=()):
    members = len(inputs)
    channels = inputs[0].shape[1]
    length = members * width
    return pl.pallas_call(
        functools.partial(forward_kernel, members, per_group, width),
        out_shape=[jax.ShapeDtypeStruct((width, channels), jnp.bfloat16)] * members,
        in_specs=[SMEM] + [VMEM] * members + [ANYWHERE] * len(after),
        out_specs=[VMEM] * members,
        scratch_shapes=[
            pltpu.VMEM((channels // per_group, length), jnp.float32),
            pltpu.VMEM((members, channels, width), jnp.bfloat16),
            pltpu.VMEM((members, channels, width), jnp.bfloat16),
        ],
        compiler_params=pltpu.CompilerParams(vmem_limit_bytes=24 * 2**20),
        cost_estimate=COST,
        name="causal_conv",
    )(plan, *inputs, *after)


def correlate(plan, inputs, cotangents, per_group, scale, after=()):
    members = len(inputs)
    width, channels = cotangents[0].shape
    length = members * width
    groups = channels // per_group
    return pl.pallas_call(
        functools.partial(backward_kernel, members, per_group, scale, width),
        out_shape=[jax.ShapeDtypeStruct(inputs[0].shape, jnp.bfloat16)] * members,
        in_specs=[SMEM] + [VMEM] * (2 * members) + [ANYWHERE] * len(after),
        out_specs=[VMEM] * members,
        scratch_shapes=[
            pltpu.VMEM((groups, length), jnp.float32),
            pltpu.VMEM((members, channels, width), jnp.bfloat16),
            pltpu.VMEM((members, channels, width), jnp.bfloat16),
            pltpu.VMEM((members, channels, width), jnp.bfloat16),
            pltpu.VMEM((groups, length), jnp.float32),
            pltpu.VMEM((2 * length // BLOCK * per_group, 2 * BLOCK), jnp.bfloat16),
        ],
        compiler_params=pltpu.CompilerParams(vmem_limit_bytes=24 * 2**20),
        cost_estimate=COST,
        name="causal_conv_grads",
    )(plan, *inputs, *cotangents, *after)


def in_hbm(array):
    return pltpu.with_memory_space_constraint(array, pltpu.HBM)


def prepare_kernel(members, scale, who_ref, key_ref, value_ref, taps_ref, *outputs):
    position = who_ref[0]
    step_no = pl.program_id(0)
    rows, channels = key_ref.shape
    share = channels // members
    groups = taps_ref.shape[0] // members
    total_width = taps_ref.shape[1]
    for step in range(members):
        at = position ^ step
        columns = pl.ds(pl.multiple_of(at * share, share), share)
        product = key_ref[:, columns].astype(jnp.float32) * value_ref[:, columns].astype(
            jnp.float32
        )
        here = pl.ds(pl.multiple_of(step_no * rows, rows), rows)
        outputs[step][here, :] = product.astype(jnp.bfloat16)

    @pl.when(step_no == 0)
    def _():
        for step in range(members):
            at = position ^ step
            taps = taps_ref[pl.ds(pl.multiple_of(at * groups, groups), groups), :]
            taps = (taps * scale).astype(jnp.bfloat16)
            for chunk in range(total_width // share):
                start = total_width + chunk * groups
                outputs[step][start : start + groups, :] = taps[
                    :, chunk * share : (chunk + 1) * share
                ]


def prepare(who, key_gate, value_input, filter_taps, members, scale):
    width, channels = key_gate.shape
    share = channels // members
    rows = width + filter_taps.size // members // share
    tile = width // 4
    part = pl.BlockSpec((tile, channels), lambda i: (i, 0))
    return pl.pallas_call(
        functools.partial(prepare_kernel, members, scale),
        out_shape=[jax.ShapeDtypeStruct((rows, share), jnp.bfloat16)] * members,
        grid=(4,),
        in_specs=[SMEM, part, part, pl.BlockSpec(filter_taps.shape[::-1], lambda i: (0, 0))],
        out_specs=[VMEM] * members,
        compiler_params=pltpu.CompilerParams(vmem_limit_bytes=24 * 2**20),
        cost_estimate=COST,
        name="gated_input",
    )(who, in_hbm(key_gate), in_hbm(value_input), in_hbm(filter_taps.T))


def finish_kernel(members, plan_ref, *refs):
    parts = refs[:members]
    key_ref, value_ref = refs[members : members + 2]
    key_out, value_out, taps_out = refs[-3:]
    position = plan_ref[POSITION]
    step_no = pl.program_id(0)
    rows, channels = key_ref.shape
    share = channels // members
    groups, width = taps_out.shape
    groups = groups // members
    here = pl.ds(pl.multiple_of(step_no * rows, rows), rows)
    for step in range(members):
        at = position ^ step
        columns = pl.ds(pl.multiple_of(at * share, share), share)
        grad = parts[step][here, :].astype(jnp.float32)
        key_out[:, columns] = (grad * value_ref[:, columns].astype(jnp.float32)).astype(
            jnp.bfloat16
        )
        value_out[:, columns] = (grad * key_ref[:, columns].astype(jnp.float32)).astype(
            jnp.bfloat16
        )

    @pl.when(step_no == 0)
    def _():
        for step in range(members):
            at = position ^ step
            taps = [
                parts[step][width + chunk * groups : width + (chunk + 1) * groups, :]
                for chunk in range(width // share)
            ]
            taps_out[pl.ds(pl.multiple_of(at * groups, groups), groups), :] = jnp.concatenate(
                taps, axis=1
            ).astype(jnp.float32)


def finished(plan, parts, key_gate, value_input, groups, after=()):
    members = len(parts)
    width, channels = key_gate.shape
    array = jax.ShapeDtypeStruct((width, channels), jnp.bfloat16)
    part = pl.BlockSpec((width // 4, channels), lambda i: (i, 0))
    grad_key, grad_value, taps = pl.pallas_call(
        functools.partial(finish_kernel, members),
        out_shape=[array, array, jax.ShapeDtypeStruct((groups, width), jnp.float32)],
        grid=(4,),
        in_specs=[SMEM] + [VMEM] * members + [part] * 2 + [ANYWHERE] * len(after),
        out_specs=[part, part, pl.BlockSpec((groups, width), lambda i: (0, 0))],
        compiler_params=pltpu.CompilerParams(vmem_limit_bytes=24 * 2**20),
        cost_estimate=COST,
        name="input_gradients",
    )(plan, *parts, in_hbm(key_gate), in_hbm(value_input), *after)
    return grad_key, grad_value, taps.T


def swapped(array, axis, step):
    size = lax.axis_size(axis)
    return lax.ppermute(array, axis, [(i, i ^ step) for i in range(size)])


def traded(pieces, axis):
    return [pieces[0]] + [swapped(pieces[step], axis, step) for step in range(1, len(pieces))]


def cut(array, position, members, axis):
    width = array.shape[axis] // members
    return [
        lax.dynamic_slice_in_dim(array, (position ^ step) * width, width, axis)
        for step in range(members)
    ]


def joined(pieces, position, axis):
    members = len(pieces)
    width = pieces[0].shape[axis]
    shape = list(pieces[0].shape)
    shape[axis] = members * width
    whole = jnp.zeros(shape, pieces[0].dtype)
    for step in range(members):
        whole = lax.dynamic_update_slice_in_dim(
            whole, pieces[step], (position ^ step) * width, axis
        )
    return whole


def wide(array):
    return array.astype(jnp.float32)


def hop(array, pairs):
    return lax.ppermute(
        array, "tp", [(2 * i + core, 2 * j + core) for i, j in pairs for core in range(2)]
    )


INWARD = ((0, 1), (3, 2))
ACROSS = ((1, 2), (2, 1))
OUTWARD = ((1, 0), (2, 3))
OWN, NEAR, MIDDLE, FAR = range(4)
CHIPS = ((0, 1, 2, 3), (1, 0, 3, 2), (2, 2, 1, 1), (3, 3, 0, 0))


def plan_kernel(who_ref, plan_ref):
    place = who_ref[1]
    chip, core = place // 2, place % 2
    for number, table in enumerate(CHIPS):
        source = jnp.where(
            chip < 2,
            jnp.where(chip == 0, table[0], table[1]),
            jnp.where(chip == 2, table[2], table[3]),
        )
        plan_ref[2 * number] = 2 * source + core
        plan_ref[2 * number + 1] = 2 * source + 1 - core
    plan_ref[POSITION] = who_ref[0]


def planned(who):
    return pl.pallas_call(
        plan_kernel,
        out_shape=jax.ShapeDtypeStruct((POSITION + 1,), jnp.int32),
        in_specs=[SMEM],
        out_specs=SMEM,
        compiler_params=pltpu.CompilerParams(vmem_limit_bytes=2**20),
        cost_estimate=COST,
        name="plan",
    )(who)


def pass_kernel(*refs):
    del refs


def held_until(values, after):
    return pl.pallas_call(
        pass_kernel,
        out_shape=[jax.ShapeDtypeStruct(value.shape, value.dtype) for value in values],
        in_specs=[ANYWHERE] * (len(values) + len(after)),
        out_specs=[ANYWHERE] * len(values),
        input_output_aliases={number: number for number in range(len(values))},
        compiler_params=pltpu.CompilerParams(vmem_limit_bytes=2**20),
        cost_estimate=COST,
        name="held",
    )(*values, *after)


def add_kernel(*refs):
    refs[-1][...] = sum(wide(ref[...]) for ref in refs[:-1]).astype(jnp.bfloat16)


def added(*arrays):
    rows, width = arrays[0].shape
    part = pl.BlockSpec((rows // 4, width), lambda i: (i, 0))
    return pl.pallas_call(
        add_kernel,
        out_shape=jax.ShapeDtypeStruct((rows, width), jnp.bfloat16),
        grid=(4,),
        in_specs=[part] * len(arrays),
        out_specs=part,
        compiler_params=pltpu.CompilerParams(vmem_limit_bytes=8 * 2**20),
        cost_estimate=COST,
        name="added",
    )(*arrays)


def gate_kernel(members, plan_ref, *refs):
    parts = refs[:members]
    query_ref, gated_ref, conv_ref = refs[members:]
    position = plan_ref[POSITION]
    share = parts[0].shape[1]
    for step in range(members):
        columns = pl.ds(pl.multiple_of((position ^ step) * share, share), share)
        conv = parts[step][...]
        conv_ref[:, columns] = conv
        gated_ref[:, columns] = (wide(conv) * wide(query_ref[:, columns])).astype(jnp.bfloat16)


def gated(plan, parts, query_gate):
    array = jax.ShapeDtypeStruct(query_gate.shape, jnp.bfloat16)
    return pl.pallas_call(
        functools.partial(gate_kernel, len(parts)),
        out_shape=[array, array],
        in_specs=[SMEM] + [VMEM] * (len(parts) + 1),
        out_specs=[VMEM] * 2,
        compiler_params=pltpu.CompilerParams(vmem_limit_bytes=8 * 2**20),
        cost_estimate=COST,
        name="gated_output",
    )(plan, *parts, query_gate)


def product_kernel(steps, joins, extra, _, data_ref, weight_ref, *refs):
    more, outputs = refs[:extra], refs[-(steps // joins) :]
    product = jnp.dot(data_ref[...], weight_ref[...], preferred_element_type=jnp.float32)
    for number in range(steps):
        out_ref = outputs[number // joins]
        wide_out = out_ref.shape[1] > product.shape[1]

        @pl.when(pl.program_id(0) == number)
        def _(number=number, out_ref=out_ref, wide_out=wide_out):
            total = product + wide(more[number][...]) if more else product
            if wide_out:
                width = product.shape[1]
                at = number % joins * width
                out_ref[:, at : at + width] = total.astype(jnp.bfloat16)
            else:
                out_ref[...] = total.astype(jnp.bfloat16)


def column_products(
    plan, data, out_weight, first, count, other, more=(), after=(), tiles=1, joins=1
):
    rows, depth = data.shape
    width = data.shape[1]
    tile = width // tiles
    steps = count * tiles

    def weights(i, at):
        return 0, at[2 * (first - i // tiles) + other] * tiles + i % tiles

    def whole(array_width):
        return pl.BlockSpec((rows, array_width), lambda i, at: (0, 0))

    return pl.pallas_call(
        functools.partial(product_kernel, steps, joins, len(more)),
        out_shape=[jax.ShapeDtypeStruct((rows, tile * joins), jnp.bfloat16)] * (steps // joins),
        grid_spec=pltpu.PrefetchScalarGridSpec(
            num_scalar_prefetch=1,
            grid=(steps,),
            in_specs=[whole(depth), pl.BlockSpec((depth, tile), weights)]
            + [whole(tile)] * len(more)
            + [ANYWHERE] * len(after),
            out_specs=[whole(tile * joins)] * (steps // joins),
        ),
        compiler_params=pltpu.CompilerParams(vmem_limit_bytes=24 * 2**20),
        cost_estimate=COST,
        name="projection_blocks",
    )(plan, data, in_hbm(out_weight), *more, *after)


def cotangent_kernel(count, begin, last, members, plan_ref, weight_ref, *refs):
    blocks, refs = refs[:count], refs[count:]
    step = pl.program_id(0)
    total = refs[-1]

    @pl.when(step == 0)
    def _():
        total[...] = jnp.zeros_like(total) if begin else refs[0][...]

    for number, block in enumerate(blocks):

        @pl.when(step == number)
        def _(block=block):
            total[...] += lax.dot_general(
                block[...], weight_ref[...], NT, preferred_element_type=jnp.float32
            )

    if last:
        conv_ref, query_ref = refs[1:3]
        grad_ref, parts = refs[-2 - members], refs[-1 - members : -1]

        @pl.when(step == count - 1)
        def _():
            dgated = wide(total[...].astype(jnp.bfloat16))
            grad_ref[...] = (dgated * wide(conv_ref[...])).astype(jnp.bfloat16)
            share = parts[0].shape[1]
            for step in range(members):
                start = pl.multiple_of((plan_ref[POSITION] ^ step) * share, share)
                columns = pl.ds(start, share)
                dgated = wide(total[:, columns].astype(jnp.bfloat16))
                parts[step][...] = (dgated * wide(query_ref[:, columns])).astype(jnp.bfloat16)


def both(blocks):
    return [part for block in blocks for part in (block, swapped(block, "tp", 1))]


def cotangent_products(
    plan, first, parts, out_weight, start=None, gates=(), after=(), members=0
):
    rows, width = parts[0].shape
    channels = out_weight.shape[0]
    count = len(parts)
    whole = pl.BlockSpec((rows, channels), lambda i, at: (0, 0))
    part = pl.BlockSpec((rows, width), lambda i, at: (0, 0))
    piece = pl.BlockSpec((rows, channels // max(members, 1)), lambda i, at: (0, 0))
    array = jax.ShapeDtypeStruct((rows, channels), jnp.bfloat16)
    cut_array = jax.ShapeDtypeStruct((rows, channels // max(members, 1)), jnp.bfloat16)
    begin, last = start is None, bool(gates)
    extra = (() if begin else (start,)) + tuple(gates)
    return pl.pallas_call(
        functools.partial(cotangent_kernel, count, begin, last, members),
        out_shape=[array] + [cut_array] * members
        if last
        else jax.ShapeDtypeStruct((rows, channels), jnp.float32),
        grid_spec=pltpu.PrefetchScalarGridSpec(
            num_scalar_prefetch=1,
            grid=(count,),
            in_specs=[pl.BlockSpec((channels, width), lambda i, at: (0, at[first + i]))]
            + [part] * count
            + [whole] * len(extra)
            + [ANYWHERE] * len(after),
            out_specs=[whole] + [piece] * members if last else whole,
            scratch_shapes=[pltpu.VMEM((rows, channels), jnp.float32)] if last else [],
        ),
        compiler_params=pltpu.CompilerParams(vmem_limit_bytes=24 * 2**20),
        cost_estimate=COST,
        name="cotangent_blocks",
    )(plan, in_hbm(out_weight), *parts, *extra, *after)


def packed_parts(position, key_gate, value_input, filter_taps, members, scale):
    length, channels = key_gate.shape
    share = channels // members
    product_in = (wide(key_gate) * wide(value_input)).astype(jnp.bfloat16)
    tap_rows = (filter_taps * scale).astype(jnp.bfloat16).T
    owned = filter_taps.shape[1] // members
    chunks = length // share
    packed = []
    pieces = cut(product_in, position, members, 1)
    for piece, taps in zip(pieces, cut(tap_rows, position, members, 0)):
        taps = taps.reshape(owned, chunks, share).transpose(1, 0, 2)
        taps = jnp.pad(taps, ((0, 0), (0, padded(owned) - owned), (0, 0)))
        packed.append(jnp.concatenate([piece, taps.reshape(-1, share)], axis=0))
    return packed


def unpacked_parts(position, parts, key_gate, value_input, groups):
    length, channels = key_gate.shape
    members = len(parts)
    share = channels // members
    owned = groups // members
    chunks = length // share
    input_grad = wide(joined([part[:length] for part in parts], position, 1))
    filter_parts = [
        part[length:]
        .reshape(chunks, padded(owned), share)[:, :owned]
        .transpose(1, 0, 2)
        .reshape(owned, length)
        for part in parts
    ]
    grad_filter = wide(joined(filter_parts, position, 0)).T
    grad_key = (input_grad * wide(value_input)).astype(jnp.bfloat16)
    grad_value = (input_grad * wide(key_gate)).astype(jnp.bfloat16)
    return grad_key, grad_value, grad_filter


def in_line(
    query_gate, key_gate, value_input, filter_taps, out_weight, out_grad, members, scale
):
    length, channels = query_gate.shape
    groups = filter_taps.shape[1]
    per_group = channels // groups
    who = jnp.stack([lax.axis_index("ctx"), lax.axis_index("tp")]).astype(jnp.int32)
    plan = planned(who)
    near, cross = hop(out_grad, INWARD + OUTWARD), hop(out_grad, ACROSS)
    total = cotangent_products(plan, 2 * OWN, both([out_grad]), out_weight)

    packed = prepare(who, key_gate, value_input, filter_taps, members, scale)
    input_parts = traded(packed, "ctx")
    conv_parts = convolve(plan, input_parts, length, per_group, (total,))
    *conv_parts, near, cross = held_until([*conv_parts, near, cross], ())
    far, skip = hop(near, ACROSS), hop(cross, OUTWARD)
    gated_out, convolved = gated(plan, traded(conv_parts, "ctx"), query_gate)

    def product(first, count, other, more=(), after=(), tiles=1, joins=1):
        return column_products(
            plan, gated_out, out_weight, first, count, other, more, after, tiles, joins
        )

    given_far, given_middle = product(FAR, 2, 1)
    far, skip = held_until([far, skip], (given_far,))
    last = hop(far, OUTWARD)
    (first,) = product(FAR, 1, 0, (swapped(given_far, "tp", 1),))
    one = hop(first, INWARD)
    (second,) = product(MIDDLE, 1, 0, (swapped(given_middle, "tp", 1),), (first,))
    beside = hop(second, ACROSS)
    near, cross = held_until([near, cross], (second,))
    total = cotangent_products(
        plan, 2 * NEAR, both([near, added(cross, skip)]), out_weight, total
    )
    given_near, given_own = product(NEAR, 2, 1, (), (second,))
    (one,) = held_until([one], (total, given_near))
    through = added(first, one)
    over_two = hop(through, ((1, 3), (2, 0)))
    (second,) = held_until([second], (one,))
    to_middle = hop(second, ((0, 2), (3, 1)))

    last, beside = held_until([last, beside], (total, given_near))
    far_block, far_other = both([added(far, last)])
    total = cotangent_products(plan, 2 * FAR, [far_block], out_weight, total, after=(through,))
    grad_query, *grad_parts = cotangent_products(
        plan,
        2 * FAR + 1,
        [far_other],
        out_weight,
        total,
        (convolved, query_gate),
        members=members,
    )
    received = (swapped(given_near, "tp", 1), swapped(given_own, "tp", 1))
    third, own = product(NEAR, 2, 0, received, (grad_parts[0],))
    grad_parts = traded(grad_parts, "ctx")
    (third,) = held_until([third], tuple(grad_parts[1:]))
    beside_near = hop(third, INWARD + OUTWARD)
    back_parts = correlate(plan, input_parts, grad_parts, per_group, scale, (third,))
    projected = added(own, beside, over_two, to_middle, beside_near)
    back_parts = traded(back_parts, "ctx")
    return projected, grad_query, *finished(plan, back_parts, key_gate, value_input, groups, (projected,))


def anywhere(
    query_gate, key_gate, value_input, filter_taps, out_weight, out_grad, members, scale
):
    length, channels = query_gate.shape
    groups = filter_taps.shape[1]
    per_group = channels // groups
    position = lax.axis_index("ctx")
    plan = jnp.full((POSITION + 1,), position, jnp.int32)
    packed = packed_parts(position, key_gate, value_input, filter_taps, members, scale)
    input_parts = traded(packed, "ctx")
    conv_parts = traded(convolve(plan, input_parts, length, per_group), "ctx")
    convolved = joined(conv_parts, position, 1)
    gated_out = (wide(query_gate) * wide(convolved)).astype(jnp.bfloat16)
    partial_value = jnp.dot(gated_out, out_weight, preferred_element_type=jnp.float32)
    projected = lax.psum_scatter(
        partial_value.astype(jnp.bfloat16), "tp", scatter_dimension=1, tiled=True
    )
    dgated = jnp.einsum(
        "tk,ck->tc",
        lax.all_gather(out_grad, "tp", axis=1, tiled=True),
        out_weight,
        preferred_element_type=jnp.float32,
    ).astype(jnp.bfloat16)
    grad_query = (wide(dgated) * wide(convolved)).astype(jnp.bfloat16)
    conv_grad = (wide(dgated) * wide(query_gate)).astype(jnp.bfloat16)
    grad_parts = traded(cut(conv_grad, position, members, 1), "ctx")
    back_parts = correlate(plan, input_parts, grad_parts, per_group, scale)
    back_parts = traded(back_parts, "ctx")
    return (
        projected,
        grad_query,
        *unpacked_parts(position, back_parts, key_gate, value_input, groups),
    )


def local(query_gate, key_gate, value_input, filter_taps, out_weight, out_grad):
    length, channels = query_gate.shape
    groups = filter_taps.shape[1]
    members = lax.axis_size("ctx")
    scale = 1.0 / math.sqrt(length * members)
    fits = channels // members % 128 == 0 and groups // members % 16 == 0
    body = in_line if lax.axis_size("tp") == 8 and fits else anywhere
    return body(
        query_gate, key_gate, value_input, filter_taps, out_weight, out_grad, members, scale
    )


def solution(mesh):
    both = P("ctx", "tp")
    return jax.shard_map(
        local,
        mesh=mesh,
        in_specs=(both, both, both, both, P("tp", None), both),
        out_specs=(both,) * 5,
        check_vma=False,
    )
```

```python
import functools
import math
import jax
import jax.numpy as jnp
from jax import lax
from jax.experimental import pallas as pl
from jax.experimental.pallas import tpu as pltpu
from jax.sharding import PartitionSpec as P

BLOCK = 128
POSITION = 8
NT = (((1,), (1,)), ((), ()))
COST = pl.CostEstimate(flops=2**20, bytes_accessed=2**12, transcendentals=0)


def lag_matrix(row, length):
    lanes = lax.broadcasted_iota(jnp.int32, (BLOCK, BLOCK), 1)
    rows = lax.broadcasted_iota(jnp.int32, (BLOCK, BLOCK), 0)
    spread = pltpu.roll(
        jnp.broadcast_to(row, (BLOCK, length)), 0, axis=1, stride=1, stride_axis=0
    )
    first = jnp.where(lanes >= rows, spread[:, :BLOCK], 0.0)
    return jnp.concatenate(
        [first.astype(jnp.bfloat16), spread[:, BLOCK:].astype(jnp.bfloat16)], axis=1
    )


def stacked(ref, start, rows, members, width):
    pieces = []
    for member in range(members):
        part = ref[member, pl.ds(start, rows), :]
        for at in range(0, width, BLOCK):
            pieces.append(part[:, at : at + BLOCK])
    return jnp.concatenate(pieces, axis=0)


def spread_out(ref, start, rows, value, members, width):
    per_member = width // BLOCK
    for member in range(members):
        base = member * per_member * rows
        parts = [value[base + i * rows : base + (i + 1) * rows] for i in range(per_member)]
        ref[member, pl.ds(start, rows), :] = jnp.concatenate(parts, axis=1)


def padded(groups):
    return -(-groups // 16) * 16


def load_taps(tap_scr, packed, at, width):
    groups, channels = tap_scr.shape[0], packed.shape[1]
    rows = padded(groups)
    parts = [
        packed[width + chunk * rows : width + (chunk + 1) * rows, :].astype(jnp.float32)
        for chunk in range(width // channels)
    ]
    start = pl.multiple_of(at * width, width)
    tap_scr[:, pl.ds(start, width)] = jnp.concatenate(parts, axis=1)[:groups]


def forward_kernel(members, per_group, width, plan_ref, *refs):
    inputs, outputs = refs[:members], refs[-members - 3 : -3]
    tap_scr, in_scr, out_scr = refs[-3:]
    position = plan_ref[POSITION]
    channels = inputs[0].shape[1]
    groups = channels // per_group
    length = members * width
    blocks = length // BLOCK
    for step in range(members):
        at = position ^ step
        in_scr[at] = inputs[step][:width].T
        load_taps(tap_scr, inputs[step], at, width)

    def one_group(group, carry):
        start = pl.multiple_of(group * per_group, per_group)
        lags = lag_matrix(tap_scr[pl.ds(group, 1), :], length)
        data = stacked(in_scr, start, per_group, members, width)
        total = [jnp.zeros((per_group, BLOCK), jnp.float32) for _ in range(blocks)]
        for offset in range(0, blocks, 2):
            rows = (blocks - offset) * per_group
            result = jnp.dot(
                data[:rows],
                lags[:, offset * BLOCK : (offset + 2) * BLOCK],
                preferred_element_type=jnp.float32,
            )
            for side in range(2):
                for source in range(blocks - offset - side):
                    total[source + offset + side] += result[
                        source * per_group : (source + 1) * per_group,
                        side * BLOCK : (side + 1) * BLOCK,
                    ]
        value = jnp.concatenate(total, axis=0).astype(jnp.bfloat16)
        spread_out(out_scr, start, per_group, value, members, width)
        return carry

    lax.fori_loop(0, groups, one_group, 0, unroll=4)
    for step in range(members):
        outputs[step][...] = out_scr[position ^ step].T


def backward_kernel(members, per_group, scale, width, plan_ref, *refs):
    inputs, cotangents = refs[:members], refs[members : 2 * members]
    outputs = refs[-members - 6 : -6]
    tap_scr, in_scr, cot_scr, out_scr, grad_scr, pad_scr = refs[-6:]
    position = plan_ref[POSITION]
    channels = inputs[0].shape[1]
    groups = channels // per_group
    length = members * width
    blocks = length // BLOCK
    depth = blocks * per_group
    for step in range(members):
        at = position ^ step
        in_scr[at] = inputs[step][:width].T
        cot_scr[at] = cotangents[step][...].T
        load_taps(tap_scr, inputs[step], at, width)
    pad_scr[...] = jnp.zeros_like(pad_scr)
    rows_of = lax.broadcasted_iota(jnp.int32, (BLOCK, BLOCK), 0)
    lanes_of = lax.broadcasted_iota(jnp.int32, (BLOCK, BLOCK), 1)
    mirror = (rows_of + lanes_of == BLOCK - 1).astype(jnp.bfloat16)

    def one_group(group, carry):
        start = pl.multiple_of(group * per_group, per_group)
        lags = lag_matrix(tap_scr[pl.ds(group, 1), :], length)
        data = stacked(in_scr, start, per_group, members, width)
        cot = stacked(cot_scr, start, per_group, members, width)
        pad_scr[:depth, :BLOCK] = cot
        pad_scr[: depth - per_group, BLOCK:] = cot[per_group:]
        flipped = lax.dot_general(
            mirror, data, NT, preferred_element_type=jnp.float32
        ).astype(jnp.bfloat16)
        total = jnp.zeros((depth, BLOCK), jnp.float32)
        products = []
        for offset in range(0, blocks, 2):
            rows = depth - offset * per_group
            pair = pad_scr[offset * per_group : offset * per_group + depth, :]
            result = lax.dot_general(
                pair[:rows],
                lags[:, offset * BLOCK : (offset + 2) * BLOCK],
                NT,
                preferred_element_type=jnp.float32,
            )
            if rows < depth:
                result = jnp.concatenate(
                    [result, jnp.zeros((depth - rows, BLOCK), jnp.float32)], axis=0
                )
            total = total + result
            products.append(jnp.dot(flipped, pair, preferred_element_type=jnp.float32))
        spread_out(
            out_scr, start, per_group, total.astype(jnp.bfloat16), members, width
        )
        kept = jnp.where(rows_of + lanes_of >= BLOCK - 1, products[0][:, :BLOCK], 0.0)
        product = jnp.concatenate([kept, products[0][:, BLOCK:], *products[1:]], axis=1)
        product = pltpu.roll(
            product, length - (BLOCK - 1), axis=1, stride=1, stride_axis=0
        )
        grad_scr[pl.ds(group, 1), :] = jnp.sum(product, axis=0, keepdims=True) * scale
        return carry

    lax.fori_loop(0, groups, one_group, 0, unroll=4)
    for step in range(members):
        at = position ^ step
        outputs[step][:width] = out_scr[at].T
        rows = padded(groups)
        whole = grad_scr[:, pl.ds(pl.multiple_of(at * width, width), width)].astype(jnp.bfloat16)
        if rows > groups:
            blank = jnp.zeros((rows - groups, width), jnp.bfloat16)
            whole = jnp.concatenate([whole, blank], axis=0)
        for chunk in range(width // channels):
            outputs[step][width + chunk * rows : width + (chunk + 1) * rows, :] = whole[
                :, chunk * channels : (chunk + 1) * channels
            ]


VMEM = pl.BlockSpec(memory_space=pltpu.VMEM)
ANYWHERE = pl.BlockSpec(memory_space=pl.ANY)
SMEM = pl.BlockSpec(memory_space=pltpu.SMEM)


def convolve(plan, inputs, width, per_group, after=()):
    members = len(inputs)
    channels = inputs[0].shape[1]
    length = members * width
    return pl.pallas_call(
        functools.partial(forward_kernel, members, per_group, width),
        out_shape=[jax.ShapeDtypeStruct((width, channels), jnp.bfloat16)] * members,
        in_specs=[SMEM] + [VMEM] * members + [ANYWHERE] * len(after),
        out_specs=[VMEM] * members,
        scratch_shapes=[
            pltpu.VMEM((channels // per_group, length), jnp.float32),
            pltpu.VMEM((members, channels, width), jnp.bfloat16),
            pltpu.VMEM((members, channels, width), jnp.bfloat16),
        ],
        compiler_params=pltpu.CompilerParams(vmem_limit_bytes=24 * 2**20),
        cost_estimate=COST,
        name="causal_conv",
    )(plan, *inputs, *after)


def correlate(plan, inputs, cotangents, per_group, scale, after=()):
    members = len(inputs)
    width, channels = cotangents[0].shape
    length = members * width
    groups = channels // per_group
    return pl.pallas_call(
        functools.partial(backward_kernel, members, per_group, scale, width),
        out_shape=[jax.ShapeDtypeStruct(inputs[0].shape, jnp.bfloat16)] * members,
        in_specs=[SMEM] + [VMEM] * (2 * members) + [ANYWHERE] * len(after),
        out_specs=[VMEM] * members,
        scratch_shapes=[
            pltpu.VMEM((groups, length), jnp.float32),
            pltpu.VMEM((members, channels, width), jnp.bfloat16),
            pltpu.VMEM((members, channels, width), jnp.bfloat16),
            pltpu.VMEM((members, channels, width), jnp.bfloat16),
            pltpu.VMEM((groups, length), jnp.float32),
            pltpu.VMEM((2 * length // BLOCK * per_group, 2 * BLOCK), jnp.bfloat16),
        ],
        compiler_params=pltpu.CompilerParams(vmem_limit_bytes=24 * 2**20),
        cost_estimate=COST,
        name="causal_conv_grads",
    )(plan, *inputs, *cotangents, *after)


def in_hbm(array):
    return pltpu.with_memory_space_constraint(array, pltpu.HBM)


def prepare_kernel(members, scale, who_ref, key_ref, value_ref, taps_ref, *outputs):
    position = who_ref[0]
    step_no = pl.program_id(0)
    rows, channels = key_ref.shape
    share = channels // members
    groups = taps_ref.shape[0] // members
    total_width = taps_ref.shape[1]
    for step in range(members):
        at = position ^ step
        columns = pl.ds(pl.multiple_of(at * share, share), share)
        product = key_ref[:, columns].astype(jnp.float32) * value_ref[:, columns].astype(
            jnp.float32
        )
        here = pl.ds(pl.multiple_of(step_no * rows, rows), rows)
        outputs[step][here, :] = product.astype(jnp.bfloat16)

    @pl.when(step_no == 0)
    def _():
        for step in range(members):
            at = position ^ step
            taps = taps_ref[pl.ds(pl.multiple_of(at * groups, groups), groups), :]
            taps = (taps * scale).astype(jnp.bfloat16)
            for chunk in range(total_width // share):
                start = total_width + chunk * groups
                outputs[step][start : start + groups, :] = taps[
                    :, chunk * share : (chunk + 1) * share
                ]


def prepare(who, key_gate, value_input, filter_taps, members, scale):
    width, channels = key_gate.shape
    share = channels // members
    rows = width + filter_taps.size // members // share
    tile = width // 4
    part = pl.BlockSpec((tile, channels), lambda i: (i, 0))
    return pl.pallas_call(
        functools.partial(prepare_kernel, members, scale),
        out_shape=[jax.ShapeDtypeStruct((rows, share), jnp.bfloat16)] * members,
        grid=(4,),
        in_specs=[SMEM, part, part, pl.BlockSpec(filter_taps.shape[::-1], lambda i: (0, 0))],
        out_specs=[VMEM] * members,
        compiler_params=pltpu.CompilerParams(vmem_limit_bytes=24 * 2**20),
        cost_estimate=COST,
        name="gated_input",
    )(who, in_hbm(key_gate), in_hbm(value_input), in_hbm(filter_taps.T))


def finish_kernel(members, plan_ref, *refs):
    parts = refs[:members]
    key_ref, value_ref = refs[members : members + 2]
    key_out, value_out, taps_out = refs[-3:]
    position = plan_ref[POSITION]
    width, channels = key_ref.shape
    share = channels // members
    groups = taps_out.shape[0] // members
    for step in range(members):
        at = position ^ step
        columns = pl.ds(pl.multiple_of(at * share, share), share)
        grad = parts[step][:width].astype(jnp.float32)
        key_out[:, columns] = (grad * value_ref[:, columns].astype(jnp.float32)).astype(
            jnp.bfloat16
        )
        value_out[:, columns] = (grad * key_ref[:, columns].astype(jnp.float32)).astype(
            jnp.bfloat16
        )
        taps = [
            parts[step][width + chunk * groups : width + (chunk + 1) * groups, :]
            for chunk in range(width // share)
        ]
        taps_out[pl.ds(pl.multiple_of(at * groups, groups), groups), :] = jnp.concatenate(
            taps, axis=1
        ).astype(jnp.float32)


def finished(plan, parts, key_gate, value_input, groups, after=()):
    members = len(parts)
    width, channels = key_gate.shape
    array = jax.ShapeDtypeStruct((width, channels), jnp.bfloat16)
    grad_key, grad_value, taps = pl.pallas_call(
        functools.partial(finish_kernel, members),
        out_shape=[array, array, jax.ShapeDtypeStruct((groups, width), jnp.float32)],
        in_specs=[SMEM] + [VMEM] * (members + 2) + [ANYWHERE] * len(after),
        out_specs=[VMEM] * 3,
        compiler_params=pltpu.CompilerParams(vmem_limit_bytes=24 * 2**20),
        cost_estimate=COST,
        name="input_gradients",
    )(plan, *parts, key_gate, value_input, *after)
    return grad_key, grad_value, taps.T


def swapped(array, axis, step):
    size = lax.axis_size(axis)
    return lax.ppermute(array, axis, [(i, i ^ step) for i in range(size)])


def traded(pieces, axis):
    return [pieces[0]] + [swapped(pieces[step], axis, step) for step in range(1, len(pieces))]


def cut(array, position, members, axis):
    width = array.shape[axis] // members
    return [
        lax.dynamic_slice_in_dim(array, (position ^ step) * width, width, axis)
        for step in range(members)
    ]


def joined(pieces, position, axis):
    members = len(pieces)
    width = pieces[0].shape[axis]
    shape = list(pieces[0].shape)
    shape[axis] = members * width
    whole = jnp.zeros(shape, pieces[0].dtype)
    for step in range(members):
        whole = lax.dynamic_update_slice_in_dim(
            whole, pieces[step], (position ^ step) * width, axis
        )
    return whole


def wide(array):
    return array.astype(jnp.float32)


def hop(array, pairs):
    return lax.ppermute(
        array, "tp", [(2 * i + core, 2 * j + core) for i, j in pairs for core in range(2)]
    )


INWARD = ((0, 1), (3, 2))
ACROSS = ((1, 2), (2, 1))
OUTWARD = ((1, 0), (2, 3))
OWN, NEAR, MIDDLE, FAR = range(4)
CHIPS = ((0, 1, 2, 3), (1, 0, 3, 2), (2, 2, 1, 1), (3, 3, 0, 0))


def plan_kernel(who_ref, plan_ref):
    place = who_ref[1]
    chip, core = place // 2, place % 2
    for number, table in enumerate(CHIPS):
        source = jnp.where(
            chip < 2,
            jnp.where(chip == 0, table[0], table[1]),
            jnp.where(chip == 2, table[2], table[3]),
        )
        plan_ref[2 * number] = 2 * source + core
        plan_ref[2 * number + 1] = 2 * source + 1 - core
    plan_ref[POSITION] = who_ref[0]


def planned(who):
    return pl.pallas_call(
        plan_kernel,
        out_shape=jax.ShapeDtypeStruct((POSITION + 1,), jnp.int32),
        in_specs=[SMEM],
        out_specs=SMEM,
        compiler_params=pltpu.CompilerParams(vmem_limit_bytes=2**20),
        cost_estimate=COST,
        name="plan",
    )(who)


def pass_kernel(*refs):
    del refs


def held_until(values, after):
    return pl.pallas_call(
        pass_kernel,
        out_shape=[jax.ShapeDtypeStruct(value.shape, value.dtype) for value in values],
        in_specs=[ANYWHERE] * (len(values) + len(after)),
        out_specs=[ANYWHERE] * len(values),
        input_output_aliases={number: number for number in range(len(values))},
        compiler_params=pltpu.CompilerParams(vmem_limit_bytes=2**20),
        cost_estimate=COST,
        name="held",
    )(*values, *after)


def add_kernel(*refs):
    refs[-1][...] = sum(wide(ref[...]) for ref in refs[:-1]).astype(jnp.bfloat16)


def added(*arrays):
    rows, width = arrays[0].shape
    part = pl.BlockSpec((rows // 4, width), lambda i: (i, 0))
    return pl.pallas_call(
        add_kernel,
        out_shape=jax.ShapeDtypeStruct((rows, width), jnp.bfloat16),
        grid=(4,),
        in_specs=[part] * len(arrays),
        out_specs=part,
        compiler_params=pltpu.CompilerParams(vmem_limit_bytes=8 * 2**20),
        cost_estimate=COST,
        name="added",
    )(*arrays)


def gate_kernel(members, plan_ref, *refs):
    parts = refs[:members]
    query_ref, gated_ref, conv_ref = refs[members:]
    position = plan_ref[POSITION]
    share = parts[0].shape[1]
    for step in range(members):
        columns = pl.ds(pl.multiple_of((position ^ step) * share, share), share)
        conv = parts[step][...]
        conv_ref[:, columns] = conv
        gated_ref[:, columns] = (wide(conv) * wide(query_ref[:, columns])).astype(jnp.bfloat16)


def gated(plan, parts, query_gate):
    array = jax.ShapeDtypeStruct(query_gate.shape, jnp.bfloat16)
    return pl.pallas_call(
        functools.partial(gate_kernel, len(parts)),
        out_shape=[array, array],
        in_specs=[SMEM] + [VMEM] * (len(parts) + 1),
        out_specs=[VMEM] * 2,
        compiler_params=pltpu.CompilerParams(vmem_limit_bytes=8 * 2**20),
        cost_estimate=COST,
        name="gated_output",
    )(plan, *parts, query_gate)


def product_kernel(steps, joins, extra, _, data_ref, weight_ref, *refs):
    more, outputs = refs[:extra], refs[-(steps // joins) :]
    product = jnp.dot(data_ref[...], weight_ref[...], preferred_element_type=jnp.float32)
    for number in range(steps):
        out_ref = outputs[number // joins]
        wide_out = out_ref.shape[1] > product.shape[1]

        @pl.when(pl.program_id(0) == number)
        def _(number=number, out_ref=out_ref, wide_out=wide_out):
            total = product + wide(more[number][...]) if more else product
            if wide_out:
                width = product.shape[1]
                at = number % joins * width
                out_ref[:, at : at + width] = total.astype(jnp.bfloat16)
            else:
                out_ref[...] = total.astype(jnp.bfloat16)


def column_products(
    plan, data, out_weight, first, count, other, more=(), after=(), tiles=1, joins=1
):
    rows, depth = data.shape
    width = data.shape[1]
    tile = width // tiles
    steps = count * tiles

    def weights(i, at):
        return 0, at[2 * (first - i // tiles) + other] * tiles + i % tiles

    def whole(array_width):
        return pl.BlockSpec((rows, array_width), lambda i, at: (0, 0))

    return pl.pallas_call(
        functools.partial(product_kernel, steps, joins, len(more)),
        out_shape=[jax.ShapeDtypeStruct((rows, tile * joins), jnp.bfloat16)] * (steps // joins),
        grid_spec=pltpu.PrefetchScalarGridSpec(
            num_scalar_prefetch=1,
            grid=(steps,),
            in_specs=[whole(depth), pl.BlockSpec((depth, tile), weights)]
            + [whole(tile)] * len(more)
            + [ANYWHERE] * len(after),
            out_specs=[whole(tile * joins)] * (steps // joins),
        ),
        compiler_params=pltpu.CompilerParams(vmem_limit_bytes=24 * 2**20),
        cost_estimate=COST,
        name="projection_blocks",
    )(plan, data, in_hbm(out_weight), *more, *after)


def cotangent_kernel(count, begin, last, members, plan_ref, weight_ref, *refs):
    blocks, refs = refs[:count], refs[count:]
    step = pl.program_id(0)
    total = refs[-1]

    @pl.when(step == 0)
    def _():
        total[...] = jnp.zeros_like(total) if begin else refs[0][...]

    for number, block in enumerate(blocks):

        @pl.when(step == number)
        def _(block=block):
            total[...] += lax.dot_general(
                block[...], weight_ref[...], NT, preferred_element_type=jnp.float32
            )

    if last:
        conv_ref, query_ref = refs[1:3]
        grad_ref, parts = refs[-2 - members], refs[-1 - members : -1]

        @pl.when(step == count - 1)
        def _():
            dgated = wide(total[...].astype(jnp.bfloat16))
            grad_ref[...] = (dgated * wide(conv_ref[...])).astype(jnp.bfloat16)
            share = parts[0].shape[1]
            for step in range(members):
                start = pl.multiple_of((plan_ref[POSITION] ^ step) * share, share)
                columns = pl.ds(start, share)
                dgated = wide(total[:, columns].astype(jnp.bfloat16))
                parts[step][...] = (dgated * wide(query_ref[:, columns])).astype(jnp.bfloat16)


def both(blocks):
    return [part for block in blocks for part in (block, swapped(block, "tp", 1))]


def cotangent_products(
    plan, first, parts, out_weight, start=None, gates=(), after=(), members=0
):
    rows, width = parts[0].shape
    channels = out_weight.shape[0]
    count = len(parts)
    whole = pl.BlockSpec((rows, channels), lambda i, at: (0, 0))
    part = pl.BlockSpec((rows, width), lambda i, at: (0, 0))
    piece = pl.BlockSpec((rows, channels // max(members, 1)), lambda i, at: (0, 0))
    array = jax.ShapeDtypeStruct((rows, channels), jnp.bfloat16)
    cut_array = jax.ShapeDtypeStruct((rows, channels // max(members, 1)), jnp.bfloat16)
    begin, last = start is None, bool(gates)
    extra = (() if begin else (start,)) + tuple(gates)
    return pl.pallas_call(
        functools.partial(cotangent_kernel, count, begin, last, members),
        out_shape=[array] + [cut_array] * members
        if last
        else jax.ShapeDtypeStruct((rows, channels), jnp.float32),
        grid_spec=pltpu.PrefetchScalarGridSpec(
            num_scalar_prefetch=1,
            grid=(count,),
            in_specs=[pl.BlockSpec((channels, width), lambda i, at: (0, at[first + i]))]
            + [part] * count
            + [whole] * len(extra)
            + [ANYWHERE] * len(after),
            out_specs=[whole] + [piece] * members if last else whole,
            scratch_shapes=[pltpu.VMEM((rows, channels), jnp.float32)] if last else [],
        ),
        compiler_params=pltpu.CompilerParams(vmem_limit_bytes=24 * 2**20),
        cost_estimate=COST,
        name="cotangent_blocks",
    )(plan, in_hbm(out_weight), *parts, *extra, *after)


def packed_parts(position, key_gate, value_input, filter_taps, members, scale):
    length, channels = key_gate.shape
    share = channels // members
    product_in = (wide(key_gate) * wide(value_input)).astype(jnp.bfloat16)
    tap_rows = (filter_taps * scale).astype(jnp.bfloat16).T
    owned = filter_taps.shape[1] // members
    chunks = length // share
    packed = []
    pieces = cut(product_in, position, members, 1)
    for piece, taps in zip(pieces, cut(tap_rows, position, members, 0)):
        taps = taps.reshape(owned, chunks, share).transpose(1, 0, 2)
        taps = jnp.pad(taps, ((0, 0), (0, padded(owned) - owned), (0, 0)))
        packed.append(jnp.concatenate([piece, taps.reshape(-1, share)], axis=0))
    return packed


def unpacked_parts(position, parts, key_gate, value_input, groups):
    length, channels = key_gate.shape
    members = len(parts)
    share = channels // members
    owned = groups // members
    chunks = length // share
    input_grad = wide(joined([part[:length] for part in parts], position, 1))
    filter_parts = [
        part[length:]
        .reshape(chunks, padded(owned), share)[:, :owned]
        .transpose(1, 0, 2)
        .reshape(owned, length)
        for part in parts
    ]
    grad_filter = wide(joined(filter_parts, position, 0)).T
    grad_key = (input_grad * wide(value_input)).astype(jnp.bfloat16)
    grad_value = (input_grad * wide(key_gate)).astype(jnp.bfloat16)
    return grad_key, grad_value, grad_filter


def in_line(
    query_gate, key_gate, value_input, filter_taps, out_weight, out_grad, members, scale
):
    length, channels = query_gate.shape
    groups = filter_taps.shape[1]
    per_group = channels // groups
    who = jnp.stack([lax.axis_index("ctx"), lax.axis_index("tp")]).astype(jnp.int32)
    plan = planned(who)
    near, cross = hop(out_grad, INWARD + OUTWARD), hop(out_grad, ACROSS)
    total = cotangent_products(plan, 2 * OWN, both([out_grad]), out_weight)

    packed = prepare(who, key_gate, value_input, filter_taps, members, scale)
    input_parts = traded(packed, "ctx")
    conv_parts = convolve(plan, input_parts, length, per_group, (total,))
    *conv_parts, near, cross = held_until([*conv_parts, near, cross], ())
    far, skip = hop(near, ACROSS), hop(cross, OUTWARD)
    gated_out, convolved = gated(plan, traded(conv_parts, "ctx"), query_gate)

    def product(first, count, other, more=(), after=(), tiles=1, joins=1):
        return column_products(
            plan, gated_out, out_weight, first, count, other, more, after, tiles, joins
        )

    given_far = product(FAR, 1, 1, tiles=2)
    received = [swapped(part, "tp", 1) for part in given_far]
    (first,) = product(FAR, 1, 0, received, tiles=2, joins=2)
    one = hop(first, INWARD)
    far, skip = held_until([far, skip], (first,))
    last = hop(far, OUTWARD)
    given_middle = product(MIDDLE, 1, 1, (), (far,), tiles=2)
    received = [swapped(part, "tp", 1) for part in given_middle]
    (second,) = product(MIDDLE, 1, 0, received, tiles=2, joins=2)
    middle_block = added(cross, skip)
    blocks = [near, swapped(near, "tp", 1), middle_block]
    total = cotangent_products(plan, 2 * NEAR, blocks, out_weight, total, after=(second,))
    given_near, given_own = product(NEAR, 2, 1, (), (second,))
    (one,) = held_until([one], (total, given_near))
    through = added(first, one)
    two_a = hop(through, ACROSS)
    (second,) = held_until([second], (one,))
    two_b = hop(second, INWARD)

    (last,) = held_until([last], (total, given_near))
    far_block, far_other = both([added(far, last)])
    blocks = [swapped(middle_block, "tp", 1), far_block]
    total = cotangent_products(
        plan, 2 * MIDDLE + 1, blocks, out_weight, total, after=(through,)
    )
    grad_query, *grad_parts = cotangent_products(
        plan,
        2 * FAR + 1,
        [far_other],
        out_weight,
        total,
        (convolved, query_gate),
        members=members,
    )
    received = (swapped(given_near, "tp", 1), swapped(given_own, "tp", 1))
    third, own = product(NEAR, 2, 0, received, (grad_parts[0],))
    grad_parts = traded(grad_parts, "ctx")

    two_a, two_b = held_until([two_a, two_b], tuple(grad_parts[1:]))
    third, second = added(third, two_a), added(second, two_b)
    back_parts = correlate(plan, input_parts, grad_parts, per_group, scale, (third, second))
    projected = added(own, hop(third, OUTWARD + INWARD), hop(second, ACROSS))
    back_parts = traded(back_parts, "ctx")
    return projected, grad_query, *finished(plan, back_parts, key_gate, value_input, groups, (projected,))


def anywhere(
    query_gate, key_gate, value_input, filter_taps, out_weight, out_grad, members, scale
):
    length, channels = query_gate.shape
    groups = filter_taps.shape[1]
    per_group = channels // groups
    position = lax.axis_index("ctx")
    plan = jnp.full((POSITION + 1,), position, jnp.int32)
    packed = packed_parts(position, key_gate, value_input, filter_taps, members, scale)
    input_parts = traded(packed, "ctx")
    conv_parts = traded(convolve(plan, input_parts, length, per_group), "ctx")
    convolved = joined(conv_parts, position, 1)
    gated_out = (wide(query_gate) * wide(convolved)).astype(jnp.bfloat16)
    partial_value = jnp.dot(gated_out, out_weight, preferred_element_type=jnp.float32)
    projected = lax.psum_scatter(
        partial_value.astype(jnp.bfloat16), "tp", scatter_dimension=1, tiled=True
    )
    dgated = jnp.einsum(
        "tk,ck->tc",
        lax.all_gather(out_grad, "tp", axis=1, tiled=True),
        out_weight,
        preferred_element_type=jnp.float32,
    ).astype(jnp.bfloat16)
    grad_query = (wide(dgated) * wide(convolved)).astype(jnp.bfloat16)
    conv_grad = (wide(dgated) * wide(query_gate)).astype(jnp.bfloat16)
    grad_parts = traded(cut(conv_grad, position, members, 1), "ctx")
    back_parts = correlate(plan, input_parts, grad_parts, per_group, scale)
    back_parts = traded(back_parts, "ctx")
    return (
        projected,
        grad_query,
        *unpacked_parts(position, back_parts, key_gate, value_input, groups),
    )


def local(query_gate, key_gate, value_input, filter_taps, out_weight, out_grad):
    length, channels = query_gate.shape
    groups = filter_taps.shape[1]
    members = lax.axis_size("ctx")
    scale = 1.0 / math.sqrt(length * members)
    fits = channels // members % 128 == 0 and groups // members % 16 == 0
    body = in_line if lax.axis_size("tp") == 8 and fits else anywhere
    return body(
        query_gate, key_gate, value_input, filter_taps, out_weight, out_grad, members, scale
    )


def solution(mesh):
    both = P("ctx", "tp")
    return jax.shard_map(
        local,
        mesh=mesh,
        in_specs=(both, both, both, both, P("tp", None), both),
        out_specs=(both,) * 5,
        check_vma=False,
    )
```

```python
import functools
import math
import jax
import jax.numpy as jnp
from jax import lax
from jax.experimental import pallas as pl
from jax.experimental.pallas import tpu as pltpu
from jax.sharding import PartitionSpec as P

BLOCK = 128
POSITION = 8
NT = (((1,), (1,)), ((), ()))
COST = pl.CostEstimate(flops=2**20, bytes_accessed=2**12, transcendentals=0)


def lag_matrix(row, length):
    lanes = lax.broadcasted_iota(jnp.int32, (BLOCK, BLOCK), 1)
    rows = lax.broadcasted_iota(jnp.int32, (BLOCK, BLOCK), 0)
    spread = pltpu.roll(
        jnp.broadcast_to(row, (BLOCK, length)), 0, axis=1, stride=1, stride_axis=0
    )
    first = jnp.where(lanes >= rows, spread[:, :BLOCK], 0.0)
    return jnp.concatenate(
        [first.astype(jnp.bfloat16), spread[:, BLOCK:].astype(jnp.bfloat16)], axis=1
    )


def stacked(ref, start, rows, members, width):
    pieces = []
    for member in range(members):
        part = ref[member, pl.ds(start, rows), :]
        for at in range(0, width, BLOCK):
            pieces.append(part[:, at : at + BLOCK])
    return jnp.concatenate(pieces, axis=0)


def spread_out(ref, start, rows, value, members, width):
    per_member = width // BLOCK
    for member in range(members):
        base = member * per_member * rows
        parts = [value[base + i * rows : base + (i + 1) * rows] for i in range(per_member)]
        ref[member, pl.ds(start, rows), :] = jnp.concatenate(parts, axis=1)


def padded(groups):
    return -(-groups // 16) * 16


def load_taps(tap_scr, packed, at, width):
    groups, channels = tap_scr.shape[0], packed.shape[1]
    rows = padded(groups)
    parts = [
        packed[width + chunk * rows : width + (chunk + 1) * rows, :].astype(jnp.float32)
        for chunk in range(width // channels)
    ]
    start = pl.multiple_of(at * width, width)
    tap_scr[:, pl.ds(start, width)] = jnp.concatenate(parts, axis=1)[:groups]


def forward_kernel(members, per_group, width, plan_ref, *refs):
    inputs, outputs = refs[:members], refs[-members - 3 : -3]
    tap_scr, in_scr, out_scr = refs[-3:]
    position = plan_ref[POSITION]
    channels = inputs[0].shape[1]
    groups = channels // per_group
    length = members * width
    blocks = length // BLOCK
    for step in range(members):
        at = position ^ step
        in_scr[at] = inputs[step][:width].T
        load_taps(tap_scr, inputs[step], at, width)

    def one_group(group, carry):
        start = pl.multiple_of(group * per_group, per_group)
        lags = lag_matrix(tap_scr[pl.ds(group, 1), :], length)
        data = stacked(in_scr, start, per_group, members, width)
        total = [jnp.zeros((per_group, BLOCK), jnp.float32) for _ in range(blocks)]
        for offset in range(0, blocks, 2):
            rows = (blocks - offset) * per_group
            result = jnp.dot(
                data[:rows],
                lags[:, offset * BLOCK : (offset + 2) * BLOCK],
                preferred_element_type=jnp.float32,
            )
            for side in range(2):
                for source in range(blocks - offset - side):
                    total[source + offset + side] += result[
                        source * per_group : (source + 1) * per_group,
                        side * BLOCK : (side + 1) * BLOCK,
                    ]
        value = jnp.concatenate(total, axis=0).astype(jnp.bfloat16)
        spread_out(out_scr, start, per_group, value, members, width)
        return carry

    lax.fori_loop(0, groups, one_group, 0, unroll=4)
    for step in range(members):
        outputs[step][...] = out_scr[position ^ step].T


def backward_kernel(members, per_group, scale, width, plan_ref, *refs):
    inputs, cotangents = refs[:members], refs[members : 2 * members]
    outputs = refs[-members - 6 : -6]
    tap_scr, in_scr, cot_scr, out_scr, grad_scr, pad_scr = refs[-6:]
    position = plan_ref[POSITION]
    channels = inputs[0].shape[1]
    groups = channels // per_group
    length = members * width
    blocks = length // BLOCK
    depth = blocks * per_group
    for step in range(members):
        at = position ^ step
        in_scr[at] = inputs[step][:width].T
        cot_scr[at] = cotangents[step][...].T
        load_taps(tap_scr, inputs[step], at, width)
    pad_scr[...] = jnp.zeros_like(pad_scr)
    rows_of = lax.broadcasted_iota(jnp.int32, (BLOCK, BLOCK), 0)
    lanes_of = lax.broadcasted_iota(jnp.int32, (BLOCK, BLOCK), 1)
    mirror = (rows_of + lanes_of == BLOCK - 1).astype(jnp.bfloat16)

    def one_group(group, carry):
        start = pl.multiple_of(group * per_group, per_group)
        lags = lag_matrix(tap_scr[pl.ds(group, 1), :], length)
        data = stacked(in_scr, start, per_group, members, width)
        cot = stacked(cot_scr, start, per_group, members, width)
        pad_scr[:depth, :BLOCK] = cot
        pad_scr[: depth - per_group, BLOCK:] = cot[per_group:]
        flipped = lax.dot_general(
            mirror, data, NT, preferred_element_type=jnp.float32
        ).astype(jnp.bfloat16)
        total = jnp.zeros((depth, BLOCK), jnp.float32)
        products = []
        for offset in range(0, blocks, 2):
            rows = depth - offset * per_group
            pair = pad_scr[offset * per_group : offset * per_group + depth, :]
            result = lax.dot_general(
                pair[:rows],
                lags[:, offset * BLOCK : (offset + 2) * BLOCK],
                NT,
                preferred_element_type=jnp.float32,
            )
            if rows < depth:
                result = jnp.concatenate(
                    [result, jnp.zeros((depth - rows, BLOCK), jnp.float32)], axis=0
                )
            total = total + result
            products.append(jnp.dot(flipped, pair, preferred_element_type=jnp.float32))
        spread_out(
            out_scr, start, per_group, total.astype(jnp.bfloat16), members, width
        )
        kept = jnp.where(rows_of + lanes_of >= BLOCK - 1, products[0][:, :BLOCK], 0.0)
        product = jnp.concatenate([kept, products[0][:, BLOCK:], *products[1:]], axis=1)
        product = pltpu.roll(
            product, length - (BLOCK - 1), axis=1, stride=1, stride_axis=0
        )
        grad_scr[pl.ds(group, 1), :] = jnp.sum(product, axis=0, keepdims=True) * scale
        return carry

    lax.fori_loop(0, groups, one_group, 0, unroll=4)
    for step in range(members):
        at = position ^ step
        outputs[step][:width] = out_scr[at].T
        rows = padded(groups)
        whole = grad_scr[:, pl.ds(pl.multiple_of(at * width, width), width)].astype(jnp.bfloat16)
        if rows > groups:
            blank = jnp.zeros((rows - groups, width), jnp.bfloat16)
            whole = jnp.concatenate([whole, blank], axis=0)
        for chunk in range(width // channels):
            outputs[step][width + chunk * rows : width + (chunk + 1) * rows, :] = whole[
                :, chunk * channels : (chunk + 1) * channels
            ]


VMEM = pl.BlockSpec(memory_space=pltpu.VMEM)
ANYWHERE = pl.BlockSpec(memory_space=pl.ANY)
SMEM = pl.BlockSpec(memory_space=pltpu.SMEM)


def convolve(plan, inputs, width, per_group, after=()):
    members = len(inputs)
    channels = inputs[0].shape[1]
    length = members * width
    return pl.pallas_call(
        functools.partial(forward_kernel, members, per_group, width),
        out_shape=[jax.ShapeDtypeStruct((width, channels), jnp.bfloat16)] * members,
        in_specs=[SMEM] + [VMEM] * members + [ANYWHERE] * len(after),
        out_specs=[VMEM] * members,
        scratch_shapes=[
            pltpu.VMEM((channels // per_group, length), jnp.float32),
            pltpu.VMEM((members, channels, width), jnp.bfloat16),
            pltpu.VMEM((members, channels, width), jnp.bfloat16),
        ],
        compiler_params=pltpu.CompilerParams(vmem_limit_bytes=24 * 2**20),
        cost_estimate=COST,
        name="causal_conv",
    )(plan, *inputs, *after)


def correlate(plan, inputs, cotangents, per_group, scale, after=()):
    members = len(inputs)
    width, channels = cotangents[0].shape
    length = members * width
    groups = channels // per_group
    return pl.pallas_call(
        functools.partial(backward_kernel, members, per_group, scale, width),
        out_shape=[jax.ShapeDtypeStruct(inputs[0].shape, jnp.bfloat16)] * members,
        in_specs=[SMEM] + [VMEM] * (2 * members) + [ANYWHERE] * len(after),
        out_specs=[VMEM] * members,
        scratch_shapes=[
            pltpu.VMEM((groups, length), jnp.float32),
            pltpu.VMEM((members, channels, width), jnp.bfloat16),
            pltpu.VMEM((members, channels, width), jnp.bfloat16),
            pltpu.VMEM((members, channels, width), jnp.bfloat16),
            pltpu.VMEM((groups, length), jnp.float32),
            pltpu.VMEM((2 * length // BLOCK * per_group, 2 * BLOCK), jnp.bfloat16),
        ],
        compiler_params=pltpu.CompilerParams(vmem_limit_bytes=24 * 2**20),
        cost_estimate=COST,
        name="causal_conv_grads",
    )(plan, *inputs, *cotangents, *after)


def in_hbm(array):
    return pltpu.with_memory_space_constraint(array, pltpu.HBM)


def prepare_kernel(members, scale, who_ref, key_ref, value_ref, taps_ref, *outputs):
    position = who_ref[0]
    step_no = pl.program_id(0)
    rows, channels = key_ref.shape
    share = channels // members
    groups = taps_ref.shape[0] // members
    total_width = taps_ref.shape[1]
    for step in range(members):
        at = position ^ step
        columns = pl.ds(pl.multiple_of(at * share, share), share)
        product = key_ref[:, columns].astype(jnp.float32) * value_ref[:, columns].astype(
            jnp.float32
        )
        here = pl.ds(pl.multiple_of(step_no * rows, rows), rows)
        outputs[step][here, :] = product.astype(jnp.bfloat16)

    @pl.when(step_no == 0)
    def _():
        for step in range(members):
            at = position ^ step
            taps = taps_ref[pl.ds(pl.multiple_of(at * groups, groups), groups), :]
            taps = (taps * scale).astype(jnp.bfloat16)
            for chunk in range(total_width // share):
                start = total_width + chunk * groups
                outputs[step][start : start + groups, :] = taps[
                    :, chunk * share : (chunk + 1) * share
                ]


def prepare(who, key_gate, value_input, filter_taps, members, scale):
    width, channels = key_gate.shape
    share = channels // members
    rows = width + filter_taps.size // members // share
    tile = width // 4
    part = pl.BlockSpec((tile, channels), lambda i: (i, 0))
    return pl.pallas_call(
        functools.partial(prepare_kernel, members, scale),
        out_shape=[jax.ShapeDtypeStruct((rows, share), jnp.bfloat16)] * members,
        grid=(4,),
        in_specs=[SMEM, part, part, pl.BlockSpec(filter_taps.shape[::-1], lambda i: (0, 0))],
        out_specs=[VMEM] * members,
        compiler_params=pltpu.CompilerParams(vmem_limit_bytes=24 * 2**20),
        cost_estimate=COST,
        name="gated_input",
    )(who, in_hbm(key_gate), in_hbm(value_input), in_hbm(filter_taps.T))


def finish_kernel(members, plan_ref, *refs):
    parts = refs[:members]
    key_ref, value_ref = refs[members : members + 2]
    key_out, value_out, taps_out = refs[-3:]
    position = plan_ref[POSITION]
    width, channels = key_ref.shape
    share = channels // members
    groups = taps_out.shape[0] // members
    for step in range(members):
        at = position ^ step
        columns = pl.ds(pl.multiple_of(at * share, share), share)
        grad = parts[step][:width].astype(jnp.float32)
        key_out[:, columns] = (grad * value_ref[:, columns].astype(jnp.float32)).astype(
            jnp.bfloat16
        )
        value_out[:, columns] = (grad * key_ref[:, columns].astype(jnp.float32)).astype(
            jnp.bfloat16
        )
        taps = [
            parts[step][width + chunk * groups : width + (chunk + 1) * groups, :]
            for chunk in range(width // share)
        ]
        taps_out[pl.ds(pl.multiple_of(at * groups, groups), groups), :] = jnp.concatenate(
            taps, axis=1
        ).astype(jnp.float32)


def finished(plan, parts, key_gate, value_input, groups, after=()):
    members = len(parts)
    width, channels = key_gate.shape
    array = jax.ShapeDtypeStruct((width, channels), jnp.bfloat16)
    grad_key, grad_value, taps = pl.pallas_call(
        functools.partial(finish_kernel, members),
        out_shape=[array, array, jax.ShapeDtypeStruct((groups, width), jnp.float32)],
        in_specs=[SMEM] + [VMEM] * (members + 2) + [ANYWHERE] * len(after),
        out_specs=[VMEM] * 3,
        compiler_params=pltpu.CompilerParams(vmem_limit_bytes=24 * 2**20),
        cost_estimate=COST,
        name="input_gradients",
    )(plan, *parts, key_gate, value_input, *after)
    return grad_key, grad_value, taps.T


def swapped(array, axis, step):
    size = lax.axis_size(axis)
    return lax.ppermute(array, axis, [(i, i ^ step) for i in range(size)])


def traded(pieces, axis):
    return [pieces[0]] + [swapped(pieces[step], axis, step) for step in range(1, len(pieces))]


def cut(array, position, members, axis):
    width = array.shape[axis] // members
    return [
        lax.dynamic_slice_in_dim(array, (position ^ step) * width, width, axis)
        for step in range(members)
    ]


def joined(pieces, position, axis):
    members = len(pieces)
    width = pieces[0].shape[axis]
    shape = list(pieces[0].shape)
    shape[axis] = members * width
    whole = jnp.zeros(shape, pieces[0].dtype)
    for step in range(members):
        whole = lax.dynamic_update_slice_in_dim(
            whole, pieces[step], (position ^ step) * width, axis
        )
    return whole


def wide(array):
    return array.astype(jnp.float32)


def hop(array, pairs):
    return lax.ppermute(
        array, "tp", [(2 * i + core, 2 * j + core) for i, j in pairs for core in range(2)]
    )


INWARD = ((0, 1), (3, 2))
ACROSS = ((1, 2), (2, 1))
OUTWARD = ((1, 0), (2, 3))
OWN, NEAR, MIDDLE, FAR = range(4)
IN_MIDDLE = POSITION + 1
CHIPS = ((0, 1, 2, 3), (1, 0, 3, 2), (2, 2, 1, 1), (3, 3, 0, 0))


def plan_kernel(who_ref, plan_ref):
    place = who_ref[1]
    chip, core = place // 2, place % 2
    for number, table in enumerate(CHIPS):
        source = jnp.where(
            chip < 2,
            jnp.where(chip == 0, table[0], table[1]),
            jnp.where(chip == 2, table[2], table[3]),
        )
        plan_ref[2 * number] = 2 * source + core
        plan_ref[2 * number + 1] = 2 * source + 1 - core
    plan_ref[POSITION] = who_ref[0]
    plan_ref[IN_MIDDLE] = ((chip == 1) | (chip == 2)).astype(jnp.int32)


def planned(who):
    return pl.pallas_call(
        plan_kernel,
        out_shape=jax.ShapeDtypeStruct((IN_MIDDLE + 1,), jnp.int32),
        in_specs=[SMEM],
        out_specs=SMEM,
        compiler_params=pltpu.CompilerParams(vmem_limit_bytes=2**20),
        cost_estimate=COST,
        name="plan",
    )(who)


def pass_kernel(*refs):
    del refs


def held_until(values, after):
    return pl.pallas_call(
        pass_kernel,
        out_shape=[jax.ShapeDtypeStruct(value.shape, value.dtype) for value in values],
        in_specs=[ANYWHERE] * (len(values) + len(after)),
        out_specs=[ANYWHERE] * len(values),
        input_output_aliases={number: number for number in range(len(values))},
        compiler_params=pltpu.CompilerParams(vmem_limit_bytes=2**20),
        cost_estimate=COST,
        name="held",
    )(*values, *after)


def add_kernel(*refs):
    refs[-1][...] = sum(wide(ref[...]) for ref in refs[:-1]).astype(jnp.bfloat16)


def added(*arrays):
    rows, width = arrays[0].shape
    part = pl.BlockSpec((rows // 4, width), lambda i: (i, 0))
    return pl.pallas_call(
        add_kernel,
        out_shape=jax.ShapeDtypeStruct((rows, width), jnp.bfloat16),
        grid=(4,),
        in_specs=[part] * len(arrays),
        out_specs=part,
        compiler_params=pltpu.CompilerParams(vmem_limit_bytes=8 * 2**20),
        cost_estimate=COST,
        name="added",
    )(*arrays)


def choice_kernel(plan_ref, middle_ref, end_ref, *refs):
    out_ref = refs[-1]
    in_middle = plan_ref[IN_MIDDLE] == 1

    @pl.when(in_middle)
    def _():
        out_ref[...] = middle_ref[...]

    @pl.when(jnp.logical_not(in_middle))
    def _():
        out_ref[...] = end_ref[...]


def chosen(plan, in_middle, at_end, after=()):
    return pl.pallas_call(
        choice_kernel,
        out_shape=jax.ShapeDtypeStruct(at_end.shape, at_end.dtype),
        in_specs=[SMEM, VMEM, VMEM] + [ANYWHERE] * len(after),
        out_specs=VMEM,
        compiler_params=pltpu.CompilerParams(vmem_limit_bytes=2**20),
        cost_estimate=COST,
        name="chosen",
    )(plan, in_middle, at_end, *after)


def gate_kernel(members, plan_ref, *refs):
    parts = refs[:members]
    query_ref, gated_ref, conv_ref = refs[members:]
    position = plan_ref[POSITION]
    share = parts[0].shape[1]
    for step in range(members):
        columns = pl.ds(pl.multiple_of((position ^ step) * share, share), share)
        conv = parts[step][...]
        conv_ref[:, columns] = conv
        gated_ref[:, columns] = (wide(conv) * wide(query_ref[:, columns])).astype(jnp.bfloat16)


def gated(plan, parts, query_gate):
    array = jax.ShapeDtypeStruct(query_gate.shape, jnp.bfloat16)
    return pl.pallas_call(
        functools.partial(gate_kernel, len(parts)),
        out_shape=[array, array],
        in_specs=[SMEM] + [VMEM] * (len(parts) + 1),
        out_specs=[VMEM] * 2,
        compiler_params=pltpu.CompilerParams(vmem_limit_bytes=8 * 2**20),
        cost_estimate=COST,
        name="gated_output",
    )(plan, *parts, query_gate)


def product_kernel(steps, joins, extra, _, data_ref, weight_ref, *refs):
    more, outputs = refs[:extra], refs[-(steps // joins) :]
    product = jnp.dot(data_ref[...], weight_ref[...], preferred_element_type=jnp.float32)
    for number in range(steps):
        out_ref = outputs[number // joins]
        wide_out = out_ref.shape[1] > product.shape[1]

        @pl.when(pl.program_id(0) == number)
        def _(number=number, out_ref=out_ref, wide_out=wide_out):
            total = product + wide(more[number][...]) if more else product
            if wide_out:
                width = product.shape[1]
                at = number % joins * width
                out_ref[:, at : at + width] = total.astype(jnp.bfloat16)
            else:
                out_ref[...] = total.astype(jnp.bfloat16)


def column_products(
    plan, data, out_weight, first, count, other, more=(), after=(), tiles=1, joins=1
):
    rows, depth = data.shape
    width = data.shape[1]
    tile = width // tiles
    steps = count * tiles

    def weights(i, at):
        return 0, at[2 * (first - i // tiles) + other] * tiles + i % tiles

    return pl.pallas_call(
        functools.partial(product_kernel, steps, joins, len(more)),
        out_shape=[jax.ShapeDtypeStruct((rows, tile * joins), jnp.bfloat16)] * (steps // joins),
        grid_spec=pltpu.PrefetchScalarGridSpec(
            num_scalar_prefetch=1,
            grid=(steps,),
            in_specs=[VMEM, pl.BlockSpec((depth, tile), weights)]
            + [VMEM] * len(more)
            + [ANYWHERE] * len(after),
            out_specs=[VMEM] * (steps // joins),
        ),
        compiler_params=pltpu.CompilerParams(vmem_limit_bytes=16 * 2**20),
        cost_estimate=COST,
        name="projection_blocks",
    )(plan, data, in_hbm(out_weight), *more, *after)


def cotangent_kernel(count, begin, _, weight_ref, *refs):
    blocks, refs = refs[:count], refs[count:]
    step = pl.program_id(0)
    total = refs[-1]

    for number, block in enumerate(blocks):

        @pl.when(step == number)
        def _(number=number, block=block):
            product = lax.dot_general(
                block[...], weight_ref[...], NT, preferred_element_type=jnp.float32
            )
            if number == 0:
                total[...] = product if begin else refs[0][...] + product
            else:
                total[...] += product


def last_cotangent_kernel(
    members, _, weight_ref, block_ref, start_ref, conv_ref, query_ref, grad_ref, *parts
):
    product = lax.dot_general(
        block_ref[...], weight_ref[...], NT, preferred_element_type=jnp.float32
    )
    dgated = wide((start_ref[...] + product).astype(jnp.bfloat16))
    grad_ref[...] = (dgated * wide(conv_ref[...])).astype(jnp.bfloat16)
    cotangent = (dgated * wide(query_ref[...])).astype(jnp.bfloat16)
    for step in range(members):

        @pl.when(pl.program_id(0) == step)
        def _(step=step):
            parts[step][...] = cotangent


def last_cotangents(plan, first, block, out_weight, start, convolved, query_gate, members):
    rows, width = block.shape
    channels = out_weight.shape[0]
    share = channels // members
    piece = pl.BlockSpec((rows, share), lambda i, at: (0, at[POSITION] ^ i))
    whole = pl.BlockSpec((rows, width), lambda i, at: (0, 0))
    part = pl.BlockSpec((rows, share), lambda i, at: (0, 0))
    return pl.pallas_call(
        functools.partial(last_cotangent_kernel, members),
        out_shape=[jax.ShapeDtypeStruct((rows, channels), jnp.bfloat16)]
        + [jax.ShapeDtypeStruct((rows, share), jnp.bfloat16)] * members,
        grid_spec=pltpu.PrefetchScalarGridSpec(
            num_scalar_prefetch=1,
            grid=(members,),
            in_specs=[
                pl.BlockSpec((share, width), lambda i, at: (at[POSITION] ^ i, at[first])),
                whole,
                piece,
                piece,
                piece,
            ],
            out_specs=[piece] + [part] * members,
        ),
        compiler_params=pltpu.CompilerParams(vmem_limit_bytes=16 * 2**20),
        cost_estimate=COST,
        name="cotangent_last",
    )(plan, in_hbm(out_weight), block, start, convolved, query_gate)


def both(blocks):
    return [part for block in blocks for part in (block, swapped(block, "tp", 1))]


def cotangent_products(plan, first, parts, out_weight, start=None, after=()):
    rows, width = parts[0].shape
    channels = out_weight.shape[0]
    count = len(parts)
    begin = start is None
    extra = () if begin else (start,)
    return pl.pallas_call(
        functools.partial(cotangent_kernel, count, begin),
        out_shape=jax.ShapeDtypeStruct((rows, channels), jnp.float32),
        grid_spec=pltpu.PrefetchScalarGridSpec(
            num_scalar_prefetch=1,
            grid=(count,),
            in_specs=[pl.BlockSpec((channels, width), lambda i, at: (0, at[first + i]))]
            + [VMEM] * (count + len(extra))
            + [ANYWHERE] * len(after),
            out_specs=VMEM,
        ),
        compiler_params=pltpu.CompilerParams(vmem_limit_bytes=16 * 2**20),
        cost_estimate=COST,
        name="cotangent_blocks",
    )(plan, in_hbm(out_weight), *parts, *extra, *after)


def packed_parts(position, key_gate, value_input, filter_taps, members, scale):
    length, channels = key_gate.shape
    share = channels // members
    product_in = (wide(key_gate) * wide(value_input)).astype(jnp.bfloat16)
    tap_rows = (filter_taps * scale).astype(jnp.bfloat16).T
    owned = filter_taps.shape[1] // members
    chunks = length // share
    packed = []
    pieces = cut(product_in, position, members, 1)
    for piece, taps in zip(pieces, cut(tap_rows, position, members, 0)):
        taps = taps.reshape(owned, chunks, share).transpose(1, 0, 2)
        taps = jnp.pad(taps, ((0, 0), (0, padded(owned) - owned), (0, 0)))
        packed.append(jnp.concatenate([piece, taps.reshape(-1, share)], axis=0))
    return packed


def unpacked_parts(position, parts, key_gate, value_input, groups):
    length, channels = key_gate.shape
    members = len(parts)
    share = channels // members
    owned = groups // members
    chunks = length // share
    input_grad = wide(joined([part[:length] for part in parts], position, 1))
    filter_parts = [
        part[length:]
        .reshape(chunks, padded(owned), share)[:, :owned]
        .transpose(1, 0, 2)
        .reshape(owned, length)
        for part in parts
    ]
    grad_filter = wide(joined(filter_parts, position, 0)).T
    grad_key = (input_grad * wide(value_input)).astype(jnp.bfloat16)
    grad_value = (input_grad * wide(key_gate)).astype(jnp.bfloat16)
    return grad_key, grad_value, grad_filter


def in_line(
    query_gate, key_gate, value_input, filter_taps, out_weight, out_grad, members, scale
):
    length, channels = query_gate.shape
    groups = filter_taps.shape[1]
    per_group = channels // groups
    who = jnp.stack([lax.axis_index("ctx"), lax.axis_index("tp")]).astype(jnp.int32)
    plan = planned(who)
    near, cross = hop(out_grad, INWARD + OUTWARD), hop(out_grad, ACROSS)
    total = cotangent_products(plan, 2 * OWN, both([out_grad]), out_weight)

    packed = prepare(who, key_gate, value_input, filter_taps, members, scale)
    input_parts = traded(packed, "ctx")
    conv_parts = convolve(plan, input_parts, length, per_group, (total,))
    *conv_parts, near, cross = held_until([*conv_parts, near, cross], ())
    far, skip = hop(near, ACROSS), hop(cross, OUTWARD)
    gated_out, convolved = gated(plan, traded(conv_parts, "ctx"), query_gate)

    def product(first, count, other, more=(), after=(), tiles=1, joins=1):
        return column_products(
            plan, gated_out, out_weight, first, count, other, more, after, tiles, joins
        )

    given_far = product(FAR, 1, 1, tiles=2)
    received = [swapped(part, "tp", 1) for part in given_far]
    (first,) = product(FAR, 1, 0, received, tiles=2, joins=2)
    far, skip, near = held_until([far, skip, near], (first,))
    mixed = chosen(plan, far, first)
    arrived = hop(mixed, OUTWARD + INWARD)
    given_middle = product(MIDDLE, 1, 1, (), (mixed,), tiles=2)
    received = [swapped(part, "tp", 1) for part in given_middle]
    (second,) = product(MIDDLE, 1, 0, received, tiles=2, joins=2)
    middle_block = added(cross, skip)
    blocks = [near, swapped(near, "tp", 1), middle_block]
    total = cotangent_products(plan, 2 * NEAR, blocks, out_weight, total, after=(second,))
    given_near, given_own = product(NEAR, 2, 1, (), (second,))
    (arrived,) = held_until([arrived], (total, given_near))
    through = added(first, arrived)
    two_a = hop(through, ACROSS)
    (second,) = held_until([second], (arrived,))
    two_b = hop(second, INWARD)

    far_block, far_other = both([chosen(plan, far, arrived, (through,))])
    blocks = [swapped(middle_block, "tp", 1), far_block]
    total = cotangent_products(
        plan, 2 * MIDDLE + 1, blocks, out_weight, total, after=(through,)
    )
    grad_query, *grad_parts = last_cotangents(
        plan, 2 * FAR + 1, far_other, out_weight, total, convolved, query_gate, members
    )
    received = (swapped(given_near, "tp", 1), swapped(given_own, "tp", 1))
    third, own = product(NEAR, 2, 0, received, (grad_parts[0],))
    grad_parts = traded(grad_parts, "ctx")

    two_a, two_b = held_until([two_a, two_b], tuple(grad_parts[1:]))
    third, second = added(third, two_a), added(second, two_b)
    back_parts = correlate(plan, input_parts, grad_parts, per_group, scale, (third, second))
    projected = added(own, hop(third, OUTWARD + INWARD), hop(second, ACROSS))
    back_parts = traded(back_parts, "ctx")
    return projected, grad_query, *finished(plan, back_parts, key_gate, value_input, groups, (projected,))


def anywhere(
    query_gate, key_gate, value_input, filter_taps, out_weight, out_grad, members, scale
):
    length, channels = query_gate.shape
    groups = filter_taps.shape[1]
    per_group = channels // groups
    position = lax.axis_index("ctx")
    plan = jnp.full((POSITION + 1,), position, jnp.int32)
    packed = packed_parts(position, key_gate, value_input, filter_taps, members, scale)
    input_parts = traded(packed, "ctx")
    conv_parts = traded(convolve(plan, input_parts, length, per_group), "ctx")
    convolved = joined(conv_parts, position, 1)
    gated_out = (wide(query_gate) * wide(convolved)).astype(jnp.bfloat16)
    partial_value = jnp.dot(gated_out, out_weight, preferred_element_type=jnp.float32)
    projected = lax.psum_scatter(
        partial_value.astype(jnp.bfloat16), "tp", scatter_dimension=1, tiled=True
    )
    dgated = jnp.einsum(
        "tk,ck->tc",
        lax.all_gather(out_grad, "tp", axis=1, tiled=True),
        out_weight,
        preferred_element_type=jnp.float32,
    ).astype(jnp.bfloat16)
    grad_query = (wide(dgated) * wide(convolved)).astype(jnp.bfloat16)
    conv_grad = (wide(dgated) * wide(query_gate)).astype(jnp.bfloat16)
    grad_parts = traded(cut(conv_grad, position, members, 1), "ctx")
    back_parts = correlate(plan, input_parts, grad_parts, per_group, scale)
    back_parts = traded(back_parts, "ctx")
    return (
        projected,
        grad_query,
        *unpacked_parts(position, back_parts, key_gate, value_input, groups),
    )


def local(query_gate, key_gate, value_input, filter_taps, out_weight, out_grad):
    length, channels = query_gate.shape
    groups = filter_taps.shape[1]
    members = lax.axis_size("ctx")
    scale = 1.0 / math.sqrt(length * members)
    fits = channels // members % 128 == 0 and groups // members % 16 == 0
    body = in_line if lax.axis_size("tp") == 8 and fits else anywhere
    return body(
        query_gate, key_gate, value_input, filter_taps, out_weight, out_grad, members, scale
    )


def solution(mesh):
    both = P("ctx", "tp")
    return jax.shard_map(
        local,
        mesh=mesh,
        in_specs=(both, both, both, both, P("tp", None), both),
        out_specs=(both,) * 5,
        check_vma=False,
    )
```

```python
import functools
import math
import jax
import jax.numpy as jnp
from jax import lax
from jax.experimental import pallas as pl
from jax.experimental.pallas import tpu as pltpu
from jax.sharding import PartitionSpec as P

BLOCK = 128
POSITION = 8
NT = (((1,), (1,)), ((), ()))
COST = pl.CostEstimate(flops=2**20, bytes_accessed=2**12, transcendentals=0)


def lag_matrix(row, length):
    lanes = lax.broadcasted_iota(jnp.int32, (BLOCK, BLOCK), 1)
    rows = lax.broadcasted_iota(jnp.int32, (BLOCK, BLOCK), 0)
    spread = pltpu.roll(
        jnp.broadcast_to(row, (BLOCK, length)), 0, axis=1, stride=1, stride_axis=0
    )
    first = jnp.where(lanes >= rows, spread[:, :BLOCK], 0.0)
    return jnp.concatenate(
        [first.astype(jnp.bfloat16), spread[:, BLOCK:].astype(jnp.bfloat16)], axis=1
    )


def stacked(ref, start, rows, members, width):
    pieces = []
    for member in range(members):
        part = ref[member, pl.ds(start, rows), :]
        for at in range(0, width, BLOCK):
            pieces.append(part[:, at : at + BLOCK])
    return jnp.concatenate(pieces, axis=0)


def spread_out(ref, start, rows, value, members, width):
    per_member = width // BLOCK
    for member in range(members):
        base = member * per_member * rows
        parts = [value[base + i * rows : base + (i + 1) * rows] for i in range(per_member)]
        ref[member, pl.ds(start, rows), :] = jnp.concatenate(parts, axis=1)


def padded(groups):
    return -(-groups // 16) * 16


def load_taps(tap_scr, packed, at, width):
    groups, channels = tap_scr.shape[0], packed.shape[1]
    rows = padded(groups)
    parts = [
        packed[width + chunk * rows : width + (chunk + 1) * rows, :].astype(jnp.float32)
        for chunk in range(width // channels)
    ]
    start = pl.multiple_of(at * width, width)
    tap_scr[:, pl.ds(start, width)] = jnp.concatenate(parts, axis=1)[:groups]


def forward_kernel(members, per_group, width, plan_ref, *refs):
    inputs, outputs = refs[:members], refs[-members - 3 : -3]
    tap_scr, in_scr, out_scr = refs[-3:]
    position = plan_ref[POSITION]
    channels = inputs[0].shape[1]
    groups = channels // per_group
    length = members * width
    blocks = length // BLOCK
    for step in range(members):
        at = position ^ step
        in_scr[at] = inputs[step][:width].T
        load_taps(tap_scr, inputs[step], at, width)

    def one_group(group, carry):
        start = pl.multiple_of(group * per_group, per_group)
        lags = lag_matrix(tap_scr[pl.ds(group, 1), :], length)
        data = stacked(in_scr, start, per_group, members, width)
        total = [jnp.zeros((per_group, BLOCK), jnp.float32) for _ in range(blocks)]
        for offset in range(0, blocks, 2):
            rows = (blocks - offset) * per_group
            result = jnp.dot(
                data[:rows],
                lags[:, offset * BLOCK : (offset + 2) * BLOCK],
                preferred_element_type=jnp.float32,
            )
            for side in range(2):
                for source in range(blocks - offset - side):
                    total[source + offset + side] += result[
                        source * per_group : (source + 1) * per_group,
                        side * BLOCK : (side + 1) * BLOCK,
                    ]
        value = jnp.concatenate(total, axis=0).astype(jnp.bfloat16)
        spread_out(out_scr, start, per_group, value, members, width)
        return carry

    lax.fori_loop(0, groups, one_group, 0, unroll=4)
    for step in range(members):
        outputs[step][...] = out_scr[position ^ step].T


def backward_kernel(members, per_group, scale, width, plan_ref, *refs):
    inputs, cotangents = refs[:members], refs[members : 2 * members]
    outputs = refs[-members - 6 : -6]
    tap_scr, in_scr, cot_scr, out_scr, grad_scr, pad_scr = refs[-6:]
    position = plan_ref[POSITION]
    channels = inputs[0].shape[1]
    groups = channels // per_group
    length = members * width
    blocks = length // BLOCK
    depth = blocks * per_group
    for step in range(members):
        at = position ^ step
        in_scr[at] = inputs[step][:width].T
        cot_scr[at] = cotangents[step][...].T
        load_taps(tap_scr, inputs[step], at, width)
    pad_scr[...] = jnp.zeros_like(pad_scr)
    rows_of = lax.broadcasted_iota(jnp.int32, (BLOCK, BLOCK), 0)
    lanes_of = lax.broadcasted_iota(jnp.int32, (BLOCK, BLOCK), 1)
    mirror = (rows_of + lanes_of == BLOCK - 1).astype(jnp.bfloat16)

    def one_group(group, carry):
        start = pl.multiple_of(group * per_group, per_group)
        lags = lag_matrix(tap_scr[pl.ds(group, 1), :], length)
        data = stacked(in_scr, start, per_group, members, width)
        cot = stacked(cot_scr, start, per_group, members, width)
        pad_scr[:depth, :BLOCK] = cot
        pad_scr[: depth - per_group, BLOCK:] = cot[per_group:]
        flipped = lax.dot_general(
            mirror, data, NT, preferred_element_type=jnp.float32
        ).astype(jnp.bfloat16)
        total = jnp.zeros((depth, BLOCK), jnp.float32)
        products = []
        for offset in range(0, blocks, 2):
            rows = depth - offset * per_group
            pair = pad_scr[offset * per_group : offset * per_group + depth, :]
            result = lax.dot_general(
                pair[:rows],
                lags[:, offset * BLOCK : (offset + 2) * BLOCK],
                NT,
                preferred_element_type=jnp.float32,
            )
            if rows < depth:
                result = jnp.concatenate(
                    [result, jnp.zeros((depth - rows, BLOCK), jnp.float32)], axis=0
                )
            total = total + result
            products.append(jnp.dot(flipped, pair, preferred_element_type=jnp.float32))
        spread_out(
            out_scr, start, per_group, total.astype(jnp.bfloat16), members, width
        )
        kept = jnp.where(rows_of + lanes_of >= BLOCK - 1, products[0][:, :BLOCK], 0.0)
        product = jnp.concatenate([kept, products[0][:, BLOCK:], *products[1:]], axis=1)
        product = pltpu.roll(
            product, length - (BLOCK - 1), axis=1, stride=1, stride_axis=0
        )
        grad_scr[pl.ds(group, 1), :] = jnp.sum(product, axis=0, keepdims=True) * scale
        return carry

    lax.fori_loop(0, groups, one_group, 0, unroll=4)
    for step in range(members):
        at = position ^ step
        outputs[step][:width] = out_scr[at].T
        rows = padded(groups)
        whole = grad_scr[:, pl.ds(pl.multiple_of(at * width, width), width)].astype(jnp.bfloat16)
        if rows > groups:
            blank = jnp.zeros((rows - groups, width), jnp.bfloat16)
            whole = jnp.concatenate([whole, blank], axis=0)
        for chunk in range(width // channels):
            outputs[step][width + chunk * rows : width + (chunk + 1) * rows, :] = whole[
                :, chunk * channels : (chunk + 1) * channels
            ]


VMEM = pl.BlockSpec(memory_space=pltpu.VMEM)
ANYWHERE = pl.BlockSpec(memory_space=pl.ANY)
SMEM = pl.BlockSpec(memory_space=pltpu.SMEM)


def convolve(plan, inputs, width, per_group, after=()):
    members = len(inputs)
    channels = inputs[0].shape[1]
    length = members * width
    return pl.pallas_call(
        functools.partial(forward_kernel, members, per_group, width),
        out_shape=[jax.ShapeDtypeStruct((width, channels), jnp.bfloat16)] * members,
        in_specs=[SMEM] + [VMEM] * members + [ANYWHERE] * len(after),
        out_specs=[VMEM] * members,
        scratch_shapes=[
            pltpu.VMEM((channels // per_group, length), jnp.float32),
            pltpu.VMEM((members, channels, width), jnp.bfloat16),
            pltpu.VMEM((members, channels, width), jnp.bfloat16),
        ],
        compiler_params=pltpu.CompilerParams(vmem_limit_bytes=24 * 2**20),
        cost_estimate=COST,
        name="causal_conv",
    )(plan, *inputs, *after)


def correlate(plan, inputs, cotangents, per_group, scale, after=()):
    members = len(inputs)
    width, channels = cotangents[0].shape
    length = members * width
    groups = channels // per_group
    return pl.pallas_call(
        functools.partial(backward_kernel, members, per_group, scale, width),
        out_shape=[jax.ShapeDtypeStruct(inputs[0].shape, jnp.bfloat16)] * members,
        in_specs=[SMEM] + [VMEM] * (2 * members) + [ANYWHERE] * len(after),
        out_specs=[VMEM] * members,
        scratch_shapes=[
            pltpu.VMEM((groups, length), jnp.float32),
            pltpu.VMEM((members, channels, width), jnp.bfloat16),
            pltpu.VMEM((members, channels, width), jnp.bfloat16),
            pltpu.VMEM((members, channels, width), jnp.bfloat16),
            pltpu.VMEM((groups, length), jnp.float32),
            pltpu.VMEM((2 * length // BLOCK * per_group, 2 * BLOCK), jnp.bfloat16),
        ],
        compiler_params=pltpu.CompilerParams(vmem_limit_bytes=24 * 2**20),
        cost_estimate=COST,
        name="causal_conv_grads",
    )(plan, *inputs, *cotangents, *after)


def in_hbm(array):
    return pltpu.with_memory_space_constraint(array, pltpu.HBM)


def prepare_kernel(members, scale, who_ref, key_ref, value_ref, taps_ref, *outputs):
    position = who_ref[0]
    step_no = pl.program_id(0)
    rows, channels = key_ref.shape
    share = channels // members
    groups = taps_ref.shape[0] // members
    total_width = taps_ref.shape[1]
    for step in range(members):
        at = position ^ step
        columns = pl.ds(pl.multiple_of(at * share, share), share)
        product = key_ref[:, columns].astype(jnp.float32) * value_ref[:, columns].astype(
            jnp.float32
        )
        here = pl.ds(pl.multiple_of(step_no * rows, rows), rows)
        outputs[step][here, :] = product.astype(jnp.bfloat16)

    @pl.when(step_no == 0)
    def _():
        for step in range(members):
            at = position ^ step
            taps = taps_ref[pl.ds(pl.multiple_of(at * groups, groups), groups), :]
            taps = (taps * scale).astype(jnp.bfloat16)
            for chunk in range(total_width // share):
                start = total_width + chunk * groups
                outputs[step][start : start + groups, :] = taps[
                    :, chunk * share : (chunk + 1) * share
                ]


def prepare(who, key_gate, value_input, filter_taps, members, scale):
    width, channels = key_gate.shape
    share = channels // members
    rows = width + filter_taps.size // members // share
    tile = width // 4
    part = pl.BlockSpec((tile, channels), lambda i: (i, 0))
    return pl.pallas_call(
        functools.partial(prepare_kernel, members, scale),
        out_shape=[jax.ShapeDtypeStruct((rows, share), jnp.bfloat16)] * members,
        grid=(4,),
        in_specs=[SMEM, part, part, pl.BlockSpec(filter_taps.shape[::-1], lambda i: (0, 0))],
        out_specs=[VMEM] * members,
        compiler_params=pltpu.CompilerParams(vmem_limit_bytes=24 * 2**20),
        cost_estimate=COST,
        name="gated_input",
    )(who, in_hbm(key_gate), in_hbm(value_input), in_hbm(filter_taps.T))


def finish_kernel(members, plan_ref, *refs):
    parts = refs[:members]
    key_ref, value_ref = refs[members : members + 2]
    key_out, value_out, taps_out = refs[-3:]
    position = plan_ref[POSITION]
    width, channels = key_ref.shape
    share = channels // members
    groups = taps_out.shape[0] // members
    for step in range(members):
        at = position ^ step
        columns = pl.ds(pl.multiple_of(at * share, share), share)
        grad = parts[step][:width].astype(jnp.float32)
        key_out[:, columns] = (grad * value_ref[:, columns].astype(jnp.float32)).astype(
            jnp.bfloat16
        )
        value_out[:, columns] = (grad * key_ref[:, columns].astype(jnp.float32)).astype(
            jnp.bfloat16
        )
        taps = [
            parts[step][width + chunk * groups : width + (chunk + 1) * groups, :]
            for chunk in range(width // share)
        ]
        taps_out[pl.ds(pl.multiple_of(at * groups, groups), groups), :] = jnp.concatenate(
            taps, axis=1
        ).astype(jnp.float32)


def finished(plan, parts, key_gate, value_input, groups, after=()):
    members = len(parts)
    width, channels = key_gate.shape
    array = jax.ShapeDtypeStruct((width, channels), jnp.bfloat16)
    grad_key, grad_value, taps = pl.pallas_call(
        functools.partial(finish_kernel, members),
        out_shape=[array, array, jax.ShapeDtypeStruct((groups, width), jnp.float32)],
        in_specs=[SMEM] + [VMEM] * (members + 2) + [ANYWHERE] * len(after),
        out_specs=[VMEM] * 3,
        compiler_params=pltpu.CompilerParams(vmem_limit_bytes=24 * 2**20),
        cost_estimate=COST,
        name="input_gradients",
    )(plan, *parts, key_gate, value_input, *after)
    return grad_key, grad_value, taps.T


def swapped(array, axis, step):
    size = lax.axis_size(axis)
    return lax.ppermute(array, axis, [(i, i ^ step) for i in range(size)])


def traded(pieces, axis):
    return [pieces[0]] + [swapped(pieces[step], axis, step) for step in range(1, len(pieces))]


def cut(array, position, members, axis):
    width = array.shape[axis] // members
    return [
        lax.dynamic_slice_in_dim(array, (position ^ step) * width, width, axis)
        for step in range(members)
    ]


def joined(pieces, position, axis):
    members = len(pieces)
    width = pieces[0].shape[axis]
    shape = list(pieces[0].shape)
    shape[axis] = members * width
    whole = jnp.zeros(shape, pieces[0].dtype)
    for step in range(members):
        whole = lax.dynamic_update_slice_in_dim(
            whole, pieces[step], (position ^ step) * width, axis
        )
    return whole


def wide(array):
    return array.astype(jnp.float32)


def hop(array, pairs):
    return lax.ppermute(
        array, "tp", [(2 * i + core, 2 * j + core) for i, j in pairs for core in range(2)]
    )


INWARD = ((0, 1), (3, 2))
ACROSS = ((1, 2), (2, 1))
OUTWARD = ((1, 0), (2, 3))
OWN, NEAR, MIDDLE, FAR = range(4)
IN_MIDDLE = POSITION + 1
CHIPS = ((0, 1, 2, 3), (1, 0, 3, 2), (2, 2, 1, 1), (3, 3, 0, 0))


def plan_kernel(who_ref, plan_ref):
    place = who_ref[1]
    chip, core = place // 2, place % 2
    for number, table in enumerate(CHIPS):
        source = jnp.where(
            chip < 2,
            jnp.where(chip == 0, table[0], table[1]),
            jnp.where(chip == 2, table[2], table[3]),
        )
        plan_ref[2 * number] = 2 * source + core
        plan_ref[2 * number + 1] = 2 * source + 1 - core
    plan_ref[POSITION] = who_ref[0]
    plan_ref[IN_MIDDLE] = ((chip == 1) | (chip == 2)).astype(jnp.int32)


def planned(who):
    return pl.pallas_call(
        plan_kernel,
        out_shape=jax.ShapeDtypeStruct((IN_MIDDLE + 1,), jnp.int32),
        in_specs=[SMEM],
        out_specs=SMEM,
        compiler_params=pltpu.CompilerParams(vmem_limit_bytes=2**20),
        cost_estimate=COST,
        name="plan",
    )(who)


def pass_kernel(*refs):
    del refs


def held_until(values, after):
    return pl.pallas_call(
        pass_kernel,
        out_shape=[jax.ShapeDtypeStruct(value.shape, value.dtype) for value in values],
        in_specs=[ANYWHERE] * (len(values) + len(after)),
        out_specs=[ANYWHERE] * len(values),
        input_output_aliases={number: number for number in range(len(values))},
        compiler_params=pltpu.CompilerParams(vmem_limit_bytes=2**20),
        cost_estimate=COST,
        name="held",
    )(*values, *after)


def add_kernel(count, *refs):
    total = sum(wide(ref[...]) for ref in refs[:count])
    if len(refs) > count + 1:
        halves = [wide(ref[...]) for ref in refs[count:-1]]
        total = total + jnp.concatenate(halves, axis=1)
    refs[-1][...] = total.astype(jnp.bfloat16)


def added(*arrays, halves=()):
    rows, width = arrays[0].shape
    part = pl.BlockSpec((rows // 4, width), lambda i: (i, 0))
    half = pl.BlockSpec((rows // 4, width // 2), lambda i: (i, 0))
    return pl.pallas_call(
        functools.partial(add_kernel, len(arrays)),
        out_shape=jax.ShapeDtypeStruct((rows, width), jnp.bfloat16),
        grid=(4,),
        in_specs=[part] * len(arrays) + [half] * len(halves),
        out_specs=part,
        compiler_params=pltpu.CompilerParams(vmem_limit_bytes=8 * 2**20),
        cost_estimate=COST,
        name="added",
    )(*arrays, *halves)


def passing_kernel(plan_ref, first_ref, arrived_ref, second_ref, *refs):
    out_ref = refs[-1]
    in_middle = plan_ref[IN_MIDDLE] == 1

    @pl.when(in_middle)
    def _():
        out_ref[...] = (wide(first_ref[...]) + wide(arrived_ref[...])).astype(jnp.bfloat16)

    @pl.when(jnp.logical_not(in_middle))
    def _():
        out_ref[...] = second_ref[...]


def passing(plan, first, arrived, second, after):
    return pl.pallas_call(
        passing_kernel,
        out_shape=jax.ShapeDtypeStruct(first.shape, first.dtype),
        in_specs=[SMEM] + [VMEM] * 3 + [ANYWHERE] * len(after),
        out_specs=VMEM,
        compiler_params=pltpu.CompilerParams(vmem_limit_bytes=4 * 2**20),
        cost_estimate=COST,
        name="passing",
    )(plan, first, arrived, second, *after)


def choice_kernel(plan_ref, middle_ref, end_ref, *refs):
    out_ref = refs[-1]
    in_middle = plan_ref[IN_MIDDLE] == 1

    @pl.when(in_middle)
    def _():
        out_ref[...] = middle_ref[...]

    @pl.when(jnp.logical_not(in_middle))
    def _():
        out_ref[...] = end_ref[...]


def chosen(plan, in_middle, at_end, after=()):
    return pl.pallas_call(
        choice_kernel,
        out_shape=jax.ShapeDtypeStruct(at_end.shape, at_end.dtype),
        in_specs=[SMEM, VMEM, VMEM] + [ANYWHERE] * len(after),
        out_specs=VMEM,
        compiler_params=pltpu.CompilerParams(vmem_limit_bytes=2**20),
        cost_estimate=COST,
        name="chosen",
    )(plan, in_middle, at_end, *after)


def gate_kernel(members, plan_ref, *refs):
    parts = refs[:members]
    query_ref, gated_ref, conv_ref = refs[members:]
    position = plan_ref[POSITION]
    share = parts[0].shape[1]
    for step in range(members):
        columns = pl.ds(pl.multiple_of((position ^ step) * share, share), share)
        conv = parts[step][...]
        conv_ref[:, columns] = conv
        gated_ref[:, columns] = (wide(conv) * wide(query_ref[:, columns])).astype(jnp.bfloat16)


def gated(plan, parts, query_gate):
    array = jax.ShapeDtypeStruct(query_gate.shape, jnp.bfloat16)
    return pl.pallas_call(
        functools.partial(gate_kernel, len(parts)),
        out_shape=[array, array],
        in_specs=[SMEM] + [VMEM] * (len(parts) + 1),
        out_specs=[VMEM] * 2,
        compiler_params=pltpu.CompilerParams(vmem_limit_bytes=8 * 2**20),
        cost_estimate=COST,
        name="gated_output",
    )(plan, *parts, query_gate)


def spans(widths, start, stop):
    found, begin = [], 0
    for number, width in enumerate(widths):
        low, high = max(start, begin), min(stop, begin + width)
        if low < high:
            found.append((number, slice(low - begin, high - begin), slice(low - start, high - start)))
        begin += width
    return found


def product_kernel(steps, more_widths, out_widths, _, data_ref, weight_ref, *refs):
    more, outputs = refs[: len(more_widths)], refs[-len(out_widths) :]
    product = jnp.dot(data_ref[...], weight_ref[...], preferred_element_type=jnp.float32)
    width = product.shape[1]
    for step in range(steps):
        start, stop = step * width, (step + 1) * width

        @pl.when(pl.program_id(0) == step)
        def _(start=start, stop=stop):
            total = product
            if more:
                parts = [wide(more[n][:, there]) for n, there, _ in spans(more_widths, start, stop)]
                total = total + jnp.concatenate(parts, axis=1)
            total = total.astype(jnp.bfloat16)
            for n, there, here in spans(out_widths, start, stop):
                outputs[n][:, there] = total[:, here]


def column_products(
    plan, data, out_weight, first, count, other, more=(), after=(), tiles=1, widths=()
):
    rows, depth = data.shape
    width = data.shape[1]
    tile = width // tiles
    steps = count * tiles
    widths = tuple(widths) or (width,) * count

    def weights(i, at):
        return 0, at[2 * (first - i // tiles) + other] * tiles + i % tiles

    return pl.pallas_call(
        functools.partial(product_kernel, steps, [part.shape[1] for part in more], widths),
        out_shape=[jax.ShapeDtypeStruct((rows, part), jnp.bfloat16) for part in widths],
        grid_spec=pltpu.PrefetchScalarGridSpec(
            num_scalar_prefetch=1,
            grid=(steps,),
            in_specs=[VMEM, pl.BlockSpec((depth, tile), weights)]
            + [VMEM] * len(more)
            + [ANYWHERE] * len(after),
            out_specs=[VMEM] * len(widths),
        ),
        compiler_params=pltpu.CompilerParams(vmem_limit_bytes=16 * 2**20),
        cost_estimate=COST,
        name="projection_blocks",
    )(plan, data, in_hbm(out_weight), *more, *after)


def cotangent_kernel(count, begin, _, weight_ref, *refs):
    blocks, refs = refs[:count], refs[count:]
    step = pl.program_id(0)
    total = refs[-1]

    for number, block in enumerate(blocks):

        @pl.when(step == number)
        def _(number=number, block=block):
            product = lax.dot_general(
                block[...], weight_ref[...], NT, preferred_element_type=jnp.float32
            )
            if number == 0:
                total[...] = product if begin else refs[0][...] + product
            else:
                total[...] += product


def last_cotangent_kernel(
    members, plan_ref, weight_ref, block_ref, start_ref, conv_ref, query_ref, *refs
):
    parts, cot_scr = refs[-1 - members : -1], refs[-1]
    grad_ref = refs[-2 - members]
    product = lax.dot_general(
        block_ref[...], weight_ref[...], NT, preferred_element_type=jnp.float32
    )
    dgated = wide((start_ref[...] + product).astype(jnp.bfloat16))
    grad_ref[...] = (dgated * wide(conv_ref[...])).astype(jnp.bfloat16)
    cot_scr[...] = (dgated * wide(query_ref[...])).astype(jnp.bfloat16)
    share = parts[0].shape[1]
    odd = plan_ref[POSITION] % 2
    for step in range(0, members, 2):

        @pl.when(pl.program_id(0) == step // 2)
        def _(step=step):
            parts[step][...] = cot_scr[:, pl.ds(pl.multiple_of(odd * share, share), share)]
            parts[step + 1][...] = cot_scr[
                :, pl.ds(pl.multiple_of((1 - odd) * share, share), share)
            ]


def last_cotangents(
    plan, first, block, out_weight, start, convolved, query_gate, members, after
):
    rows, width = block.shape
    channels = out_weight.shape[0]
    share = channels // members
    pair = pl.BlockSpec((rows, 2 * share), lambda i, at: (0, at[POSITION] // 2 ^ i))
    return pl.pallas_call(
        functools.partial(last_cotangent_kernel, members),
        out_shape=[jax.ShapeDtypeStruct((rows, channels), jnp.bfloat16)]
        + [jax.ShapeDtypeStruct((rows, share), jnp.bfloat16)] * members,
        grid_spec=pltpu.PrefetchScalarGridSpec(
            num_scalar_prefetch=1,
            grid=(members // 2,),
            in_specs=[
                pl.BlockSpec((2 * share, width), lambda i, at: (at[POSITION] // 2 ^ i, at[first])),
                VMEM,
                pair,
                pair,
                pair,
            ]
            + [ANYWHERE] * len(after),
            out_specs=[pair] + [VMEM] * members,
            scratch_shapes=[pltpu.VMEM((rows, 2 * share), jnp.bfloat16)],
        ),
        compiler_params=pltpu.CompilerParams(vmem_limit_bytes=24 * 2**20),
        cost_estimate=COST,
        name="cotangent_last",
    )(plan, in_hbm(out_weight), block, start, convolved, query_gate, *after)


def both(blocks):
    return [part for block in blocks for part in (block, swapped(block, "tp", 1))]


def cotangent_products(plan, first, parts, out_weight, start=None, after=()):
    rows, width = parts[0].shape
    channels = out_weight.shape[0]
    count = len(parts)
    begin = start is None
    extra = () if begin else (start,)
    return pl.pallas_call(
        functools.partial(cotangent_kernel, count, begin),
        out_shape=jax.ShapeDtypeStruct((rows, channels), jnp.float32),
        grid_spec=pltpu.PrefetchScalarGridSpec(
            num_scalar_prefetch=1,
            grid=(count,),
            in_specs=[pl.BlockSpec((channels, width), lambda i, at: (0, at[first + i]))]
            + [VMEM] * (count + len(extra))
            + [ANYWHERE] * len(after),
            out_specs=VMEM,
        ),
        compiler_params=pltpu.CompilerParams(vmem_limit_bytes=16 * 2**20),
        cost_estimate=COST,
        name="cotangent_blocks",
    )(plan, in_hbm(out_weight), *parts, *extra, *after)


def packed_parts(position, key_gate, value_input, filter_taps, members, scale):
    length, channels = key_gate.shape
    share = channels // members
    product_in = (wide(key_gate) * wide(value_input)).astype(jnp.bfloat16)
    tap_rows = (filter_taps * scale).astype(jnp.bfloat16).T
    owned = filter_taps.shape[1] // members
    chunks = length // share
    packed = []
    pieces = cut(product_in, position, members, 1)
    for piece, taps in zip(pieces, cut(tap_rows, position, members, 0)):
        taps = taps.reshape(owned, chunks, share).transpose(1, 0, 2)
        taps = jnp.pad(taps, ((0, 0), (0, padded(owned) - owned), (0, 0)))
        packed.append(jnp.concatenate([piece, taps.reshape(-1, share)], axis=0))
    return packed


def unpacked_parts(position, parts, key_gate, value_input, groups):
    length, channels = key_gate.shape
    members = len(parts)
    share = channels // members
    owned = groups // members
    chunks = length // share
    input_grad = wide(joined([part[:length] for part in parts], position, 1))
    filter_parts = [
        part[length:]
        .reshape(chunks, padded(owned), share)[:, :owned]
        .transpose(1, 0, 2)
        .reshape(owned, length)
        for part in parts
    ]
    grad_filter = wide(joined(filter_parts, position, 0)).T
    grad_key = (input_grad * wide(value_input)).astype(jnp.bfloat16)
    grad_value = (input_grad * wide(key_gate)).astype(jnp.bfloat16)
    return grad_key, grad_value, grad_filter


def in_line(
    query_gate, key_gate, value_input, filter_taps, out_weight, out_grad, members, scale
):
    length, channels = query_gate.shape
    groups = filter_taps.shape[1]
    per_group = channels // groups
    who = jnp.stack([lax.axis_index("ctx"), lax.axis_index("tp")]).astype(jnp.int32)
    plan = planned(who)
    near, cross = hop(out_grad, INWARD + OUTWARD), hop(out_grad, ACROSS)
    total = cotangent_products(plan, 2 * OWN, both([out_grad]), out_weight)

    packed = prepare(who, key_gate, value_input, filter_taps, members, scale)
    input_parts = traded(packed, "ctx")
    conv_parts = convolve(plan, input_parts, length, per_group, (total,))
    *conv_parts, near, cross = held_until([*conv_parts, near, cross], ())
    far, skip = hop(near, ACROSS), hop(cross, OUTWARD)
    gated_out, convolved = gated(plan, traded(conv_parts, "ctx"), query_gate)

    def product(first, count, other, more=(), after=(), tiles=1, widths=()):
        return column_products(
            plan, gated_out, out_weight, first, count, other, more, after, tiles, widths
        )

    third_part = 2 * channels // 3 // 128 * 128
    widths = (2 * channels - 2 * third_part, third_part, third_part)
    given = product(FAR, 2, 1, tiles=2, widths=widths)
    received = [swapped(part, "tp", 1) for part in given]
    first, second = product(FAR, 2, 0, received, tiles=2)
    far, skip, near = held_until([far, skip, near], (first,))
    mixed = chosen(plan, far, first)
    arrived = hop(mixed, OUTWARD + INWARD)
    beside = hop(second, ACROSS)
    middle_block = added(cross, skip)
    blocks = [near, swapped(near, "tp", 1), middle_block]
    total = cotangent_products(plan, 2 * NEAR, blocks, out_weight, total, after=(mixed,))
    given = product(NEAR, 2, 1, (), (mixed,))
    (arrived,) = held_until([arrived], (total, given[0]))
    passed = passing(plan, first, arrived, second, (beside,))
    jumped = hop(passed, ((0, 2), (1, 3), (2, 0), (3, 1)))

    far_block, far_other = both([chosen(plan, far, arrived, (passed,))])
    blocks = [swapped(middle_block, "tp", 1), far_block]
    total = cotangent_products(
        plan, 2 * MIDDLE + 1, blocks, out_weight, total, after=(passed,)
    )
    received = [swapped(part, "tp", 1) for part in given]
    grad_query, *grad_parts = last_cotangents(
        plan, 2 * FAR + 1, far_other, out_weight, total, convolved, query_gate, members, received
    )
    widths = (channels // 2, channels // 2, channels)
    *halves, own = product(NEAR, 2, 0, received, (grad_parts[0],), widths=widths)
    halves_near = [hop(half, INWARD + OUTWARD) for half in halves]
    grad_parts = traded(grad_parts, "ctx")
    back_parts = correlate(plan, input_parts, grad_parts, per_group, scale, (own,))
    back_parts = held_until(back_parts, (halves_near[0],))
    projected = added(own, beside, jumped, halves=halves_near)
    back_parts = traded(back_parts, "ctx")
    return projected, grad_query, *finished(plan, back_parts, key_gate, value_input, groups, (projected,))


def anywhere(
    query_gate, key_gate, value_input, filter_taps, out_weight, out_grad, members, scale
):
    length, channels = query_gate.shape
    groups = filter_taps.shape[1]
    per_group = channels // groups
    position = lax.axis_index("ctx")
    plan = jnp.full((POSITION + 1,), position, jnp.int32)
    packed = packed_parts(position, key_gate, value_input, filter_taps, members, scale)
    input_parts = traded(packed, "ctx")
    conv_parts = traded(convolve(plan, input_parts, length, per_group), "ctx")
    convolved = joined(conv_parts, position, 1)
    gated_out = (wide(query_gate) * wide(convolved)).astype(jnp.bfloat16)
    partial_value = jnp.dot(gated_out, out_weight, preferred_element_type=jnp.float32)
    projected = lax.psum_scatter(
        partial_value.astype(jnp.bfloat16), "tp", scatter_dimension=1, tiled=True
    )
    dgated = jnp.einsum(
        "tk,ck->tc",
        lax.all_gather(out_grad, "tp", axis=1, tiled=True),
        out_weight,
        preferred_element_type=jnp.float32,
    ).astype(jnp.bfloat16)
    grad_query = (wide(dgated) * wide(convolved)).astype(jnp.bfloat16)
    conv_grad = (wide(dgated) * wide(query_gate)).astype(jnp.bfloat16)
    grad_parts = traded(cut(conv_grad, position, members, 1), "ctx")
    back_parts = correlate(plan, input_parts, grad_parts, per_group, scale)
    back_parts = traded(back_parts, "ctx")
    return (
        projected,
        grad_query,
        *unpacked_parts(position, back_parts, key_gate, value_input, groups),
    )


def local(query_gate, key_gate, value_input, filter_taps, out_weight, out_grad):
    length, channels = query_gate.shape
    groups = filter_taps.shape[1]
    members = lax.axis_size("ctx")
    scale = 1.0 / math.sqrt(length * members)
    fits = channels // members % 128 == 0 and groups // members % 16 == 0
    body = in_line if lax.axis_size("tp") == 8 and fits else anywhere
    return body(
        query_gate, key_gate, value_input, filter_taps, out_weight, out_grad, members, scale
    )


def solution(mesh):
    both = P("ctx", "tp")
    return jax.shard_map(
        local,
        mesh=mesh,
        in_specs=(both, both, both, both, P("tp", None), both),
        out_specs=(both,) * 5,
        check_vma=False,
    )
```

```python
import functools
import math
import jax
import jax.numpy as jnp
from jax import lax
from jax.experimental import pallas as pl
from jax.experimental.pallas import tpu as pltpu
from jax.sharding import PartitionSpec as P

BLOCK = 128
POSITION = 8
NT = (((1,), (1,)), ((), ()))
COST = pl.CostEstimate(flops=2**20, bytes_accessed=2**12, transcendentals=0)


def lag_matrix(row, length):
    lanes = lax.broadcasted_iota(jnp.int32, (BLOCK, BLOCK), 1)
    rows = lax.broadcasted_iota(jnp.int32, (BLOCK, BLOCK), 0)
    spread = pltpu.roll(
        jnp.broadcast_to(row, (BLOCK, length)), 0, axis=1, stride=1, stride_axis=0
    )
    first = jnp.where(lanes >= rows, spread[:, :BLOCK], 0.0)
    return jnp.concatenate(
        [first.astype(jnp.bfloat16), spread[:, BLOCK:].astype(jnp.bfloat16)], axis=1
    )


def stacked(ref, start, rows, members, width):
    pieces = []
    for member in range(members):
        part = ref[member, pl.ds(start, rows), :]
        for at in range(0, width, BLOCK):
            pieces.append(part[:, at : at + BLOCK])
    return jnp.concatenate(pieces, axis=0)


def spread_out(ref, start, rows, value, members, width):
    per_member = width // BLOCK
    for member in range(members):
        base = member * per_member * rows
        parts = [value[base + i * rows : base + (i + 1) * rows] for i in range(per_member)]
        ref[member, pl.ds(start, rows), :] = jnp.concatenate(parts, axis=1)


def padded(groups):
    return -(-groups // 16) * 16


def load_taps(tap_scr, packed, at, width):
    groups, channels = tap_scr.shape[0], packed.shape[1]
    rows = padded(groups)
    parts = [
        packed[width + chunk * rows : width + (chunk + 1) * rows, :].astype(jnp.float32)
        for chunk in range(width // channels)
    ]
    start = pl.multiple_of(at * width, width)
    tap_scr[:, pl.ds(start, width)] = jnp.concatenate(parts, axis=1)[:groups]


def forward_kernel(members, per_group, width, plan_ref, *refs):
    inputs, outputs = refs[:members], refs[-members - 3 : -3]
    in_scr, tap_scr, out_scr = refs[-3:]
    position = plan_ref[POSITION]
    channels = inputs[0].shape[1]
    groups = channels // per_group
    length = members * width
    blocks = length // BLOCK
    for step in range(members):
        at = position ^ step
        in_scr[at] = inputs[step][:width].T
        load_taps(tap_scr, inputs[step], at, width)

    def one_group(group, carry):
        start = pl.multiple_of(group * per_group, per_group)
        lags = lag_matrix(tap_scr[pl.ds(group, 1), :], length)
        data = stacked(in_scr, start, per_group, members, width)
        total = [jnp.zeros((per_group, BLOCK), jnp.float32) for _ in range(blocks)]
        for offset in range(0, blocks, 2):
            rows = (blocks - offset) * per_group
            result = jnp.dot(
                data[:rows],
                lags[:, offset * BLOCK : (offset + 2) * BLOCK],
                preferred_element_type=jnp.float32,
            )
            for side in range(2):
                for source in range(blocks - offset - side):
                    total[source + offset + side] += result[
                        source * per_group : (source + 1) * per_group,
                        side * BLOCK : (side + 1) * BLOCK,
                    ]
        value = jnp.concatenate(total, axis=0).astype(jnp.bfloat16)
        spread_out(out_scr, start, per_group, value, members, width)
        return carry

    lax.fori_loop(0, groups, one_group, 0, unroll=4)
    for step in range(members):
        outputs[step][...] = out_scr[position ^ step].T


def backward_kernel(members, per_group, scale, width, plan_ref, in_scr, tap_scr, *refs):
    cotangents = refs[:members]
    outputs = refs[-members - 4 : -4]
    cot_scr, out_scr, grad_scr, pad_scr = refs[-4:]
    position = plan_ref[POSITION]
    channels = cotangents[0].shape[1]
    groups = channels // per_group
    length = members * width
    blocks = length // BLOCK
    depth = blocks * per_group
    for step in range(members):
        at = position ^ step
        cot_scr[at] = cotangents[step][...].T
    pad_scr[...] = jnp.zeros_like(pad_scr)
    rows_of = lax.broadcasted_iota(jnp.int32, (BLOCK, BLOCK), 0)
    lanes_of = lax.broadcasted_iota(jnp.int32, (BLOCK, BLOCK), 1)
    mirror = (rows_of + lanes_of == BLOCK - 1).astype(jnp.bfloat16)

    def one_group(group, carry):
        start = pl.multiple_of(group * per_group, per_group)
        lags = lag_matrix(tap_scr[pl.ds(group, 1), :], length)
        data = stacked(in_scr, start, per_group, members, width)
        cot = stacked(cot_scr, start, per_group, members, width)
        pad_scr[:depth, :BLOCK] = cot
        pad_scr[: depth - per_group, BLOCK:] = cot[per_group:]
        flipped = lax.dot_general(
            mirror, data, NT, preferred_element_type=jnp.float32
        ).astype(jnp.bfloat16)
        total = jnp.zeros((depth, BLOCK), jnp.float32)
        products = []
        for offset in range(0, blocks, 2):
            rows = depth - offset * per_group
            pair = pad_scr[offset * per_group : offset * per_group + depth, :]
            result = lax.dot_general(
                pair[:rows],
                lags[:, offset * BLOCK : (offset + 2) * BLOCK],
                NT,
                preferred_element_type=jnp.float32,
            )
            if rows < depth:
                result = jnp.concatenate(
                    [result, jnp.zeros((depth - rows, BLOCK), jnp.float32)], axis=0
                )
            total = total + result
            products.append(jnp.dot(flipped, pair, preferred_element_type=jnp.float32))
        spread_out(
            out_scr, start, per_group, total.astype(jnp.bfloat16), members, width
        )
        kept = jnp.where(rows_of + lanes_of >= BLOCK - 1, products[0][:, :BLOCK], 0.0)
        product = jnp.concatenate([kept, products[0][:, BLOCK:], *products[1:]], axis=1)
        product = pltpu.roll(
            product, length - (BLOCK - 1), axis=1, stride=1, stride_axis=0
        )
        grad_scr[pl.ds(group, 1), :] = jnp.sum(product, axis=0, keepdims=True) * scale
        return carry

    lax.fori_loop(0, groups, one_group, 0, unroll=4)
    for step in range(members):
        at = position ^ step
        outputs[step][:width] = out_scr[at].T
        rows = padded(groups)
        whole = grad_scr[:, pl.ds(pl.multiple_of(at * width, width), width)].astype(jnp.bfloat16)
        if rows > groups:
            blank = jnp.zeros((rows - groups, width), jnp.bfloat16)
            whole = jnp.concatenate([whole, blank], axis=0)
        for chunk in range(width // channels):
            outputs[step][width + chunk * rows : width + (chunk + 1) * rows, :] = whole[
                :, chunk * channels : (chunk + 1) * channels
            ]


VMEM = pl.BlockSpec(memory_space=pltpu.VMEM)
ANYWHERE = pl.BlockSpec(memory_space=pl.ANY)
SMEM = pl.BlockSpec(memory_space=pltpu.SMEM)


def convolve(plan, inputs, width, per_group, after=()):
    members = len(inputs)
    channels = inputs[0].shape[1]
    length = members * width
    *parts, turned, taps = pl.pallas_call(
        functools.partial(forward_kernel, members, per_group, width),
        out_shape=[jax.ShapeDtypeStruct((width, channels), jnp.bfloat16)] * members
        + [
            jax.ShapeDtypeStruct((members, channels, width), jnp.bfloat16),
            jax.ShapeDtypeStruct((channels // per_group, length), jnp.float32),
        ],
        in_specs=[SMEM] + [VMEM] * members + [ANYWHERE] * len(after),
        out_specs=[VMEM] * (members + 2),
        scratch_shapes=[pltpu.VMEM((members, channels, width), jnp.bfloat16)],
        compiler_params=pltpu.CompilerParams(vmem_limit_bytes=24 * 2**20),
        cost_estimate=COST,
        name="causal_conv",
    )(plan, *inputs, *after)
    return parts, turned, taps


def correlate(plan, turned, taps, cotangents, per_group, scale, after=()):
    members = len(cotangents)
    width, channels = cotangents[0].shape
    length = members * width
    groups = channels // per_group
    rows = width + padded(groups) * width // channels
    return pl.pallas_call(
        functools.partial(backward_kernel, members, per_group, scale, width),
        out_shape=[jax.ShapeDtypeStruct((rows, channels), jnp.bfloat16)] * members,
        in_specs=[SMEM] + [VMEM] * (members + 2) + [ANYWHERE] * len(after),
        out_specs=[VMEM] * members,
        scratch_shapes=[
            pltpu.VMEM((members, channels, width), jnp.bfloat16),
            pltpu.VMEM((members, channels, width), jnp.bfloat16),
            pltpu.VMEM((groups, length), jnp.float32),
            pltpu.VMEM((2 * length // BLOCK * per_group, 2 * BLOCK), jnp.bfloat16),
        ],
        compiler_params=pltpu.CompilerParams(vmem_limit_bytes=24 * 2**20),
        cost_estimate=COST,
        name="causal_conv_grads",
    )(plan, turned, taps, *cotangents, *after)


def in_hbm(array):
    return pltpu.with_memory_space_constraint(array, pltpu.HBM)


def prepare_kernel(members, scale, who_ref, key_ref, value_ref, taps_ref, *outputs):
    position = who_ref[0]
    step_no = pl.program_id(0)
    rows, channels = key_ref.shape
    share = channels // members
    groups = taps_ref.shape[0] // members
    total_width = taps_ref.shape[1]
    for step in range(members):
        at = position ^ step
        columns = pl.ds(pl.multiple_of(at * share, share), share)
        product = key_ref[:, columns].astype(jnp.float32) * value_ref[:, columns].astype(
            jnp.float32
        )
        here = pl.ds(pl.multiple_of(step_no * rows, rows), rows)
        outputs[step][here, :] = product.astype(jnp.bfloat16)

    @pl.when(step_no == 0)
    def _():
        for step in range(members):
            at = position ^ step
            taps = taps_ref[pl.ds(pl.multiple_of(at * groups, groups), groups), :]
            taps = (taps * scale).astype(jnp.bfloat16)
            for chunk in range(total_width // share):
                start = total_width + chunk * groups
                outputs[step][start : start + groups, :] = taps[
                    :, chunk * share : (chunk + 1) * share
                ]


def prepare(who, key_gate, value_input, filter_taps, members, scale):
    width, channels = key_gate.shape
    share = channels // members
    rows = width + filter_taps.size // members // share
    tile = width // 4
    part = pl.BlockSpec((tile, channels), lambda i: (i, 0))
    return pl.pallas_call(
        functools.partial(prepare_kernel, members, scale),
        out_shape=[jax.ShapeDtypeStruct((rows, share), jnp.bfloat16)] * members,
        grid=(4,),
        in_specs=[SMEM, part, part, pl.BlockSpec(filter_taps.shape[::-1], lambda i: (0, 0))],
        out_specs=[VMEM] * members,
        compiler_params=pltpu.CompilerParams(vmem_limit_bytes=24 * 2**20),
        cost_estimate=COST,
        name="gated_input",
    )(who, in_hbm(key_gate), in_hbm(value_input), in_hbm(filter_taps.T))


def finish_kernel(members, plan_ref, *refs):
    parts = refs[:members]
    key_ref, value_ref = refs[members : members + 2]
    key_out, value_out, taps_out = refs[-3:]
    position = plan_ref[POSITION]
    width, channels = key_ref.shape
    share = channels // members
    groups = taps_out.shape[0] // members
    for step in range(members):
        at = position ^ step
        columns = pl.ds(pl.multiple_of(at * share, share), share)
        grad = parts[step][:width].astype(jnp.float32)
        key_out[:, columns] = (grad * value_ref[:, columns].astype(jnp.float32)).astype(
            jnp.bfloat16
        )
        value_out[:, columns] = (grad * key_ref[:, columns].astype(jnp.float32)).astype(
            jnp.bfloat16
        )
        taps = [
            parts[step][width + chunk * groups : width + (chunk + 1) * groups, :]
            for chunk in range(width // share)
        ]
        taps_out[pl.ds(pl.multiple_of(at * groups, groups), groups), :] = jnp.concatenate(
            taps, axis=1
        ).astype(jnp.float32)


def finished(plan, parts, key_gate, value_input, groups, after=()):
    members = len(parts)
    width, channels = key_gate.shape
    array = jax.ShapeDtypeStruct((width, channels), jnp.bfloat16)
    grad_key, grad_value, taps = pl.pallas_call(
        functools.partial(finish_kernel, members),
        out_shape=[array, array, jax.ShapeDtypeStruct((groups, width), jnp.float32)],
        in_specs=[SMEM] + [VMEM] * (members + 2) + [ANYWHERE] * len(after),
        out_specs=[VMEM] * 3,
        compiler_params=pltpu.CompilerParams(vmem_limit_bytes=24 * 2**20),
        cost_estimate=COST,
        name="input_gradients",
    )(plan, *parts, key_gate, value_input, *after)
    return grad_key, grad_value, taps.T


def swapped(array, axis, step):
    size = lax.axis_size(axis)
    return lax.ppermute(array, axis, [(i, i ^ step) for i in range(size)])


def traded(pieces, axis):
    return [pieces[0]] + [swapped(pieces[step], axis, step) for step in range(1, len(pieces))]


def cut(array, position, members, axis):
    width = array.shape[axis] // members
    return [
        lax.dynamic_slice_in_dim(array, (position ^ step) * width, width, axis)
        for step in range(members)
    ]


def joined(pieces, position, axis):
    members = len(pieces)
    width = pieces[0].shape[axis]
    shape = list(pieces[0].shape)
    shape[axis] = members * width
    whole = jnp.zeros(shape, pieces[0].dtype)
    for step in range(members):
        whole = lax.dynamic_update_slice_in_dim(
            whole, pieces[step], (position ^ step) * width, axis
        )
    return whole


def wide(array):
    return array.astype(jnp.float32)


def hop(array, pairs):
    return lax.ppermute(
        array, "tp", [(2 * i + core, 2 * j + core) for i, j in pairs for core in range(2)]
    )


INWARD = ((0, 1), (3, 2))
ACROSS = ((1, 2), (2, 1))
OUTWARD = ((1, 0), (2, 3))
OWN, NEAR, MIDDLE, FAR = range(4)
IN_MIDDLE = POSITION + 1
CHIPS = ((0, 1, 2, 3), (1, 0, 3, 2), (2, 2, 1, 1), (3, 3, 0, 0))


def plan_kernel(who_ref, plan_ref):
    place = who_ref[1]
    chip, core = place // 2, place % 2
    for number, table in enumerate(CHIPS):
        source = jnp.where(
            chip < 2,
            jnp.where(chip == 0, table[0], table[1]),
            jnp.where(chip == 2, table[2], table[3]),
        )
        plan_ref[2 * number] = 2 * source + core
        plan_ref[2 * number + 1] = 2 * source + 1 - core
    plan_ref[POSITION] = who_ref[0]
    plan_ref[IN_MIDDLE] = ((chip == 1) | (chip == 2)).astype(jnp.int32)


def planned(who):
    return pl.pallas_call(
        plan_kernel,
        out_shape=jax.ShapeDtypeStruct((IN_MIDDLE + 1,), jnp.int32),
        in_specs=[SMEM],
        out_specs=SMEM,
        compiler_params=pltpu.CompilerParams(vmem_limit_bytes=2**20),
        cost_estimate=COST,
        name="plan",
    )(who)


def pass_kernel(*refs):
    del refs


def held_until(values, after):
    return pl.pallas_call(
        pass_kernel,
        out_shape=[jax.ShapeDtypeStruct(value.shape, value.dtype) for value in values],
        in_specs=[ANYWHERE] * (len(values) + len(after)),
        out_specs=[ANYWHERE] * len(values),
        input_output_aliases={number: number for number in range(len(values))},
        compiler_params=pltpu.CompilerParams(vmem_limit_bytes=2**20),
        cost_estimate=COST,
        name="held",
    )(*values, *after)


def add_kernel(*refs):
    refs[-1][...] = sum(wide(ref[...]) for ref in refs[:-1]).astype(jnp.bfloat16)


def added(*arrays):
    rows, width = arrays[0].shape
    part = pl.BlockSpec((rows // 4, width), lambda i: (i, 0))
    return pl.pallas_call(
        add_kernel,
        out_shape=jax.ShapeDtypeStruct((rows, width), jnp.bfloat16),
        grid=(4,),
        in_specs=[part] * len(arrays),
        out_specs=part,
        compiler_params=pltpu.CompilerParams(vmem_limit_bytes=8 * 2**20),
        cost_estimate=COST,
        name="added",
    )(*arrays)


def choice_kernel(plan_ref, middle_ref, end_ref, *refs):
    out_ref = refs[-1]
    in_middle = plan_ref[IN_MIDDLE] == 1

    @pl.when(in_middle)
    def _():
        out_ref[...] = middle_ref[...]

    @pl.when(jnp.logical_not(in_middle))
    def _():
        out_ref[...] = end_ref[...]


def chosen(plan, in_middle, at_end, after=()):
    return pl.pallas_call(
        choice_kernel,
        out_shape=jax.ShapeDtypeStruct(at_end.shape, at_end.dtype),
        in_specs=[SMEM, VMEM, VMEM] + [ANYWHERE] * len(after),
        out_specs=VMEM,
        compiler_params=pltpu.CompilerParams(vmem_limit_bytes=2**20),
        cost_estimate=COST,
        name="chosen",
    )(plan, in_middle, at_end, *after)


def gate_kernel(members, plan_ref, *refs):
    parts = refs[:members]
    query_ref, gated_ref, conv_ref = refs[members:]
    position = plan_ref[POSITION]
    share = parts[0].shape[1]
    for step in range(members):
        columns = pl.ds(pl.multiple_of((position ^ step) * share, share), share)
        conv = parts[step][...]
        conv_ref[:, columns] = conv
        gated_ref[:, columns] = (wide(conv) * wide(query_ref[:, columns])).astype(jnp.bfloat16)


def gated(plan, parts, query_gate):
    array = jax.ShapeDtypeStruct(query_gate.shape, jnp.bfloat16)
    return pl.pallas_call(
        functools.partial(gate_kernel, len(parts)),
        out_shape=[array, array],
        in_specs=[SMEM] + [VMEM] * (len(parts) + 1),
        out_specs=[VMEM] * 2,
        compiler_params=pltpu.CompilerParams(vmem_limit_bytes=8 * 2**20),
        cost_estimate=COST,
        name="gated_output",
    )(plan, *parts, query_gate)


def spans(widths, start, stop):
    found, begin = [], 0
    for number, width in enumerate(widths):
        low, high = max(start, begin), min(stop, begin + width)
        if low < high:
            found.append((number, slice(low - begin, high - begin), slice(low - start, high - start)))
        begin += width
    return found


def product_kernel(steps, more_widths, out_widths, _, data_ref, weight_ref, *refs):
    more, outputs = refs[: len(more_widths)], refs[-len(out_widths) :]
    product = jnp.dot(data_ref[...], weight_ref[...], preferred_element_type=jnp.float32)
    width = product.shape[1]
    for step in range(steps):
        start, stop = step * width, (step + 1) * width

        @pl.when(pl.program_id(0) == step)
        def _(start=start, stop=stop):
            total = product
            if more:
                parts = [wide(more[n][:, there]) for n, there, _ in spans(more_widths, start, stop)]
                total = total + jnp.concatenate(parts, axis=1)
            total = total.astype(jnp.bfloat16)
            for n, there, here in spans(out_widths, start, stop):
                outputs[n][:, there] = total[:, here]


def column_products(
    plan, data, out_weight, first, count, other, more=(), after=(), tiles=1, widths=()
):
    rows, depth = data.shape
    width = data.shape[1]
    tile = width // tiles
    steps = count * tiles
    widths = tuple(widths) or (width,) * count

    def weights(i, at):
        return 0, at[2 * (first - i // tiles) + other] * tiles + i % tiles

    return pl.pallas_call(
        functools.partial(product_kernel, steps, [part.shape[1] for part in more], widths),
        out_shape=[jax.ShapeDtypeStruct((rows, part), jnp.bfloat16) for part in widths],
        grid_spec=pltpu.PrefetchScalarGridSpec(
            num_scalar_prefetch=1,
            grid=(steps,),
            in_specs=[VMEM, pl.BlockSpec((depth, tile), weights)]
            + [VMEM] * len(more)
            + [ANYWHERE] * len(after),
            out_specs=[VMEM] * len(widths),
        ),
        compiler_params=pltpu.CompilerParams(vmem_limit_bytes=16 * 2**20),
        cost_estimate=COST,
        name="projection_blocks",
    )(plan, data, in_hbm(out_weight), *more, *after)


def cotangent_kernel(count, begin, _, weight_ref, *refs):
    blocks, refs = refs[:count], refs[count:]
    step = pl.program_id(0)
    total = refs[-1]

    for number, block in enumerate(blocks):

        @pl.when(step == number)
        def _(number=number, block=block):
            product = lax.dot_general(
                block[...], weight_ref[...], NT, preferred_element_type=jnp.float32
            )
            if number == 0:
                total[...] = product if begin else refs[0][...] + product
            else:
                total[...] += product


def last_cotangent_kernel(
    members, plan_ref, weight_ref, block_ref, start_ref, conv_ref, query_ref, *refs
):
    parts, cot_scr = refs[-1 - members : -1], refs[-1]
    grad_ref = refs[-2 - members]
    product = lax.dot_general(
        block_ref[...], weight_ref[...], NT, preferred_element_type=jnp.float32
    )
    dgated = wide((start_ref[...] + product).astype(jnp.bfloat16))
    grad_ref[...] = (dgated * wide(conv_ref[...])).astype(jnp.bfloat16)
    cot_scr[...] = (dgated * wide(query_ref[...])).astype(jnp.bfloat16)
    share = parts[0].shape[1]
    odd = plan_ref[POSITION] % 2
    for step in range(0, members, 2):

        @pl.when(pl.program_id(0) == step // 2)
        def _(step=step):
            parts[step][...] = cot_scr[:, pl.ds(pl.multiple_of(odd * share, share), share)]
            parts[step + 1][...] = cot_scr[
                :, pl.ds(pl.multiple_of((1 - odd) * share, share), share)
            ]


def last_cotangents(
    plan, first, block, out_weight, start, convolved, query_gate, members, after
):
    rows, width = block.shape
    channels = out_weight.shape[0]
    share = channels // members
    pair = pl.BlockSpec((rows, 2 * share), lambda i, at: (0, at[POSITION] // 2 ^ i))
    return pl.pallas_call(
        functools.partial(last_cotangent_kernel, members),
        out_shape=[jax.ShapeDtypeStruct((rows, channels), jnp.bfloat16)]
        + [jax.ShapeDtypeStruct((rows, share), jnp.bfloat16)] * members,
        grid_spec=pltpu.PrefetchScalarGridSpec(
            num_scalar_prefetch=1,
            grid=(members // 2,),
            in_specs=[
                pl.BlockSpec((2 * share, width), lambda i, at: (at[POSITION] // 2 ^ i, at[first])),
                VMEM,
                pair,
                pair,
                pair,
            ]
            + [ANYWHERE] * len(after),
            out_specs=[pair] + [VMEM] * members,
            scratch_shapes=[pltpu.VMEM((rows, 2 * share), jnp.bfloat16)],
        ),
        compiler_params=pltpu.CompilerParams(vmem_limit_bytes=24 * 2**20),
        cost_estimate=COST,
        name="cotangent_last",
    )(plan, in_hbm(out_weight), block, start, convolved, query_gate, *after)


def both(blocks):
    return [part for block in blocks for part in (block, swapped(block, "tp", 1))]


def cotangent_products(plan, first, parts, out_weight, start=None, after=()):
    rows, width = parts[0].shape
    channels = out_weight.shape[0]
    count = len(parts)
    begin = start is None
    extra = () if begin else (start,)
    return pl.pallas_call(
        functools.partial(cotangent_kernel, count, begin),
        out_shape=jax.ShapeDtypeStruct((rows, channels), jnp.float32),
        grid_spec=pltpu.PrefetchScalarGridSpec(
            num_scalar_prefetch=1,
            grid=(count,),
            in_specs=[pl.BlockSpec((channels, width), lambda i, at: (0, at[first + i]))]
            + [VMEM] * (count + len(extra))
            + [ANYWHERE] * len(after),
            out_specs=VMEM,
        ),
        compiler_params=pltpu.CompilerParams(vmem_limit_bytes=16 * 2**20),
        cost_estimate=COST,
        name="cotangent_blocks",
    )(plan, in_hbm(out_weight), *parts, *extra, *after)


def packed_parts(position, key_gate, value_input, filter_taps, members, scale):
    length, channels = key_gate.shape
    share = channels // members
    product_in = (wide(key_gate) * wide(value_input)).astype(jnp.bfloat16)
    tap_rows = (filter_taps * scale).astype(jnp.bfloat16).T
    owned = filter_taps.shape[1] // members
    chunks = length // share
    packed = []
    pieces = cut(product_in, position, members, 1)
    for piece, taps in zip(pieces, cut(tap_rows, position, members, 0)):
        taps = taps.reshape(owned, chunks, share).transpose(1, 0, 2)
        taps = jnp.pad(taps, ((0, 0), (0, padded(owned) - owned), (0, 0)))
        packed.append(jnp.concatenate([piece, taps.reshape(-1, share)], axis=0))
    return packed


def unpacked_parts(position, parts, key_gate, value_input, groups):
    length, channels = key_gate.shape
    members = len(parts)
    share = channels // members
    owned = groups // members
    chunks = length // share
    input_grad = wide(joined([part[:length] for part in parts], position, 1))
    filter_parts = [
        part[length:]
        .reshape(chunks, padded(owned), share)[:, :owned]
        .transpose(1, 0, 2)
        .reshape(owned, length)
        for part in parts
    ]
    grad_filter = wide(joined(filter_parts, position, 0)).T
    grad_key = (input_grad * wide(value_input)).astype(jnp.bfloat16)
    grad_value = (input_grad * wide(key_gate)).astype(jnp.bfloat16)
    return grad_key, grad_value, grad_filter


def in_line(
    query_gate, key_gate, value_input, filter_taps, out_weight, out_grad, members, scale
):
    length, channels = query_gate.shape
    groups = filter_taps.shape[1]
    per_group = channels // groups
    who = jnp.stack([lax.axis_index("ctx"), lax.axis_index("tp")]).astype(jnp.int32)
    plan = planned(who)
    near, cross = hop(out_grad, INWARD + OUTWARD), hop(out_grad, ACROSS)
    total = cotangent_products(plan, 2 * OWN, both([out_grad]), out_weight)

    packed = prepare(who, key_gate, value_input, filter_taps, members, scale)
    input_parts = traded(packed, "ctx")
    conv_parts, turned, taps = convolve(plan, input_parts, length, per_group, (total,))
    *conv_parts, near, cross = held_until([*conv_parts, near, cross], ())
    far, skip = hop(near, ACROSS), hop(cross, OUTWARD)
    gated_out, convolved = gated(plan, traded(conv_parts, "ctx"), query_gate)

    def product(first, count, other, more=(), after=(), tiles=1, widths=()):
        return column_products(
            plan, gated_out, out_weight, first, count, other, more, after, tiles, widths
        )

    quarter, half = channels // 4, channels // 2
    given_far = product(FAR, 1, 1, tiles=2, widths=(3 * quarter, quarter))
    received = [swapped(part, "tp", 1) for part in given_far]
    (first,) = product(FAR, 1, 0, received, tiles=2)
    far, skip, near = held_until([far, skip, near], (first,))
    mixed = chosen(plan, far, first)
    arrived = hop(mixed, OUTWARD + INWARD)
    given_middle = product(MIDDLE, 1, 1, (), (mixed,), tiles=2, widths=(half, half))
    received = [swapped(part, "tp", 1) for part in given_middle]
    (second,) = product(MIDDLE, 1, 0, received, tiles=2)
    middle_block = added(cross, skip)
    blocks = [near, swapped(near, "tp", 1), middle_block]
    total = cotangent_products(plan, 2 * NEAR, blocks, out_weight, total, after=(second,))
    given_near, given_own = product(NEAR, 2, 1, (), (second,))
    (arrived,) = held_until([arrived], (total, given_near))
    through = added(first, arrived)
    two_a = hop(through, ACROSS)
    (second,) = held_until([second], (arrived,))
    two_b = hop(second, INWARD)

    far_block, far_other = both([chosen(plan, far, arrived, (through,))])
    blocks = [swapped(middle_block, "tp", 1), far_block]
    total = cotangent_products(
        plan, 2 * MIDDLE + 1, blocks, out_weight, total, after=(through,)
    )
    grad_query, *grad_parts = last_cotangents(
        plan, 2 * FAR + 1, far_other, out_weight, total, convolved, query_gate, members, ()
    )
    received = (swapped(given_near, "tp", 1), swapped(given_own, "tp", 1))
    third, own = product(NEAR, 2, 0, received, (grad_parts[0],))
    grad_parts = traded(grad_parts, "ctx")

    two_a, two_b = held_until([two_a, two_b], tuple(grad_parts[1:]))
    third, second = added(third, two_a), added(second, two_b)
    back_parts = correlate(plan, turned, taps, grad_parts, per_group, scale, (third, second))
    projected = added(own, hop(third, OUTWARD + INWARD), hop(second, ACROSS))
    back_parts = traded(back_parts, "ctx")
    return projected, grad_query, *finished(plan, back_parts, key_gate, value_input, groups, (in_hbm(projected),))


def anywhere(
    query_gate, key_gate, value_input, filter_taps, out_weight, out_grad, members, scale
):
    length, channels = query_gate.shape
    groups = filter_taps.shape[1]
    per_group = channels // groups
    position = lax.axis_index("ctx")
    plan = jnp.full((POSITION + 1,), position, jnp.int32)
    packed = packed_parts(position, key_gate, value_input, filter_taps, members, scale)
    input_parts = traded(packed, "ctx")
    conv_parts, turned, taps = convolve(plan, input_parts, length, per_group)
    conv_parts = traded(conv_parts, "ctx")
    convolved = joined(conv_parts, position, 1)
    gated_out = (wide(query_gate) * wide(convolved)).astype(jnp.bfloat16)
    partial_value = jnp.dot(gated_out, out_weight, preferred_element_type=jnp.float32)
    projected = lax.psum_scatter(
        partial_value.astype(jnp.bfloat16), "tp", scatter_dimension=1, tiled=True
    )
    dgated = jnp.einsum(
        "tk,ck->tc",
        lax.all_gather(out_grad, "tp", axis=1, tiled=True),
        out_weight,
        preferred_element_type=jnp.float32,
    ).astype(jnp.bfloat16)
    grad_query = (wide(dgated) * wide(convolved)).astype(jnp.bfloat16)
    conv_grad = (wide(dgated) * wide(query_gate)).astype(jnp.bfloat16)
    grad_parts = traded(cut(conv_grad, position, members, 1), "ctx")
    back_parts = correlate(plan, turned, taps, grad_parts, per_group, scale)
    back_parts = traded(back_parts, "ctx")
    return (
        projected,
        grad_query,
        *unpacked_parts(position, back_parts, key_gate, value_input, groups),
    )


def local(query_gate, key_gate, value_input, filter_taps, out_weight, out_grad):
    length, channels = query_gate.shape
    groups = filter_taps.shape[1]
    members = lax.axis_size("ctx")
    scale = 1.0 / math.sqrt(length * members)
    fits = channels // members % 128 == 0 and groups // members % 16 == 0
    body = in_line if lax.axis_size("tp") == 8 and fits else anywhere
    return body(
        query_gate, key_gate, value_input, filter_taps, out_weight, out_grad, members, scale
    )


def solution(mesh):
    both = P("ctx", "tp")
    return jax.shard_map(
        local,
        mesh=mesh,
        in_specs=(both, both, both, both, P("tp", None), both),
        out_specs=(both,) * 5,
        check_vma=False,
    )
```

```python
import functools
import math
import jax
import jax.numpy as jnp
from jax import lax
from jax.experimental import pallas as pl
from jax.experimental.pallas import tpu as pltpu
from jax.sharding import PartitionSpec as P

BLOCK = 128
POSITION = 8
NT = (((1,), (1,)), ((), ()))
COST = pl.CostEstimate(flops=2**20, bytes_accessed=2**12, transcendentals=0)


def lag_matrix(row, length):
    lanes = lax.broadcasted_iota(jnp.int32, (BLOCK, BLOCK), 1)
    rows = lax.broadcasted_iota(jnp.int32, (BLOCK, BLOCK), 0)
    spread = pltpu.roll(
        jnp.broadcast_to(row, (BLOCK, length)), 0, axis=1, stride=1, stride_axis=0
    )
    first = jnp.where(lanes >= rows, spread[:, :BLOCK], 0.0)
    return jnp.concatenate(
        [first.astype(jnp.bfloat16), spread[:, BLOCK:].astype(jnp.bfloat16)], axis=1
    )


def stacked(ref, start, rows, members, width):
    pieces = []
    for member in range(members):
        part = ref[member, pl.ds(start, rows), :]
        for at in range(0, width, BLOCK):
            pieces.append(part[:, at : at + BLOCK])
    return jnp.concatenate(pieces, axis=0)


def spread_out(ref, start, rows, value, members, width):
    per_member = width // BLOCK
    for member in range(members):
        base = member * per_member * rows
        parts = [value[base + i * rows : base + (i + 1) * rows] for i in range(per_member)]
        ref[member, pl.ds(start, rows), :] = jnp.concatenate(parts, axis=1)


def padded(groups):
    return -(-groups // 16) * 16


def load_taps(tap_scr, packed, at, width):
    groups, channels = tap_scr.shape[0], packed.shape[1]
    rows = padded(groups)
    parts = [
        packed[width + chunk * rows : width + (chunk + 1) * rows, :].astype(jnp.float32)
        for chunk in range(width // channels)
    ]
    start = pl.multiple_of(at * width, width)
    tap_scr[:, pl.ds(start, width)] = jnp.concatenate(parts, axis=1)[:groups]


def forward_kernel(members, per_group, width, plan_ref, *refs):
    inputs, outputs = refs[:members], refs[-members - 3 : -3]
    in_scr, tap_scr, out_scr = refs[-3:]
    position = plan_ref[POSITION]
    channels = inputs[0].shape[1]
    groups = channels // per_group
    length = members * width
    blocks = length // BLOCK
    for step in range(members):
        at = position ^ step
        in_scr[at] = inputs[step][:width].T
        load_taps(tap_scr, inputs[step], at, width)

    def one_group(group, carry):
        start = pl.multiple_of(group * per_group, per_group)
        lags = lag_matrix(tap_scr[pl.ds(group, 1), :], length)
        data = stacked(in_scr, start, per_group, members, width)
        total = [jnp.zeros((per_group, BLOCK), jnp.float32) for _ in range(blocks)]
        for offset in range(0, blocks, 2):
            rows = (blocks - offset) * per_group
            result = jnp.dot(
                data[:rows],
                lags[:, offset * BLOCK : (offset + 2) * BLOCK],
                preferred_element_type=jnp.float32,
            )
            for side in range(2):
                for source in range(blocks - offset - side):
                    total[source + offset + side] += result[
                        source * per_group : (source + 1) * per_group,
                        side * BLOCK : (side + 1) * BLOCK,
                    ]
        value = jnp.concatenate(total, axis=0).astype(jnp.bfloat16)
        spread_out(out_scr, start, per_group, value, members, width)
        return carry

    lax.fori_loop(0, groups, one_group, 0, unroll=4)
    for step in range(members):
        outputs[step][...] = out_scr[position ^ step].T


def backward_kernel(members, pieces, per_group, scale, width, plan_ref, in_scr, tap_scr, *refs):
    cotangents = refs[:pieces]
    outputs = refs[-members - 4 : -4]
    cot_scr, out_scr, grad_scr, pad_scr = refs[-4:]
    position = plan_ref[POSITION]
    channels = cotangents[0].shape[1]
    groups = channels // per_group
    length = members * width
    blocks = length // BLOCK
    depth = blocks * per_group
    for step in range(members):
        at = position ^ step
        rows = cotangents[step].shape[0]
        for part in range(pieces // members):
            cot_scr[at, :, part * rows : (part + 1) * rows] = cotangents[
                part * members + step
            ][...].T
    pad_scr[...] = jnp.zeros_like(pad_scr)
    rows_of = lax.broadcasted_iota(jnp.int32, (BLOCK, BLOCK), 0)
    lanes_of = lax.broadcasted_iota(jnp.int32, (BLOCK, BLOCK), 1)
    mirror = (rows_of + lanes_of == BLOCK - 1).astype(jnp.bfloat16)

    def one_group(group, carry):
        start = pl.multiple_of(group * per_group, per_group)
        lags = lag_matrix(tap_scr[pl.ds(group, 1), :], length)
        data = stacked(in_scr, start, per_group, members, width)
        cot = stacked(cot_scr, start, per_group, members, width)
        pad_scr[:depth, :BLOCK] = cot
        pad_scr[: depth - per_group, BLOCK:] = cot[per_group:]
        flipped = lax.dot_general(
            mirror, data, NT, preferred_element_type=jnp.float32
        ).astype(jnp.bfloat16)
        total = jnp.zeros((depth, BLOCK), jnp.float32)
        products = []
        for offset in range(0, blocks, 2):
            rows = depth - offset * per_group
            pair = pad_scr[offset * per_group : offset * per_group + depth, :]
            result = lax.dot_general(
                pair[:rows],
                lags[:, offset * BLOCK : (offset + 2) * BLOCK],
                NT,
                preferred_element_type=jnp.float32,
            )
            if rows < depth:
                result = jnp.concatenate(
                    [result, jnp.zeros((depth - rows, BLOCK), jnp.float32)], axis=0
                )
            total = total + result
            products.append(jnp.dot(flipped, pair, preferred_element_type=jnp.float32))
        spread_out(
            out_scr, start, per_group, total.astype(jnp.bfloat16), members, width
        )
        kept = jnp.where(rows_of + lanes_of >= BLOCK - 1, products[0][:, :BLOCK], 0.0)
        product = jnp.concatenate([kept, products[0][:, BLOCK:], *products[1:]], axis=1)
        product = pltpu.roll(
            product, length - (BLOCK - 1), axis=1, stride=1, stride_axis=0
        )
        grad_scr[pl.ds(group, 1), :] = jnp.sum(product, axis=0, keepdims=True) * scale
        return carry

    lax.fori_loop(0, groups, one_group, 0, unroll=4)
    for step in range(members):
        at = position ^ step
        outputs[step][:width] = out_scr[at].T
        rows = padded(groups)
        whole = grad_scr[:, pl.ds(pl.multiple_of(at * width, width), width)].astype(jnp.bfloat16)
        if rows > groups:
            blank = jnp.zeros((rows - groups, width), jnp.bfloat16)
            whole = jnp.concatenate([whole, blank], axis=0)
        for chunk in range(width // channels):
            outputs[step][width + chunk * rows : width + (chunk + 1) * rows, :] = whole[
                :, chunk * channels : (chunk + 1) * channels
            ]


VMEM = pl.BlockSpec(memory_space=pltpu.VMEM)
ANYWHERE = pl.BlockSpec(memory_space=pl.ANY)
SMEM = pl.BlockSpec(memory_space=pltpu.SMEM)


def convolve(plan, inputs, width, per_group, after=()):
    members = len(inputs)
    channels = inputs[0].shape[1]
    length = members * width
    *parts, turned, taps = pl.pallas_call(
        functools.partial(forward_kernel, members, per_group, width),
        out_shape=[jax.ShapeDtypeStruct((width, channels), jnp.bfloat16)] * members
        + [
            jax.ShapeDtypeStruct((members, channels, width), jnp.bfloat16),
            jax.ShapeDtypeStruct((channels // per_group, length), jnp.float32),
        ],
        in_specs=[SMEM] + [VMEM] * members + [ANYWHERE] * len(after),
        out_specs=[VMEM] * (members + 2),
        scratch_shapes=[pltpu.VMEM((members, channels, width), jnp.bfloat16)],
        compiler_params=pltpu.CompilerParams(vmem_limit_bytes=24 * 2**20),
        cost_estimate=COST,
        name="causal_conv",
    )(plan, *inputs, *after)
    return parts, turned, taps


def correlate(plan, turned, taps, cotangents, per_group, scale, after=()):
    members, channels, width = turned.shape
    length = members * width
    groups = channels // per_group
    rows = width + padded(groups) * width // channels
    return pl.pallas_call(
        functools.partial(backward_kernel, members, len(cotangents), per_group, scale, width),
        out_shape=[jax.ShapeDtypeStruct((rows, channels), jnp.bfloat16)] * members,
        in_specs=[SMEM] + [VMEM] * (len(cotangents) + 2) + [ANYWHERE] * len(after),
        out_specs=[VMEM] * members,
        scratch_shapes=[
            pltpu.VMEM((members, channels, width), jnp.bfloat16),
            pltpu.VMEM((members, channels, width), jnp.bfloat16),
            pltpu.VMEM((groups, length), jnp.float32),
            pltpu.VMEM((2 * length // BLOCK * per_group, 2 * BLOCK), jnp.bfloat16),
        ],
        compiler_params=pltpu.CompilerParams(vmem_limit_bytes=24 * 2**20),
        cost_estimate=COST,
        name="causal_conv_grads",
    )(plan, turned, taps, *cotangents, *after)


def in_hbm(array):
    return pltpu.with_memory_space_constraint(array, pltpu.HBM)


def prepare_kernel(members, scale, who_ref, key_ref, value_ref, taps_ref, *outputs):
    position = who_ref[0]
    step_no = pl.program_id(0)
    rows, channels = key_ref.shape
    share = channels // members
    groups = taps_ref.shape[0] // members
    total_width = taps_ref.shape[1]
    for step in range(members):
        at = position ^ step
        columns = pl.ds(pl.multiple_of(at * share, share), share)
        product = key_ref[:, columns].astype(jnp.float32) * value_ref[:, columns].astype(
            jnp.float32
        )
        here = pl.ds(pl.multiple_of(step_no * rows, rows), rows)
        outputs[step][here, :] = product.astype(jnp.bfloat16)

    @pl.when(step_no == 0)
    def _():
        for step in range(members):
            at = position ^ step
            taps = taps_ref[pl.ds(pl.multiple_of(at * groups, groups), groups), :]
            taps = (taps * scale).astype(jnp.bfloat16)
            for chunk in range(total_width // share):
                start = total_width + chunk * groups
                outputs[step][start : start + groups, :] = taps[
                    :, chunk * share : (chunk + 1) * share
                ]


def prepare(who, key_gate, value_input, filter_taps, members, scale):
    width, channels = key_gate.shape
    share = channels // members
    rows = width + filter_taps.size // members // share
    tile = width // 4
    part = pl.BlockSpec((tile, channels), lambda i: (i, 0))
    return pl.pallas_call(
        functools.partial(prepare_kernel, members, scale),
        out_shape=[jax.ShapeDtypeStruct((rows, share), jnp.bfloat16)] * members,
        grid=(4,),
        in_specs=[SMEM, part, part, pl.BlockSpec(filter_taps.shape[::-1], lambda i: (0, 0))],
        out_specs=[VMEM] * members,
        compiler_params=pltpu.CompilerParams(vmem_limit_bytes=24 * 2**20),
        cost_estimate=COST,
        name="gated_input",
    )(who, in_hbm(key_gate), in_hbm(value_input), in_hbm(filter_taps.T))


def finish_kernel(members, plan_ref, *refs):
    parts = refs[:members]
    key_ref, value_ref = refs[members : members + 2]
    key_out, value_out, taps_out = refs[-3:]
    position = plan_ref[POSITION]
    width, channels = key_ref.shape
    share = channels // members
    groups = taps_out.shape[0] // members
    for step in range(members):
        at = position ^ step
        columns = pl.ds(pl.multiple_of(at * share, share), share)
        grad = parts[step][:width].astype(jnp.float32)
        key_out[:, columns] = (grad * value_ref[:, columns].astype(jnp.float32)).astype(
            jnp.bfloat16
        )
        value_out[:, columns] = (grad * key_ref[:, columns].astype(jnp.float32)).astype(
            jnp.bfloat16
        )
        taps = [
            parts[step][width + chunk * groups : width + (chunk + 1) * groups, :]
            for chunk in range(width // share)
        ]
        taps_out[pl.ds(pl.multiple_of(at * groups, groups), groups), :] = jnp.concatenate(
            taps, axis=1
        ).astype(jnp.float32)


def finished(plan, parts, key_gate, value_input, groups, after=()):
    members = len(parts)
    width, channels = key_gate.shape
    array = jax.ShapeDtypeStruct((width, channels), jnp.bfloat16)
    grad_key, grad_value, taps = pl.pallas_call(
        functools.partial(finish_kernel, members),
        out_shape=[array, array, jax.ShapeDtypeStruct((groups, width), jnp.float32)],
        in_specs=[SMEM] + [VMEM] * (members + 2) + [ANYWHERE] * len(after),
        out_specs=[VMEM] * 3,
        compiler_params=pltpu.CompilerParams(vmem_limit_bytes=24 * 2**20),
        cost_estimate=COST,
        name="input_gradients",
    )(plan, *parts, key_gate, value_input, *after)
    return grad_key, grad_value, taps.T


def swapped(array, axis, step):
    size = lax.axis_size(axis)
    return lax.ppermute(array, axis, [(i, i ^ step) for i in range(size)])


def traded(pieces, axis):
    return [pieces[0]] + [swapped(pieces[step], axis, step) for step in range(1, len(pieces))]


def cut(array, position, members, axis):
    width = array.shape[axis] // members
    return [
        lax.dynamic_slice_in_dim(array, (position ^ step) * width, width, axis)
        for step in range(members)
    ]


def joined(pieces, position, axis):
    members = len(pieces)
    width = pieces[0].shape[axis]
    shape = list(pieces[0].shape)
    shape[axis] = members * width
    whole = jnp.zeros(shape, pieces[0].dtype)
    for step in range(members):
        whole = lax.dynamic_update_slice_in_dim(
            whole, pieces[step], (position ^ step) * width, axis
        )
    return whole


def wide(array):
    return array.astype(jnp.float32)


def hop(array, pairs):
    return lax.ppermute(
        array, "tp", [(2 * i + core, 2 * j + core) for i, j in pairs for core in range(2)]
    )


INWARD = ((0, 1), (3, 2))
ACROSS = ((1, 2), (2, 1))
OUTWARD = ((1, 0), (2, 3))
OWN, NEAR, MIDDLE, FAR = range(4)
IN_MIDDLE = POSITION + 1
CHIPS = ((0, 1, 2, 3), (1, 0, 3, 2), (2, 2, 1, 1), (3, 3, 0, 0))


def plan_kernel(who_ref, plan_ref):
    place = who_ref[1]
    chip, core = place // 2, place % 2
    for number, table in enumerate(CHIPS):
        source = jnp.where(
            chip < 2,
            jnp.where(chip == 0, table[0], table[1]),
            jnp.where(chip == 2, table[2], table[3]),
        )
        plan_ref[2 * number] = 2 * source + core
        plan_ref[2 * number + 1] = 2 * source + 1 - core
    plan_ref[POSITION] = who_ref[0]
    plan_ref[IN_MIDDLE] = ((chip == 1) | (chip == 2)).astype(jnp.int32)


def planned(who):
    return pl.pallas_call(
        plan_kernel,
        out_shape=jax.ShapeDtypeStruct((IN_MIDDLE + 1,), jnp.int32),
        in_specs=[SMEM],
        out_specs=SMEM,
        compiler_params=pltpu.CompilerParams(vmem_limit_bytes=2**20),
        cost_estimate=COST,
        name="plan",
    )(who)


def pass_kernel(*refs):
    del refs


def held_until(values, after):
    return pl.pallas_call(
        pass_kernel,
        out_shape=[jax.ShapeDtypeStruct(value.shape, value.dtype) for value in values],
        in_specs=[ANYWHERE] * (len(values) + len(after)),
        out_specs=[ANYWHERE] * len(values),
        input_output_aliases={number: number for number in range(len(values))},
        compiler_params=pltpu.CompilerParams(vmem_limit_bytes=2**20),
        cost_estimate=COST,
        name="held",
    )(*values, *after)


def add_kernel(*refs):
    refs[-1][...] = sum(wide(ref[...]) for ref in refs[:-1]).astype(jnp.bfloat16)


def added(*arrays):
    rows, width = arrays[0].shape
    part = pl.BlockSpec((rows // 4, width), lambda i: (i, 0))
    return pl.pallas_call(
        add_kernel,
        out_shape=jax.ShapeDtypeStruct((rows, width), jnp.bfloat16),
        grid=(4,),
        in_specs=[part] * len(arrays),
        out_specs=part,
        compiler_params=pltpu.CompilerParams(vmem_limit_bytes=8 * 2**20),
        cost_estimate=COST,
        name="added",
    )(*arrays)


def choice_kernel(plan_ref, middle_ref, end_ref, *refs):
    out_ref = refs[-1]
    in_middle = plan_ref[IN_MIDDLE] == 1

    @pl.when(in_middle)
    def _():
        out_ref[...] = middle_ref[...]

    @pl.when(jnp.logical_not(in_middle))
    def _():
        out_ref[...] = end_ref[...]


def chosen(plan, in_middle, at_end, after=()):
    return pl.pallas_call(
        choice_kernel,
        out_shape=jax.ShapeDtypeStruct(at_end.shape, at_end.dtype),
        in_specs=[SMEM, VMEM, VMEM] + [ANYWHERE] * len(after),
        out_specs=VMEM,
        compiler_params=pltpu.CompilerParams(vmem_limit_bytes=2**20),
        cost_estimate=COST,
        name="chosen",
    )(plan, in_middle, at_end, *after)


def gate_kernel(members, plan_ref, *refs):
    parts = refs[:members]
    query_ref, gated_ref, conv_ref = refs[members:]
    position = plan_ref[POSITION]
    share = parts[0].shape[1]
    for step in range(members):
        columns = pl.ds(pl.multiple_of((position ^ step) * share, share), share)
        conv = parts[step][...]
        conv_ref[:, columns] = conv
        gated_ref[:, columns] = (wide(conv) * wide(query_ref[:, columns])).astype(jnp.bfloat16)


def gated(plan, parts, query_gate):
    array = jax.ShapeDtypeStruct(query_gate.shape, jnp.bfloat16)
    return pl.pallas_call(
        functools.partial(gate_kernel, len(parts)),
        out_shape=[array, array],
        in_specs=[SMEM] + [VMEM] * (len(parts) + 1),
        out_specs=[VMEM] * 2,
        compiler_params=pltpu.CompilerParams(vmem_limit_bytes=8 * 2**20),
        cost_estimate=COST,
        name="gated_output",
    )(plan, *parts, query_gate)


def spans(widths, start, stop):
    found, begin = [], 0
    for number, width in enumerate(widths):
        low, high = max(start, begin), min(stop, begin + width)
        if low < high:
            found.append((number, slice(low - begin, high - begin), slice(low - start, high - start)))
        begin += width
    return found


def product_kernel(steps, more_widths, out_widths, _, data_ref, weight_ref, *refs):
    more, outputs = refs[: len(more_widths)], refs[-len(out_widths) :]
    product = jnp.dot(data_ref[...], weight_ref[...], preferred_element_type=jnp.float32)
    width = product.shape[1]
    for step in range(steps):
        start, stop = step * width, (step + 1) * width

        @pl.when(pl.program_id(0) == step)
        def _(start=start, stop=stop):
            total = product
            if more:
                parts = [wide(more[n][:, there]) for n, there, _ in spans(more_widths, start, stop)]
                total = total + jnp.concatenate(parts, axis=1)
            total = total.astype(jnp.bfloat16)
            for n, there, here in spans(out_widths, start, stop):
                outputs[n][:, there] = total[:, here]


def column_products(
    plan, data, out_weight, first, count, other, more=(), after=(), tiles=1, widths=()
):
    rows, depth = data.shape
    width = data.shape[1]
    tile = width // tiles
    steps = count * tiles
    widths = tuple(widths) or (width,) * count

    def weights(i, at):
        return 0, at[2 * (first - i // tiles) + other] * tiles + i % tiles

    return pl.pallas_call(
        functools.partial(product_kernel, steps, [part.shape[1] for part in more], widths),
        out_shape=[jax.ShapeDtypeStruct((rows, part), jnp.bfloat16) for part in widths],
        grid_spec=pltpu.PrefetchScalarGridSpec(
            num_scalar_prefetch=1,
            grid=(steps,),
            in_specs=[VMEM, pl.BlockSpec((depth, tile), weights)]
            + [VMEM] * len(more)
            + [ANYWHERE] * len(after),
            out_specs=[VMEM] * len(widths),
        ),
        compiler_params=pltpu.CompilerParams(vmem_limit_bytes=16 * 2**20),
        cost_estimate=COST,
        name="projection_blocks",
    )(plan, data, in_hbm(out_weight), *more, *after)


def cotangent_kernel(members, plan_ref, data_ref, weight_ref, conv_ref, query_ref, *refs):
    grad_ref, parts = refs[-3 - members], refs[-2 - members : -2]
    total, cot_scr = refs[-2:]
    step = pl.program_id(0)
    product = lax.dot_general(
        data_ref[...], weight_ref[...], NT, preferred_element_type=jnp.float32
    )

    @pl.when(step == 0)
    def _():
        total[...] = product

    @pl.when(step > 0)
    def _():
        total[...] += product

    @pl.when(step == pl.num_programs(0) - 1)
    def _():
        dgated = wide(total[...].astype(jnp.bfloat16))
        grad_ref[...] = (dgated * wide(conv_ref[...])).astype(jnp.bfloat16)
        cot_scr[...] = (dgated * wide(query_ref[...])).astype(jnp.bfloat16)
        share = parts[0].shape[1]
        for number in range(members):
            start = pl.multiple_of((plan_ref[POSITION] ^ number) * share, share)
            parts[number][...] = cot_scr[:, pl.ds(start, share)]


def cotangents(plan, number, gathered, out_weight, convolved, query_gate, members, begun, after):
    rows, depth = gathered.shape
    length, channels = convolved.shape
    share = channels // members
    tile = min(depth, 1024)
    place = pl.BlockSpec((rows, channels), lambda i, at: (number, 0))
    return pl.pallas_call(
        functools.partial(cotangent_kernel, members),
        out_shape=[jax.ShapeDtypeStruct((length, channels), jnp.bfloat16)]
        + [jax.ShapeDtypeStruct((rows, share), jnp.bfloat16)] * members,
        grid_spec=pltpu.PrefetchScalarGridSpec(
            num_scalar_prefetch=1,
            grid=(depth // tile,),
            in_specs=[
                pl.BlockSpec((rows, tile), lambda i, at: (0, i)),
                pl.BlockSpec((channels, tile), lambda i, at: (0, i)),
                place,
                place,
            ]
            + [ANYWHERE] * (len(begun) + len(after)),
            out_specs=[place] + [VMEM] * members,
            scratch_shapes=[
                pltpu.VMEM((rows, channels), jnp.float32),
                pltpu.VMEM((rows, channels), jnp.bfloat16),
            ],
        ),
        input_output_aliases={5: 0} if begun else {},
        compiler_params=pltpu.CompilerParams(vmem_limit_bytes=24 * 2**20),
        cost_estimate=COST,
        name="cotangents",
    )(plan, in_hbm(gathered), in_hbm(out_weight), convolved, query_gate, *begun, *after)


def packed_parts(position, key_gate, value_input, filter_taps, members, scale):
    length, channels = key_gate.shape
    share = channels // members
    product_in = (wide(key_gate) * wide(value_input)).astype(jnp.bfloat16)
    tap_rows = (filter_taps * scale).astype(jnp.bfloat16).T
    owned = filter_taps.shape[1] // members
    chunks = length // share
    packed = []
    pieces = cut(product_in, position, members, 1)
    for piece, taps in zip(pieces, cut(tap_rows, position, members, 0)):
        taps = taps.reshape(owned, chunks, share).transpose(1, 0, 2)
        taps = jnp.pad(taps, ((0, 0), (0, padded(owned) - owned), (0, 0)))
        packed.append(jnp.concatenate([piece, taps.reshape(-1, share)], axis=0))
    return packed


def unpacked_parts(position, parts, key_gate, value_input, groups):
    length, channels = key_gate.shape
    members = len(parts)
    share = channels // members
    owned = groups // members
    chunks = length // share
    input_grad = wide(joined([part[:length] for part in parts], position, 1))
    filter_parts = [
        part[length:]
        .reshape(chunks, padded(owned), share)[:, :owned]
        .transpose(1, 0, 2)
        .reshape(owned, length)
        for part in parts
    ]
    grad_filter = wide(joined(filter_parts, position, 0)).T
    grad_key = (input_grad * wide(value_input)).astype(jnp.bfloat16)
    grad_value = (input_grad * wide(key_gate)).astype(jnp.bfloat16)
    return grad_key, grad_value, grad_filter


def in_line(
    query_gate, key_gate, value_input, filter_taps, out_weight, out_grad, members, scale
):
    length, channels = query_gate.shape
    groups = filter_taps.shape[1]
    per_group = channels // groups
    who = jnp.stack([lax.axis_index("ctx"), lax.axis_index("tp")]).astype(jnp.int32)
    plan = planned(who)
    count = 2
    rows = length // count
    gathered = [
        lax.all_gather(out_grad[part * rows : (part + 1) * rows], "tp", axis=1, tiled=True)
        for part in range(count)
    ]
    packed = prepare(who, key_gate, value_input, filter_taps, members, scale)
    input_parts = traded(packed, "ctx")
    conv_parts, turned, taps = convolve(plan, input_parts, length, per_group)
    gated_out, convolved = gated(plan, traded(conv_parts, "ctx"), query_gate)

    def product(first, count, other, more=(), after=(), tiles=1, widths=()):
        return column_products(
            plan, gated_out, out_weight, first, count, other, more, after, tiles, widths
        )

    (given,) = product(FAR, 1, 1, tiles=2)
    (first,) = product(FAR, 1, 0, [swapped(given, "tp", 1)], tiles=2)
    one = hop(first, INWARD)
    given = product(MIDDLE, 3, 1, (), (first,), widths=(3 * channels // 4,) * 4)
    received = [swapped(part, "tp", 1) for part in given]
    second, third, own = product(MIDDLE, 3, 0, received)
    grad_query, grad_parts = (), []
    after = own
    for part in range(count):
        if part == count - 1:
            (one,) = held_until([one], (after,))
            through = added(first, one)
            two_a = hop(through, ACROSS)
            (second,) = held_until([second], (one,))
            two_b = hop(second, INWARD)
            after = through
        received = grad_parts[1:]
        results = cotangents(
            plan,
            part,
            gathered[part],
            out_weight,
            convolved,
            query_gate,
            members,
            grad_query,
            (after, *received),
        )
        grad_query, pieces = results[:1], results[1:]
        after = pieces[0]
        grad_parts += traded(pieces, "ctx")
    (grad_query,) = grad_query
    two_a, two_b = held_until([two_a, two_b], tuple(grad_parts[1 - members :]))
    third, second = added(third, two_a), added(second, two_b)
    back_parts = correlate(plan, turned, taps, grad_parts, per_group, scale, (third, second))
    projected = added(own, hop(third, OUTWARD + INWARD), hop(second, ACROSS))
    back_parts = traded(back_parts, "ctx")
    return projected, grad_query, *finished(plan, back_parts, key_gate, value_input, groups, (in_hbm(projected),))


def anywhere(
    query_gate, key_gate, value_input, filter_taps, out_weight, out_grad, members, scale
):
    length, channels = query_gate.shape
    groups = filter_taps.shape[1]
    per_group = channels // groups
    position = lax.axis_index("ctx")
    plan = jnp.full((POSITION + 1,), position, jnp.int32)
    packed = packed_parts(position, key_gate, value_input, filter_taps, members, scale)
    input_parts = traded(packed, "ctx")
    conv_parts, turned, taps = convolve(plan, input_parts, length, per_group)
    conv_parts = traded(conv_parts, "ctx")
    convolved = joined(conv_parts, position, 1)
    gated_out = (wide(query_gate) * wide(convolved)).astype(jnp.bfloat16)
    partial_value = jnp.dot(gated_out, out_weight, preferred_element_type=jnp.float32)
    projected = lax.psum_scatter(
        partial_value.astype(jnp.bfloat16), "tp", scatter_dimension=1, tiled=True
    )
    dgated = jnp.einsum(
        "tk,ck->tc",
        lax.all_gather(out_grad, "tp", axis=1, tiled=True),
        out_weight,
        preferred_element_type=jnp.float32,
    ).astype(jnp.bfloat16)
    grad_query = (wide(dgated) * wide(convolved)).astype(jnp.bfloat16)
    conv_grad = (wide(dgated) * wide(query_gate)).astype(jnp.bfloat16)
    grad_parts = traded(cut(conv_grad, position, members, 1), "ctx")
    back_parts = correlate(plan, turned, taps, grad_parts, per_group, scale)
    back_parts = traded(back_parts, "ctx")
    return (
        projected,
        grad_query,
        *unpacked_parts(position, back_parts, key_gate, value_input, groups),
    )


def local(query_gate, key_gate, value_input, filter_taps, out_weight, out_grad):
    length, channels = query_gate.shape
    groups = filter_taps.shape[1]
    members = lax.axis_size("ctx")
    scale = 1.0 / math.sqrt(length * members)
    fits = channels // members % 128 == 0 and groups // members % 16 == 0
    body = in_line if lax.axis_size("tp") == 8 and fits else anywhere
    return body(
        query_gate, key_gate, value_input, filter_taps, out_weight, out_grad, members, scale
    )


def solution(mesh):
    both = P("ctx", "tp")
    return jax.shard_map(
        local,
        mesh=mesh,
        in_specs=(both, both, both, both, P("tp", None), both),
        out_specs=(both,) * 5,
        check_vma=False,
    )
```

```python
import functools
import math
import jax
import jax.numpy as jnp
from jax import lax
from jax.experimental import pallas as pl
from jax.experimental.pallas import tpu as pltpu
from jax.sharding import PartitionSpec as P

BLOCK = 128
POSITION = 8
NT = (((1,), (1,)), ((), ()))
COST = pl.CostEstimate(flops=2**20, bytes_accessed=2**12, transcendentals=0)


def lag_matrix(row, length):
    lanes = lax.broadcasted_iota(jnp.int32, (BLOCK, BLOCK), 1)
    rows = lax.broadcasted_iota(jnp.int32, (BLOCK, BLOCK), 0)
    spread = pltpu.roll(
        jnp.broadcast_to(row, (BLOCK, length)), 0, axis=1, stride=1, stride_axis=0
    )
    first = jnp.where(lanes >= rows, spread[:, :BLOCK], 0.0)
    return jnp.concatenate(
        [first.astype(jnp.bfloat16), spread[:, BLOCK:].astype(jnp.bfloat16)], axis=1
    )


def stacked(ref, start, rows, members, width):
    pieces = []
    for member in range(members):
        part = ref[member, pl.ds(start, rows), :]
        for at in range(0, width, BLOCK):
            pieces.append(part[:, at : at + BLOCK])
    return jnp.concatenate(pieces, axis=0)


def spread_out(ref, start, rows, value, members, width):
    per_member = width // BLOCK
    for member in range(members):
        base = member * per_member * rows
        parts = [value[base + i * rows : base + (i + 1) * rows] for i in range(per_member)]
        ref[member, pl.ds(start, rows), :] = jnp.concatenate(parts, axis=1)


def padded(groups):
    return -(-groups // 16) * 16


def load_taps(tap_scr, packed, at, width):
    groups, channels = tap_scr.shape[0], packed.shape[1]
    rows = padded(groups)
    parts = [
        packed[width + chunk * rows : width + (chunk + 1) * rows, :].astype(jnp.float32)
        for chunk in range(width // channels)
    ]
    start = pl.multiple_of(at * width, width)
    tap_scr[:, pl.ds(start, width)] = jnp.concatenate(parts, axis=1)[:groups]


def forward_kernel(members, per_group, width, plan_ref, *refs):
    inputs, outputs = refs[:members], refs[-members - 3 : -3]
    in_scr, tap_scr, out_scr = refs[-3:]
    position = plan_ref[POSITION]
    channels = inputs[0].shape[1]
    groups = channels // per_group
    length = members * width
    blocks = length // BLOCK
    for step in range(members):
        at = position ^ step
        in_scr[at] = inputs[step][:width].T
        load_taps(tap_scr, inputs[step], at, width)

    def one_group(group, carry):
        start = pl.multiple_of(group * per_group, per_group)
        lags = lag_matrix(tap_scr[pl.ds(group, 1), :], length)
        data = stacked(in_scr, start, per_group, members, width)
        total = [jnp.zeros((per_group, BLOCK), jnp.float32) for _ in range(blocks)]
        for offset in range(0, blocks, 2):
            rows = (blocks - offset) * per_group
            result = jnp.dot(
                data[:rows],
                lags[:, offset * BLOCK : (offset + 2) * BLOCK],
                preferred_element_type=jnp.float32,
            )
            for side in range(2):
                for source in range(blocks - offset - side):
                    total[source + offset + side] += result[
                        source * per_group : (source + 1) * per_group,
                        side * BLOCK : (side + 1) * BLOCK,
                    ]
        value = jnp.concatenate(total, axis=0).astype(jnp.bfloat16)
        spread_out(out_scr, start, per_group, value, members, width)
        return carry

    lax.fori_loop(0, groups, one_group, 0, unroll=4)
    for step in range(members):
        outputs[step][...] = out_scr[position ^ step].T


def backward_kernel(members, batch, per_group, scale, width, plan_ref, in_scr, lag_ref, *refs):
    cotangents = refs[:members]
    outputs = refs[-members - 4 : -4]
    cot_scr, out_scr, grad_scr, pad_scr = refs[-4:]
    position = plan_ref[POSITION]
    channels = cotangents[0].shape[1]
    groups = channels // per_group
    length = members * width
    blocks = length // BLOCK
    depth = blocks * per_group
    rows_of = lax.broadcasted_iota(jnp.int32, (BLOCK, BLOCK), 0)
    lanes_of = lax.broadcasted_iota(jnp.int32, (BLOCK, BLOCK), 1)
    mirror = (rows_of + lanes_of == BLOCK - 1).astype(jnp.bfloat16)

    @pl.when(pl.program_id(0) == 0)
    def _():
        for step in range(members):
            cot_scr[position ^ step] = cotangents[step][...].T
        pad_scr[...] = jnp.zeros_like(pad_scr)

    for local_group in range(batch):
        group = pl.program_id(0) * batch + local_group
        start = pl.multiple_of(group * per_group, per_group)
        lags = lag_ref[local_group]
        padded_cot = pad_scr.at[local_group]
        data = stacked(in_scr, start, per_group, members, width)
        cot = stacked(cot_scr, start, per_group, members, width)
        padded_cot[:depth, :BLOCK] = cot
        padded_cot[: depth - per_group, BLOCK:] = cot[per_group:]
        flipped = lax.dot_general(
            mirror, data, NT, preferred_element_type=jnp.float32
        ).astype(jnp.bfloat16)
        total = jnp.zeros((depth, BLOCK), jnp.float32)
        products = []
        for offset in range(0, blocks, 2):
            rows = depth - offset * per_group
            pair = padded_cot[offset * per_group : offset * per_group + depth, :]
            result = lax.dot_general(
                pair[:rows],
                lags[:, offset * BLOCK : (offset + 2) * BLOCK],
                NT,
                preferred_element_type=jnp.float32,
            )
            if rows < depth:
                result = jnp.concatenate(
                    [result, jnp.zeros((depth - rows, BLOCK), jnp.float32)], axis=0
                )
            total = total + result
            products.append(jnp.dot(flipped, pair, preferred_element_type=jnp.float32))
        spread_out(out_scr, start, per_group, total.astype(jnp.bfloat16), members, width)
        kept = jnp.where(rows_of + lanes_of >= BLOCK - 1, products[0][:, :BLOCK], 0.0)
        product = jnp.concatenate([kept, products[0][:, BLOCK:], *products[1:]], axis=1)
        product = pltpu.roll(
            product, length - (BLOCK - 1), axis=1, stride=1, stride_axis=0
        )
        grad_scr[pl.ds(group, 1), :] = jnp.sum(product, axis=0, keepdims=True) * scale

    @pl.when(pl.program_id(0) == pl.num_programs(0) - 1)
    def _():
        for step in range(members):
            at = position ^ step
            outputs[step][:width] = out_scr[at].T
            rows = padded(groups)
            whole = grad_scr[:, pl.ds(pl.multiple_of(at * width, width), width)]
            whole = whole.astype(jnp.bfloat16)
            if rows > groups:
                blank = jnp.zeros((rows - groups, width), jnp.bfloat16)
                whole = jnp.concatenate([whole, blank], axis=0)
            for chunk in range(width // channels):
                outputs[step][width + chunk * rows : width + (chunk + 1) * rows, :] = whole[
                    :, chunk * channels : (chunk + 1) * channels
                ]


def lag_kernel(taps_ref, out_ref):
    row = taps_ref[pl.ds(pl.program_id(0), 1), :]
    out_ref[0] = lag_matrix(row, taps_ref.shape[1])


VMEM = pl.BlockSpec(memory_space=pltpu.VMEM)
ANYWHERE = pl.BlockSpec(memory_space=pl.ANY)
SMEM = pl.BlockSpec(memory_space=pltpu.SMEM)


def convolve(plan, inputs, width, per_group, after=()):
    members = len(inputs)
    channels = inputs[0].shape[1]
    length = members * width
    *parts, turned, taps = pl.pallas_call(
        functools.partial(forward_kernel, members, per_group, width),
        out_shape=[jax.ShapeDtypeStruct((width, channels), jnp.bfloat16)] * members
        + [
            jax.ShapeDtypeStruct((members, channels, width), jnp.bfloat16),
            jax.ShapeDtypeStruct((channels // per_group, length), jnp.float32),
        ],
        in_specs=[SMEM] + [VMEM] * members + [ANYWHERE] * len(after),
        out_specs=[VMEM] * (members + 2),
        scratch_shapes=[pltpu.VMEM((members, channels, width), jnp.bfloat16)],
        compiler_params=pltpu.CompilerParams(vmem_limit_bytes=24 * 2**20),
        cost_estimate=COST,
        name="causal_conv",
    )(plan, *inputs, *after)
    return parts, turned, taps


def lag_matrices(taps):
    groups, length = taps.shape
    return pl.pallas_call(
        lag_kernel,
        out_shape=jax.ShapeDtypeStruct((groups, BLOCK, length), jnp.bfloat16),
        grid=(groups,),
        in_specs=[VMEM],
        out_specs=pl.BlockSpec((1, BLOCK, length), lambda i: (i, 0, 0)),
        compiler_params=pltpu.CompilerParams(vmem_limit_bytes=12 * 2**20),
        cost_estimate=COST,
        name="lag_matrices",
    )(taps)


def correlate(plan, turned, lags, cotangents, per_group, scale, after=()):
    members = len(cotangents)
    width, channels = cotangents[0].shape
    length = members * width
    groups = channels // per_group
    batch = 4 if groups % 4 == 0 else 1
    rows = width + padded(groups) * width // channels
    return pl.pallas_call(
        functools.partial(backward_kernel, members, batch, per_group, scale, width),
        out_shape=[jax.ShapeDtypeStruct((rows, channels), jnp.bfloat16)] * members,
        grid=(groups // batch,),
        in_specs=[SMEM, VMEM, pl.BlockSpec((batch, BLOCK, length), lambda i: (i, 0, 0))]
        + [VMEM] * members
        + [ANYWHERE] * len(after),
        out_specs=[VMEM] * members,
        scratch_shapes=[
            pltpu.VMEM((members, channels, width), jnp.bfloat16),
            pltpu.VMEM((members, channels, width), jnp.bfloat16),
            pltpu.VMEM((groups, length), jnp.float32),
            pltpu.VMEM((batch, 2 * length // BLOCK * per_group, 2 * BLOCK), jnp.bfloat16),
        ],
        compiler_params=pltpu.CompilerParams(vmem_limit_bytes=24 * 2**20),
        cost_estimate=COST,
        name="causal_conv_grads",
    )(plan, turned, lags, *cotangents, *after)


def in_hbm(array):
    return pltpu.with_memory_space_constraint(array, pltpu.HBM)


def prepare_kernel(members, scale, who_ref, key_ref, value_ref, taps_ref, *outputs):
    position = who_ref[0]
    step_no = pl.program_id(0)
    rows, channels = key_ref.shape
    share = channels // members
    groups = taps_ref.shape[0] // members
    total_width = taps_ref.shape[1]
    for step in range(members):
        at = position ^ step
        columns = pl.ds(pl.multiple_of(at * share, share), share)
        product = key_ref[:, columns].astype(jnp.float32) * value_ref[:, columns].astype(
            jnp.float32
        )
        here = pl.ds(pl.multiple_of(step_no * rows, rows), rows)
        outputs[step][here, :] = product.astype(jnp.bfloat16)

    @pl.when(step_no == 0)
    def _():
        for step in range(members):
            at = position ^ step
            taps = taps_ref[pl.ds(pl.multiple_of(at * groups, groups), groups), :]
            taps = (taps * scale).astype(jnp.bfloat16)
            for chunk in range(total_width // share):
                start = total_width + chunk * groups
                outputs[step][start : start + groups, :] = taps[
                    :, chunk * share : (chunk + 1) * share
                ]


def prepare(who, key_gate, value_input, filter_taps, members, scale):
    width, channels = key_gate.shape
    share = channels // members
    rows = width + filter_taps.size // members // share
    tile = width // 4
    part = pl.BlockSpec((tile, channels), lambda i: (i, 0))
    return pl.pallas_call(
        functools.partial(prepare_kernel, members, scale),
        out_shape=[jax.ShapeDtypeStruct((rows, share), jnp.bfloat16)] * members,
        grid=(4,),
        in_specs=[SMEM, part, part, pl.BlockSpec(filter_taps.shape[::-1], lambda i: (0, 0))],
        out_specs=[VMEM] * members,
        compiler_params=pltpu.CompilerParams(vmem_limit_bytes=24 * 2**20),
        cost_estimate=COST,
        name="gated_input",
    )(who, in_hbm(key_gate), in_hbm(value_input), in_hbm(filter_taps.T))


def finish_kernel(members, plan_ref, *refs):
    parts = refs[:members]
    key_ref, value_ref = refs[members : members + 2]
    key_out, value_out, taps_out = refs[-3:]
    position = plan_ref[POSITION]
    width, channels = key_ref.shape
    share = channels // members
    groups = taps_out.shape[0] // members
    for step in range(members):
        at = position ^ step
        columns = pl.ds(pl.multiple_of(at * share, share), share)
        grad = parts[step][:width].astype(jnp.float32)
        key_out[:, columns] = (grad * value_ref[:, columns].astype(jnp.float32)).astype(
            jnp.bfloat16
        )
        value_out[:, columns] = (grad * key_ref[:, columns].astype(jnp.float32)).astype(
            jnp.bfloat16
        )
        taps = [
            parts[step][width + chunk * groups : width + (chunk + 1) * groups, :]
            for chunk in range(width // share)
        ]
        taps_out[pl.ds(pl.multiple_of(at * groups, groups), groups), :] = jnp.concatenate(
            taps, axis=1
        ).astype(jnp.float32)


def finished(plan, parts, key_gate, value_input, groups, after=()):
    members = len(parts)
    width, channels = key_gate.shape
    array = jax.ShapeDtypeStruct((width, channels), jnp.bfloat16)
    grad_key, grad_value, taps = pl.pallas_call(
        functools.partial(finish_kernel, members),
        out_shape=[array, array, jax.ShapeDtypeStruct((groups, width), jnp.float32)],
        in_specs=[SMEM] + [VMEM] * (members + 2) + [ANYWHERE] * len(after),
        out_specs=[VMEM] * 3,
        compiler_params=pltpu.CompilerParams(vmem_limit_bytes=24 * 2**20),
        cost_estimate=COST,
        name="input_gradients",
    )(plan, *parts, key_gate, value_input, *after)
    return grad_key, grad_value, taps.T


def swapped(array, axis, step):
    size = lax.axis_size(axis)
    return lax.ppermute(array, axis, [(i, i ^ step) for i in range(size)])


def traded(pieces, axis):
    return [pieces[0]] + [swapped(pieces[step], axis, step) for step in range(1, len(pieces))]


def cut(array, position, members, axis):
    width = array.shape[axis] // members
    return [
        lax.dynamic_slice_in_dim(array, (position ^ step) * width, width, axis)
        for step in range(members)
    ]


def joined(pieces, position, axis):
    members = len(pieces)
    width = pieces[0].shape[axis]
    shape = list(pieces[0].shape)
    shape[axis] = members * width
    whole = jnp.zeros(shape, pieces[0].dtype)
    for step in range(members):
        whole = lax.dynamic_update_slice_in_dim(
            whole, pieces[step], (position ^ step) * width, axis
        )
    return whole


def wide(array):
    return array.astype(jnp.float32)


def hop(array, pairs):
    return lax.ppermute(
        array, "tp", [(2 * i + core, 2 * j + core) for i, j in pairs for core in range(2)]
    )


INWARD = ((0, 1), (3, 2))
ACROSS = ((1, 2), (2, 1))
OUTWARD = ((1, 0), (2, 3))
OWN, NEAR, MIDDLE, FAR = range(4)
IN_MIDDLE = POSITION + 1
CHIPS = ((0, 1, 2, 3), (1, 0, 3, 2), (2, 2, 1, 1), (3, 3, 0, 0))


def plan_kernel(who_ref, plan_ref):
    place = who_ref[1]
    chip, core = place // 2, place % 2
    for number, table in enumerate(CHIPS):
        source = jnp.where(
            chip < 2,
            jnp.where(chip == 0, table[0], table[1]),
            jnp.where(chip == 2, table[2], table[3]),
        )
        plan_ref[2 * number] = 2 * source + core
        plan_ref[2 * number + 1] = 2 * source + 1 - core
    plan_ref[POSITION] = who_ref[0]
    plan_ref[IN_MIDDLE] = ((chip == 1) | (chip == 2)).astype(jnp.int32)


def planned(who):
    return pl.pallas_call(
        plan_kernel,
        out_shape=jax.ShapeDtypeStruct((IN_MIDDLE + 1,), jnp.int32),
        in_specs=[SMEM],
        out_specs=SMEM,
        compiler_params=pltpu.CompilerParams(vmem_limit_bytes=2**20),
        cost_estimate=COST,
        name="plan",
    )(who)


def pass_kernel(*refs):
    del refs


def held_until(values, after):
    return pl.pallas_call(
        pass_kernel,
        out_shape=[jax.ShapeDtypeStruct(value.shape, value.dtype) for value in values],
        in_specs=[ANYWHERE] * (len(values) + len(after)),
        out_specs=[ANYWHERE] * len(values),
        input_output_aliases={number: number for number in range(len(values))},
        compiler_params=pltpu.CompilerParams(vmem_limit_bytes=2**20),
        cost_estimate=COST,
        name="held",
    )(*values, *after)


def add_kernel(*refs):
    refs[-1][...] = sum(wide(ref[...]) for ref in refs[:-1]).astype(jnp.bfloat16)


def added(*arrays):
    rows, width = arrays[0].shape
    part = pl.BlockSpec((rows // 4, width), lambda i: (i, 0))
    return pl.pallas_call(
        add_kernel,
        out_shape=jax.ShapeDtypeStruct((rows, width), jnp.bfloat16),
        grid=(4,),
        in_specs=[part] * len(arrays),
        out_specs=part,
        compiler_params=pltpu.CompilerParams(vmem_limit_bytes=8 * 2**20),
        cost_estimate=COST,
        name="added",
    )(*arrays)


def choice_kernel(plan_ref, middle_ref, end_ref, *refs):
    out_ref = refs[-1]
    in_middle = plan_ref[IN_MIDDLE] == 1

    @pl.when(in_middle)
    def _():
        out_ref[...] = middle_ref[...]

    @pl.when(jnp.logical_not(in_middle))
    def _():
        out_ref[...] = end_ref[...]


def chosen(plan, in_middle, at_end, after=()):
    return pl.pallas_call(
        choice_kernel,
        out_shape=jax.ShapeDtypeStruct(at_end.shape, at_end.dtype),
        in_specs=[SMEM, VMEM, VMEM] + [ANYWHERE] * len(after),
        out_specs=VMEM,
        compiler_params=pltpu.CompilerParams(vmem_limit_bytes=2**20),
        cost_estimate=COST,
        name="chosen",
    )(plan, in_middle, at_end, *after)


def gate_kernel(members, plan_ref, *refs):
    parts = refs[:members]
    query_ref, gated_ref, conv_ref = refs[members], *refs[-2:]
    position = plan_ref[POSITION]
    share = parts[0].shape[1]
    for step in range(members):
        columns = pl.ds(pl.multiple_of((position ^ step) * share, share), share)
        conv = parts[step][...]
        conv_ref[:, columns] = conv
        gated_ref[:, columns] = (wide(conv) * wide(query_ref[:, columns])).astype(jnp.bfloat16)


def gated(plan, parts, query_gate, after):
    array = jax.ShapeDtypeStruct(query_gate.shape, jnp.bfloat16)
    return pl.pallas_call(
        functools.partial(gate_kernel, len(parts)),
        out_shape=[array, array],
        in_specs=[SMEM] + [VMEM] * (len(parts) + 1) + [ANYWHERE] * len(after),
        out_specs=[VMEM] * 2,
        compiler_params=pltpu.CompilerParams(vmem_limit_bytes=8 * 2**20),
        cost_estimate=COST,
        name="gated_output",
    )(plan, *parts, query_gate, *after)


def spans(widths, start, stop):
    found, begin = [], 0
    for number, width in enumerate(widths):
        low, high = max(start, begin), min(stop, begin + width)
        if low < high:
            found.append((number, slice(low - begin, high - begin), slice(low - start, high - start)))
        begin += width
    return found


def product_kernel(steps, more_widths, out_widths, _, data_ref, weight_ref, *refs):
    more, outputs = refs[: len(more_widths)], refs[-len(out_widths) :]
    product = jnp.dot(data_ref[...], weight_ref[...], preferred_element_type=jnp.float32)
    width = product.shape[1]
    for step in range(steps):
        start, stop = step * width, (step + 1) * width

        @pl.when(pl.program_id(0) == step)
        def _(start=start, stop=stop):
            total = product
            if more:
                parts = [wide(more[n][:, there]) for n, there, _ in spans(more_widths, start, stop)]
                total = total + jnp.concatenate(parts, axis=1)
            total = total.astype(jnp.bfloat16)
            for n, there, here in spans(out_widths, start, stop):
                outputs[n][:, there] = total[:, here]


def column_products(
    plan, data, out_weight, first, count, other, more=(), after=(), tiles=1, widths=()
):
    rows, depth = data.shape
    width = data.shape[1]
    tile = width // tiles
    steps = count * tiles
    widths = tuple(widths) or (width,) * count

    def weights(i, at):
        return 0, at[2 * (first - i // tiles) + other] * tiles + i % tiles

    return pl.pallas_call(
        functools.partial(product_kernel, steps, [part.shape[1] for part in more], widths),
        out_shape=[jax.ShapeDtypeStruct((rows, part), jnp.bfloat16) for part in widths],
        grid_spec=pltpu.PrefetchScalarGridSpec(
            num_scalar_prefetch=1,
            grid=(steps,),
            in_specs=[VMEM, pl.BlockSpec((depth, tile), weights)]
            + [VMEM] * len(more)
            + [ANYWHERE] * len(after),
            out_specs=[VMEM] * len(widths),
        ),
        compiler_params=pltpu.CompilerParams(vmem_limit_bytes=16 * 2**20),
        cost_estimate=COST,
        name="projection_blocks",
    )(plan, data, in_hbm(out_weight), *more, *after)


def cotangent_kernel(count, begin, _, weight_ref, *refs):
    blocks, refs = refs[:count], refs[count:]
    step = pl.program_id(0)
    total = refs[-1]

    for number, block in enumerate(blocks):

        @pl.when(step == number)
        def _(number=number, block=block):
            product = lax.dot_general(
                block[...], weight_ref[...], NT, preferred_element_type=jnp.float32
            )
            if number == 0:
                total[...] = product if begin else refs[0][...] + product
            else:
                total[...] += product


def last_cotangent_kernel(
    members, plan_ref, weight_ref, block_ref, start_ref, conv_ref, query_ref, *refs
):
    parts, cot_scr = refs[-1 - members : -1], refs[-1]
    grad_ref = refs[-2 - members]
    product = lax.dot_general(
        block_ref[...], weight_ref[...], NT, preferred_element_type=jnp.float32
    )
    dgated = wide((start_ref[...] + product).astype(jnp.bfloat16))
    grad_ref[...] = (dgated * wide(conv_ref[...])).astype(jnp.bfloat16)
    cot_scr[...] = (dgated * wide(query_ref[...])).astype(jnp.bfloat16)
    share = parts[0].shape[1]
    odd = plan_ref[POSITION] % 2
    for step in range(0, members, 2):

        @pl.when(pl.program_id(0) == step // 2)
        def _(step=step):
            parts[step][...] = cot_scr[:, pl.ds(pl.multiple_of(odd * share, share), share)]
            parts[step + 1][...] = cot_scr[
                :, pl.ds(pl.multiple_of((1 - odd) * share, share), share)
            ]


def last_cotangents(
    plan, first, block, out_weight, start, convolved, query_gate, members, after
):
    rows, width = block.shape
    channels = out_weight.shape[0]
    share = channels // members
    pair = pl.BlockSpec((rows, 2 * share), lambda i, at: (0, at[POSITION] // 2 ^ i))
    return pl.pallas_call(
        functools.partial(last_cotangent_kernel, members),
        out_shape=[jax.ShapeDtypeStruct((rows, channels), jnp.bfloat16)]
        + [jax.ShapeDtypeStruct((rows, share), jnp.bfloat16)] * members,
        grid_spec=pltpu.PrefetchScalarGridSpec(
            num_scalar_prefetch=1,
            grid=(members // 2,),
            in_specs=[
                pl.BlockSpec((2 * share, width), lambda i, at: (at[POSITION] // 2 ^ i, at[first])),
                VMEM,
                pair,
                pair,
                pair,
            ]
            + [ANYWHERE] * len(after),
            out_specs=[pair] + [VMEM] * members,
            scratch_shapes=[pltpu.VMEM((rows, 2 * share), jnp.bfloat16)],
        ),
        compiler_params=pltpu.CompilerParams(vmem_limit_bytes=24 * 2**20),
        cost_estimate=COST,
        name="cotangent_last",
    )(plan, in_hbm(out_weight), block, start, convolved, query_gate, *after)


def both(blocks):
    return [part for block in blocks for part in (block, swapped(block, "tp", 1))]


def cotangent_products(plan, first, parts, out_weight, start=None, after=()):
    rows, width = parts[0].shape
    channels = out_weight.shape[0]
    count = len(parts)
    begin = start is None
    extra = () if begin else (start,)
    return pl.pallas_call(
        functools.partial(cotangent_kernel, count, begin),
        out_shape=jax.ShapeDtypeStruct((rows, channels), jnp.float32),
        grid_spec=pltpu.PrefetchScalarGridSpec(
            num_scalar_prefetch=1,
            grid=(count,),
            in_specs=[pl.BlockSpec((channels, width), lambda i, at: (0, at[first + i]))]
            + [VMEM] * (count + len(extra))
            + [ANYWHERE] * len(after),
            out_specs=VMEM,
        ),
        compiler_params=pltpu.CompilerParams(vmem_limit_bytes=16 * 2**20),
        cost_estimate=COST,
        name="cotangent_blocks",
    )(plan, in_hbm(out_weight), *parts, *extra, *after)


def packed_parts(position, key_gate, value_input, filter_taps, members, scale):
    length, channels = key_gate.shape
    share = channels // members
    product_in = (wide(key_gate) * wide(value_input)).astype(jnp.bfloat16)
    tap_rows = (filter_taps * scale).astype(jnp.bfloat16).T
    owned = filter_taps.shape[1] // members
    chunks = length // share
    packed = []
    pieces = cut(product_in, position, members, 1)
    for piece, taps in zip(pieces, cut(tap_rows, position, members, 0)):
        taps = taps.reshape(owned, chunks, share).transpose(1, 0, 2)
        taps = jnp.pad(taps, ((0, 0), (0, padded(owned) - owned), (0, 0)))
        packed.append(jnp.concatenate([piece, taps.reshape(-1, share)], axis=0))
    return packed


def unpacked_parts(position, parts, key_gate, value_input, groups):
    length, channels = key_gate.shape
    members = len(parts)
    share = channels // members
    owned = groups // members
    chunks = length // share
    input_grad = wide(joined([part[:length] for part in parts], position, 1))
    filter_parts = [
        part[length:]
        .reshape(chunks, padded(owned), share)[:, :owned]
        .transpose(1, 0, 2)
        .reshape(owned, length)
        for part in parts
    ]
    grad_filter = wide(joined(filter_parts, position, 0)).T
    grad_key = (input_grad * wide(value_input)).astype(jnp.bfloat16)
    grad_value = (input_grad * wide(key_gate)).astype(jnp.bfloat16)
    return grad_key, grad_value, grad_filter


def in_line(
    query_gate, key_gate, value_input, filter_taps, out_weight, out_grad, members, scale
):
    length, channels = query_gate.shape
    groups = filter_taps.shape[1]
    per_group = channels // groups
    who = jnp.stack([lax.axis_index("ctx"), lax.axis_index("tp")]).astype(jnp.int32)
    plan = planned(who)
    near, cross = hop(out_grad, INWARD + OUTWARD), hop(out_grad, ACROSS)
    total = cotangent_products(plan, 2 * OWN, both([out_grad]), out_weight)

    packed = prepare(who, key_gate, value_input, filter_taps, members, scale)
    input_parts = traded(packed, "ctx")
    conv_parts, turned, taps = convolve(plan, input_parts, length, per_group, (total,))
    *conv_parts, near, cross = held_until([*conv_parts, near, cross], ())
    far, skip = hop(near, ACROSS), hop(cross, OUTWARD)
    lags = lag_matrices(taps)
    gated_out, convolved = gated(plan, traded(conv_parts, "ctx"), query_gate, (lags,))

    def product(first, count, other, more=(), after=(), tiles=1, widths=()):
        return column_products(
            plan, gated_out, out_weight, first, count, other, more, after, tiles, widths
        )

    quarter, half = channels // 4, channels // 2
    given_far = product(FAR, 1, 1, tiles=2, widths=(3 * quarter, quarter))
    received = [swapped(part, "tp", 1) for part in given_far]
    (first,) = product(FAR, 1, 0, received, tiles=2)
    far, skip = held_until([far, skip], (first,))
    mixed = chosen(plan, far, first)
    arrived = hop(mixed, OUTWARD + INWARD)
    given_middle = product(MIDDLE, 1, 1, (), (mixed,), tiles=2, widths=(half, half))
    received = [swapped(part, "tp", 1) for part in given_middle]
    (second,) = product(MIDDLE, 1, 0, received, tiles=2)
    middle_block = added(cross, skip)
    blocks = [near, swapped(near, "tp", 1), middle_block]
    total = cotangent_products(plan, 2 * NEAR, blocks, out_weight, total, after=(second,))
    given_near, given_own = product(NEAR, 2, 1, (), (second,))
    (arrived,) = held_until([arrived], (total, given_near))
    through = added(first, arrived)
    two_a = hop(through, ACROSS)
    (second,) = held_until([second], (arrived,))
    two_b = hop(second, INWARD)

    far_block, far_other = both([chosen(plan, far, arrived, (through,))])
    blocks = [swapped(middle_block, "tp", 1), far_block]
    total = cotangent_products(
        plan, 2 * MIDDLE + 1, blocks, out_weight, total, after=(through,)
    )
    grad_query, *grad_parts = last_cotangents(
        plan, 2 * FAR + 1, far_other, out_weight, total, convolved, query_gate, members, ()
    )
    received = (swapped(given_near, "tp", 1), swapped(given_own, "tp", 1))
    third, own = product(NEAR, 2, 0, received, (grad_parts[0],))
    grad_parts = traded(grad_parts, "ctx")

    two_a, two_b = held_until([two_a, two_b], tuple(grad_parts[1:]))
    third, second = added(third, two_a), added(second, two_b)
    back_parts = correlate(plan, turned, lags, grad_parts, per_group, scale, (third, second))
    projected = added(own, hop(third, OUTWARD + INWARD), hop(second, ACROSS))
    back_parts = traded(back_parts, "ctx")
    return projected, grad_query, *finished(plan, back_parts, key_gate, value_input, groups, (in_hbm(projected),))


def anywhere(
    query_gate, key_gate, value_input, filter_taps, out_weight, out_grad, members, scale
):
    length, channels = query_gate.shape
    groups = filter_taps.shape[1]
    per_group = channels // groups
    position = lax.axis_index("ctx")
    plan = jnp.full((POSITION + 1,), position, jnp.int32)
    packed = packed_parts(position, key_gate, value_input, filter_taps, members, scale)
    input_parts = traded(packed, "ctx")
    conv_parts, turned, taps = convolve(plan, input_parts, length, per_group)
    conv_parts = traded(conv_parts, "ctx")
    convolved = joined(conv_parts, position, 1)
    gated_out = (wide(query_gate) * wide(convolved)).astype(jnp.bfloat16)
    partial_value = jnp.dot(gated_out, out_weight, preferred_element_type=jnp.float32)
    projected = lax.psum_scatter(
        partial_value.astype(jnp.bfloat16), "tp", scatter_dimension=1, tiled=True
    )
    dgated = jnp.einsum(
        "tk,ck->tc",
        lax.all_gather(out_grad, "tp", axis=1, tiled=True),
        out_weight,
        preferred_element_type=jnp.float32,
    ).astype(jnp.bfloat16)
    grad_query = (wide(dgated) * wide(convolved)).astype(jnp.bfloat16)
    conv_grad = (wide(dgated) * wide(query_gate)).astype(jnp.bfloat16)
    grad_parts = traded(cut(conv_grad, position, members, 1), "ctx")
    back_parts = correlate(plan, turned, lag_matrices(taps), grad_parts, per_group, scale)
    back_parts = traded(back_parts, "ctx")
    return (
        projected,
        grad_query,
        *unpacked_parts(position, back_parts, key_gate, value_input, groups),
    )


def local(query_gate, key_gate, value_input, filter_taps, out_weight, out_grad):
    length, channels = query_gate.shape
    groups = filter_taps.shape[1]
    members = lax.axis_size("ctx")
    scale = 1.0 / math.sqrt(length * members)
    fits = channels // members % 128 == 0 and groups // members % 16 == 0
    body = in_line if lax.axis_size("tp") == 8 and fits else anywhere
    return body(
        query_gate, key_gate, value_input, filter_taps, out_weight, out_grad, members, scale
    )


def solution(mesh):
    both = P("ctx", "tp")
    return jax.shard_map(
        local,
        mesh=mesh,
        in_specs=(both, both, both, both, P("tp", None), both),
        out_specs=(both,) * 5,
        check_vma=False,
    )
```

```python
import functools
import math
import jax
import jax.numpy as jnp
from jax import lax
from jax.experimental import pallas as pl
from jax.experimental.pallas import tpu as pltpu
from jax.sharding import PartitionSpec as P

BLOCK = 128
POSITION = 8
NT = (((1,), (1,)), ((), ()))
COST = pl.CostEstimate(flops=2**20, bytes_accessed=2**12, transcendentals=0)


def lag_matrix(row, length):
    lanes = lax.broadcasted_iota(jnp.int32, (BLOCK, BLOCK), 1)
    rows = lax.broadcasted_iota(jnp.int32, (BLOCK, BLOCK), 0)
    spread = pltpu.roll(
        jnp.broadcast_to(row, (BLOCK, length)), 0, axis=1, stride=1, stride_axis=0
    )
    first = jnp.where(lanes >= rows, spread[:, :BLOCK], 0.0)
    return jnp.concatenate(
        [first.astype(jnp.bfloat16), spread[:, BLOCK:].astype(jnp.bfloat16)], axis=1
    )


def stacked(ref, start, rows, members, width):
    pieces = []
    for member in range(members):
        part = ref[member, pl.ds(start, rows), :]
        for at in range(0, width, BLOCK):
            pieces.append(part[:, at : at + BLOCK])
    return jnp.concatenate(pieces, axis=0)


def spread_out(ref, start, rows, value, members, width):
    per_member = width // BLOCK
    for member in range(members):
        base = member * per_member * rows
        parts = [value[base + i * rows : base + (i + 1) * rows] for i in range(per_member)]
        ref[member, pl.ds(start, rows), :] = jnp.concatenate(parts, axis=1)


def padded(groups):
    return -(-groups // 16) * 16


def load_taps(tap_scr, packed, at, width):
    groups, channels = tap_scr.shape[0], packed.shape[1]
    rows = padded(groups)
    parts = [
        packed[width + chunk * rows : width + (chunk + 1) * rows, :].astype(jnp.float32)
        for chunk in range(width // channels)
    ]
    start = pl.multiple_of(at * width, width)
    tap_scr[:, pl.ds(start, width)] = jnp.concatenate(parts, axis=1)[:groups]


def forward_kernel(members, per_group, width, plan_ref, *refs):
    inputs, outputs = refs[:members], refs[-members - 3 : -3]
    in_scr, tap_scr, out_scr = refs[-3:]
    position = plan_ref[POSITION]
    channels = inputs[0].shape[1]
    groups = channels // per_group
    length = members * width
    blocks = length // BLOCK
    for step in range(members):
        at = position ^ step
        in_scr[at] = inputs[step][:width].T
        load_taps(tap_scr, inputs[step], at, width)

    def one_group(group, carry):
        start = pl.multiple_of(group * per_group, per_group)
        lags = lag_matrix(tap_scr[pl.ds(group, 1), :], length)
        data = stacked(in_scr, start, per_group, members, width)
        total = [jnp.zeros((per_group, BLOCK), jnp.float32) for _ in range(blocks)]
        for offset in range(0, blocks, 2):
            rows = (blocks - offset) * per_group
            result = jnp.dot(
                data[:rows],
                lags[:, offset * BLOCK : (offset + 2) * BLOCK],
                preferred_element_type=jnp.float32,
            )
            for side in range(2):
                for source in range(blocks - offset - side):
                    total[source + offset + side] += result[
                        source * per_group : (source + 1) * per_group,
                        side * BLOCK : (side + 1) * BLOCK,
                    ]
        value = jnp.concatenate(total, axis=0).astype(jnp.bfloat16)
        spread_out(out_scr, start, per_group, value, members, width)
        return carry

    lax.fori_loop(0, groups, one_group, 0, unroll=4)
    for step in range(members):
        outputs[step][...] = out_scr[position ^ step].T


def backward_kernel(members, batch, per_group, scale, width, plan_ref, in_scr, lag_ref, *refs):
    cotangents = refs[:members]
    outputs = refs[-members - 4 : -4]
    cot_scr, out_scr, grad_scr, pad_scr = refs[-4:]
    position = plan_ref[POSITION]
    channels = cotangents[0].shape[1]
    groups = channels // per_group
    length = members * width
    blocks = length // BLOCK
    depth = blocks * per_group
    rows_of = lax.broadcasted_iota(jnp.int32, (BLOCK, BLOCK), 0)
    lanes_of = lax.broadcasted_iota(jnp.int32, (BLOCK, BLOCK), 1)
    mirror = (rows_of + lanes_of == BLOCK - 1).astype(jnp.bfloat16)

    @pl.when(pl.program_id(0) == 0)
    def _():
        for step in range(members):
            cot_scr[position ^ step] = cotangents[step][...].T
        pad_scr[...] = jnp.zeros_like(pad_scr)

    for local_group in range(batch):
        group = pl.program_id(0) * batch + local_group
        start = pl.multiple_of(group * per_group, per_group)
        lags = lag_ref[local_group]
        padded_cot = pad_scr.at[local_group]
        data = stacked(in_scr, start, per_group, members, width)
        cot = stacked(cot_scr, start, per_group, members, width)
        padded_cot[:depth, :BLOCK] = cot
        padded_cot[: depth - per_group, BLOCK:] = cot[per_group:]
        flipped = lax.dot_general(
            mirror, data, NT, preferred_element_type=jnp.float32
        ).astype(jnp.bfloat16)
        total = jnp.zeros((depth, BLOCK), jnp.float32)
        products = []
        for offset in range(0, blocks, 2):
            rows = depth - offset * per_group
            pair = padded_cot[offset * per_group : offset * per_group + depth, :]
            result = lax.dot_general(
                pair[:rows],
                lags[:, offset * BLOCK : (offset + 2) * BLOCK],
                NT,
                preferred_element_type=jnp.float32,
            )
            if rows < depth:
                result = jnp.concatenate(
                    [result, jnp.zeros((depth - rows, BLOCK), jnp.float32)], axis=0
                )
            total = total + result
            products.append(jnp.dot(flipped, pair, preferred_element_type=jnp.float32))
        spread_out(out_scr, start, per_group, total.astype(jnp.bfloat16), members, width)
        kept = jnp.where(rows_of + lanes_of >= BLOCK - 1, products[0][:, :BLOCK], 0.0)
        product = jnp.concatenate([kept, products[0][:, BLOCK:], *products[1:]], axis=1)
        product = pltpu.roll(
            product, length - (BLOCK - 1), axis=1, stride=1, stride_axis=0
        )
        grad_scr[pl.ds(group, 1), :] = jnp.sum(product, axis=0, keepdims=True) * scale

    @pl.when(pl.program_id(0) == pl.num_programs(0) - 1)
    def _():
        for step in range(members):
            at = position ^ step
            outputs[step][:width] = out_scr[at].T
            rows = padded(groups)
            whole = grad_scr[:, pl.ds(pl.multiple_of(at * width, width), width)]
            whole = whole.astype(jnp.bfloat16)
            if rows > groups:
                blank = jnp.zeros((rows - groups, width), jnp.bfloat16)
                whole = jnp.concatenate([whole, blank], axis=0)
            for chunk in range(width // channels):
                outputs[step][width + chunk * rows : width + (chunk + 1) * rows, :] = whole[
                    :, chunk * channels : (chunk + 1) * channels
                ]


def lag_kernel(taps_ref, out_ref):
    row = taps_ref[pl.ds(pl.program_id(0), 1), :]
    out_ref[0] = lag_matrix(row, taps_ref.shape[1])


VMEM = pl.BlockSpec(memory_space=pltpu.VMEM)
ANYWHERE = pl.BlockSpec(memory_space=pl.ANY)
SMEM = pl.BlockSpec(memory_space=pltpu.SMEM)


def convolve(plan, inputs, width, per_group, after=()):
    members = len(inputs)
    channels = inputs[0].shape[1]
    length = members * width
    *parts, turned, taps = pl.pallas_call(
        functools.partial(forward_kernel, members, per_group, width),
        out_shape=[jax.ShapeDtypeStruct((width, channels), jnp.bfloat16)] * members
        + [
            jax.ShapeDtypeStruct((members, channels, width), jnp.bfloat16),
            jax.ShapeDtypeStruct((channels // per_group, length), jnp.float32),
        ],
        in_specs=[SMEM] + [VMEM] * members + [ANYWHERE] * len(after),
        out_specs=[VMEM] * (members + 2),
        scratch_shapes=[pltpu.VMEM((members, channels, width), jnp.bfloat16)],
        compiler_params=pltpu.CompilerParams(vmem_limit_bytes=24 * 2**20),
        cost_estimate=COST,
        name="causal_conv",
    )(plan, *inputs, *after)
    return parts, turned, taps


def lag_matrices(taps):
    groups, length = taps.shape
    return pl.pallas_call(
        lag_kernel,
        out_shape=jax.ShapeDtypeStruct((groups, BLOCK, length), jnp.bfloat16),
        grid=(groups,),
        in_specs=[VMEM],
        out_specs=pl.BlockSpec((1, BLOCK, length), lambda i: (i, 0, 0)),
        compiler_params=pltpu.CompilerParams(vmem_limit_bytes=12 * 2**20),
        cost_estimate=COST,
        name="lag_matrices",
    )(taps)


def correlate(plan, turned, lags, cotangents, per_group, scale, after=()):
    members = len(cotangents)
    width, channels = cotangents[0].shape
    length = members * width
    groups = channels // per_group
    batch = 4 if groups % 4 == 0 else 1
    rows = width + padded(groups) * width // channels
    return pl.pallas_call(
        functools.partial(backward_kernel, members, batch, per_group, scale, width),
        out_shape=[jax.ShapeDtypeStruct((rows, channels), jnp.bfloat16)] * members,
        grid=(groups // batch,),
        in_specs=[SMEM, VMEM, pl.BlockSpec((batch, BLOCK, length), lambda i: (i, 0, 0))]
        + [VMEM] * members
        + [ANYWHERE] * len(after),
        out_specs=[VMEM] * members,
        scratch_shapes=[
            pltpu.VMEM((members, channels, width), jnp.bfloat16),
            pltpu.VMEM((members, channels, width), jnp.bfloat16),
            pltpu.VMEM((groups, length), jnp.float32),
            pltpu.VMEM((batch, 2 * length // BLOCK * per_group, 2 * BLOCK), jnp.bfloat16),
        ],
        compiler_params=pltpu.CompilerParams(vmem_limit_bytes=24 * 2**20),
        cost_estimate=COST,
        name="causal_conv_grads",
    )(plan, turned, lags, *cotangents, *after)


def in_hbm(array):
    return pltpu.with_memory_space_constraint(array, pltpu.HBM)


def prepare_kernel(
    members, scale, who_ref, key_ref, value_ref, taps_ref, passed_ref, *outputs
):
    position = who_ref[0]
    step_no = pl.program_id(0)
    rows, channels = key_ref.shape
    share = channels // members
    groups = taps_ref.shape[0] // members
    total_width = taps_ref.shape[1]
    outputs[members][pl.ds(pl.multiple_of(step_no * rows, rows), rows), :] = passed_ref[...]
    for step in range(members):
        at = position ^ step
        columns = pl.ds(pl.multiple_of(at * share, share), share)
        product = key_ref[:, columns].astype(jnp.float32) * value_ref[:, columns].astype(
            jnp.float32
        )
        here = pl.ds(pl.multiple_of(step_no * rows, rows), rows)
        outputs[step][here, :] = product.astype(jnp.bfloat16)

    @pl.when(step_no == 0)
    def _():
        for step in range(members):
            at = position ^ step
            taps = taps_ref[pl.ds(pl.multiple_of(at * groups, groups), groups), :]
            taps = (taps * scale).astype(jnp.bfloat16)
            for chunk in range(total_width // share):
                start = total_width + chunk * groups
                outputs[step][start : start + groups, :] = taps[
                    :, chunk * share : (chunk + 1) * share
                ]


def prepare(who, key_gate, value_input, filter_taps, passed, members, scale):
    width, channels = key_gate.shape
    share = channels // members
    rows = width + filter_taps.size // members // share
    tile = width // 4
    part = pl.BlockSpec((tile, channels), lambda i: (i, 0))
    return pl.pallas_call(
        functools.partial(prepare_kernel, members, scale),
        out_shape=[jax.ShapeDtypeStruct((rows, share), jnp.bfloat16)] * members
        + [jax.ShapeDtypeStruct(passed.shape, passed.dtype)],
        grid=(4,),
        in_specs=[SMEM, part, part, pl.BlockSpec(filter_taps.shape[::-1], lambda i: (0, 0)), part],
        out_specs=[VMEM] * (members + 1),
        compiler_params=pltpu.CompilerParams(vmem_limit_bytes=24 * 2**20),
        cost_estimate=COST,
        name="gated_input",
    )(who, in_hbm(key_gate), in_hbm(value_input), in_hbm(filter_taps.T), in_hbm(passed))


def finish_kernel(members, plan_ref, *refs):
    parts = refs[:members]
    key_ref, value_ref = refs[members : members + 2]
    key_out, value_out, taps_out = refs[-3:]
    position = plan_ref[POSITION]
    width, channels = key_ref.shape
    share = channels // members
    groups = taps_out.shape[0] // members
    for step in range(members):
        at = position ^ step
        columns = pl.ds(pl.multiple_of(at * share, share), share)
        grad = parts[step][:width].astype(jnp.float32)
        key_out[:, columns] = (grad * value_ref[:, columns].astype(jnp.float32)).astype(
            jnp.bfloat16
        )
        value_out[:, columns] = (grad * key_ref[:, columns].astype(jnp.float32)).astype(
            jnp.bfloat16
        )
        taps = [
            parts[step][width + chunk * groups : width + (chunk + 1) * groups, :]
            for chunk in range(width // share)
        ]
        taps_out[pl.ds(pl.multiple_of(at * groups, groups), groups), :] = jnp.concatenate(
            taps, axis=1
        ).astype(jnp.float32)


def finished(plan, parts, key_gate, value_input, groups, after=()):
    members = len(parts)
    width, channels = key_gate.shape
    array = jax.ShapeDtypeStruct((width, channels), jnp.bfloat16)
    grad_key, grad_value, taps = pl.pallas_call(
        functools.partial(finish_kernel, members),
        out_shape=[array, array, jax.ShapeDtypeStruct((groups, width), jnp.float32)],
        in_specs=[SMEM] + [VMEM] * (members + 2) + [ANYWHERE] * len(after),
        out_specs=[VMEM] * 3,
        compiler_params=pltpu.CompilerParams(vmem_limit_bytes=24 * 2**20),
        cost_estimate=COST,
        name="input_gradients",
    )(plan, *parts, key_gate, value_input, *after)
    return grad_key, grad_value, taps.T


def swapped(array, axis, step):
    size = lax.axis_size(axis)
    return lax.ppermute(array, axis, [(i, i ^ step) for i in range(size)])


def traded(pieces, axis):
    return [pieces[0]] + [swapped(pieces[step], axis, step) for step in range(1, len(pieces))]


def cut(array, position, members, axis):
    width = array.shape[axis] // members
    return [
        lax.dynamic_slice_in_dim(array, (position ^ step) * width, width, axis)
        for step in range(members)
    ]


def joined(pieces, position, axis):
    members = len(pieces)
    width = pieces[0].shape[axis]
    shape = list(pieces[0].shape)
    shape[axis] = members * width
    whole = jnp.zeros(shape, pieces[0].dtype)
    for step in range(members):
        whole = lax.dynamic_update_slice_in_dim(
            whole, pieces[step], (position ^ step) * width, axis
        )
    return whole


def wide(array):
    return array.astype(jnp.float32)


def hop(array, pairs):
    return lax.ppermute(
        array, "tp", [(2 * i + core, 2 * j + core) for i, j in pairs for core in range(2)]
    )


INWARD = ((0, 1), (3, 2))
ACROSS = ((1, 2), (2, 1))
OUTWARD = ((1, 0), (2, 3))
OWN, NEAR, MIDDLE, FAR = range(4)
IN_MIDDLE = POSITION + 1
CHIPS = ((0, 1, 2, 3), (1, 0, 3, 2), (2, 2, 1, 1), (3, 3, 0, 0))


def plan_kernel(who_ref, plan_ref):
    place = who_ref[1]
    chip, core = place // 2, place % 2
    for number, table in enumerate(CHIPS):
        source = jnp.where(
            chip < 2,
            jnp.where(chip == 0, table[0], table[1]),
            jnp.where(chip == 2, table[2], table[3]),
        )
        plan_ref[2 * number] = 2 * source + core
        plan_ref[2 * number + 1] = 2 * source + 1 - core
    plan_ref[POSITION] = who_ref[0]
    plan_ref[IN_MIDDLE] = ((chip == 1) | (chip == 2)).astype(jnp.int32)


def planned(who):
    return pl.pallas_call(
        plan_kernel,
        out_shape=jax.ShapeDtypeStruct((IN_MIDDLE + 1,), jnp.int32),
        in_specs=[SMEM],
        out_specs=SMEM,
        compiler_params=pltpu.CompilerParams(vmem_limit_bytes=2**20),
        cost_estimate=COST,
        name="plan",
    )(who)


def pass_kernel(*refs):
    del refs


def held_until(values, after):
    return pl.pallas_call(
        pass_kernel,
        out_shape=[jax.ShapeDtypeStruct(value.shape, value.dtype) for value in values],
        in_specs=[ANYWHERE] * (len(values) + len(after)),
        out_specs=[ANYWHERE] * len(values),
        input_output_aliases={number: number for number in range(len(values))},
        compiler_params=pltpu.CompilerParams(vmem_limit_bytes=2**20),
        cost_estimate=COST,
        name="held",
    )(*values, *after)


def add_kernel(*refs):
    refs[-1][...] = sum(wide(ref[...]) for ref in refs[:-1]).astype(jnp.bfloat16)


def added(*arrays):
    rows, width = arrays[0].shape
    part = pl.BlockSpec((rows // 4, width), lambda i: (i, 0))
    return pl.pallas_call(
        add_kernel,
        out_shape=jax.ShapeDtypeStruct((rows, width), jnp.bfloat16),
        grid=(4,),
        in_specs=[part] * len(arrays),
        out_specs=part,
        compiler_params=pltpu.CompilerParams(vmem_limit_bytes=8 * 2**20),
        cost_estimate=COST,
        name="added",
    )(*arrays)


def choice_kernel(plan_ref, middle_ref, end_ref, *refs):
    out_ref = refs[-1]
    in_middle = plan_ref[IN_MIDDLE] == 1

    @pl.when(in_middle)
    def _():
        out_ref[...] = middle_ref[...]

    @pl.when(jnp.logical_not(in_middle))
    def _():
        out_ref[...] = end_ref[...]


def chosen(plan, in_middle, at_end, after=()):
    return pl.pallas_call(
        choice_kernel,
        out_shape=jax.ShapeDtypeStruct(at_end.shape, at_end.dtype),
        in_specs=[SMEM, VMEM, VMEM] + [ANYWHERE] * len(after),
        out_specs=VMEM,
        compiler_params=pltpu.CompilerParams(vmem_limit_bytes=2**20),
        cost_estimate=COST,
        name="chosen",
    )(plan, in_middle, at_end, *after)


def gate_kernel(members, plan_ref, *refs):
    parts = refs[:members]
    query_ref, gated_ref, conv_ref = refs[members], *refs[-2:]
    position = plan_ref[POSITION]
    share = parts[0].shape[1]
    for step in range(members):
        columns = pl.ds(pl.multiple_of((position ^ step) * share, share), share)
        conv = parts[step][...]
        conv_ref[:, columns] = conv
        gated_ref[:, columns] = (wide(conv) * wide(query_ref[:, columns])).astype(jnp.bfloat16)


def gated(plan, parts, query_gate, after):
    array = jax.ShapeDtypeStruct(query_gate.shape, jnp.bfloat16)
    return pl.pallas_call(
        functools.partial(gate_kernel, len(parts)),
        out_shape=[array, array],
        in_specs=[SMEM] + [VMEM] * (len(parts) + 1) + [ANYWHERE] * len(after),
        out_specs=[VMEM] * 2,
        compiler_params=pltpu.CompilerParams(vmem_limit_bytes=8 * 2**20),
        cost_estimate=COST,
        name="gated_output",
    )(plan, *parts, query_gate, *after)


def spans(widths, start, stop):
    found, begin = [], 0
    for number, width in enumerate(widths):
        low, high = max(start, begin), min(stop, begin + width)
        if low < high:
            found.append((number, slice(low - begin, high - begin), slice(low - start, high - start)))
        begin += width
    return found


def product_kernel(steps, more_widths, out_widths, _, data_ref, weight_ref, *refs):
    more, outputs = refs[: len(more_widths)], refs[-len(out_widths) :]
    product = jnp.dot(data_ref[...], weight_ref[...], preferred_element_type=jnp.float32)
    width = product.shape[1]
    for step in range(steps):
        start, stop = step * width, (step + 1) * width

        @pl.when(pl.program_id(0) == step)
        def _(start=start, stop=stop):
            total = product
            if more:
                parts = [wide(more[n][:, there]) for n, there, _ in spans(more_widths, start, stop)]
                total = total + jnp.concatenate(parts, axis=1)
            total = total.astype(jnp.bfloat16)
            for n, there, here in spans(out_widths, start, stop):
                outputs[n][:, there] = total[:, here]


def column_products(
    plan, data, out_weight, first, count, other, more=(), after=(), tiles=1, widths=()
):
    rows, depth = data.shape
    width = data.shape[1]
    tile = width // tiles
    steps = count * tiles
    widths = tuple(widths) or (width,) * count

    def weights(i, at):
        return 0, at[2 * (first - i // tiles) + other] * tiles + i % tiles

    return pl.pallas_call(
        functools.partial(product_kernel, steps, [part.shape[1] for part in more], widths),
        out_shape=[jax.ShapeDtypeStruct((rows, part), jnp.bfloat16) for part in widths],
        grid_spec=pltpu.PrefetchScalarGridSpec(
            num_scalar_prefetch=1,
            grid=(steps,),
            in_specs=[VMEM, pl.BlockSpec((depth, tile), weights)]
            + [VMEM] * len(more)
            + [ANYWHERE] * len(after),
            out_specs=[VMEM] * len(widths),
        ),
        compiler_params=pltpu.CompilerParams(vmem_limit_bytes=16 * 2**20),
        cost_estimate=COST,
        name="projection_blocks",
    )(plan, data, in_hbm(out_weight), *more, *after)


def cotangent_kernel(count, begin, _, weight_ref, *refs):
    blocks, refs = refs[:count], refs[count:]
    step = pl.program_id(0)
    total = refs[-1]

    for number, block in enumerate(blocks):

        @pl.when(step == number)
        def _(number=number, block=block):
            product = lax.dot_general(
                block[...], weight_ref[...], NT, preferred_element_type=jnp.float32
            )
            if number == 0:
                total[...] = product if begin else refs[0][...] + product
            else:
                total[...] += product


def last_cotangent_kernel(
    members, plan_ref, weight_ref, block_ref, start_ref, conv_ref, query_ref, *refs
):
    parts, cot_scr = refs[-1 - members : -1], refs[-1]
    grad_ref = refs[-2 - members]
    product = lax.dot_general(
        block_ref[...], weight_ref[...], NT, preferred_element_type=jnp.float32
    )
    dgated = wide((start_ref[...] + product).astype(jnp.bfloat16))
    grad_ref[...] = (dgated * wide(conv_ref[...])).astype(jnp.bfloat16)
    cot_scr[...] = (dgated * wide(query_ref[...])).astype(jnp.bfloat16)
    share = parts[0].shape[1]
    odd = plan_ref[POSITION] % 2
    for step in range(0, members, 2):

        @pl.when(pl.program_id(0) == step // 2)
        def _(step=step):
            parts[step][...] = cot_scr[:, pl.ds(pl.multiple_of(odd * share, share), share)]
            parts[step + 1][...] = cot_scr[
                :, pl.ds(pl.multiple_of((1 - odd) * share, share), share)
            ]


def last_cotangents(
    plan, first, block, out_weight, start, convolved, query_gate, members, after
):
    rows, width = block.shape
    channels = out_weight.shape[0]
    share = channels // members
    pair = pl.BlockSpec((rows, 2 * share), lambda i, at: (0, at[POSITION] // 2 ^ i))
    return pl.pallas_call(
        functools.partial(last_cotangent_kernel, members),
        out_shape=[jax.ShapeDtypeStruct((rows, channels), jnp.bfloat16)]
        + [jax.ShapeDtypeStruct((rows, share), jnp.bfloat16)] * members,
        grid_spec=pltpu.PrefetchScalarGridSpec(
            num_scalar_prefetch=1,
            grid=(members // 2,),
            in_specs=[
                pl.BlockSpec((2 * share, width), lambda i, at: (at[POSITION] // 2 ^ i, at[first])),
                VMEM,
                pair,
                pair,
                pair,
            ]
            + [ANYWHERE] * len(after),
            out_specs=[pair] + [VMEM] * members,
            scratch_shapes=[pltpu.VMEM((rows, 2 * share), jnp.bfloat16)],
        ),
        compiler_params=pltpu.CompilerParams(vmem_limit_bytes=24 * 2**20),
        cost_estimate=COST,
        name="cotangent_last",
    )(plan, in_hbm(out_weight), block, start, convolved, query_gate, *after)


def both(blocks):
    return [part for block in blocks for part in (block, swapped(block, "tp", 1))]


def cotangent_products(plan, first, parts, out_weight, start=None, after=()):
    rows, width = parts[0].shape
    channels = out_weight.shape[0]
    count = len(parts)
    begin = start is None
    extra = () if begin else (start,)
    return pl.pallas_call(
        functools.partial(cotangent_kernel, count, begin),
        out_shape=jax.ShapeDtypeStruct((rows, channels), jnp.float32),
        grid_spec=pltpu.PrefetchScalarGridSpec(
            num_scalar_prefetch=1,
            grid=(count,),
            in_specs=[pl.BlockSpec((channels, width), lambda i, at: (0, at[first + i]))]
            + [VMEM] * (count + len(extra))
            + [ANYWHERE] * len(after),
            out_specs=VMEM,
        ),
        compiler_params=pltpu.CompilerParams(vmem_limit_bytes=16 * 2**20),
        cost_estimate=COST,
        name="cotangent_blocks",
    )(plan, in_hbm(out_weight), *parts, *extra, *after)


def packed_parts(position, key_gate, value_input, filter_taps, members, scale):
    length, channels = key_gate.shape
    share = channels // members
    product_in = (wide(key_gate) * wide(value_input)).astype(jnp.bfloat16)
    tap_rows = (filter_taps * scale).astype(jnp.bfloat16).T
    owned = filter_taps.shape[1] // members
    chunks = length // share
    packed = []
    pieces = cut(product_in, position, members, 1)
    for piece, taps in zip(pieces, cut(tap_rows, position, members, 0)):
        taps = taps.reshape(owned, chunks, share).transpose(1, 0, 2)
        taps = jnp.pad(taps, ((0, 0), (0, padded(owned) - owned), (0, 0)))
        packed.append(jnp.concatenate([piece, taps.reshape(-1, share)], axis=0))
    return packed


def unpacked_parts(position, parts, key_gate, value_input, groups):
    length, channels = key_gate.shape
    members = len(parts)
    share = channels // members
    owned = groups // members
    chunks = length // share
    input_grad = wide(joined([part[:length] for part in parts], position, 1))
    filter_parts = [
        part[length:]
        .reshape(chunks, padded(owned), share)[:, :owned]
        .transpose(1, 0, 2)
        .reshape(owned, length)
        for part in parts
    ]
    grad_filter = wide(joined(filter_parts, position, 0)).T
    grad_key = (input_grad * wide(value_input)).astype(jnp.bfloat16)
    grad_value = (input_grad * wide(key_gate)).astype(jnp.bfloat16)
    return grad_key, grad_value, grad_filter


def in_line(
    query_gate, key_gate, value_input, filter_taps, out_weight, out_grad, members, scale
):
    length, channels = query_gate.shape
    groups = filter_taps.shape[1]
    per_group = channels // groups
    who = jnp.stack([lax.axis_index("ctx"), lax.axis_index("tp")]).astype(jnp.int32)
    plan = planned(who)
    *packed, out_grad = prepare(
        who, key_gate, value_input, filter_taps, out_grad, members, scale
    )
    near, cross = hop(out_grad, INWARD + OUTWARD), hop(out_grad, ACROSS)
    total = cotangent_products(plan, 2 * OWN, both([out_grad]), out_weight)

    input_parts = traded(packed, "ctx")
    conv_parts, turned, taps = convolve(plan, input_parts, length, per_group, (total,))
    *conv_parts, near, cross = held_until([*conv_parts, near, cross], ())
    far, skip = hop(near, ACROSS), hop(cross, OUTWARD)
    lags = lag_matrices(taps)
    gated_out, convolved = gated(plan, traded(conv_parts, "ctx"), query_gate, (lags,))

    def product(first, count, other, more=(), after=(), tiles=1, widths=()):
        return column_products(
            plan, gated_out, out_weight, first, count, other, more, after, tiles, widths
        )

    half = channels // 2
    given_far = product(FAR, 1, 1, tiles=2, widths=(half, half))
    received = [swapped(part, "tp", 1) for part in given_far]
    (first,) = product(FAR, 1, 0, received, tiles=2)
    far, skip = held_until([far, skip], (first,))
    mixed = chosen(plan, far, first)
    arrived = hop(mixed, OUTWARD + INWARD)
    given_middle = product(MIDDLE, 1, 1, (), (mixed,), tiles=2, widths=(half, half))
    received = [swapped(part, "tp", 1) for part in given_middle]
    (second,) = product(MIDDLE, 1, 0, received, tiles=2)
    middle_block = added(cross, skip)
    blocks = [near, swapped(near, "tp", 1), middle_block]
    total = cotangent_products(plan, 2 * NEAR, blocks, out_weight, total, after=(second,))
    given_near, given_own = product(NEAR, 2, 1, (), (second,))
    (arrived,) = held_until([arrived], (total, given_near))
    through = added(first, arrived)
    two_a = hop(through, ACROSS)
    (second,) = held_until([second], (arrived,))
    two_b = hop(second, INWARD)

    far_block, far_other = both([chosen(plan, far, arrived, (through,))])
    blocks = [swapped(middle_block, "tp", 1), far_block]
    total = cotangent_products(
        plan, 2 * MIDDLE + 1, blocks, out_weight, total, after=(through,)
    )
    grad_query, *grad_parts = last_cotangents(
        plan, 2 * FAR + 1, far_other, out_weight, total, convolved, query_gate, members, ()
    )
    received = (swapped(given_near, "tp", 1), swapped(given_own, "tp", 1))
    third, own = product(NEAR, 2, 0, received, (grad_parts[0],))
    grad_parts = traded(grad_parts, "ctx")

    two_a, two_b = held_until([two_a, two_b], tuple(grad_parts[1:]))
    third, second = added(third, two_a), added(second, two_b)
    back_parts = correlate(plan, turned, lags, grad_parts, per_group, scale, (third, second))
    projected = added(own, hop(third, OUTWARD + INWARD), hop(second, ACROSS))
    back_parts = traded(back_parts, "ctx")
    return projected, grad_query, *finished(plan, back_parts, key_gate, value_input, groups, (in_hbm(projected),))


def anywhere(
    query_gate, key_gate, value_input, filter_taps, out_weight, out_grad, members, scale
):
    length, channels = query_gate.shape
    groups = filter_taps.shape[1]
    per_group = channels // groups
    position = lax.axis_index("ctx")
    plan = jnp.full((POSITION + 1,), position, jnp.int32)
    packed = packed_parts(position, key_gate, value_input, filter_taps, members, scale)
    input_parts = traded(packed, "ctx")
    conv_parts, turned, taps = convolve(plan, input_parts, length, per_group)
    conv_parts = traded(conv_parts, "ctx")
    convolved = joined(conv_parts, position, 1)
    gated_out = (wide(query_gate) * wide(convolved)).astype(jnp.bfloat16)
    partial_value = jnp.dot(gated_out, out_weight, preferred_element_type=jnp.float32)
    projected = lax.psum_scatter(
        partial_value.astype(jnp.bfloat16), "tp", scatter_dimension=1, tiled=True
    )
    dgated = jnp.einsum(
        "tk,ck->tc",
        lax.all_gather(out_grad, "tp", axis=1, tiled=True),
        out_weight,
        preferred_element_type=jnp.float32,
    ).astype(jnp.bfloat16)
    grad_query = (wide(dgated) * wide(convolved)).astype(jnp.bfloat16)
    conv_grad = (wide(dgated) * wide(query_gate)).astype(jnp.bfloat16)
    grad_parts = traded(cut(conv_grad, position, members, 1), "ctx")
    back_parts = correlate(plan, turned, lag_matrices(taps), grad_parts, per_group, scale)
    back_parts = traded(back_parts, "ctx")
    return (
        projected,
        grad_query,
        *unpacked_parts(position, back_parts, key_gate, value_input, groups),
    )


def local(query_gate, key_gate, value_input, filter_taps, out_weight, out_grad):
    length, channels = query_gate.shape
    groups = filter_taps.shape[1]
    members = lax.axis_size("ctx")
    scale = 1.0 / math.sqrt(length * members)
    fits = channels // members % 128 == 0 and groups // members % 16 == 0
    body = in_line if lax.axis_size("tp") == 8 and fits else anywhere
    return body(
        query_gate, key_gate, value_input, filter_taps, out_weight, out_grad, members, scale
    )


def solution(mesh):
    both = P("ctx", "tp")
    return jax.shard_map(
        local,
        mesh=mesh,
        in_specs=(both, both, both, both, P("tp", None), both),
        out_specs=(both,) * 5,
        check_vma=False,
    )
```

```python
import functools
import math
import jax
import jax.numpy as jnp
from jax import lax
from jax.experimental import pallas as pl
from jax.experimental.pallas import tpu as pltpu
from jax.sharding import PartitionSpec as P

BLOCK = 128
POSITION = 8
NT = (((1,), (1,)), ((), ()))
COST = pl.CostEstimate(flops=2**20, bytes_accessed=2**12, transcendentals=0)


def lag_matrix(row, length):
    lanes = lax.broadcasted_iota(jnp.int32, (BLOCK, BLOCK), 1)
    rows = lax.broadcasted_iota(jnp.int32, (BLOCK, BLOCK), 0)
    spread = pltpu.roll(
        jnp.broadcast_to(row, (BLOCK, length)), 0, axis=1, stride=1, stride_axis=0
    )
    first = jnp.where(lanes >= rows, spread[:, :BLOCK], 0.0)
    return jnp.concatenate(
        [first.astype(jnp.bfloat16), spread[:, BLOCK:].astype(jnp.bfloat16)], axis=1
    )


def stacked(ref, start, rows, members, width):
    pieces = []
    for member in range(members):
        part = ref[member, pl.ds(start, rows), :]
        for at in range(0, width, BLOCK):
            pieces.append(part[:, at : at + BLOCK])
    return jnp.concatenate(pieces, axis=0)


def spread_out(ref, start, rows, value, members, width):
    per_member = width // BLOCK
    for member in range(members):
        base = member * per_member * rows
        parts = [value[base + i * rows : base + (i + 1) * rows] for i in range(per_member)]
        ref[member, pl.ds(start, rows), :] = jnp.concatenate(parts, axis=1)


def padded(groups):
    return -(-groups // 16) * 16


def load_taps(tap_scr, packed, at, width):
    groups, channels = tap_scr.shape[0], packed.shape[1]
    rows = padded(groups)
    parts = [
        packed[width + chunk * rows : width + (chunk + 1) * rows, :].astype(jnp.float32)
        for chunk in range(width // channels)
    ]
    start = pl.multiple_of(at * width, width)
    tap_scr[:, pl.ds(start, width)] = jnp.concatenate(parts, axis=1)[:groups]


def forward_kernel(members, per_group, width, plan_ref, *refs):
    inputs, outputs = refs[:members], refs[-members - 3 : -3]
    in_scr, tap_scr, out_scr = refs[-3:]
    position = plan_ref[POSITION]
    channels = inputs[0].shape[1]
    groups = channels // per_group
    length = members * width
    blocks = length // BLOCK
    for step in range(members):
        at = position ^ step
        in_scr[at] = inputs[step][:width].T
        load_taps(tap_scr, inputs[step], at, width)

    def one_group(group, carry):
        start = pl.multiple_of(group * per_group, per_group)
        lags = lag_matrix(tap_scr[pl.ds(group, 1), :], length)
        data = stacked(in_scr, start, per_group, members, width)
        total = [jnp.zeros((per_group, BLOCK), jnp.float32) for _ in range(blocks)]
        for offset in range(0, blocks, 2):
            rows = (blocks - offset) * per_group
            result = jnp.dot(
                data[:rows],
                lags[:, offset * BLOCK : (offset + 2) * BLOCK],
                preferred_element_type=jnp.float32,
            )
            for side in range(2):
                for source in range(blocks - offset - side):
                    total[source + offset + side] += result[
                        source * per_group : (source + 1) * per_group,
                        side * BLOCK : (side + 1) * BLOCK,
                    ]
        value = jnp.concatenate(total, axis=0).astype(jnp.bfloat16)
        spread_out(out_scr, start, per_group, value, members, width)
        return carry

    lax.fori_loop(0, groups, one_group, 0, unroll=4)
    for step in range(members):
        outputs[step][...] = out_scr[position ^ step].T


def backward_kernel(members, batch, per_group, scale, width, plan_ref, in_scr, lag_ref, *refs):
    cotangents = refs[:members]
    outputs = refs[-members - 4 : -4]
    cot_scr, out_scr, grad_scr, pad_scr = refs[-4:]
    position = plan_ref[POSITION]
    channels = cotangents[0].shape[1]
    groups = channels // per_group
    length = members * width
    blocks = length // BLOCK
    depth = blocks * per_group
    rows_of = lax.broadcasted_iota(jnp.int32, (BLOCK, BLOCK), 0)
    lanes_of = lax.broadcasted_iota(jnp.int32, (BLOCK, BLOCK), 1)
    mirror = (rows_of + lanes_of == BLOCK - 1).astype(jnp.bfloat16)

    @pl.when(pl.program_id(0) == 0)
    def _():
        for step in range(members):
            cot_scr[position ^ step] = cotangents[step][...].T
        pad_scr[...] = jnp.zeros_like(pad_scr)

    for local_group in range(batch):
        group = pl.program_id(0) * batch + local_group
        start = pl.multiple_of(group * per_group, per_group)
        lags = lag_ref[local_group]
        padded_cot = pad_scr.at[local_group]
        data = stacked(in_scr, start, per_group, members, width)
        cot = stacked(cot_scr, start, per_group, members, width)
        padded_cot[:depth, :BLOCK] = cot
        padded_cot[: depth - per_group, BLOCK:] = cot[per_group:]
        flipped = lax.dot_general(
            mirror, data, NT, preferred_element_type=jnp.float32
        ).astype(jnp.bfloat16)
        total = jnp.zeros((depth, BLOCK), jnp.float32)
        products = []
        for offset in range(0, blocks, 2):
            rows = depth - offset * per_group
            pair = padded_cot[offset * per_group : offset * per_group + depth, :]
            result = lax.dot_general(
                pair[:rows],
                lags[:, offset * BLOCK : (offset + 2) * BLOCK],
                NT,
                preferred_element_type=jnp.float32,
            )
            if rows < depth:
                result = jnp.concatenate(
                    [result, jnp.zeros((depth - rows, BLOCK), jnp.float32)], axis=0
                )
            total = total + result
            products.append(jnp.dot(flipped, pair, preferred_element_type=jnp.float32))
        spread_out(out_scr, start, per_group, total.astype(jnp.bfloat16), members, width)
        kept = jnp.where(rows_of + lanes_of >= BLOCK - 1, products[0][:, :BLOCK], 0.0)
        product = jnp.concatenate([kept, products[0][:, BLOCK:], *products[1:]], axis=1)
        product = pltpu.roll(
            product, length - (BLOCK - 1), axis=1, stride=1, stride_axis=0
        )
        grad_scr[pl.ds(group, 1), :] = jnp.sum(product, axis=0, keepdims=True) * scale

    @pl.when(pl.program_id(0) == pl.num_programs(0) - 1)
    def _():
        for step in range(members):
            at = position ^ step
            outputs[step][:width] = out_scr[at].T
            rows = padded(groups)
            whole = grad_scr[:, pl.ds(pl.multiple_of(at * width, width), width)]
            whole = whole.astype(jnp.bfloat16)
            if rows > groups:
                blank = jnp.zeros((rows - groups, width), jnp.bfloat16)
                whole = jnp.concatenate([whole, blank], axis=0)
            for chunk in range(width // channels):
                outputs[step][width + chunk * rows : width + (chunk + 1) * rows, :] = whole[
                    :, chunk * channels : (chunk + 1) * channels
                ]


def lag_kernel(taps_ref, out_ref):
    row = taps_ref[pl.ds(pl.program_id(0), 1), :]
    out_ref[0] = lag_matrix(row, taps_ref.shape[1])


VMEM = pl.BlockSpec(memory_space=pltpu.VMEM)
ANYWHERE = pl.BlockSpec(memory_space=pl.ANY)
SMEM = pl.BlockSpec(memory_space=pltpu.SMEM)


def convolve(plan, inputs, width, per_group, after=()):
    members = len(inputs)
    channels = inputs[0].shape[1]
    length = members * width
    *parts, turned, taps = pl.pallas_call(
        functools.partial(forward_kernel, members, per_group, width),
        out_shape=[jax.ShapeDtypeStruct((width, channels), jnp.bfloat16)] * members
        + [
            jax.ShapeDtypeStruct((members, channels, width), jnp.bfloat16),
            jax.ShapeDtypeStruct((channels // per_group, length), jnp.float32),
        ],
        in_specs=[SMEM] + [VMEM] * members + [ANYWHERE] * len(after),
        out_specs=[VMEM] * (members + 2),
        scratch_shapes=[pltpu.VMEM((members, channels, width), jnp.bfloat16)],
        compiler_params=pltpu.CompilerParams(vmem_limit_bytes=24 * 2**20),
        cost_estimate=COST,
        name="causal_conv",
    )(plan, *inputs, *after)
    return parts, turned, taps


def lag_matrices(taps):
    groups, length = taps.shape
    return pl.pallas_call(
        lag_kernel,
        out_shape=jax.ShapeDtypeStruct((groups, BLOCK, length), jnp.bfloat16),
        grid=(groups,),
        in_specs=[VMEM],
        out_specs=pl.BlockSpec((1, BLOCK, length), lambda i: (i, 0, 0)),
        compiler_params=pltpu.CompilerParams(vmem_limit_bytes=12 * 2**20),
        cost_estimate=COST,
        name="lag_matrices",
    )(taps)


def correlate(plan, turned, lags, cotangents, per_group, scale, after=()):
    members = len(cotangents)
    width, channels = cotangents[0].shape
    length = members * width
    groups = channels // per_group
    batch = 4 if groups % 4 == 0 else 1
    rows = width + padded(groups) * width // channels
    return pl.pallas_call(
        functools.partial(backward_kernel, members, batch, per_group, scale, width),
        out_shape=[jax.ShapeDtypeStruct((rows, channels), jnp.bfloat16)] * members,
        grid=(groups // batch,),
        in_specs=[SMEM, VMEM, pl.BlockSpec((batch, BLOCK, length), lambda i: (i, 0, 0))]
        + [VMEM] * members
        + [ANYWHERE] * len(after),
        out_specs=[VMEM] * members,
        scratch_shapes=[
            pltpu.VMEM((members, channels, width), jnp.bfloat16),
            pltpu.VMEM((members, channels, width), jnp.bfloat16),
            pltpu.VMEM((groups, length), jnp.float32),
            pltpu.VMEM((batch, 2 * length // BLOCK * per_group, 2 * BLOCK), jnp.bfloat16),
        ],
        compiler_params=pltpu.CompilerParams(vmem_limit_bytes=24 * 2**20),
        cost_estimate=COST,
        name="causal_conv_grads",
    )(plan, turned, lags, *cotangents, *after)


def in_hbm(array):
    return pltpu.with_memory_space_constraint(array, pltpu.HBM)


def prepare_kernel(members, scale, who_ref, key_ref, value_ref, taps_ref, *outputs):
    position = who_ref[0]
    step_no = pl.program_id(0)
    rows, channels = key_ref.shape
    share = channels // members
    groups = taps_ref.shape[0] // members
    total_width = taps_ref.shape[1]
    for step in range(members):
        at = position ^ step
        columns = pl.ds(pl.multiple_of(at * share, share), share)
        product = key_ref[:, columns].astype(jnp.float32) * value_ref[:, columns].astype(
            jnp.float32
        )
        here = pl.ds(pl.multiple_of(step_no * rows, rows), rows)
        outputs[step][here, :] = product.astype(jnp.bfloat16)

    @pl.when(step_no == 0)
    def _():
        for step in range(members):
            at = position ^ step
            taps = taps_ref[pl.ds(pl.multiple_of(at * groups, groups), groups), :]
            taps = (taps * scale).astype(jnp.bfloat16)
            for chunk in range(total_width // share):
                start = total_width + chunk * groups
                outputs[step][start : start + groups, :] = taps[
                    :, chunk * share : (chunk + 1) * share
                ]


def prepare(who, key_gate, value_input, filter_taps, members, scale):
    width, channels = key_gate.shape
    share = channels // members
    rows = width + filter_taps.size // members // share
    tile = width // 4
    part = pl.BlockSpec((tile, channels), lambda i: (i, 0))
    return pl.pallas_call(
        functools.partial(prepare_kernel, members, scale),
        out_shape=[jax.ShapeDtypeStruct((rows, share), jnp.bfloat16)] * members,
        grid=(4,),
        in_specs=[SMEM, part, part, pl.BlockSpec(filter_taps.shape[::-1], lambda i: (0, 0))],
        out_specs=[VMEM] * members,
        compiler_params=pltpu.CompilerParams(vmem_limit_bytes=24 * 2**20),
        cost_estimate=COST,
        name="gated_input",
    )(who, in_hbm(key_gate), in_hbm(value_input), in_hbm(filter_taps.T))


def finish_kernel(members, plan_ref, *refs):
    parts = refs[:members]
    key_ref, value_ref = refs[members : members + 2]
    key_out, value_out, taps_out = refs[-3:]
    position = plan_ref[POSITION]
    width, channels = key_ref.shape
    share = channels // members
    groups = taps_out.shape[0] // members
    for step in range(members):
        at = position ^ step
        columns = pl.ds(pl.multiple_of(at * share, share), share)
        grad = parts[step][:width].astype(jnp.float32)
        key_out[:, columns] = (grad * value_ref[:, columns].astype(jnp.float32)).astype(
            jnp.bfloat16
        )
        value_out[:, columns] = (grad * key_ref[:, columns].astype(jnp.float32)).astype(
            jnp.bfloat16
        )
        taps = [
            parts[step][width + chunk * groups : width + (chunk + 1) * groups, :]
            for chunk in range(width // share)
        ]
        taps_out[pl.ds(pl.multiple_of(at * groups, groups), groups), :] = jnp.concatenate(
            taps, axis=1
        ).astype(jnp.float32)


def finished(plan, parts, key_gate, value_input, groups, after=()):
    members = len(parts)
    width, channels = key_gate.shape
    array = jax.ShapeDtypeStruct((width, channels), jnp.bfloat16)
    grad_key, grad_value, taps = pl.pallas_call(
        functools.partial(finish_kernel, members),
        out_shape=[array, array, jax.ShapeDtypeStruct((groups, width), jnp.float32)],
        in_specs=[SMEM] + [VMEM] * (members + 2) + [ANYWHERE] * len(after),
        out_specs=[VMEM] * 3,
        compiler_params=pltpu.CompilerParams(vmem_limit_bytes=24 * 2**20),
        cost_estimate=COST,
        name="input_gradients",
    )(plan, *parts, key_gate, value_input, *after)
    return grad_key, grad_value, taps.T


def swapped(array, axis, step):
    size = lax.axis_size(axis)
    return lax.ppermute(array, axis, [(i, i ^ step) for i in range(size)])


def traded(pieces, axis):
    return [pieces[0]] + [swapped(pieces[step], axis, step) for step in range(1, len(pieces))]


def cut(array, position, members, axis):
    width = array.shape[axis] // members
    return [
        lax.dynamic_slice_in_dim(array, (position ^ step) * width, width, axis)
        for step in range(members)
    ]


def joined(pieces, position, axis):
    members = len(pieces)
    width = pieces[0].shape[axis]
    shape = list(pieces[0].shape)
    shape[axis] = members * width
    whole = jnp.zeros(shape, pieces[0].dtype)
    for step in range(members):
        whole = lax.dynamic_update_slice_in_dim(
            whole, pieces[step], (position ^ step) * width, axis
        )
    return whole


def wide(array):
    return array.astype(jnp.float32)


def hop(array, pairs):
    return lax.ppermute(
        array, "tp", [(2 * i + core, 2 * j + core) for i, j in pairs for core in range(2)]
    )


INWARD = ((0, 1), (3, 2))
ACROSS = ((1, 2), (2, 1))
OUTWARD = ((1, 0), (2, 3))
OWN, NEAR, MIDDLE, FAR = range(4)
IN_MIDDLE = POSITION + 1
CHIPS = ((0, 1, 2, 3), (1, 0, 3, 2), (2, 2, 1, 1), (3, 3, 0, 0))


def plan_kernel(who_ref, plan_ref):
    place = who_ref[1]
    chip, core = place // 2, place % 2
    for number, table in enumerate(CHIPS):
        source = jnp.where(
            chip < 2,
            jnp.where(chip == 0, table[0], table[1]),
            jnp.where(chip == 2, table[2], table[3]),
        )
        plan_ref[2 * number] = 2 * source + core
        plan_ref[2 * number + 1] = 2 * source + 1 - core
    plan_ref[POSITION] = who_ref[0]
    plan_ref[IN_MIDDLE] = ((chip == 1) | (chip == 2)).astype(jnp.int32)


def planned(who):
    return pl.pallas_call(
        plan_kernel,
        out_shape=jax.ShapeDtypeStruct((IN_MIDDLE + 1,), jnp.int32),
        in_specs=[SMEM],
        out_specs=SMEM,
        compiler_params=pltpu.CompilerParams(vmem_limit_bytes=2**20),
        cost_estimate=COST,
        name="plan",
    )(who)


def pass_kernel(*refs):
    del refs


def held_until(values, after):
    return pl.pallas_call(
        pass_kernel,
        out_shape=[jax.ShapeDtypeStruct(value.shape, value.dtype) for value in values],
        in_specs=[ANYWHERE] * (len(values) + len(after)),
        out_specs=[ANYWHERE] * len(values),
        input_output_aliases={number: number for number in range(len(values))},
        compiler_params=pltpu.CompilerParams(vmem_limit_bytes=2**20),
        cost_estimate=COST,
        name="held",
    )(*values, *after)


def add_kernel(*refs):
    refs[-1][...] = sum(wide(ref[...]) for ref in refs[:-1]).astype(jnp.bfloat16)


def added(*arrays):
    rows, width = arrays[0].shape
    part = pl.BlockSpec((rows // 4, width), lambda i: (i, 0))
    return pl.pallas_call(
        add_kernel,
        out_shape=jax.ShapeDtypeStruct((rows, width), jnp.bfloat16),
        grid=(4,),
        in_specs=[part] * len(arrays),
        out_specs=part,
        compiler_params=pltpu.CompilerParams(vmem_limit_bytes=8 * 2**20),
        cost_estimate=COST,
        name="added",
    )(*arrays)


def choice_kernel(plan_ref, middle_ref, end_ref, *refs):
    out_ref = refs[-1]
    in_middle = plan_ref[IN_MIDDLE] == 1

    @pl.when(in_middle)
    def _():
        out_ref[...] = middle_ref[...]

    @pl.when(jnp.logical_not(in_middle))
    def _():
        out_ref[...] = end_ref[...]


def chosen(plan, in_middle, at_end, after=()):
    return pl.pallas_call(
        choice_kernel,
        out_shape=jax.ShapeDtypeStruct(at_end.shape, at_end.dtype),
        in_specs=[SMEM, VMEM, VMEM] + [ANYWHERE] * len(after),
        out_specs=VMEM,
        compiler_params=pltpu.CompilerParams(vmem_limit_bytes=2**20),
        cost_estimate=COST,
        name="chosen",
    )(plan, in_middle, at_end, *after)


def gate_kernel(members, plan_ref, *refs):
    parts = refs[:members]
    query_ref, gated_ref, conv_ref = refs[members], *refs[-2:]
    position = plan_ref[POSITION]
    share = parts[0].shape[1]
    for step in range(members):
        columns = pl.ds(pl.multiple_of((position ^ step) * share, share), share)
        conv = parts[step][...]
        conv_ref[:, columns] = conv
        gated_ref[:, columns] = (wide(conv) * wide(query_ref[:, columns])).astype(jnp.bfloat16)


def gated(plan, parts, query_gate, after):
    array = jax.ShapeDtypeStruct(query_gate.shape, jnp.bfloat16)
    return pl.pallas_call(
        functools.partial(gate_kernel, len(parts)),
        out_shape=[array, array],
        in_specs=[SMEM] + [VMEM] * (len(parts) + 1) + [ANYWHERE] * len(after),
        out_specs=[VMEM] * 2,
        compiler_params=pltpu.CompilerParams(vmem_limit_bytes=8 * 2**20),
        cost_estimate=COST,
        name="gated_output",
    )(plan, *parts, query_gate, *after)


def spans(widths, start, stop):
    found, begin = [], 0
    for number, width in enumerate(widths):
        low, high = max(start, begin), min(stop, begin + width)
        if low < high:
            found.append((number, slice(low - begin, high - begin), slice(low - start, high - start)))
        begin += width
    return found


def product_kernel(steps, more_widths, out_widths, _, data_ref, weight_ref, *refs):
    more, outputs = refs[: len(more_widths)], refs[-len(out_widths) :]
    product = jnp.dot(data_ref[...], weight_ref[...], preferred_element_type=jnp.float32)
    width = product.shape[1]
    for step in range(steps):
        start, stop = step * width, (step + 1) * width

        @pl.when(pl.program_id(0) == step)
        def _(start=start, stop=stop):
            total = product
            if more:
                parts = [wide(more[n][:, there]) for n, there, _ in spans(more_widths, start, stop)]
                total = total + jnp.concatenate(parts, axis=1)
            total = total.astype(jnp.bfloat16)
            for n, there, here in spans(out_widths, start, stop):
                outputs[n][:, there] = total[:, here]


def column_products(
    plan, data, out_weight, first, count, other, more=(), after=(), tiles=1, widths=()
):
    rows, depth = data.shape
    width = data.shape[1]
    tile = width // tiles
    steps = count * tiles
    widths = tuple(widths) or (width,) * count

    def weights(i, at):
        return 0, at[2 * (first - i // tiles) + other] * tiles + i % tiles

    return pl.pallas_call(
        functools.partial(product_kernel, steps, [part.shape[1] for part in more], widths),
        out_shape=[jax.ShapeDtypeStruct((rows, part), jnp.bfloat16) for part in widths],
        grid_spec=pltpu.PrefetchScalarGridSpec(
            num_scalar_prefetch=1,
            grid=(steps,),
            in_specs=[VMEM, pl.BlockSpec((depth, tile), weights)]
            + [VMEM] * len(more)
            + [ANYWHERE] * len(after),
            out_specs=[VMEM] * len(widths),
        ),
        compiler_params=pltpu.CompilerParams(vmem_limit_bytes=16 * 2**20),
        cost_estimate=COST,
        name="projection_blocks",
    )(plan, data, in_hbm(out_weight), *more, *after)


def cotangent_kernel(count, begin, _, weight_ref, *refs):
    blocks, refs = refs[:count], refs[count:]
    step = pl.program_id(0)
    total = refs[-1]

    for number, block in enumerate(blocks):

        @pl.when(step == number)
        def _(number=number, block=block):
            product = lax.dot_general(
                block[...], weight_ref[...], NT, preferred_element_type=jnp.float32
            )
            if number == 0:
                total[...] = product if begin else refs[0][...] + product
            else:
                total[...] += product


def last_cotangent_kernel(
    members, plan_ref, weight_ref, block_ref, start_ref, conv_ref, query_ref, *refs
):
    parts, cot_scr = refs[-1 - members : -1], refs[-1]
    grad_ref = refs[-2 - members]
    product = lax.dot_general(
        block_ref[...], weight_ref[...], NT, preferred_element_type=jnp.float32
    )
    dgated = wide((start_ref[...] + product).astype(jnp.bfloat16))
    grad_ref[...] = (dgated * wide(conv_ref[...])).astype(jnp.bfloat16)
    cot_scr[...] = (dgated * wide(query_ref[...])).astype(jnp.bfloat16)
    share = parts[0].shape[1]
    odd = plan_ref[POSITION] % 2
    for step in range(0, members, 2):

        @pl.when(pl.program_id(0) == step // 2)
        def _(step=step):
            parts[step][...] = cot_scr[:, pl.ds(pl.multiple_of(odd * share, share), share)]
            parts[step + 1][...] = cot_scr[
                :, pl.ds(pl.multiple_of((1 - odd) * share, share), share)
            ]


def last_cotangents(
    plan, first, block, out_weight, start, convolved, query_gate, members, after
):
    rows, width = block.shape
    channels = out_weight.shape[0]
    share = channels // members
    pair = pl.BlockSpec((rows, 2 * share), lambda i, at: (0, at[POSITION] // 2 ^ i))
    return pl.pallas_call(
        functools.partial(last_cotangent_kernel, members),
        out_shape=[jax.ShapeDtypeStruct((rows, channels), jnp.bfloat16)]
        + [jax.ShapeDtypeStruct((rows, share), jnp.bfloat16)] * members,
        grid_spec=pltpu.PrefetchScalarGridSpec(
            num_scalar_prefetch=1,
            grid=(members // 2,),
            in_specs=[
                pl.BlockSpec((2 * share, width), lambda i, at: (at[POSITION] // 2 ^ i, at[first])),
                VMEM,
                pair,
                pair,
                pair,
            ]
            + [ANYWHERE] * len(after),
            out_specs=[pair] + [VMEM] * members,
            scratch_shapes=[pltpu.VMEM((rows, 2 * share), jnp.bfloat16)],
        ),
        compiler_params=pltpu.CompilerParams(vmem_limit_bytes=24 * 2**20),
        cost_estimate=COST,
        name="cotangent_last",
    )(plan, in_hbm(out_weight), block, start, convolved, query_gate, *after)


def both(blocks):
    return [part for block in blocks for part in (block, swapped(block, "tp", 1))]


def cotangent_products(plan, first, parts, out_weight, start=None, after=()):
    rows, width = parts[0].shape
    channels = out_weight.shape[0]
    count = len(parts)
    begin = start is None
    extra = () if begin else (start,)
    return pl.pallas_call(
        functools.partial(cotangent_kernel, count, begin),
        out_shape=jax.ShapeDtypeStruct((rows, channels), jnp.float32),
        grid_spec=pltpu.PrefetchScalarGridSpec(
            num_scalar_prefetch=1,
            grid=(count,),
            in_specs=[pl.BlockSpec((channels, width), lambda i, at: (0, at[first + i]))]
            + [VMEM] * (count + len(extra))
            + [ANYWHERE] * len(after),
            out_specs=VMEM,
        ),
        compiler_params=pltpu.CompilerParams(vmem_limit_bytes=16 * 2**20),
        cost_estimate=COST,
        name="cotangent_blocks",
    )(plan, in_hbm(out_weight), *parts, *extra, *after)


def packed_parts(position, key_gate, value_input, filter_taps, members, scale):
    length, channels = key_gate.shape
    share = channels // members
    product_in = (wide(key_gate) * wide(value_input)).astype(jnp.bfloat16)
    tap_rows = (filter_taps * scale).astype(jnp.bfloat16).T
    owned = filter_taps.shape[1] // members
    chunks = length // share
    packed = []
    pieces = cut(product_in, position, members, 1)
    for piece, taps in zip(pieces, cut(tap_rows, position, members, 0)):
        taps = taps.reshape(owned, chunks, share).transpose(1, 0, 2)
        taps = jnp.pad(taps, ((0, 0), (0, padded(owned) - owned), (0, 0)))
        packed.append(jnp.concatenate([piece, taps.reshape(-1, share)], axis=0))
    return packed


def unpacked_parts(position, parts, key_gate, value_input, groups):
    length, channels = key_gate.shape
    members = len(parts)
    share = channels // members
    owned = groups // members
    chunks = length // share
    input_grad = wide(joined([part[:length] for part in parts], position, 1))
    filter_parts = [
        part[length:]
        .reshape(chunks, padded(owned), share)[:, :owned]
        .transpose(1, 0, 2)
        .reshape(owned, length)
        for part in parts
    ]
    grad_filter = wide(joined(filter_parts, position, 0)).T
    grad_key = (input_grad * wide(value_input)).astype(jnp.bfloat16)
    grad_value = (input_grad * wide(key_gate)).astype(jnp.bfloat16)
    return grad_key, grad_value, grad_filter


def in_line(
    query_gate, key_gate, value_input, filter_taps, out_weight, out_grad, members, scale
):
    length, channels = query_gate.shape
    groups = filter_taps.shape[1]
    per_group = channels // groups
    who = jnp.stack([lax.axis_index("ctx"), lax.axis_index("tp")]).astype(jnp.int32)
    plan = planned(who)
    near, cross = hop(out_grad, INWARD + OUTWARD), hop(out_grad, ACROSS)
    total = cotangent_products(plan, 2 * OWN, both([out_grad]), out_weight)

    packed = prepare(who, key_gate, value_input, filter_taps, members, scale)
    input_parts = traded(packed, "ctx")
    conv_parts, turned, taps = convolve(plan, input_parts, length, per_group, (total,))
    *conv_parts, near = held_until([*conv_parts, near], ())
    (cross,) = held_until([cross], (near,))
    far, skip = hop(near, ACROSS), hop(cross, OUTWARD)
    lags = lag_matrices(taps)
    gated_out, convolved = gated(plan, traded(conv_parts, "ctx"), query_gate, (lags,))

    def product(first, count, other, more=(), after=(), tiles=1, widths=()):
        return column_products(
            plan, gated_out, out_weight, first, count, other, more, after, tiles, widths
        )

    half = channels // 2
    given_far = product(FAR, 1, 1, tiles=2, widths=(half, half))
    received = [swapped(part, "tp", 1) for part in given_far]
    (first,) = product(FAR, 1, 0, received, tiles=2)
    far, skip = held_until([far, skip], (first,))
    mixed = chosen(plan, far, first)
    arrived = hop(mixed, OUTWARD + INWARD)
    given_middle = product(MIDDLE, 1, 1, (), (mixed,), tiles=2, widths=(half, half))
    received = [swapped(part, "tp", 1) for part in given_middle]
    (second,) = product(MIDDLE, 1, 0, received, tiles=2)
    middle_block = added(cross, skip)
    blocks = [near, swapped(near, "tp", 1), middle_block]
    total = cotangent_products(plan, 2 * NEAR, blocks, out_weight, total, after=(second,))
    given_near, given_own = product(NEAR, 2, 1, (), (second,))
    (arrived,) = held_until([arrived], (total, given_near))
    through = added(first, arrived)
    two_a = hop(through, ACROSS)
    (second,) = held_until([second], (arrived,))
    two_b = hop(second, INWARD)

    far_block, far_other = both([chosen(plan, far, arrived, (through,))])
    blocks = [swapped(middle_block, "tp", 1), far_block]
    total = cotangent_products(
        plan, 2 * MIDDLE + 1, blocks, out_weight, total, after=(through,)
    )
    grad_query, *grad_parts = last_cotangents(
        plan, 2 * FAR + 1, far_other, out_weight, total, convolved, query_gate, members, ()
    )
    received = (swapped(given_near, "tp", 1), swapped(given_own, "tp", 1))
    third, own = product(NEAR, 2, 0, received, (grad_parts[0],))
    grad_parts = traded(grad_parts, "ctx")

    two_a, two_b = held_until([two_a, two_b], tuple(grad_parts[1:]))
    third, second = added(third, two_a), added(second, two_b)
    back_parts = correlate(plan, turned, lags, grad_parts, per_group, scale, (third, second))
    projected = added(own, hop(third, OUTWARD + INWARD), hop(second, ACROSS))
    back_parts = traded(back_parts, "ctx")
    return projected, grad_query, *finished(plan, back_parts, key_gate, value_input, groups, (in_hbm(projected),))


def anywhere(
    query_gate, key_gate, value_input, filter_taps, out_weight, out_grad, members, scale
):
    length, channels = query_gate.shape
    groups = filter_taps.shape[1]
    per_group = channels // groups
    position = lax.axis_index("ctx")
    plan = jnp.full((POSITION + 1,), position, jnp.int32)
    packed = packed_parts(position, key_gate, value_input, filter_taps, members, scale)
    input_parts = traded(packed, "ctx")
    conv_parts, turned, taps = convolve(plan, input_parts, length, per_group)
    conv_parts = traded(conv_parts, "ctx")
    convolved = joined(conv_parts, position, 1)
    gated_out = (wide(query_gate) * wide(convolved)).astype(jnp.bfloat16)
    partial_value = jnp.dot(gated_out, out_weight, preferred_element_type=jnp.float32)
    projected = lax.psum_scatter(
        partial_value.astype(jnp.bfloat16), "tp", scatter_dimension=1, tiled=True
    )
    dgated = jnp.einsum(
        "tk,ck->tc",
        lax.all_gather(out_grad, "tp", axis=1, tiled=True),
        out_weight,
        preferred_element_type=jnp.float32,
    ).astype(jnp.bfloat16)
    grad_query = (wide(dgated) * wide(convolved)).astype(jnp.bfloat16)
    conv_grad = (wide(dgated) * wide(query_gate)).astype(jnp.bfloat16)
    grad_parts = traded(cut(conv_grad, position, members, 1), "ctx")
    back_parts = correlate(plan, turned, lag_matrices(taps), grad_parts, per_group, scale)
    back_parts = traded(back_parts, "ctx")
    return (
        projected,
        grad_query,
        *unpacked_parts(position, back_parts, key_gate, value_input, groups),
    )


def local(query_gate, key_gate, value_input, filter_taps, out_weight, out_grad):
    length, channels = query_gate.shape
    groups = filter_taps.shape[1]
    members = lax.axis_size("ctx")
    scale = 1.0 / math.sqrt(length * members)
    fits = channels // members % 128 == 0 and groups // members % 16 == 0
    body = in_line if lax.axis_size("tp") == 8 and fits else anywhere
    return body(
        query_gate, key_gate, value_input, filter_taps, out_weight, out_grad, members, scale
    )


def solution(mesh):
    both = P("ctx", "tp")
    return jax.shard_map(
        local,
        mesh=mesh,
        in_specs=(both, both, both, both, P("tp", None), both),
        out_specs=(both,) * 5,
        check_vma=False,
    )
```

```python
import functools
import math
import jax
import jax.numpy as jnp
from jax import lax
from jax.experimental import pallas as pl
from jax.experimental.pallas import tpu as pltpu
from jax.sharding import PartitionSpec as P

BLOCK = 128
POSITION = 8
NT = (((1,), (1,)), ((), ()))
COST = pl.CostEstimate(flops=2**20, bytes_accessed=2**12, transcendentals=0)


def lag_matrix(row, length):
    lanes = lax.broadcasted_iota(jnp.int32, (BLOCK, BLOCK), 1)
    rows = lax.broadcasted_iota(jnp.int32, (BLOCK, BLOCK), 0)
    spread = pltpu.roll(
        jnp.broadcast_to(row, (BLOCK, length)), 0, axis=1, stride=1, stride_axis=0
    )
    first = jnp.where(lanes >= rows, spread[:, :BLOCK], 0.0)
    return jnp.concatenate(
        [first.astype(jnp.bfloat16), spread[:, BLOCK:].astype(jnp.bfloat16)], axis=1
    )


def stacked(ref, start, rows, members, width):
    pieces = []
    for member in range(members):
        part = ref[member, pl.ds(start, rows), :]
        for at in range(0, width, BLOCK):
            pieces.append(part[:, at : at + BLOCK])
    return jnp.concatenate(pieces, axis=0)


def spread_out(ref, start, rows, value, members, width):
    per_member = width // BLOCK
    for member in range(members):
        base = member * per_member * rows
        parts = [value[base + i * rows : base + (i + 1) * rows] for i in range(per_member)]
        ref[member, pl.ds(start, rows), :] = jnp.concatenate(parts, axis=1)


def padded(groups):
    return -(-groups // 16) * 16


def load_taps(tap_scr, packed, at, width):
    groups, channels = tap_scr.shape[0], packed.shape[1]
    rows = padded(groups)
    parts = [
        packed[width + chunk * rows : width + (chunk + 1) * rows, :].astype(jnp.float32)
        for chunk in range(width // channels)
    ]
    start = pl.multiple_of(at * width, width)
    tap_scr[:, pl.ds(start, width)] = jnp.concatenate(parts, axis=1)[:groups]


def forward_kernel(members, per_group, width, plan_ref, *refs):
    inputs, outputs = refs[:members], refs[-members - 3 : -3]
    in_scr, tap_scr, out_scr = refs[-3:]
    position = plan_ref[POSITION]
    channels = inputs[0].shape[1]
    groups = channels // per_group
    length = members * width
    blocks = length // BLOCK
    for step in range(members):
        at = position ^ step
        in_scr[at] = inputs[step][:width].T
        load_taps(tap_scr, inputs[step], at, width)

    def one_group(group, carry):
        start = pl.multiple_of(group * per_group, per_group)
        lags = lag_matrix(tap_scr[pl.ds(group, 1), :], length)
        data = stacked(in_scr, start, per_group, members, width)
        total = [jnp.zeros((per_group, BLOCK), jnp.float32) for _ in range(blocks)]
        for offset in range(0, blocks, 2):
            rows = (blocks - offset) * per_group
            result = jnp.dot(
                data[:rows],
                lags[:, offset * BLOCK : (offset + 2) * BLOCK],
                preferred_element_type=jnp.float32,
            )
            for side in range(2):
                for source in range(blocks - offset - side):
                    total[source + offset + side] += result[
                        source * per_group : (source + 1) * per_group,
                        side * BLOCK : (side + 1) * BLOCK,
                    ]
        value = jnp.concatenate(total, axis=0).astype(jnp.bfloat16)
        spread_out(out_scr, start, per_group, value, members, width)
        return carry

    lax.fori_loop(0, groups, one_group, 0, unroll=8)
    for step in range(members):
        outputs[step][...] = out_scr[position ^ step].T


def backward_kernel(members, batch, per_group, scale, width, plan_ref, in_scr, lag_ref, *refs):
    cotangents = refs[:members]
    outputs = refs[-members - 4 : -4]
    cot_scr, out_scr, grad_scr, pad_scr = refs[-4:]
    position = plan_ref[POSITION]
    channels = cotangents[0].shape[1]
    groups = channels // per_group
    length = members * width
    blocks = length // BLOCK
    depth = blocks * per_group
    rows_of = lax.broadcasted_iota(jnp.int32, (BLOCK, BLOCK), 0)
    lanes_of = lax.broadcasted_iota(jnp.int32, (BLOCK, BLOCK), 1)
    mirror = (rows_of + lanes_of == BLOCK - 1).astype(jnp.bfloat16)

    @pl.when(pl.program_id(0) == 0)
    def _():
        for step in range(members):
            cot_scr[position ^ step] = cotangents[step][...].T
        pad_scr[...] = jnp.zeros_like(pad_scr)

    for local_group in range(batch):
        group = pl.program_id(0) * batch + local_group
        start = pl.multiple_of(group * per_group, per_group)
        lags = lag_ref[local_group]
        padded_cot = pad_scr.at[local_group]
        data = stacked(in_scr, start, per_group, members, width)
        cot = stacked(cot_scr, start, per_group, members, width)
        padded_cot[:depth, :BLOCK] = cot
        padded_cot[: depth - per_group, BLOCK:] = cot[per_group:]
        flipped = lax.dot_general(
            mirror, data, NT, preferred_element_type=jnp.float32
        ).astype(jnp.bfloat16)
        total = jnp.zeros((depth, BLOCK), jnp.float32)
        products = []
        for offset in range(0, blocks, 2):
            rows = depth - offset * per_group
            pair = padded_cot[offset * per_group : offset * per_group + depth, :]
            result = lax.dot_general(
                pair[:rows],
                lags[:, offset * BLOCK : (offset + 2) * BLOCK],
                NT,
                preferred_element_type=jnp.float32,
            )
            if rows < depth:
                result = jnp.concatenate(
                    [result, jnp.zeros((depth - rows, BLOCK), jnp.float32)], axis=0
                )
            total = total + result
            products.append(jnp.dot(flipped, pair, preferred_element_type=jnp.float32))
        spread_out(out_scr, start, per_group, total.astype(jnp.bfloat16), members, width)
        kept = jnp.where(rows_of + lanes_of >= BLOCK - 1, products[0][:, :BLOCK], 0.0)
        product = jnp.concatenate([kept, products[0][:, BLOCK:], *products[1:]], axis=1)
        product = pltpu.roll(
            product, length - (BLOCK - 1), axis=1, stride=1, stride_axis=0
        )
        grad_scr[pl.ds(group, 1), :] = jnp.sum(product, axis=0, keepdims=True) * scale

    @pl.when(pl.program_id(0) == pl.num_programs(0) - 1)
    def _():
        for step in range(members):
            at = position ^ step
            outputs[step][:width] = out_scr[at].T
            rows = padded(groups)
            whole = grad_scr[:, pl.ds(pl.multiple_of(at * width, width), width)]
            whole = whole.astype(jnp.bfloat16)
            if rows > groups:
                blank = jnp.zeros((rows - groups, width), jnp.bfloat16)
                whole = jnp.concatenate([whole, blank], axis=0)
            for chunk in range(width // channels):
                outputs[step][width + chunk * rows : width + (chunk + 1) * rows, :] = whole[
                    :, chunk * channels : (chunk + 1) * channels
                ]


def lag_kernel(taps_ref, out_ref):
    row = taps_ref[pl.ds(pl.program_id(0), 1), :]
    out_ref[0] = lag_matrix(row, taps_ref.shape[1])


VMEM = pl.BlockSpec(memory_space=pltpu.VMEM)
ANYWHERE = pl.BlockSpec(memory_space=pl.ANY)
SMEM = pl.BlockSpec(memory_space=pltpu.SMEM)


def convolve(plan, inputs, width, per_group, after=()):
    members = len(inputs)
    channels = inputs[0].shape[1]
    length = members * width
    *parts, turned, taps = pl.pallas_call(
        functools.partial(forward_kernel, members, per_group, width),
        out_shape=[jax.ShapeDtypeStruct((width, channels), jnp.bfloat16)] * members
        + [
            jax.ShapeDtypeStruct((members, channels, width), jnp.bfloat16),
            jax.ShapeDtypeStruct((channels // per_group, length), jnp.float32),
        ],
        in_specs=[SMEM] + [VMEM] * members + [ANYWHERE] * len(after),
        out_specs=[VMEM] * (members + 2),
        scratch_shapes=[pltpu.VMEM((members, channels, width), jnp.bfloat16)],
        compiler_params=pltpu.CompilerParams(vmem_limit_bytes=24 * 2**20),
        cost_estimate=COST,
        name="causal_conv",
    )(plan, *inputs, *after)
    return parts, turned, taps


def lag_matrices(taps):
    groups, length = taps.shape
    return pl.pallas_call(
        lag_kernel,
        out_shape=jax.ShapeDtypeStruct((groups, BLOCK, length), jnp.bfloat16),
        grid=(groups,),
        in_specs=[VMEM],
        out_specs=pl.BlockSpec((1, BLOCK, length), lambda i: (i, 0, 0)),
        compiler_params=pltpu.CompilerParams(vmem_limit_bytes=12 * 2**20),
        cost_estimate=COST,
        name="lag_matrices",
    )(taps)


def correlate(plan, turned, lags, cotangents, per_group, scale, after=()):
    members = len(cotangents)
    width, channels = cotangents[0].shape
    length = members * width
    groups = channels // per_group
    batch = 4 if groups % 4 == 0 else 1
    rows = width + padded(groups) * width // channels
    return pl.pallas_call(
        functools.partial(backward_kernel, members, batch, per_group, scale, width),
        out_shape=[jax.ShapeDtypeStruct((rows, channels), jnp.bfloat16)] * members,
        grid=(groups // batch,),
        in_specs=[SMEM, VMEM, pl.BlockSpec((batch, BLOCK, length), lambda i: (i, 0, 0))]
        + [VMEM] * members
        + [ANYWHERE] * len(after),
        out_specs=[VMEM] * members,
        scratch_shapes=[
            pltpu.VMEM((members, channels, width), jnp.bfloat16),
            pltpu.VMEM((members, channels, width), jnp.bfloat16),
            pltpu.VMEM((groups, length), jnp.float32),
            pltpu.VMEM((batch, 2 * length // BLOCK * per_group, 2 * BLOCK), jnp.bfloat16),
        ],
        compiler_params=pltpu.CompilerParams(vmem_limit_bytes=24 * 2**20),
        cost_estimate=COST,
        name="causal_conv_grads",
    )(plan, turned, lags, *cotangents, *after)


def in_hbm(array):
    return pltpu.with_memory_space_constraint(array, pltpu.HBM)


def prepare_kernel(members, scale, who_ref, key_ref, value_ref, taps_ref, *outputs):
    position = who_ref[0]
    step_no = pl.program_id(0)
    rows, channels = key_ref.shape
    share = channels // members
    groups = taps_ref.shape[0] // members
    total_width = taps_ref.shape[1]
    for step in range(members):
        at = position ^ step
        columns = pl.ds(pl.multiple_of(at * share, share), share)
        product = key_ref[:, columns].astype(jnp.float32) * value_ref[:, columns].astype(
            jnp.float32
        )
        here = pl.ds(pl.multiple_of(step_no * rows, rows), rows)
        outputs[step][here, :] = product.astype(jnp.bfloat16)

    @pl.when(step_no == 0)
    def _():
        for step in range(members):
            at = position ^ step
            taps = taps_ref[pl.ds(pl.multiple_of(at * groups, groups), groups), :]
            taps = (taps * scale).astype(jnp.bfloat16)
            for chunk in range(total_width // share):
                start = total_width + chunk * groups
                outputs[step][start : start + groups, :] = taps[
                    :, chunk * share : (chunk + 1) * share
                ]


def prepare(who, key_gate, value_input, filter_taps, members, scale):
    width, channels = key_gate.shape
    share = channels // members
    rows = width + filter_taps.size // members // share
    tile = width // 4
    part = pl.BlockSpec((tile, channels), lambda i: (i, 0))
    return pl.pallas_call(
        functools.partial(prepare_kernel, members, scale),
        out_shape=[jax.ShapeDtypeStruct((rows, share), jnp.bfloat16)] * members,
        grid=(4,),
        in_specs=[SMEM, part, part, pl.BlockSpec(filter_taps.shape[::-1], lambda i: (0, 0))],
        out_specs=[VMEM] * members,
        compiler_params=pltpu.CompilerParams(vmem_limit_bytes=24 * 2**20),
        cost_estimate=COST,
        name="gated_input",
    )(who, in_hbm(key_gate), in_hbm(value_input), in_hbm(filter_taps.T))


def finish_kernel(members, plan_ref, *refs):
    parts = refs[:members]
    key_ref, value_ref = refs[members : members + 2]
    summands = refs[members + 2 : -4]
    key_out, value_out, projected_out, taps_out = refs[-4:]
    position = plan_ref[POSITION]
    width = key_ref.shape[0]
    share = key_out.shape[1]
    groups = taps_out.shape[0] // members
    here = pl.ds(pl.multiple_of(pl.program_id(0) * share, share), share)
    projected = sum(ref[:, here].astype(jnp.float32) for ref in summands)
    projected_out[...] = projected.astype(jnp.bfloat16)
    for step in range(members):

        @pl.when(pl.program_id(0) == step)
        def _(step=step):
            at = position ^ step
            columns = pl.ds(pl.multiple_of(at * share, share), share)
            grad = parts[step][:width].astype(jnp.float32)
            key_out[...] = (grad * value_ref[:, columns].astype(jnp.float32)).astype(jnp.bfloat16)
            value_out[...] = (grad * key_ref[:, columns].astype(jnp.float32)).astype(jnp.bfloat16)
            taps = [
                parts[step][width + chunk * groups : width + (chunk + 1) * groups, :]
                for chunk in range(width // share)
            ]
            taps_out[pl.ds(pl.multiple_of(at * groups, groups), groups), :] = jnp.concatenate(
                taps, axis=1
            ).astype(jnp.float32)


def finished(plan, parts, key_gate, value_input, summands, groups):
    members = len(parts)
    width, channels = key_gate.shape
    share = channels // members
    array = jax.ShapeDtypeStruct((width, channels), jnp.bfloat16)
    swapped_piece = pl.BlockSpec((width, share), lambda i, at: (0, at[POSITION] ^ i))
    piece = pl.BlockSpec((width, share), lambda i, at: (0, i))
    grad_key, grad_value, projected, taps = pl.pallas_call(
        functools.partial(finish_kernel, members),
        out_shape=[array] * 3 + [jax.ShapeDtypeStruct((groups, width), jnp.float32)],
        grid_spec=pltpu.PrefetchScalarGridSpec(
            num_scalar_prefetch=1,
            grid=(members,),
            in_specs=[VMEM] * (members + 2 + len(summands)),
            out_specs=[swapped_piece, swapped_piece, piece, VMEM],
        ),
        compiler_params=pltpu.CompilerParams(vmem_limit_bytes=24 * 2**20),
        cost_estimate=COST,
        name="input_gradients",
    )(plan, *parts, key_gate, value_input, *summands)
    return projected, grad_key, grad_value, taps.T


def swapped(array, axis, step):
    size = lax.axis_size(axis)
    return lax.ppermute(array, axis, [(i, i ^ step) for i in range(size)])


def traded(pieces, axis):
    return [pieces[0]] + [swapped(pieces[step], axis, step) for step in range(1, len(pieces))]


def cut(array, position, members, axis):
    width = array.shape[axis] // members
    return [
        lax.dynamic_slice_in_dim(array, (position ^ step) * width, width, axis)
        for step in range(members)
    ]


def joined(pieces, position, axis):
    members = len(pieces)
    width = pieces[0].shape[axis]
    shape = list(pieces[0].shape)
    shape[axis] = members * width
    whole = jnp.zeros(shape, pieces[0].dtype)
    for step in range(members):
        whole = lax.dynamic_update_slice_in_dim(
            whole, pieces[step], (position ^ step) * width, axis
        )
    return whole


def wide(array):
    return array.astype(jnp.float32)


def hop(array, pairs):
    return lax.ppermute(
        array, "tp", [(2 * i + core, 2 * j + core) for i, j in pairs for core in range(2)]
    )


INWARD = ((0, 1), (3, 2))
ACROSS = ((1, 2), (2, 1))
OUTWARD = ((1, 0), (2, 3))
OWN, NEAR, MIDDLE, FAR = range(4)
IN_MIDDLE = POSITION + 1
CHIPS = ((0, 1, 2, 3), (1, 0, 3, 2), (2, 2, 1, 1), (3, 3, 0, 0))


def plan_kernel(who_ref, plan_ref):
    place = who_ref[1]
    chip, core = place // 2, place % 2
    for number, table in enumerate(CHIPS):
        source = jnp.where(
            chip < 2,
            jnp.where(chip == 0, table[0], table[1]),
            jnp.where(chip == 2, table[2], table[3]),
        )
        plan_ref[2 * number] = 2 * source + core
        plan_ref[2 * number + 1] = 2 * source + 1 - core
    plan_ref[POSITION] = who_ref[0]
    plan_ref[IN_MIDDLE] = ((chip == 1) | (chip == 2)).astype(jnp.int32)


def planned(who):
    return pl.pallas_call(
        plan_kernel,
        out_shape=jax.ShapeDtypeStruct((IN_MIDDLE + 1,), jnp.int32),
        in_specs=[SMEM],
        out_specs=SMEM,
        compiler_params=pltpu.CompilerParams(vmem_limit_bytes=2**20),
        cost_estimate=COST,
        name="plan",
    )(who)


def pass_kernel(*refs):
    del refs


def held_until(values, after):
    return pl.pallas_call(
        pass_kernel,
        out_shape=[jax.ShapeDtypeStruct(value.shape, value.dtype) for value in values],
        in_specs=[ANYWHERE] * (len(values) + len(after)),
        out_specs=[ANYWHERE] * len(values),
        input_output_aliases={number: number for number in range(len(values))},
        compiler_params=pltpu.CompilerParams(vmem_limit_bytes=2**20),
        cost_estimate=COST,
        name="held",
    )(*values, *after)


def add_kernel(*refs):
    refs[-1][...] = sum(wide(ref[...]) for ref in refs[:-1]).astype(jnp.bfloat16)


def added(*arrays):
    rows, width = arrays[0].shape
    part = pl.BlockSpec((rows // 4, width), lambda i: (i, 0))
    return pl.pallas_call(
        add_kernel,
        out_shape=jax.ShapeDtypeStruct((rows, width), jnp.bfloat16),
        grid=(4,),
        in_specs=[part] * len(arrays),
        out_specs=part,
        compiler_params=pltpu.CompilerParams(vmem_limit_bytes=8 * 2**20),
        cost_estimate=COST,
        name="added",
    )(*arrays)


def choice_kernel(plan_ref, middle_ref, end_ref, *refs):
    out_ref = refs[-1]
    in_middle = plan_ref[IN_MIDDLE] == 1

    @pl.when(in_middle)
    def _():
        out_ref[...] = middle_ref[...]

    @pl.when(jnp.logical_not(in_middle))
    def _():
        out_ref[...] = end_ref[...]


def chosen(plan, in_middle, at_end, after=()):
    return pl.pallas_call(
        choice_kernel,
        out_shape=jax.ShapeDtypeStruct(at_end.shape, at_end.dtype),
        in_specs=[SMEM, VMEM, VMEM] + [ANYWHERE] * len(after),
        out_specs=VMEM,
        compiler_params=pltpu.CompilerParams(vmem_limit_bytes=2**20),
        cost_estimate=COST,
        name="chosen",
    )(plan, in_middle, at_end, *after)


def gate_kernel(members, plan_ref, *refs):
    parts = refs[:members]
    query_ref, gated_ref, conv_ref = refs[members], *refs[-2:]
    position = plan_ref[POSITION]
    share = parts[0].shape[1]
    for step in range(members):
        columns = pl.ds(pl.multiple_of((position ^ step) * share, share), share)
        conv = parts[step][...]
        conv_ref[:, columns] = conv
        gated_ref[:, columns] = (wide(conv) * wide(query_ref[:, columns])).astype(jnp.bfloat16)


def gated(plan, parts, query_gate, after):
    array = jax.ShapeDtypeStruct(query_gate.shape, jnp.bfloat16)
    return pl.pallas_call(
        functools.partial(gate_kernel, len(parts)),
        out_shape=[array, array],
        in_specs=[SMEM] + [VMEM] * (len(parts) + 1) + [ANYWHERE] * len(after),
        out_specs=[VMEM] * 2,
        compiler_params=pltpu.CompilerParams(vmem_limit_bytes=8 * 2**20),
        cost_estimate=COST,
        name="gated_output",
    )(plan, *parts, query_gate, *after)


def spans(widths, start, stop):
    found, begin = [], 0
    for number, width in enumerate(widths):
        low, high = max(start, begin), min(stop, begin + width)
        if low < high:
            found.append((number, slice(low - begin, high - begin), slice(low - start, high - start)))
        begin += width
    return found


def product_kernel(steps, more_widths, out_widths, _, data_ref, weight_ref, *refs):
    more, outputs = refs[: len(more_widths)], refs[-len(out_widths) :]
    product = jnp.dot(data_ref[...], weight_ref[...], preferred_element_type=jnp.float32)
    width = product.shape[1]
    for step in range(steps):
        start, stop = step * width, (step + 1) * width

        @pl.when(pl.program_id(0) == step)
        def _(start=start, stop=stop):
            total = product
            if more:
                parts = [wide(more[n][:, there]) for n, there, _ in spans(more_widths, start, stop)]
                total = total + jnp.concatenate(parts, axis=1)
            total = total.astype(jnp.bfloat16)
            for n, there, here in spans(out_widths, start, stop):
                outputs[n][:, there] = total[:, here]


def column_products(
    plan, data, out_weight, first, count, other, more=(), after=(), tiles=1, widths=()
):
    rows, depth = data.shape
    width = data.shape[1]
    tile = width // tiles
    steps = count * tiles
    widths = tuple(widths) or (width,) * count

    def weights(i, at):
        return 0, at[2 * (first - i // tiles) + other] * tiles + i % tiles

    return pl.pallas_call(
        functools.partial(product_kernel, steps, [part.shape[1] for part in more], widths),
        out_shape=[jax.ShapeDtypeStruct((rows, part), jnp.bfloat16) for part in widths],
        grid_spec=pltpu.PrefetchScalarGridSpec(
            num_scalar_prefetch=1,
            grid=(steps,),
            in_specs=[VMEM, pl.BlockSpec((depth, tile), weights)]
            + [VMEM] * len(more)
            + [ANYWHERE] * len(after),
            out_specs=[VMEM] * len(widths),
        ),
        compiler_params=pltpu.CompilerParams(vmem_limit_bytes=16 * 2**20),
        cost_estimate=COST,
        name="projection_blocks",
    )(plan, data, in_hbm(out_weight), *more, *after)


def cotangent_kernel(count, begin, _, weight_ref, *refs):
    blocks, refs = refs[:count], refs[count:]
    step = pl.program_id(0)
    total = refs[-1]

    for number, block in enumerate(blocks):

        @pl.when(step == number)
        def _(number=number, block=block):
            product = lax.dot_general(
                block[...], weight_ref[...], NT, preferred_element_type=jnp.float32
            )
            if number == 0:
                total[...] = product if begin else refs[0][...] + product
            else:
                total[...] += product


def last_cotangent_kernel(
    members, plan_ref, weight_ref, block_ref, start_ref, conv_ref, query_ref, *refs
):
    parts, cot_scr = refs[-1 - members : -1], refs[-1]
    grad_ref = refs[-2 - members]
    product = lax.dot_general(
        block_ref[...], weight_ref[...], NT, preferred_element_type=jnp.float32
    )
    dgated = wide((start_ref[...] + product).astype(jnp.bfloat16))
    grad_ref[...] = (dgated * wide(conv_ref[...])).astype(jnp.bfloat16)
    cot_scr[...] = (dgated * wide(query_ref[...])).astype(jnp.bfloat16)
    share = parts[0].shape[1]
    odd = plan_ref[POSITION] % 2
    for step in range(0, members, 2):

        @pl.when(pl.program_id(0) == step // 2)
        def _(step=step):
            parts[step][...] = cot_scr[:, pl.ds(pl.multiple_of(odd * share, share), share)]
            parts[step + 1][...] = cot_scr[
                :, pl.ds(pl.multiple_of((1 - odd) * share, share), share)
            ]


def last_cotangents(
    plan, first, block, out_weight, start, convolved, query_gate, members, after
):
    rows, width = block.shape
    channels = out_weight.shape[0]
    share = channels // members
    pair = pl.BlockSpec((rows, 2 * share), lambda i, at: (0, at[POSITION] // 2 ^ i))
    return pl.pallas_call(
        functools.partial(last_cotangent_kernel, members),
        out_shape=[jax.ShapeDtypeStruct((rows, channels), jnp.bfloat16)]
        + [jax.ShapeDtypeStruct((rows, share), jnp.bfloat16)] * members,
        grid_spec=pltpu.PrefetchScalarGridSpec(
            num_scalar_prefetch=1,
            grid=(members // 2,),
            in_specs=[
                pl.BlockSpec((2 * share, width), lambda i, at: (at[POSITION] // 2 ^ i, at[first])),
                VMEM,
                pair,
                pair,
                pair,
            ]
            + [ANYWHERE] * len(after),
            out_specs=[pair] + [VMEM] * members,
            scratch_shapes=[pltpu.VMEM((rows, 2 * share), jnp.bfloat16)],
        ),
        compiler_params=pltpu.CompilerParams(vmem_limit_bytes=24 * 2**20),
        cost_estimate=COST,
        name="cotangent_last",
    )(plan, in_hbm(out_weight), block, start, convolved, query_gate, *after)


def both(blocks):
    return [part for block in blocks for part in (block, swapped(block, "tp", 1))]


def cotangent_products(plan, first, parts, out_weight, start=None, after=()):
    rows, width = parts[0].shape
    channels = out_weight.shape[0]
    count = len(parts)
    begin = start is None
    extra = () if begin else (start,)
    return pl.pallas_call(
        functools.partial(cotangent_kernel, count, begin),
        out_shape=jax.ShapeDtypeStruct((rows, channels), jnp.float32),
        grid_spec=pltpu.PrefetchScalarGridSpec(
            num_scalar_prefetch=1,
            grid=(count,),
            in_specs=[pl.BlockSpec((channels, width), lambda i, at: (0, at[first + i]))]
            + [VMEM] * (count + len(extra))
            + [ANYWHERE] * len(after),
            out_specs=VMEM,
        ),
        compiler_params=pltpu.CompilerParams(vmem_limit_bytes=16 * 2**20),
        cost_estimate=COST,
        name="cotangent_blocks",
    )(plan, in_hbm(out_weight), *parts, *extra, *after)


def packed_parts(position, key_gate, value_input, filter_taps, members, scale):
    length, channels = key_gate.shape
    share = channels // members
    product_in = (wide(key_gate) * wide(value_input)).astype(jnp.bfloat16)
    tap_rows = (filter_taps * scale).astype(jnp.bfloat16).T
    owned = filter_taps.shape[1] // members
    chunks = length // share
    packed = []
    pieces = cut(product_in, position, members, 1)
    for piece, taps in zip(pieces, cut(tap_rows, position, members, 0)):
        taps = taps.reshape(owned, chunks, share).transpose(1, 0, 2)
        taps = jnp.pad(taps, ((0, 0), (0, padded(owned) - owned), (0, 0)))
        packed.append(jnp.concatenate([piece, taps.reshape(-1, share)], axis=0))
    return packed


def unpacked_parts(position, parts, key_gate, value_input, groups):
    length, channels = key_gate.shape
    members = len(parts)
    share = channels // members
    owned = groups // members
    chunks = length // share
    input_grad = wide(joined([part[:length] for part in parts], position, 1))
    filter_parts = [
        part[length:]
        .reshape(chunks, padded(owned), share)[:, :owned]
        .transpose(1, 0, 2)
        .reshape(owned, length)
        for part in parts
    ]
    grad_filter = wide(joined(filter_parts, position, 0)).T
    grad_key = (input_grad * wide(value_input)).astype(jnp.bfloat16)
    grad_value = (input_grad * wide(key_gate)).astype(jnp.bfloat16)
    return grad_key, grad_value, grad_filter


def in_line(
    query_gate, key_gate, value_input, filter_taps, out_weight, out_grad, members, scale
):
    length, channels = query_gate.shape
    groups = filter_taps.shape[1]
    per_group = channels // groups
    who = jnp.stack([lax.axis_index("ctx"), lax.axis_index("tp")]).astype(jnp.int32)
    plan = planned(who)
    near, cross = hop(out_grad, INWARD + OUTWARD), hop(out_grad, ACROSS)
    total = cotangent_products(plan, 2 * OWN, both([out_grad]), out_weight)

    packed = prepare(who, key_gate, value_input, filter_taps, members, scale)
    input_parts = traded(packed, "ctx")
    conv_parts, turned, taps = convolve(plan, input_parts, length, per_group, (total,))
    *conv_parts, near, cross = held_until([*conv_parts, near, cross], ())
    far, skip = hop(near, ACROSS), hop(cross, OUTWARD)
    lags = lag_matrices(taps)
    gated_out, convolved = gated(plan, traded(conv_parts, "ctx"), query_gate, (lags,))

    def product(first, count, other, more=(), after=(), tiles=1, widths=()):
        return column_products(
            plan, gated_out, out_weight, first, count, other, more, after, tiles, widths
        )

    quarter, half = channels // 4, channels // 2
    given_far = product(FAR, 1, 1, tiles=2, widths=(3 * quarter, quarter))
    received = [swapped(part, "tp", 1) for part in given_far]
    (first,) = product(FAR, 1, 0, received, tiles=2)
    far, skip = held_until([far, skip], (first,))
    mixed = chosen(plan, far, first)
    arrived = hop(mixed, OUTWARD + INWARD)
    given_middle = product(MIDDLE, 1, 1, (), (mixed,), tiles=2, widths=(half, half))
    received = [swapped(part, "tp", 1) for part in given_middle]
    (second,) = product(MIDDLE, 1, 0, received, tiles=2)
    middle_block = added(cross, skip)
    blocks = [near, swapped(near, "tp", 1), middle_block]
    total = cotangent_products(plan, 2 * NEAR, blocks, out_weight, total, after=(second,))
    given_near, given_own = product(NEAR, 2, 1, (), (second,))
    (arrived,) = held_until([arrived], (total, given_near))
    through = added(first, arrived)
    two_a = hop(through, ACROSS)
    (second,) = held_until([second], (arrived,))
    two_b = hop(second, INWARD)

    far_block, far_other = both([chosen(plan, far, arrived, (through,))])
    blocks = [swapped(middle_block, "tp", 1), far_block]
    total = cotangent_products(
        plan, 2 * MIDDLE + 1, blocks, out_weight, total, after=(through,)
    )
    grad_query, *grad_parts = last_cotangents(
        plan, 2 * FAR + 1, far_other, out_weight, total, convolved, query_gate, members, ()
    )
    received = (swapped(given_near, "tp", 1), swapped(given_own, "tp", 1))
    third, own = product(NEAR, 2, 0, received, (grad_parts[0],))
    grad_parts = traded(grad_parts, "ctx")

    two_a, two_b = held_until([two_a, two_b], tuple(grad_parts[1:]))
    third, second = added(third, two_a), added(second, two_b)
    back_parts = correlate(plan, turned, lags, grad_parts, per_group, scale, (third, second))
    summands = (own, hop(third, OUTWARD + INWARD), hop(second, ACROSS))
    back_parts = traded(back_parts, "ctx")
    projected, *gradients = finished(
        plan, back_parts, key_gate, value_input, summands, groups
    )
    return projected, grad_query, *gradients


def anywhere(
    query_gate, key_gate, value_input, filter_taps, out_weight, out_grad, members, scale
):
    length, channels = query_gate.shape
    groups = filter_taps.shape[1]
    per_group = channels // groups
    position = lax.axis_index("ctx")
    plan = jnp.full((POSITION + 1,), position, jnp.int32)
    packed = packed_parts(position, key_gate, value_input, filter_taps, members, scale)
    input_parts = traded(packed, "ctx")
    conv_parts, turned, taps = convolve(plan, input_parts, length, per_group)
    conv_parts = traded(conv_parts, "ctx")
    convolved = joined(conv_parts, position, 1)
    gated_out = (wide(query_gate) * wide(convolved)).astype(jnp.bfloat16)
    partial_value = jnp.dot(gated_out, out_weight, preferred_element_type=jnp.float32)
    projected = lax.psum_scatter(
        partial_value.astype(jnp.bfloat16), "tp", scatter_dimension=1, tiled=True
    )
    dgated = jnp.einsum(
        "tk,ck->tc",
        lax.all_gather(out_grad, "tp", axis=1, tiled=True),
        out_weight,
        preferred_element_type=jnp.float32,
    ).astype(jnp.bfloat16)
    grad_query = (wide(dgated) * wide(convolved)).astype(jnp.bfloat16)
    conv_grad = (wide(dgated) * wide(query_gate)).astype(jnp.bfloat16)
    grad_parts = traded(cut(conv_grad, position, members, 1), "ctx")
    back_parts = correlate(plan, turned, lag_matrices(taps), grad_parts, per_group, scale)
    back_parts = traded(back_parts, "ctx")
    return (
        projected,
        grad_query,
        *unpacked_parts(position, back_parts, key_gate, value_input, groups),
    )


def local(query_gate, key_gate, value_input, filter_taps, out_weight, out_grad):
    length, channels = query_gate.shape
    groups = filter_taps.shape[1]
    members = lax.axis_size("ctx")
    scale = 1.0 / math.sqrt(length * members)
    fits = channels // members % 128 == 0 and groups // members % 16 == 0
    body = in_line if lax.axis_size("tp") == 8 and fits else anywhere
    return body(
        query_gate, key_gate, value_input, filter_taps, out_weight, out_grad, members, scale
    )


def solution(mesh):
    both = P("ctx", "tp")
    return jax.shard_map(
        local,
        mesh=mesh,
        in_specs=(both, both, both, both, P("tp", None), both),
        out_specs=(both,) * 5,
        check_vma=False,
    )
```

```python
import functools
import math
import jax
import jax.numpy as jnp
from jax import lax
from jax.experimental import pallas as pl
from jax.experimental.pallas import tpu as pltpu
from jax.sharding import PartitionSpec as P

BLOCK = 128
POSITION = 8
NT = (((1,), (1,)), ((), ()))
COST = pl.CostEstimate(flops=2**20, bytes_accessed=2**12, transcendentals=0)


def lag_matrix(row, length):
    lanes = lax.broadcasted_iota(jnp.int32, (BLOCK, BLOCK), 1)
    rows = lax.broadcasted_iota(jnp.int32, (BLOCK, BLOCK), 0)
    spread = pltpu.roll(
        jnp.broadcast_to(row, (BLOCK, length)), 0, axis=1, stride=1, stride_axis=0
    )
    first = jnp.where(lanes >= rows, spread[:, :BLOCK], 0.0)
    return jnp.concatenate(
        [first.astype(jnp.bfloat16), spread[:, BLOCK:].astype(jnp.bfloat16)], axis=1
    )


def stacked(ref, start, rows, members, width):
    pieces = []
    for member in range(members):
        part = ref[member, pl.ds(start, rows), :]
        for at in range(0, width, BLOCK):
            pieces.append(part[:, at : at + BLOCK])
    return jnp.concatenate(pieces, axis=0)


def spread_out(ref, start, rows, value, members, width):
    per_member = width // BLOCK
    for member in range(members):
        base = member * per_member * rows
        parts = [value[base + i * rows : base + (i + 1) * rows] for i in range(per_member)]
        ref[member, pl.ds(start, rows), :] = jnp.concatenate(parts, axis=1)


def padded(groups):
    return -(-groups // 16) * 16


def load_taps(tap_scr, packed, at, width):
    groups, channels = tap_scr.shape[0], packed.shape[1]
    rows = padded(groups)
    parts = [
        packed[width + chunk * rows : width + (chunk + 1) * rows, :].astype(jnp.float32)
        for chunk in range(width // channels)
    ]
    start = pl.multiple_of(at * width, width)
    tap_scr[:, pl.ds(start, width)] = jnp.concatenate(parts, axis=1)[:groups]


def forward_kernel(members, per_group, width, plan_ref, *refs):
    inputs, outputs = refs[:members], refs[-members - 3 : -3]
    in_scr, tap_scr, out_scr = refs[-3:]
    position = plan_ref[POSITION]
    channels = inputs[0].shape[1]
    groups = channels // per_group
    length = members * width
    blocks = length // BLOCK
    for step in range(members):
        at = position ^ step
        in_scr[at] = inputs[step][:width].T
        load_taps(tap_scr, inputs[step], at, width)

    def one_group(group, carry):
        start = pl.multiple_of(group * per_group, per_group)
        lags = lag_matrix(tap_scr[pl.ds(group, 1), :], length)
        data = stacked(in_scr, start, per_group, members, width)
        total = [jnp.zeros((per_group, BLOCK), jnp.float32) for _ in range(blocks)]
        for offset in range(0, blocks, 2):
            rows = (blocks - offset) * per_group
            result = jnp.dot(
                data[:rows],
                lags[:, offset * BLOCK : (offset + 2) * BLOCK],
                preferred_element_type=jnp.float32,
            )
            for side in range(2):
                for source in range(blocks - offset - side):
                    total[source + offset + side] += result[
                        source * per_group : (source + 1) * per_group,
                        side * BLOCK : (side + 1) * BLOCK,
                    ]
        value = jnp.concatenate(total, axis=0).astype(jnp.bfloat16)
        spread_out(out_scr, start, per_group, value, members, width)
        return carry

    lax.fori_loop(0, groups, one_group, 0, unroll=8)
    for step in range(members):
        outputs[step][...] = out_scr[position ^ step].T


def backward_kernel(members, batch, per_group, scale, width, plan_ref, in_scr, lag_ref, *refs):
    cotangents = refs[:members]
    outputs = refs[-members - 4 : -4]
    cot_scr, out_scr, grad_scr, pad_scr = refs[-4:]
    position = plan_ref[POSITION]
    channels = cotangents[0].shape[1]
    groups = channels // per_group
    length = members * width
    blocks = length // BLOCK
    depth = blocks * per_group
    rows_of = lax.broadcasted_iota(jnp.int32, (BLOCK, BLOCK), 0)
    lanes_of = lax.broadcasted_iota(jnp.int32, (BLOCK, BLOCK), 1)
    mirror = (rows_of + lanes_of == BLOCK - 1).astype(jnp.bfloat16)

    @pl.when(pl.program_id(0) == 0)
    def _():
        for step in range(members):
            cot_scr[position ^ step] = cotangents[step][...].T
        pad_scr[...] = jnp.zeros_like(pad_scr)

    for local_group in range(batch):
        group = pl.program_id(0) * batch + local_group
        start = pl.multiple_of(group * per_group, per_group)
        lags = lag_ref[local_group]
        padded_cot = pad_scr.at[local_group]
        data = stacked(in_scr, start, per_group, members, width)
        cot = stacked(cot_scr, start, per_group, members, width)
        padded_cot[:depth, :BLOCK] = cot
        padded_cot[: depth - per_group, BLOCK:] = cot[per_group:]
        flipped = lax.dot_general(
            mirror, data, NT, preferred_element_type=jnp.float32
        ).astype(jnp.bfloat16)
        total = jnp.zeros((depth, BLOCK), jnp.float32)
        products = []
        for offset in range(0, blocks, 2):
            rows = depth - offset * per_group
            pair = padded_cot[offset * per_group : offset * per_group + depth, :]
            result = lax.dot_general(
                pair[:rows],
                lags[:, offset * BLOCK : (offset + 2) * BLOCK],
                NT,
                preferred_element_type=jnp.float32,
            )
            if rows < depth:
                result = jnp.concatenate(
                    [result, jnp.zeros((depth - rows, BLOCK), jnp.float32)], axis=0
                )
            total = total + result
            products.append(jnp.dot(flipped, pair, preferred_element_type=jnp.float32))
        spread_out(out_scr, start, per_group, total.astype(jnp.bfloat16), members, width)
        kept = jnp.where(rows_of + lanes_of >= BLOCK - 1, products[0][:, :BLOCK], 0.0)
        product = jnp.concatenate([kept, products[0][:, BLOCK:], *products[1:]], axis=1)
        product = pltpu.roll(
            product, length - (BLOCK - 1), axis=1, stride=1, stride_axis=0
        )
        grad_scr[pl.ds(group, 1), :] = jnp.sum(product, axis=0, keepdims=True) * scale

    @pl.when(pl.program_id(0) == pl.num_programs(0) - 1)
    def _():
        for step in range(members):
            at = position ^ step
            outputs[step][:width] = out_scr[at].T
            rows = padded(groups)
            whole = grad_scr[:, pl.ds(pl.multiple_of(at * width, width), width)]
            whole = whole.astype(jnp.bfloat16)
            if rows > groups:
                blank = jnp.zeros((rows - groups, width), jnp.bfloat16)
                whole = jnp.concatenate([whole, blank], axis=0)
            for chunk in range(width // channels):
                outputs[step][width + chunk * rows : width + (chunk + 1) * rows, :] = whole[
                    :, chunk * channels : (chunk + 1) * channels
                ]


def lag_kernel(taps_ref, out_ref):
    row = taps_ref[pl.ds(pl.program_id(0), 1), :]
    out_ref[0] = lag_matrix(row, taps_ref.shape[1])


VMEM = pl.BlockSpec(memory_space=pltpu.VMEM)
ANYWHERE = pl.BlockSpec(memory_space=pl.ANY)
SMEM = pl.BlockSpec(memory_space=pltpu.SMEM)


def convolve(plan, inputs, width, per_group, after=()):
    members = len(inputs)
    channels = inputs[0].shape[1]
    length = members * width
    *parts, turned, taps = pl.pallas_call(
        functools.partial(forward_kernel, members, per_group, width),
        out_shape=[jax.ShapeDtypeStruct((width, channels), jnp.bfloat16)] * members
        + [
            jax.ShapeDtypeStruct((members, channels, width), jnp.bfloat16),
            jax.ShapeDtypeStruct((channels // per_group, length), jnp.float32),
        ],
        in_specs=[SMEM] + [VMEM] * members + [ANYWHERE] * len(after),
        out_specs=[VMEM] * (members + 2),
        scratch_shapes=[pltpu.VMEM((members, channels, width), jnp.bfloat16)],
        compiler_params=pltpu.CompilerParams(vmem_limit_bytes=24 * 2**20),
        cost_estimate=COST,
        name="causal_conv",
    )(plan, *inputs, *after)
    return parts, turned, taps


def lag_matrices(taps):
    groups, length = taps.shape
    return pl.pallas_call(
        lag_kernel,
        out_shape=jax.ShapeDtypeStruct((groups, BLOCK, length), jnp.bfloat16),
        grid=(groups,),
        in_specs=[VMEM],
        out_specs=pl.BlockSpec((1, BLOCK, length), lambda i: (i, 0, 0)),
        compiler_params=pltpu.CompilerParams(vmem_limit_bytes=12 * 2**20),
        cost_estimate=COST,
        name="lag_matrices",
    )(taps)


def correlate(plan, turned, lags, cotangents, per_group, scale, after=()):
    members = len(cotangents)
    width, channels = cotangents[0].shape
    length = members * width
    groups = channels // per_group
    batch = 4 if groups % 4 == 0 else 1
    rows = width + padded(groups) * width // channels
    return pl.pallas_call(
        functools.partial(backward_kernel, members, batch, per_group, scale, width),
        out_shape=[jax.ShapeDtypeStruct((rows, channels), jnp.bfloat16)] * members,
        grid=(groups // batch,),
        in_specs=[SMEM, VMEM, pl.BlockSpec((batch, BLOCK, length), lambda i: (i, 0, 0))]
        + [VMEM] * members
        + [ANYWHERE] * len(after),
        out_specs=[VMEM] * members,
        scratch_shapes=[
            pltpu.VMEM((members, channels, width), jnp.bfloat16),
            pltpu.VMEM((members, channels, width), jnp.bfloat16),
            pltpu.VMEM((groups, length), jnp.float32),
            pltpu.VMEM((batch, 2 * length // BLOCK * per_group, 2 * BLOCK), jnp.bfloat16),
        ],
        compiler_params=pltpu.CompilerParams(vmem_limit_bytes=24 * 2**20),
        cost_estimate=pl.CostEstimate(flops=10**10, bytes_accessed=2**12, transcendentals=0),
        name="causal_conv_grads",
    )(plan, turned, lags, *cotangents, *after)


def in_hbm(array):
    return pltpu.with_memory_space_constraint(array, pltpu.HBM)


def prepare_kernel(members, scale, who_ref, key_ref, value_ref, taps_ref, *outputs):
    position = who_ref[0]
    step_no = pl.program_id(0)
    rows, channels = key_ref.shape
    share = channels // members
    groups = taps_ref.shape[0] // members
    total_width = taps_ref.shape[1]
    for step in range(members):
        at = position ^ step
        columns = pl.ds(pl.multiple_of(at * share, share), share)
        product = key_ref[:, columns].astype(jnp.float32) * value_ref[:, columns].astype(
            jnp.float32
        )
        here = pl.ds(pl.multiple_of(step_no * rows, rows), rows)
        outputs[step][here, :] = product.astype(jnp.bfloat16)

    @pl.when(step_no == 0)
    def _():
        for step in range(members):
            at = position ^ step
            taps = taps_ref[pl.ds(pl.multiple_of(at * groups, groups), groups), :]
            taps = (taps * scale).astype(jnp.bfloat16)
            for chunk in range(total_width // share):
                start = total_width + chunk * groups
                outputs[step][start : start + groups, :] = taps[
                    :, chunk * share : (chunk + 1) * share
                ]


def prepare(who, key_gate, value_input, filter_taps, members, scale):
    width, channels = key_gate.shape
    share = channels // members
    rows = width + filter_taps.size // members // share
    tile = width // 4
    part = pl.BlockSpec((tile, channels), lambda i: (i, 0))
    return pl.pallas_call(
        functools.partial(prepare_kernel, members, scale),
        out_shape=[jax.ShapeDtypeStruct((rows, share), jnp.bfloat16)] * members,
        grid=(4,),
        in_specs=[SMEM, part, part, pl.BlockSpec(filter_taps.shape[::-1], lambda i: (0, 0))],
        out_specs=[VMEM] * members,
        compiler_params=pltpu.CompilerParams(vmem_limit_bytes=24 * 2**20),
        cost_estimate=COST,
        name="gated_input",
    )(who, in_hbm(key_gate), in_hbm(value_input), in_hbm(filter_taps.T))


def finish_kernel(members, plan_ref, *refs):
    parts = refs[:members]
    key_ref, value_ref = refs[members : members + 2]
    summands = refs[members + 2 : -4]
    key_out, value_out, projected_out, taps_out = refs[-4:]
    position = plan_ref[POSITION]
    width = key_ref.shape[0]
    share = key_out.shape[1]
    groups = taps_out.shape[0] // members
    here = pl.ds(pl.multiple_of(pl.program_id(0) * share, share), share)
    projected = sum(ref[:, here].astype(jnp.float32) for ref in summands)
    projected_out[...] = projected.astype(jnp.bfloat16)
    for step in range(members):

        @pl.when(pl.program_id(0) == step)
        def _(step=step):
            at = position ^ step
            columns = pl.ds(pl.multiple_of(at * share, share), share)
            grad = parts[step][:width].astype(jnp.float32)
            key_out[...] = (grad * value_ref[:, columns].astype(jnp.float32)).astype(jnp.bfloat16)
            value_out[...] = (grad * key_ref[:, columns].astype(jnp.float32)).astype(jnp.bfloat16)
            taps = [
                parts[step][width + chunk * groups : width + (chunk + 1) * groups, :]
                for chunk in range(width // share)
            ]
            taps_out[pl.ds(pl.multiple_of(at * groups, groups), groups), :] = jnp.concatenate(
                taps, axis=1
            ).astype(jnp.float32)


def finished(plan, parts, key_gate, value_input, summands, groups):
    members = len(parts)
    width, channels = key_gate.shape
    share = channels // members
    array = jax.ShapeDtypeStruct((width, channels), jnp.bfloat16)
    swapped_piece = pl.BlockSpec((width, share), lambda i, at: (0, at[POSITION] ^ i))
    piece = pl.BlockSpec((width, share), lambda i, at: (0, i))
    grad_key, grad_value, projected, taps = pl.pallas_call(
        functools.partial(finish_kernel, members),
        out_shape=[array] * 3 + [jax.ShapeDtypeStruct((groups, width), jnp.float32)],
        grid_spec=pltpu.PrefetchScalarGridSpec(
            num_scalar_prefetch=1,
            grid=(members,),
            in_specs=[VMEM] * (members + 2 + len(summands)),
            out_specs=[swapped_piece, swapped_piece, piece, VMEM],
        ),
        compiler_params=pltpu.CompilerParams(vmem_limit_bytes=24 * 2**20),
        cost_estimate=COST,
        name="input_gradients",
    )(plan, *parts, key_gate, value_input, *summands)
    return projected, grad_key, grad_value, taps.T


def swapped(array, axis, step):
    size = lax.axis_size(axis)
    return lax.ppermute(array, axis, [(i, i ^ step) for i in range(size)])


def traded(pieces, axis):
    return [pieces[0]] + [swapped(pieces[step], axis, step) for step in range(1, len(pieces))]


def cut(array, position, members, axis):
    width = array.shape[axis] // members
    return [
        lax.dynamic_slice_in_dim(array, (position ^ step) * width, width, axis)
        for step in range(members)
    ]


def joined(pieces, position, axis):
    members = len(pieces)
    width = pieces[0].shape[axis]
    shape = list(pieces[0].shape)
    shape[axis] = members * width
    whole = jnp.zeros(shape, pieces[0].dtype)
    for step in range(members):
        whole = lax.dynamic_update_slice_in_dim(
            whole, pieces[step], (position ^ step) * width, axis
        )
    return whole


def wide(array):
    return array.astype(jnp.float32)


def hop(array, pairs):
    return lax.ppermute(
        array, "tp", [(2 * i + core, 2 * j + core) for i, j in pairs for core in range(2)]
    )


INWARD = ((0, 1), (3, 2))
ACROSS = ((1, 2), (2, 1))
OUTWARD = ((1, 0), (2, 3))
OWN, NEAR, MIDDLE, FAR = range(4)
IN_MIDDLE = POSITION + 1
CHIPS = ((0, 1, 2, 3), (1, 0, 3, 2), (2, 2, 1, 1), (3, 3, 0, 0))


def plan_kernel(who_ref, plan_ref):
    place = who_ref[1]
    chip, core = place // 2, place % 2
    for number, table in enumerate(CHIPS):
        source = jnp.where(
            chip < 2,
            jnp.where(chip == 0, table[0], table[1]),
            jnp.where(chip == 2, table[2], table[3]),
        )
        plan_ref[2 * number] = 2 * source + core
        plan_ref[2 * number + 1] = 2 * source + 1 - core
    plan_ref[POSITION] = who_ref[0]
    plan_ref[IN_MIDDLE] = ((chip == 1) | (chip == 2)).astype(jnp.int32)


def planned(who):
    return pl.pallas_call(
        plan_kernel,
        out_shape=jax.ShapeDtypeStruct((IN_MIDDLE + 1,), jnp.int32),
        in_specs=[SMEM],
        out_specs=SMEM,
        compiler_params=pltpu.CompilerParams(vmem_limit_bytes=2**20),
        cost_estimate=COST,
        name="plan",
    )(who)


def pass_kernel(*refs):
    del refs


def held_until(values, after):
    return pl.pallas_call(
        pass_kernel,
        out_shape=[jax.ShapeDtypeStruct(value.shape, value.dtype) for value in values],
        in_specs=[ANYWHERE] * (len(values) + len(after)),
        out_specs=[ANYWHERE] * len(values),
        input_output_aliases={number: number for number in range(len(values))},
        compiler_params=pltpu.CompilerParams(vmem_limit_bytes=2**20),
        cost_estimate=COST,
        name="held",
    )(*values, *after)


def add_kernel(*refs):
    refs[-1][...] = sum(wide(ref[...]) for ref in refs[:-1]).astype(jnp.bfloat16)


def added(*arrays):
    rows, width = arrays[0].shape
    part = pl.BlockSpec((rows // 4, width), lambda i: (i, 0))
    return pl.pallas_call(
        add_kernel,
        out_shape=jax.ShapeDtypeStruct((rows, width), jnp.bfloat16),
        grid=(4,),
        in_specs=[part] * len(arrays),
        out_specs=part,
        compiler_params=pltpu.CompilerParams(vmem_limit_bytes=8 * 2**20),
        cost_estimate=COST,
        name="added",
    )(*arrays)


def choice_kernel(plan_ref, middle_ref, end_ref, *refs):
    out_ref = refs[-1]
    in_middle = plan_ref[IN_MIDDLE] == 1

    @pl.when(in_middle)
    def _():
        out_ref[...] = middle_ref[...]

    @pl.when(jnp.logical_not(in_middle))
    def _():
        out_ref[...] = end_ref[...]


def chosen(plan, in_middle, at_end, after=()):
    return pl.pallas_call(
        choice_kernel,
        out_shape=jax.ShapeDtypeStruct(at_end.shape, at_end.dtype),
        in_specs=[SMEM, VMEM, VMEM] + [ANYWHERE] * len(after),
        out_specs=VMEM,
        compiler_params=pltpu.CompilerParams(vmem_limit_bytes=2**20),
        cost_estimate=COST,
        name="chosen",
    )(plan, in_middle, at_end, *after)


def gate_kernel(members, plan_ref, *refs):
    parts = refs[:members]
    query_ref, gated_ref, conv_ref = refs[members], *refs[-2:]
    position = plan_ref[POSITION]
    share = parts[0].shape[1]
    for step in range(members):
        columns = pl.ds(pl.multiple_of((position ^ step) * share, share), share)
        conv = parts[step][...]
        conv_ref[:, columns] = conv
        gated_ref[:, columns] = (wide(conv) * wide(query_ref[:, columns])).astype(jnp.bfloat16)


def gated(plan, parts, query_gate, after):
    array = jax.ShapeDtypeStruct(query_gate.shape, jnp.bfloat16)
    return pl.pallas_call(
        functools.partial(gate_kernel, len(parts)),
        out_shape=[array, array],
        in_specs=[SMEM] + [VMEM] * (len(parts) + 1) + [ANYWHERE] * len(after),
        out_specs=[VMEM] * 2,
        compiler_params=pltpu.CompilerParams(vmem_limit_bytes=8 * 2**20),
        cost_estimate=COST,
        name="gated_output",
    )(plan, *parts, query_gate, *after)


def spans(widths, start, stop):
    found, begin = [], 0
    for number, width in enumerate(widths):
        low, high = max(start, begin), min(stop, begin + width)
        if low < high:
            found.append((number, slice(low - begin, high - begin), slice(low - start, high - start)))
        begin += width
    return found


def product_kernel(steps, more_widths, out_widths, _, data_ref, weight_ref, *refs):
    more, outputs = refs[: len(more_widths)], refs[-len(out_widths) :]
    product = jnp.dot(data_ref[...], weight_ref[...], preferred_element_type=jnp.float32)
    width = product.shape[1]
    for step in range(steps):
        start, stop = step * width, (step + 1) * width

        @pl.when(pl.program_id(0) == step)
        def _(start=start, stop=stop):
            total = product
            if more:
                parts = [wide(more[n][:, there]) for n, there, _ in spans(more_widths, start, stop)]
                total = total + jnp.concatenate(parts, axis=1)
            total = total.astype(jnp.bfloat16)
            for n, there, here in spans(out_widths, start, stop):
                outputs[n][:, there] = total[:, here]


def column_products(
    plan, data, out_weight, first, count, other, more=(), after=(), tiles=1, widths=()
):
    rows, depth = data.shape
    width = data.shape[1]
    tile = width // tiles
    steps = count * tiles
    widths = tuple(widths) or (width,) * count

    def weights(i, at):
        return 0, at[2 * (first - i // tiles) + other] * tiles + i % tiles

    return pl.pallas_call(
        functools.partial(product_kernel, steps, [part.shape[1] for part in more], widths),
        out_shape=[jax.ShapeDtypeStruct((rows, part), jnp.bfloat16) for part in widths],
        grid_spec=pltpu.PrefetchScalarGridSpec(
            num_scalar_prefetch=1,
            grid=(steps,),
            in_specs=[VMEM, pl.BlockSpec((depth, tile), weights)]
            + [VMEM] * len(more)
            + [ANYWHERE] * len(after),
            out_specs=[VMEM] * len(widths),
        ),
        compiler_params=pltpu.CompilerParams(vmem_limit_bytes=16 * 2**20),
        cost_estimate=COST,
        name="projection_blocks",
    )(plan, data, in_hbm(out_weight), *more, *after)


def cotangent_kernel(count, begin, _, weight_ref, *refs):
    blocks, refs = refs[:count], refs[count:]
    step = pl.program_id(0)
    total = refs[-1]

    for number, block in enumerate(blocks):

        @pl.when(step == number)
        def _(number=number, block=block):
            product = lax.dot_general(
                block[...], weight_ref[...], NT, preferred_element_type=jnp.float32
            )
            if number == 0:
                total[...] = product if begin else refs[0][...] + product
            else:
                total[...] += product


def last_cotangent_kernel(
    members, plan_ref, weight_ref, block_ref, start_ref, conv_ref, query_ref, *refs
):
    parts, cot_scr = refs[-1 - members : -1], refs[-1]
    grad_ref = refs[-2 - members]
    product = lax.dot_general(
        block_ref[...], weight_ref[...], NT, preferred_element_type=jnp.float32
    )
    dgated = wide((start_ref[...] + product).astype(jnp.bfloat16))
    grad_ref[...] = (dgated * wide(conv_ref[...])).astype(jnp.bfloat16)
    cot_scr[...] = (dgated * wide(query_ref[...])).astype(jnp.bfloat16)
    share = parts[0].shape[1]
    odd = plan_ref[POSITION] % 2
    for step in range(0, members, 2):

        @pl.when(pl.program_id(0) == step // 2)
        def _(step=step):
            parts[step][...] = cot_scr[:, pl.ds(pl.multiple_of(odd * share, share), share)]
            parts[step + 1][...] = cot_scr[
                :, pl.ds(pl.multiple_of((1 - odd) * share, share), share)
            ]


def last_cotangents(
    plan, first, block, out_weight, start, convolved, query_gate, members, after
):
    rows, width = block.shape
    channels = out_weight.shape[0]
    share = channels // members
    pair = pl.BlockSpec((rows, 2 * share), lambda i, at: (0, at[POSITION] // 2 ^ i))
    return pl.pallas_call(
        functools.partial(last_cotangent_kernel, members),
        out_shape=[jax.ShapeDtypeStruct((rows, channels), jnp.bfloat16)]
        + [jax.ShapeDtypeStruct((rows, share), jnp.bfloat16)] * members,
        grid_spec=pltpu.PrefetchScalarGridSpec(
            num_scalar_prefetch=1,
            grid=(members // 2,),
            in_specs=[
                pl.BlockSpec((2 * share, width), lambda i, at: (at[POSITION] // 2 ^ i, at[first])),
                VMEM,
                pair,
                pair,
                pair,
            ]
            + [ANYWHERE] * len(after),
            out_specs=[pair] + [VMEM] * members,
            scratch_shapes=[pltpu.VMEM((rows, 2 * share), jnp.bfloat16)],
        ),
        compiler_params=pltpu.CompilerParams(vmem_limit_bytes=24 * 2**20),
        cost_estimate=COST,
        name="cotangent_last",
    )(plan, in_hbm(out_weight), block, start, convolved, query_gate, *after)


def both(blocks):
    return [part for block in blocks for part in (block, swapped(block, "tp", 1))]


def cotangent_products(plan, first, parts, out_weight, start=None, after=()):
    rows, width = parts[0].shape
    channels = out_weight.shape[0]
    count = len(parts)
    begin = start is None
    extra = () if begin else (start,)
    return pl.pallas_call(
        functools.partial(cotangent_kernel, count, begin),
        out_shape=jax.ShapeDtypeStruct((rows, channels), jnp.float32),
        grid_spec=pltpu.PrefetchScalarGridSpec(
            num_scalar_prefetch=1,
            grid=(count,),
            in_specs=[pl.BlockSpec((channels, width), lambda i, at: (0, at[first + i]))]
            + [VMEM] * (count + len(extra))
            + [ANYWHERE] * len(after),
            out_specs=VMEM,
        ),
        compiler_params=pltpu.CompilerParams(vmem_limit_bytes=16 * 2**20),
        cost_estimate=COST,
        name="cotangent_blocks",
    )(plan, in_hbm(out_weight), *parts, *extra, *after)


def packed_parts(position, key_gate, value_input, filter_taps, members, scale):
    length, channels = key_gate.shape
    share = channels // members
    product_in = (wide(key_gate) * wide(value_input)).astype(jnp.bfloat16)
    tap_rows = (filter_taps * scale).astype(jnp.bfloat16).T
    owned = filter_taps.shape[1] // members
    chunks = length // share
    packed = []
    pieces = cut(product_in, position, members, 1)
    for piece, taps in zip(pieces, cut(tap_rows, position, members, 0)):
        taps = taps.reshape(owned, chunks, share).transpose(1, 0, 2)
        taps = jnp.pad(taps, ((0, 0), (0, padded(owned) - owned), (0, 0)))
        packed.append(jnp.concatenate([piece, taps.reshape(-1, share)], axis=0))
    return packed


def unpacked_parts(position, parts, key_gate, value_input, groups):
    length, channels = key_gate.shape
    members = len(parts)
    share = channels // members
    owned = groups // members
    chunks = length // share
    input_grad = wide(joined([part[:length] for part in parts], position, 1))
    filter_parts = [
        part[length:]
        .reshape(chunks, padded(owned), share)[:, :owned]
        .transpose(1, 0, 2)
        .reshape(owned, length)
        for part in parts
    ]
    grad_filter = wide(joined(filter_parts, position, 0)).T
    grad_key = (input_grad * wide(value_input)).astype(jnp.bfloat16)
    grad_value = (input_grad * wide(key_gate)).astype(jnp.bfloat16)
    return grad_key, grad_value, grad_filter


def in_line(
    query_gate, key_gate, value_input, filter_taps, out_weight, out_grad, members, scale
):
    length, channels = query_gate.shape
    groups = filter_taps.shape[1]
    per_group = channels // groups
    who = jnp.stack([lax.axis_index("ctx"), lax.axis_index("tp")]).astype(jnp.int32)
    plan = planned(who)
    near, cross = hop(out_grad, INWARD + OUTWARD), hop(out_grad, ACROSS)
    total = cotangent_products(plan, 2 * OWN, both([out_grad]), out_weight)

    packed = prepare(who, key_gate, value_input, filter_taps, members, scale)
    input_parts = traded(packed, "ctx")
    conv_parts, turned, taps = convolve(plan, input_parts, length, per_group, (total,))
    *conv_parts, near, cross = held_until([*conv_parts, near, cross], ())
    far, skip = hop(near, ACROSS), hop(cross, OUTWARD)
    lags = lag_matrices(taps)
    gated_out, convolved = gated(plan, traded(conv_parts, "ctx"), query_gate, (lags,))

    def product(first, count, other, more=(), after=(), tiles=1, widths=()):
        return column_products(
            plan, gated_out, out_weight, first, count, other, more, after, tiles, widths
        )

    quarter, half = channels // 4, channels // 2
    given_far = product(FAR, 1, 1, tiles=2, widths=(3 * quarter, quarter))
    received = [swapped(part, "tp", 1) for part in given_far]
    (first,) = product(FAR, 1, 0, received, tiles=2)
    far, skip = held_until([far, skip], (first,))
    mixed = chosen(plan, far, first)
    arrived = hop(mixed, OUTWARD + INWARD)
    given_middle = product(MIDDLE, 1, 1, (), (mixed,), tiles=2, widths=(half, half))
    received = [swapped(part, "tp", 1) for part in given_middle]
    (second,) = product(MIDDLE, 1, 0, received, tiles=2)
    middle_block = added(cross, skip)
    blocks = [near, swapped(near, "tp", 1), middle_block]
    total = cotangent_products(plan, 2 * NEAR, blocks, out_weight, total, after=(second,))
    given_near, given_own = product(NEAR, 2, 1, (), (second,))
    (arrived,) = held_until([arrived], (total, given_near))
    through = added(first, arrived)
    two_a = hop(through, ACROSS)
    (second,) = held_until([second], (arrived,))
    two_b = hop(second, INWARD)

    far_block, far_other = both([chosen(plan, far, arrived, (through,))])
    blocks = [swapped(middle_block, "tp", 1), far_block]
    total = cotangent_products(
        plan, 2 * MIDDLE + 1, blocks, out_weight, total, after=(through,)
    )
    received = [swapped(part, "tp", 1) for part in (given_near, given_own)]
    grad_query, *grad_parts = last_cotangents(
        plan, 2 * FAR + 1, far_other, out_weight, total, convolved, query_gate, members, received
    )
    third, own = product(NEAR, 2, 0, received, (grad_parts[0],))
    grad_parts = traded(grad_parts, "ctx")

    two_a, two_b = held_until([two_a, two_b], (own,))
    third, second = added(third, two_a), added(second, two_b)
    back_parts = correlate(plan, turned, lags, grad_parts, per_group, scale, (third, second))
    summands = (own, hop(third, OUTWARD + INWARD), hop(second, ACROSS))
    back_parts = traded(back_parts, "ctx")
    projected, *gradients = finished(
        plan, back_parts, key_gate, value_input, summands, groups
    )
    return projected, grad_query, *gradients


def anywhere(
    query_gate, key_gate, value_input, filter_taps, out_weight, out_grad, members, scale
):
    length, channels = query_gate.shape
    groups = filter_taps.shape[1]
    per_group = channels // groups
    position = lax.axis_index("ctx")
    plan = jnp.full((POSITION + 1,), position, jnp.int32)
    packed = packed_parts(position, key_gate, value_input, filter_taps, members, scale)
    input_parts = traded(packed, "ctx")
    conv_parts, turned, taps = convolve(plan, input_parts, length, per_group)
    conv_parts = traded(conv_parts, "ctx")
    convolved = joined(conv_parts, position, 1)
    gated_out = (wide(query_gate) * wide(convolved)).astype(jnp.bfloat16)
    partial_value = jnp.dot(gated_out, out_weight, preferred_element_type=jnp.float32)
    projected = lax.psum_scatter(
        partial_value.astype(jnp.bfloat16), "tp", scatter_dimension=1, tiled=True
    )
    dgated = jnp.einsum(
        "tk,ck->tc",
        lax.all_gather(out_grad, "tp", axis=1, tiled=True),
        out_weight,
        preferred_element_type=jnp.float32,
    ).astype(jnp.bfloat16)
    grad_query = (wide(dgated) * wide(convolved)).astype(jnp.bfloat16)
    conv_grad = (wide(dgated) * wide(query_gate)).astype(jnp.bfloat16)
    grad_parts = traded(cut(conv_grad, position, members, 1), "ctx")
    back_parts = correlate(plan, turned, lag_matrices(taps), grad_parts, per_group, scale)
    back_parts = traded(back_parts, "ctx")
    return (
        projected,
        grad_query,
        *unpacked_parts(position, back_parts, key_gate, value_input, groups),
    )


def local(query_gate, key_gate, value_input, filter_taps, out_weight, out_grad):
    length, channels = query_gate.shape
    groups = filter_taps.shape[1]
    members = lax.axis_size("ctx")
    scale = 1.0 / math.sqrt(length * members)
    fits = channels // members % 128 == 0 and groups // members % 16 == 0
    body = in_line if lax.axis_size("tp") == 8 and fits else anywhere
    return body(
        query_gate, key_gate, value_input, filter_taps, out_weight, out_grad, members, scale
    )


def solution(mesh):
    both = P("ctx", "tp")
    return jax.shard_map(
        local,
        mesh=mesh,
        in_specs=(both, both, both, both, P("tp", None), both),
        out_specs=(both,) * 5,
        check_vma=False,
    )
```

```python
import functools
import math
import jax
import jax.numpy as jnp
from jax import lax
from jax.experimental import pallas as pl
from jax.experimental.pallas import tpu as pltpu
from jax.sharding import PartitionSpec as P

BLOCK = 128
POSITION = 8
NT = (((1,), (1,)), ((), ()))
COST = pl.CostEstimate(flops=2**20, bytes_accessed=2**12, transcendentals=0)


def lag_matrix(row, length):
    lanes = lax.broadcasted_iota(jnp.int32, (BLOCK, BLOCK), 1)
    rows = lax.broadcasted_iota(jnp.int32, (BLOCK, BLOCK), 0)
    spread = pltpu.roll(
        jnp.broadcast_to(row, (BLOCK, length)), 0, axis=1, stride=1, stride_axis=0
    )
    first = jnp.where(lanes >= rows, spread[:, :BLOCK], 0.0)
    return jnp.concatenate(
        [first.astype(jnp.bfloat16), spread[:, BLOCK:].astype(jnp.bfloat16)], axis=1
    )


def stacked(ref, start, rows, members, width):
    pieces = []
    for member in range(members):
        part = ref[member, pl.ds(start, rows), :]
        for at in range(0, width, BLOCK):
            pieces.append(part[:, at : at + BLOCK])
    return jnp.concatenate(pieces, axis=0)


def spread_out(ref, start, rows, value, members, width):
    per_member = width // BLOCK
    for member in range(members):
        base = member * per_member * rows
        parts = [value[base + i * rows : base + (i + 1) * rows] for i in range(per_member)]
        ref[member, pl.ds(start, rows), :] = jnp.concatenate(parts, axis=1)


def padded(groups):
    return -(-groups // 16) * 16


def load_taps(tap_scr, packed, at, width):
    groups, channels = tap_scr.shape[0], packed.shape[1]
    rows = padded(groups)
    parts = [
        packed[width + chunk * rows : width + (chunk + 1) * rows, :].astype(jnp.float32)
        for chunk in range(width // channels)
    ]
    start = pl.multiple_of(at * width, width)
    tap_scr[:, pl.ds(start, width)] = jnp.concatenate(parts, axis=1)[:groups]


def forward_kernel(members, per_group, width, plan_ref, *refs):
    inputs, outputs = refs[:members], refs[-members - 3 : -3]
    in_scr, tap_scr, out_scr = refs[-3:]
    position = plan_ref[POSITION]
    channels = inputs[0].shape[1]
    groups = channels // per_group
    length = members * width
    blocks = length // BLOCK
    for step in range(members):
        at = position ^ step
        in_scr[at] = inputs[step][:width].T
        load_taps(tap_scr, inputs[step], at, width)

    def one_group(group, carry):
        start = pl.multiple_of(group * per_group, per_group)
        lags = lag_matrix(tap_scr[pl.ds(group, 1), :], length)
        data = stacked(in_scr, start, per_group, members, width)
        total = [jnp.zeros((per_group, BLOCK), jnp.float32) for _ in range(blocks)]
        for offset in range(0, blocks, 2):
            rows = (blocks - offset) * per_group
            result = jnp.dot(
                data[:rows],
                lags[:, offset * BLOCK : (offset + 2) * BLOCK],
                preferred_element_type=jnp.float32,
            )
            for side in range(2):
                for source in range(blocks - offset - side):
                    total[source + offset + side] += result[
                        source * per_group : (source + 1) * per_group,
                        side * BLOCK : (side + 1) * BLOCK,
                    ]
        value = jnp.concatenate(total, axis=0).astype(jnp.bfloat16)
        spread_out(out_scr, start, per_group, value, members, width)
        return carry

    lax.fori_loop(0, groups, one_group, 0, unroll=8)
    for step in range(members):
        outputs[step][...] = out_scr[position ^ step].T


def backward_kernel(members, batch, per_group, scale, width, plan_ref, in_scr, lag_ref, *refs):
    cotangents = refs[:members]
    outputs = refs[-members - 4 : -4]
    cot_scr, out_scr, grad_scr, pad_scr = refs[-4:]
    position = plan_ref[POSITION]
    channels = cotangents[0].shape[1]
    groups = channels // per_group
    length = members * width
    blocks = length // BLOCK
    depth = blocks * per_group
    rows_of = lax.broadcasted_iota(jnp.int32, (BLOCK, BLOCK), 0)
    lanes_of = lax.broadcasted_iota(jnp.int32, (BLOCK, BLOCK), 1)
    mirror = (rows_of + lanes_of == BLOCK - 1).astype(jnp.bfloat16)

    @pl.when(pl.program_id(0) == 0)
    def _():
        for step in range(members):
            cot_scr[position ^ step] = cotangents[step][...].T
        pad_scr[...] = jnp.zeros_like(pad_scr)

    for local_group in range(batch):
        group = pl.program_id(0) * batch + local_group
        start = pl.multiple_of(group * per_group, per_group)
        lags = lag_ref[local_group]
        padded_cot = pad_scr.at[local_group]
        data = stacked(in_scr, start, per_group, members, width)
        cot = stacked(cot_scr, start, per_group, members, width)
        padded_cot[:depth, :BLOCK] = cot
        padded_cot[: depth - per_group, BLOCK:] = cot[per_group:]
        flipped = lax.dot_general(
            mirror, data, NT, preferred_element_type=jnp.float32
        ).astype(jnp.bfloat16)
        total = jnp.zeros((depth, BLOCK), jnp.float32)
        products = []
        for offset in range(0, blocks, 2):
            rows = depth - offset * per_group
            pair = padded_cot[offset * per_group : offset * per_group + depth, :]
            result = lax.dot_general(
                pair[:rows],
                lags[:, offset * BLOCK : (offset + 2) * BLOCK],
                NT,
                preferred_element_type=jnp.float32,
            )
            if rows < depth:
                result = jnp.concatenate(
                    [result, jnp.zeros((depth - rows, BLOCK), jnp.float32)], axis=0
                )
            total = total + result
            products.append(jnp.dot(flipped, pair, preferred_element_type=jnp.float32))
        spread_out(out_scr, start, per_group, total.astype(jnp.bfloat16), members, width)
        kept = jnp.where(rows_of + lanes_of >= BLOCK - 1, products[0][:, :BLOCK], 0.0)
        product = jnp.concatenate([kept, products[0][:, BLOCK:], *products[1:]], axis=1)
        product = pltpu.roll(
            product, length - (BLOCK - 1), axis=1, stride=1, stride_axis=0
        )
        grad_scr[pl.ds(group, 1), :] = jnp.sum(product, axis=0, keepdims=True) * scale

    @pl.when(pl.program_id(0) == pl.num_programs(0) - 1)
    def _():
        for step in range(members):
            at = position ^ step
            outputs[step][:width] = out_scr[at].T
            rows = padded(groups)
            whole = grad_scr[:, pl.ds(pl.multiple_of(at * width, width), width)]
            whole = whole.astype(jnp.bfloat16)
            if rows > groups:
                blank = jnp.zeros((rows - groups, width), jnp.bfloat16)
                whole = jnp.concatenate([whole, blank], axis=0)
            for chunk in range(width // channels):
                outputs[step][width + chunk * rows : width + (chunk + 1) * rows, :] = whole[
                    :, chunk * channels : (chunk + 1) * channels
                ]


def lag_kernel(taps_ref, out_ref):
    row = taps_ref[pl.ds(pl.program_id(0), 1), :]
    out_ref[0] = lag_matrix(row, taps_ref.shape[1])


VMEM = pl.BlockSpec(memory_space=pltpu.VMEM)
ANYWHERE = pl.BlockSpec(memory_space=pl.ANY)
SMEM = pl.BlockSpec(memory_space=pltpu.SMEM)


def convolve(plan, inputs, width, per_group, after=()):
    members = len(inputs)
    channels = inputs[0].shape[1]
    length = members * width
    *parts, turned, taps = pl.pallas_call(
        functools.partial(forward_kernel, members, per_group, width),
        out_shape=[jax.ShapeDtypeStruct((width, channels), jnp.bfloat16)] * members
        + [
            jax.ShapeDtypeStruct((members, channels, width), jnp.bfloat16),
            jax.ShapeDtypeStruct((channels // per_group, length), jnp.float32),
        ],
        in_specs=[SMEM] + [VMEM] * members + [ANYWHERE] * len(after),
        out_specs=[VMEM] * (members + 2),
        scratch_shapes=[pltpu.VMEM((members, channels, width), jnp.bfloat16)],
        compiler_params=pltpu.CompilerParams(vmem_limit_bytes=24 * 2**20),
        cost_estimate=pl.CostEstimate(flops=9*10**9, bytes_accessed=2**12, transcendentals=0),
        name="causal_conv",
    )(plan, *inputs, *after)
    return parts, turned, taps


def lag_matrices(taps):
    groups, length = taps.shape
    return pl.pallas_call(
        lag_kernel,
        out_shape=jax.ShapeDtypeStruct((groups, BLOCK, length), jnp.bfloat16),
        grid=(groups,),
        in_specs=[VMEM],
        out_specs=pl.BlockSpec((1, BLOCK, length), lambda i: (i, 0, 0)),
        compiler_params=pltpu.CompilerParams(vmem_limit_bytes=12 * 2**20),
        cost_estimate=COST,
        name="lag_matrices",
    )(taps)


def correlate(plan, turned, lags, cotangents, per_group, scale, after=()):
    members = len(cotangents)
    width, channels = cotangents[0].shape
    length = members * width
    groups = channels // per_group
    batch = 4 if groups % 4 == 0 else 1
    rows = width + padded(groups) * width // channels
    return pl.pallas_call(
        functools.partial(backward_kernel, members, batch, per_group, scale, width),
        out_shape=[jax.ShapeDtypeStruct((rows, channels), jnp.bfloat16)] * members,
        grid=(groups // batch,),
        in_specs=[SMEM, VMEM, pl.BlockSpec((batch, BLOCK, length), lambda i: (i, 0, 0))]
        + [VMEM] * members
        + [ANYWHERE] * len(after),
        out_specs=[VMEM] * members,
        scratch_shapes=[
            pltpu.VMEM((members, channels, width), jnp.bfloat16),
            pltpu.VMEM((members, channels, width), jnp.bfloat16),
            pltpu.VMEM((groups, length), jnp.float32),
            pltpu.VMEM((batch, 2 * length // BLOCK * per_group, 2 * BLOCK), jnp.bfloat16),
        ],
        compiler_params=pltpu.CompilerParams(vmem_limit_bytes=24 * 2**20),
        cost_estimate=pl.CostEstimate(flops=10**10, bytes_accessed=2**12, transcendentals=0),
        name="causal_conv_grads",
    )(plan, turned, lags, *cotangents, *after)


def in_hbm(array):
    return pltpu.with_memory_space_constraint(array, pltpu.HBM)


def prepare_kernel(members, scale, who_ref, key_ref, value_ref, taps_ref, *outputs):
    position = who_ref[0]
    step_no = pl.program_id(0)
    rows, channels = key_ref.shape
    share = channels // members
    groups = taps_ref.shape[0] // members
    total_width = taps_ref.shape[1]
    for step in range(members):
        at = position ^ step
        columns = pl.ds(pl.multiple_of(at * share, share), share)
        product = key_ref[:, columns].astype(jnp.float32) * value_ref[:, columns].astype(
            jnp.float32
        )
        here = pl.ds(pl.multiple_of(step_no * rows, rows), rows)
        outputs[step][here, :] = product.astype(jnp.bfloat16)

    @pl.when(step_no == 0)
    def _():
        for step in range(members):
            at = position ^ step
            taps = taps_ref[pl.ds(pl.multiple_of(at * groups, groups), groups), :]
            taps = (taps * scale).astype(jnp.bfloat16)
            for chunk in range(total_width // share):
                start = total_width + chunk * groups
                outputs[step][start : start + groups, :] = taps[
                    :, chunk * share : (chunk + 1) * share
                ]


def prepare(who, key_gate, value_input, filter_taps, members, scale):
    width, channels = key_gate.shape
    share = channels // members
    rows = width + filter_taps.size // members // share
    tile = width // 4
    part = pl.BlockSpec((tile, channels), lambda i: (i, 0))
    return pl.pallas_call(
        functools.partial(prepare_kernel, members, scale),
        out_shape=[jax.ShapeDtypeStruct((rows, share), jnp.bfloat16)] * members,
        grid=(4,),
        in_specs=[SMEM, part, part, pl.BlockSpec(filter_taps.shape[::-1], lambda i: (0, 0))],
        out_specs=[VMEM] * members,
        compiler_params=pltpu.CompilerParams(vmem_limit_bytes=24 * 2**20),
        cost_estimate=COST,
        name="gated_input",
    )(who, in_hbm(key_gate), in_hbm(value_input), in_hbm(filter_taps.T))


def finish_kernel(members, plan_ref, *refs):
    parts = refs[:members]
    key_ref, value_ref = refs[members : members + 2]
    summands = refs[members + 2 : -4]
    key_out, value_out, projected_out, taps_out = refs[-4:]
    position = plan_ref[POSITION]
    width = key_ref.shape[0]
    share = key_out.shape[1]
    groups = taps_out.shape[0] // members
    here = pl.ds(pl.multiple_of(pl.program_id(0) * share, share), share)
    projected = sum(ref[:, here].astype(jnp.float32) for ref in summands)
    projected_out[...] = projected.astype(jnp.bfloat16)
    for step in range(members):

        @pl.when(pl.program_id(0) == step)
        def _(step=step):
            at = position ^ step
            columns = pl.ds(pl.multiple_of(at * share, share), share)
            grad = parts[step][:width].astype(jnp.float32)
            key_out[...] = (grad * value_ref[:, columns].astype(jnp.float32)).astype(jnp.bfloat16)
            value_out[...] = (grad * key_ref[:, columns].astype(jnp.float32)).astype(jnp.bfloat16)
            taps = [
                parts[step][width + chunk * groups : width + (chunk + 1) * groups, :]
                for chunk in range(width // share)
            ]
            taps_out[pl.ds(pl.multiple_of(at * groups, groups), groups), :] = jnp.concatenate(
                taps, axis=1
            ).astype(jnp.float32)


def finished(plan, parts, key_gate, value_input, summands, groups):
    members = len(parts)
    width, channels = key_gate.shape
    share = channels // members
    array = jax.ShapeDtypeStruct((width, channels), jnp.bfloat16)
    swapped_piece = pl.BlockSpec((width, share), lambda i, at: (0, at[POSITION] ^ i))
    piece = pl.BlockSpec((width, share), lambda i, at: (0, i))
    grad_key, grad_value, projected, taps = pl.pallas_call(
        functools.partial(finish_kernel, members),
        out_shape=[array] * 3 + [jax.ShapeDtypeStruct((groups, width), jnp.float32)],
        grid_spec=pltpu.PrefetchScalarGridSpec(
            num_scalar_prefetch=1,
            grid=(members,),
            in_specs=[VMEM] * (members + 2 + len(summands)),
            out_specs=[swapped_piece, swapped_piece, piece, VMEM],
        ),
        compiler_params=pltpu.CompilerParams(vmem_limit_bytes=24 * 2**20),
        cost_estimate=COST,
        name="input_gradients",
    )(plan, *parts, key_gate, value_input, *summands)
    return projected, grad_key, grad_value, taps.T


def swapped(array, axis, step):
    size = lax.axis_size(axis)
    return lax.ppermute(array, axis, [(i, i ^ step) for i in range(size)])


def traded(pieces, axis):
    return [pieces[0]] + [swapped(pieces[step], axis, step) for step in range(1, len(pieces))]


def cut(array, position, members, axis):
    width = array.shape[axis] // members
    return [
        lax.dynamic_slice_in_dim(array, (position ^ step) * width, width, axis)
        for step in range(members)
    ]


def joined(pieces, position, axis):
    members = len(pieces)
    width = pieces[0].shape[axis]
    shape = list(pieces[0].shape)
    shape[axis] = members * width
    whole = jnp.zeros(shape, pieces[0].dtype)
    for step in range(members):
        whole = lax.dynamic_update_slice_in_dim(
            whole, pieces[step], (position ^ step) * width, axis
        )
    return whole


def wide(array):
    return array.astype(jnp.float32)


def hop(array, pairs):
    return lax.ppermute(
        array, "tp", [(2 * i + core, 2 * j + core) for i, j in pairs for core in range(2)]
    )


INWARD = ((0, 1), (3, 2))
ACROSS = ((1, 2), (2, 1))
OUTWARD = ((1, 0), (2, 3))
OWN, NEAR, MIDDLE, FAR = range(4)
IN_MIDDLE = POSITION + 1
CHIPS = ((0, 1, 2, 3), (1, 0, 3, 2), (2, 2, 1, 1), (3, 3, 0, 0))


def plan_kernel(who_ref, plan_ref):
    place = who_ref[1]
    chip, core = place // 2, place % 2
    for number, table in enumerate(CHIPS):
        source = jnp.where(
            chip < 2,
            jnp.where(chip == 0, table[0], table[1]),
            jnp.where(chip == 2, table[2], table[3]),
        )
        plan_ref[2 * number] = 2 * source + core
        plan_ref[2 * number + 1] = 2 * source + 1 - core
    plan_ref[POSITION] = who_ref[0]
    plan_ref[IN_MIDDLE] = ((chip == 1) | (chip == 2)).astype(jnp.int32)


def planned(who):
    return pl.pallas_call(
        plan_kernel,
        out_shape=jax.ShapeDtypeStruct((IN_MIDDLE + 1,), jnp.int32),
        in_specs=[SMEM],
        out_specs=SMEM,
        compiler_params=pltpu.CompilerParams(vmem_limit_bytes=2**20),
        cost_estimate=COST,
        name="plan",
    )(who)


def pass_kernel(*refs):
    del refs


def held_until(values, after):
    return pl.pallas_call(
        pass_kernel,
        out_shape=[jax.ShapeDtypeStruct(value.shape, value.dtype) for value in values],
        in_specs=[ANYWHERE] * (len(values) + len(after)),
        out_specs=[ANYWHERE] * len(values),
        input_output_aliases={number: number for number in range(len(values))},
        compiler_params=pltpu.CompilerParams(vmem_limit_bytes=2**20),
        cost_estimate=COST,
        name="held",
    )(*values, *after)


def add_kernel(*refs):
    refs[-1][...] = sum(wide(ref[...]) for ref in refs[:-1]).astype(jnp.bfloat16)


def added(*arrays):
    rows, width = arrays[0].shape
    part = pl.BlockSpec((rows // 4, width), lambda i: (i, 0))
    return pl.pallas_call(
        add_kernel,
        out_shape=jax.ShapeDtypeStruct((rows, width), jnp.bfloat16),
        grid=(4,),
        in_specs=[part] * len(arrays),
        out_specs=part,
        compiler_params=pltpu.CompilerParams(vmem_limit_bytes=8 * 2**20),
        cost_estimate=COST,
        name="added",
    )(*arrays)


def choice_kernel(plan_ref, middle_ref, end_ref, *refs):
    out_ref = refs[-1]
    in_middle = plan_ref[IN_MIDDLE] == 1

    @pl.when(in_middle)
    def _():
        out_ref[...] = middle_ref[...]

    @pl.when(jnp.logical_not(in_middle))
    def _():
        out_ref[...] = end_ref[...]


def chosen(plan, in_middle, at_end, after=()):
    return pl.pallas_call(
        choice_kernel,
        out_shape=jax.ShapeDtypeStruct(at_end.shape, at_end.dtype),
        in_specs=[SMEM, VMEM, VMEM] + [ANYWHERE] * len(after),
        out_specs=VMEM,
        compiler_params=pltpu.CompilerParams(vmem_limit_bytes=2**20),
        cost_estimate=COST,
        name="chosen",
    )(plan, in_middle, at_end, *after)


def gate_kernel(members, plan_ref, *refs):
    parts = refs[:members]
    query_ref, gated_ref, conv_ref = refs[members], *refs[-2:]
    position = plan_ref[POSITION]
    share = parts[0].shape[1]
    for step in range(members):
        columns = pl.ds(pl.multiple_of((position ^ step) * share, share), share)
        conv = parts[step][...]
        conv_ref[:, columns] = conv
        gated_ref[:, columns] = (wide(conv) * wide(query_ref[:, columns])).astype(jnp.bfloat16)


def gated(plan, parts, query_gate, after):
    array = jax.ShapeDtypeStruct(query_gate.shape, jnp.bfloat16)
    return pl.pallas_call(
        functools.partial(gate_kernel, len(parts)),
        out_shape=[array, array],
        in_specs=[SMEM] + [VMEM] * (len(parts) + 1) + [ANYWHERE] * len(after),
        out_specs=[VMEM] * 2,
        compiler_params=pltpu.CompilerParams(vmem_limit_bytes=8 * 2**20),
        cost_estimate=COST,
        name="gated_output",
    )(plan, *parts, query_gate, *after)


def spans(widths, start, stop):
    found, begin = [], 0
    for number, width in enumerate(widths):
        low, high = max(start, begin), min(stop, begin + width)
        if low < high:
            found.append((number, slice(low - begin, high - begin), slice(low - start, high - start)))
        begin += width
    return found


def product_kernel(steps, more_widths, out_widths, _, data_ref, weight_ref, *refs):
    more, outputs = refs[: len(more_widths)], refs[-len(out_widths) :]
    product = jnp.dot(data_ref[...], weight_ref[...], preferred_element_type=jnp.float32)
    width = product.shape[1]
    for step in range(steps):
        start, stop = step * width, (step + 1) * width

        @pl.when(pl.program_id(0) == step)
        def _(start=start, stop=stop):
            total = product
            if more:
                parts = [wide(more[n][:, there]) for n, there, _ in spans(more_widths, start, stop)]
                total = total + jnp.concatenate(parts, axis=1)
            total = total.astype(jnp.bfloat16)
            for n, there, here in spans(out_widths, start, stop):
                outputs[n][:, there] = total[:, here]


def column_products(
    plan, data, out_weight, first, count, other, more=(), after=(), tiles=1, widths=()
):
    rows, depth = data.shape
    width = data.shape[1]
    tile = width // tiles
    steps = count * tiles
    widths = tuple(widths) or (width,) * count

    def weights(i, at):
        return 0, at[2 * (first - i // tiles) + other] * tiles + i % tiles

    return pl.pallas_call(
        functools.partial(product_kernel, steps, [part.shape[1] for part in more], widths),
        out_shape=[jax.ShapeDtypeStruct((rows, part), jnp.bfloat16) for part in widths],
        grid_spec=pltpu.PrefetchScalarGridSpec(
            num_scalar_prefetch=1,
            grid=(steps,),
            in_specs=[VMEM, pl.BlockSpec((depth, tile), weights)]
            + [VMEM] * len(more)
            + [ANYWHERE] * len(after),
            out_specs=[VMEM] * len(widths),
        ),
        compiler_params=pltpu.CompilerParams(vmem_limit_bytes=16 * 2**20),
        cost_estimate=COST,
        name="projection_blocks",
    )(plan, data, in_hbm(out_weight), *more, *after)


def cotangent_kernel(count, begin, _, weight_ref, *refs):
    blocks, refs = refs[:count], refs[count:]
    step = pl.program_id(0)
    total = refs[-1]

    for number, block in enumerate(blocks):

        @pl.when(step == number)
        def _(number=number, block=block):
            product = lax.dot_general(
                block[...], weight_ref[...], NT, preferred_element_type=jnp.float32
            )
            if number == 0:
                total[...] = product if begin else refs[0][...] + product
            else:
                total[...] += product


def last_cotangent_kernel(
    members, plan_ref, weight_ref, block_ref, start_ref, conv_ref, query_ref, *refs
):
    parts, cot_scr = refs[-1 - members : -1], refs[-1]
    grad_ref = refs[-2 - members]
    product = lax.dot_general(
        block_ref[...], weight_ref[...], NT, preferred_element_type=jnp.float32
    )
    dgated = wide((start_ref[...] + product).astype(jnp.bfloat16))
    grad_ref[...] = (dgated * wide(conv_ref[...])).astype(jnp.bfloat16)
    cot_scr[...] = (dgated * wide(query_ref[...])).astype(jnp.bfloat16)
    share = parts[0].shape[1]
    odd = plan_ref[POSITION] % 2
    for step in range(0, members, 2):

        @pl.when(pl.program_id(0) == step // 2)
        def _(step=step):
            parts[step][...] = cot_scr[:, pl.ds(pl.multiple_of(odd * share, share), share)]
            parts[step + 1][...] = cot_scr[
                :, pl.ds(pl.multiple_of((1 - odd) * share, share), share)
            ]


def last_cotangents(
    plan, first, block, out_weight, start, convolved, query_gate, members, after
):
    rows, width = block.shape
    channels = out_weight.shape[0]
    share = channels // members
    pair = pl.BlockSpec((rows, 2 * share), lambda i, at: (0, at[POSITION] // 2 ^ i))
    return pl.pallas_call(
        functools.partial(last_cotangent_kernel, members),
        out_shape=[jax.ShapeDtypeStruct((rows, channels), jnp.bfloat16)]
        + [jax.ShapeDtypeStruct((rows, share), jnp.bfloat16)] * members,
        grid_spec=pltpu.PrefetchScalarGridSpec(
            num_scalar_prefetch=1,
            grid=(members // 2,),
            in_specs=[
                pl.BlockSpec((2 * share, width), lambda i, at: (at[POSITION] // 2 ^ i, at[first])),
                VMEM,
                pair,
                pair,
                pair,
            ]
            + [ANYWHERE] * len(after),
            out_specs=[pair] + [VMEM] * members,
            scratch_shapes=[pltpu.VMEM((rows, 2 * share), jnp.bfloat16)],
        ),
        compiler_params=pltpu.CompilerParams(vmem_limit_bytes=24 * 2**20),
        cost_estimate=COST,
        name="cotangent_last",
    )(plan, in_hbm(out_weight), block, start, convolved, query_gate, *after)


def both(blocks):
    return [part for block in blocks for part in (block, swapped(block, "tp", 1))]


def cotangent_products(plan, first, parts, out_weight, start=None, after=()):
    rows, width = parts[0].shape
    channels = out_weight.shape[0]
    count = len(parts)
    begin = start is None
    extra = () if begin else (start,)
    return pl.pallas_call(
        functools.partial(cotangent_kernel, count, begin),
        out_shape=jax.ShapeDtypeStruct((rows, channels), jnp.float32),
        grid_spec=pltpu.PrefetchScalarGridSpec(
            num_scalar_prefetch=1,
            grid=(count,),
            in_specs=[pl.BlockSpec((channels, width), lambda i, at: (0, at[first + i]))]
            + [VMEM] * (count + len(extra))
            + [ANYWHERE] * len(after),
            out_specs=VMEM,
        ),
        compiler_params=pltpu.CompilerParams(vmem_limit_bytes=16 * 2**20),
        cost_estimate=COST,
        name="cotangent_blocks",
    )(plan, in_hbm(out_weight), *parts, *extra, *after)


def packed_parts(position, key_gate, value_input, filter_taps, members, scale):
    length, channels = key_gate.shape
    share = channels // members
    product_in = (wide(key_gate) * wide(value_input)).astype(jnp.bfloat16)
    tap_rows = (filter_taps * scale).astype(jnp.bfloat16).T
    owned = filter_taps.shape[1] // members
    chunks = length // share
    packed = []
    pieces = cut(product_in, position, members, 1)
    for piece, taps in zip(pieces, cut(tap_rows, position, members, 0)):
        taps = taps.reshape(owned, chunks, share).transpose(1, 0, 2)
        taps = jnp.pad(taps, ((0, 0), (0, padded(owned) - owned), (0, 0)))
        packed.append(jnp.concatenate([piece, taps.reshape(-1, share)], axis=0))
    return packed


def unpacked_parts(position, parts, key_gate, value_input, groups):
    length, channels = key_gate.shape
    members = len(parts)
    share = channels // members
    owned = groups // members
    chunks = length // share
    input_grad = wide(joined([part[:length] for part in parts], position, 1))
    filter_parts = [
        part[length:]
        .reshape(chunks, padded(owned), share)[:, :owned]
        .transpose(1, 0, 2)
        .reshape(owned, length)
        for part in parts
    ]
    grad_filter = wide(joined(filter_parts, position, 0)).T
    grad_key = (input_grad * wide(value_input)).astype(jnp.bfloat16)
    grad_value = (input_grad * wide(key_gate)).astype(jnp.bfloat16)
    return grad_key, grad_value, grad_filter


def in_line(
    query_gate, key_gate, value_input, filter_taps, out_weight, out_grad, members, scale
):
    length, channels = query_gate.shape
    groups = filter_taps.shape[1]
    per_group = channels // groups
    who = jnp.stack([lax.axis_index("ctx"), lax.axis_index("tp")]).astype(jnp.int32)
    plan = planned(who)
    near, cross = hop(out_grad, INWARD + OUTWARD), hop(out_grad, ACROSS)
    total = cotangent_products(plan, 2 * OWN, both([out_grad]), out_weight)

    packed = prepare(who, key_gate, value_input, filter_taps, members, scale)
    input_parts = traded(packed, "ctx")
    conv_parts, turned, taps = convolve(plan, input_parts, length, per_group, (total,))
    conv_parts = traded(conv_parts, "ctx")
    lags = lag_matrices(taps)
    gated_out, convolved = gated(plan, conv_parts, query_gate, ())
    near, cross = held_until([near, cross], (lags,))
    far, skip = hop(near, ACROSS), hop(cross, OUTWARD)

    def product(first, count, other, more=(), after=(), tiles=1, widths=()):
        return column_products(
            plan, gated_out, out_weight, first, count, other, more, after, tiles, widths
        )

    quarter, half = channels // 4, channels // 2
    given_far = product(FAR, 1, 1, tiles=2, widths=(3 * quarter, quarter))
    received = [swapped(part, "tp", 1) for part in given_far]
    (first,) = product(FAR, 1, 0, received, tiles=2)
    one = hop(first, INWARD)
    far, skip, near = held_until([far, skip, near], (first,))
    last = hop(far, OUTWARD)
    given_middle = product(MIDDLE, 1, 1, (), (far,), tiles=2, widths=(half, half))
    received = [swapped(part, "tp", 1) for part in given_middle]
    (second,) = product(MIDDLE, 1, 0, received, tiles=2)
    middle_block = added(cross, skip)
    given_near, given_own = product(NEAR, 2, 1, (), (second,))
    (one,) = held_until([one], (given_near,))
    through = added(first, one)
    two_a = hop(through, ACROSS)
    (second,) = held_until([second], (one,))
    two_b = hop(second, INWARD)
    blocks = [near, swapped(near, "tp", 1), middle_block]
    total = cotangent_products(plan, 2 * NEAR, blocks, out_weight, total, after=(through,))
    last, middle_block = held_until([last, middle_block], (total,))
    far_block, far_other = both([added(far, last)])
    blocks = [swapped(middle_block, "tp", 1), far_block]
    total = cotangent_products(plan, 2 * MIDDLE + 1, blocks, out_weight, total)
    received = [swapped(part, "tp", 1) for part in (given_near, given_own)]
    grad_query, *grad_parts = last_cotangents(
        plan, 2 * FAR + 1, far_other, out_weight, total, convolved, query_gate, members, received
    )
    third, own = product(NEAR, 2, 0, received, (grad_parts[0],))
    grad_parts = traded(grad_parts, "ctx")

    two_a, two_b = held_until([two_a, two_b], (own,))
    third, second = added(third, two_a), added(second, two_b)
    back_parts = correlate(plan, turned, lags, grad_parts, per_group, scale, (third, second))
    summands = (own, hop(third, OUTWARD + INWARD), hop(second, ACROSS))
    back_parts = traded(back_parts, "ctx")
    projected, *gradients = finished(
        plan, back_parts, key_gate, value_input, summands, groups
    )
    return projected, grad_query, *gradients


def anywhere(
    query_gate, key_gate, value_input, filter_taps, out_weight, out_grad, members, scale
):
    length, channels = query_gate.shape
    groups = filter_taps.shape[1]
    per_group = channels // groups
    position = lax.axis_index("ctx")
    plan = jnp.full((POSITION + 1,), position, jnp.int32)
    packed = packed_parts(position, key_gate, value_input, filter_taps, members, scale)
    input_parts = traded(packed, "ctx")
    conv_parts, turned, taps = convolve(plan, input_parts, length, per_group)
    conv_parts = traded(conv_parts, "ctx")
    convolved = joined(conv_parts, position, 1)
    gated_out = (wide(query_gate) * wide(convolved)).astype(jnp.bfloat16)
    partial_value = jnp.dot(gated_out, out_weight, preferred_element_type=jnp.float32)
    projected = lax.psum_scatter(
        partial_value.astype(jnp.bfloat16), "tp", scatter_dimension=1, tiled=True
    )
    dgated = jnp.einsum(
        "tk,ck->tc",
        lax.all_gather(out_grad, "tp", axis=1, tiled=True),
        out_weight,
        preferred_element_type=jnp.float32,
    ).astype(jnp.bfloat16)
    grad_query = (wide(dgated) * wide(convolved)).astype(jnp.bfloat16)
    conv_grad = (wide(dgated) * wide(query_gate)).astype(jnp.bfloat16)
    grad_parts = traded(cut(conv_grad, position, members, 1), "ctx")
    back_parts = correlate(plan, turned, lag_matrices(taps), grad_parts, per_group, scale)
    back_parts = traded(back_parts, "ctx")
    return (
        projected,
        grad_query,
        *unpacked_parts(position, back_parts, key_gate, value_input, groups),
    )


def local(query_gate, key_gate, value_input, filter_taps, out_weight, out_grad):
    length, channels = query_gate.shape
    groups = filter_taps.shape[1]
    members = lax.axis_size("ctx")
    scale = 1.0 / math.sqrt(length * members)
    fits = channels // members % 128 == 0 and groups // members % 16 == 0
    body = in_line if lax.axis_size("tp") == 8 and fits else anywhere
    return body(
        query_gate, key_gate, value_input, filter_taps, out_weight, out_grad, members, scale
    )


def solution(mesh):
    both = P("ctx", "tp")
    return jax.shard_map(
        local,
        mesh=mesh,
        in_specs=(both, both, both, both, P("tp", None), both),
        out_specs=(both,) * 5,
        check_vma=False,
    )
```

```python
import functools
import math
import jax
import jax.numpy as jnp
from jax import lax
from jax.experimental import pallas as pl
from jax.experimental.pallas import tpu as pltpu
from jax.sharding import PartitionSpec as P

BLOCK = 128
POSITION = 8
NT = (((1,), (1,)), ((), ()))
COST = pl.CostEstimate(flops=2**20, bytes_accessed=2**12, transcendentals=0)


def lag_matrix(row, length):
    lanes = lax.broadcasted_iota(jnp.int32, (BLOCK, BLOCK), 1)
    rows = lax.broadcasted_iota(jnp.int32, (BLOCK, BLOCK), 0)
    spread = pltpu.roll(
        jnp.broadcast_to(row, (BLOCK, length)), 0, axis=1, stride=1, stride_axis=0
    )
    first = jnp.where(lanes >= rows, spread[:, :BLOCK], 0.0)
    return jnp.concatenate(
        [first.astype(jnp.bfloat16), spread[:, BLOCK:].astype(jnp.bfloat16)], axis=1
    )


def stacked(ref, start, rows, members, width):
    pieces = []
    for member in range(members):
        part = ref[member, pl.ds(start, rows), :]
        for at in range(0, width, BLOCK):
            pieces.append(part[:, at : at + BLOCK])
    return jnp.concatenate(pieces, axis=0)


def spread_out(ref, start, rows, value, members, width):
    per_member = width // BLOCK
    for member in range(members):
        base = member * per_member * rows
        parts = [value[base + i * rows : base + (i + 1) * rows] for i in range(per_member)]
        ref[member, pl.ds(start, rows), :] = jnp.concatenate(parts, axis=1)


def padded(groups):
    return -(-groups // 16) * 16


def load_taps(tap_scr, packed, at, width):
    groups, channels = tap_scr.shape[0], packed.shape[1]
    rows = padded(groups)
    parts = [
        packed[width + chunk * rows : width + (chunk + 1) * rows, :].astype(jnp.float32)
        for chunk in range(width // channels)
    ]
    start = pl.multiple_of(at * width, width)
    tap_scr[:, pl.ds(start, width)] = jnp.concatenate(parts, axis=1)[:groups]


def forward_kernel(members, per_group, width, plan_ref, *refs):
    inputs, outputs = refs[:members], refs[-members - 3 : -3]
    in_scr, tap_scr, out_scr = refs[-3:]
    position = plan_ref[POSITION]
    channels = inputs[0].shape[1]
    groups = channels // per_group
    length = members * width
    blocks = length // BLOCK
    for step in range(members):
        at = position ^ step
        in_scr[at] = inputs[step][:width].T
        load_taps(tap_scr, inputs[step], at, width)

    def one_group(group, carry):
        start = pl.multiple_of(group * per_group, per_group)
        lags = lag_matrix(tap_scr[pl.ds(group, 1), :], length)
        data = stacked(in_scr, start, per_group, members, width)
        total = [jnp.zeros((per_group, BLOCK), jnp.float32) for _ in range(blocks)]
        for offset in range(0, blocks, 2):
            rows = (blocks - offset) * per_group
            result = jnp.dot(
                data[:rows],
                lags[:, offset * BLOCK : (offset + 2) * BLOCK],
                preferred_element_type=jnp.float32,
            )
            for side in range(2):
                for source in range(blocks - offset - side):
                    total[source + offset + side] += result[
                        source * per_group : (source + 1) * per_group,
                        side * BLOCK : (side + 1) * BLOCK,
                    ]
        value = jnp.concatenate(total, axis=0).astype(jnp.bfloat16)
        spread_out(out_scr, start, per_group, value, members, width)
        return carry

    lax.fori_loop(0, groups, one_group, 0, unroll=8)
    for step in range(members):
        outputs[step][...] = out_scr[position ^ step].T


def backward_kernel(members, batch, per_group, scale, width, plan_ref, in_scr, lag_ref, *refs):
    cotangents = refs[:members]
    outputs = refs[-members - 4 : -4]
    cot_scr, out_scr, grad_scr, pad_scr = refs[-4:]
    position = plan_ref[POSITION]
    channels = cotangents[0].shape[1]
    groups = channels // per_group
    length = members * width
    blocks = length // BLOCK
    depth = blocks * per_group
    rows_of = lax.broadcasted_iota(jnp.int32, (BLOCK, BLOCK), 0)
    lanes_of = lax.broadcasted_iota(jnp.int32, (BLOCK, BLOCK), 1)
    mirror = (rows_of + lanes_of == BLOCK - 1).astype(jnp.bfloat16)

    @pl.when(pl.program_id(0) == 0)
    def _():
        for step in range(members):
            cot_scr[position ^ step] = cotangents[step][...].T
        pad_scr[...] = jnp.zeros_like(pad_scr)

    for local_group in range(batch):
        group = pl.program_id(0) * batch + local_group
        start = pl.multiple_of(group * per_group, per_group)
        lags = lag_ref[local_group]
        padded_cot = pad_scr.at[local_group]
        data = stacked(in_scr, start, per_group, members, width)
        cot = stacked(cot_scr, start, per_group, members, width)
        padded_cot[:depth, :BLOCK] = cot
        padded_cot[: depth - per_group, BLOCK:] = cot[per_group:]
        flipped = lax.dot_general(
            mirror, data, NT, preferred_element_type=jnp.float32
        ).astype(jnp.bfloat16)
        total = jnp.zeros((depth, BLOCK), jnp.float32)
        products = []
        for offset in range(0, blocks, 2):
            rows = depth - offset * per_group
            pair = padded_cot[offset * per_group : offset * per_group + depth, :]
            result = lax.dot_general(
                pair[:rows],
                lags[:, offset * BLOCK : (offset + 2) * BLOCK],
                NT,
                preferred_element_type=jnp.float32,
            )
            if rows < depth:
                result = jnp.concatenate(
                    [result, jnp.zeros((depth - rows, BLOCK), jnp.float32)], axis=0
                )
            total = total + result
            products.append(jnp.dot(flipped, pair, preferred_element_type=jnp.float32))
        spread_out(out_scr, start, per_group, total.astype(jnp.bfloat16), members, width)
        kept = jnp.where(rows_of + lanes_of >= BLOCK - 1, products[0][:, :BLOCK], 0.0)
        product = jnp.concatenate([kept, products[0][:, BLOCK:], *products[1:]], axis=1)
        product = pltpu.roll(
            product, length - (BLOCK - 1), axis=1, stride=1, stride_axis=0
        )
        grad_scr[pl.ds(group, 1), :] = jnp.sum(product, axis=0, keepdims=True) * scale

    @pl.when(pl.program_id(0) == pl.num_programs(0) - 1)
    def _():
        for step in range(members):
            at = position ^ step
            outputs[step][:width] = out_scr[at].T
            rows = padded(groups)
            whole = grad_scr[:, pl.ds(pl.multiple_of(at * width, width), width)]
            whole = whole.astype(jnp.bfloat16)
            if rows > groups:
                blank = jnp.zeros((rows - groups, width), jnp.bfloat16)
                whole = jnp.concatenate([whole, blank], axis=0)
            for chunk in range(width // channels):
                outputs[step][width + chunk * rows : width + (chunk + 1) * rows, :] = whole[
                    :, chunk * channels : (chunk + 1) * channels
                ]


def lag_kernel(taps_ref, out_ref):
    row = taps_ref[pl.ds(pl.program_id(0), 1), :]
    out_ref[0] = lag_matrix(row, taps_ref.shape[1])


VMEM = pl.BlockSpec(memory_space=pltpu.VMEM)
ANYWHERE = pl.BlockSpec(memory_space=pl.ANY)
SMEM = pl.BlockSpec(memory_space=pltpu.SMEM)


def convolve(plan, inputs, width, per_group, after=()):
    members = len(inputs)
    channels = inputs[0].shape[1]
    length = members * width
    *parts, turned, taps = pl.pallas_call(
        functools.partial(forward_kernel, members, per_group, width),
        out_shape=[jax.ShapeDtypeStruct((width, channels), jnp.bfloat16)] * members
        + [
            jax.ShapeDtypeStruct((members, channels, width), jnp.bfloat16),
            jax.ShapeDtypeStruct((channels // per_group, length), jnp.float32),
        ],
        in_specs=[SMEM] + [VMEM] * members + [ANYWHERE] * len(after),
        out_specs=[VMEM] * (members + 2),
        scratch_shapes=[pltpu.VMEM((members, channels, width), jnp.bfloat16)],
        compiler_params=pltpu.CompilerParams(vmem_limit_bytes=24 * 2**20),
        cost_estimate=pl.CostEstimate(flops=9*10**9, bytes_accessed=2**12, transcendentals=0),
        name="causal_conv",
    )(plan, *inputs, *after)
    return parts, turned, taps


def lag_matrices(taps):
    groups, length = taps.shape
    return pl.pallas_call(
        lag_kernel,
        out_shape=jax.ShapeDtypeStruct((groups, BLOCK, length), jnp.bfloat16),
        grid=(groups,),
        in_specs=[VMEM],
        out_specs=pl.BlockSpec((1, BLOCK, length), lambda i: (i, 0, 0)),
        compiler_params=pltpu.CompilerParams(vmem_limit_bytes=12 * 2**20),
        cost_estimate=COST,
        name="lag_matrices",
    )(taps)


def correlate(plan, turned, lags, cotangents, per_group, scale, after=()):
    members = len(cotangents)
    width, channels = cotangents[0].shape
    length = members * width
    groups = channels // per_group
    batch = 4 if groups % 4 == 0 else 1
    rows = width + padded(groups) * width // channels
    return pl.pallas_call(
        functools.partial(backward_kernel, members, batch, per_group, scale, width),
        out_shape=[jax.ShapeDtypeStruct((rows, channels), jnp.bfloat16)] * members,
        grid=(groups // batch,),
        in_specs=[SMEM, VMEM, pl.BlockSpec((batch, BLOCK, length), lambda i: (i, 0, 0))]
        + [VMEM] * members
        + [ANYWHERE] * len(after),
        out_specs=[VMEM] * members,
        scratch_shapes=[
            pltpu.VMEM((members, channels, width), jnp.bfloat16),
            pltpu.VMEM((members, channels, width), jnp.bfloat16),
            pltpu.VMEM((groups, length), jnp.float32),
            pltpu.VMEM((batch, 2 * length // BLOCK * per_group, 2 * BLOCK), jnp.bfloat16),
        ],
        compiler_params=pltpu.CompilerParams(vmem_limit_bytes=24 * 2**20),
        cost_estimate=pl.CostEstimate(flops=10**10, bytes_accessed=2**12, transcendentals=0),
        name="causal_conv_grads",
    )(plan, turned, lags, *cotangents, *after)


def in_hbm(array):
    return pltpu.with_memory_space_constraint(array, pltpu.HBM)


def prepare_kernel(members, scale, who_ref, key_ref, value_ref, taps_ref, *outputs):
    position = who_ref[0]
    step_no = pl.program_id(0)
    rows, channels = key_ref.shape
    share = channels // members
    groups = taps_ref.shape[0] // members
    total_width = taps_ref.shape[1]
    for step in range(members):
        at = position ^ step
        columns = pl.ds(pl.multiple_of(at * share, share), share)
        product = key_ref[:, columns].astype(jnp.float32) * value_ref[:, columns].astype(
            jnp.float32
        )
        here = pl.ds(pl.multiple_of(step_no * rows, rows), rows)
        outputs[step][here, :] = product.astype(jnp.bfloat16)

    @pl.when(step_no == 0)
    def _():
        for step in range(members):
            at = position ^ step
            taps = taps_ref[pl.ds(pl.multiple_of(at * groups, groups), groups), :]
            taps = (taps * scale).astype(jnp.bfloat16)
            for chunk in range(total_width // share):
                start = total_width + chunk * groups
                outputs[step][start : start + groups, :] = taps[
                    :, chunk * share : (chunk + 1) * share
                ]


def prepare(who, key_gate, value_input, filter_taps, members, scale):
    width, channels = key_gate.shape
    share = channels // members
    rows = width + filter_taps.size // members // share
    tile = width // 4
    part = pl.BlockSpec((tile, channels), lambda i: (i, 0))
    return pl.pallas_call(
        functools.partial(prepare_kernel, members, scale),
        out_shape=[jax.ShapeDtypeStruct((rows, share), jnp.bfloat16)] * members,
        grid=(4,),
        in_specs=[SMEM, part, part, pl.BlockSpec(filter_taps.shape[::-1], lambda i: (0, 0))],
        out_specs=[VMEM] * members,
        compiler_params=pltpu.CompilerParams(vmem_limit_bytes=24 * 2**20),
        cost_estimate=COST,
        name="gated_input",
    )(who, in_hbm(key_gate), in_hbm(value_input), in_hbm(filter_taps.T))


def finish_kernel(members, plan_ref, *refs):
    parts = refs[:members]
    key_ref, value_ref = refs[members : members + 2]
    summands = refs[members + 2 : -4]
    key_out, value_out, projected_out, taps_out = refs[-4:]
    position = plan_ref[POSITION]
    width = key_ref.shape[0]
    share = key_out.shape[1]
    groups = taps_out.shape[0] // members
    here = pl.ds(pl.multiple_of(pl.program_id(0) * share, share), share)
    projected = sum(ref[:, here].astype(jnp.float32) for ref in summands)
    projected_out[...] = projected.astype(jnp.bfloat16)
    for step in range(members):

        @pl.when(pl.program_id(0) == step)
        def _(step=step):
            at = position ^ step
            columns = pl.ds(pl.multiple_of(at * share, share), share)
            grad = parts[step][:width].astype(jnp.float32)
            key_out[...] = (grad * value_ref[:, columns].astype(jnp.float32)).astype(jnp.bfloat16)
            value_out[...] = (grad * key_ref[:, columns].astype(jnp.float32)).astype(jnp.bfloat16)
            taps = [
                parts[step][width + chunk * groups : width + (chunk + 1) * groups, :]
                for chunk in range(width // share)
            ]
            taps_out[pl.ds(pl.multiple_of(at * groups, groups), groups), :] = jnp.concatenate(
                taps, axis=1
            ).astype(jnp.float32)


def finished(plan, parts, key_gate, value_input, summands, groups):
    members = len(parts)
    width, channels = key_gate.shape
    share = channels // members
    array = jax.ShapeDtypeStruct((width, channels), jnp.bfloat16)
    swapped_piece = pl.BlockSpec((width, share), lambda i, at: (0, at[POSITION] ^ i))
    piece = pl.BlockSpec((width, share), lambda i, at: (0, i))
    grad_key, grad_value, projected, taps = pl.pallas_call(
        functools.partial(finish_kernel, members),
        out_shape=[array] * 3 + [jax.ShapeDtypeStruct((groups, width), jnp.float32)],
        grid_spec=pltpu.PrefetchScalarGridSpec(
            num_scalar_prefetch=1,
            grid=(members,),
            in_specs=[VMEM] * (members + 2 + len(summands)),
            out_specs=[swapped_piece, swapped_piece, piece, VMEM],
        ),
        compiler_params=pltpu.CompilerParams(vmem_limit_bytes=24 * 2**20),
        cost_estimate=COST,
        name="input_gradients",
    )(plan, *parts, key_gate, value_input, *summands)
    return projected, grad_key, grad_value, taps.T


def swapped(array, axis, step):
    size = lax.axis_size(axis)
    return lax.ppermute(array, axis, [(i, i ^ step) for i in range(size)])


def traded(pieces, axis):
    return [pieces[0]] + [swapped(pieces[step], axis, step) for step in range(1, len(pieces))]


def cut(array, position, members, axis):
    width = array.shape[axis] // members
    return [
        lax.dynamic_slice_in_dim(array, (position ^ step) * width, width, axis)
        for step in range(members)
    ]


def joined(pieces, position, axis):
    members = len(pieces)
    width = pieces[0].shape[axis]
    shape = list(pieces[0].shape)
    shape[axis] = members * width
    whole = jnp.zeros(shape, pieces[0].dtype)
    for step in range(members):
        whole = lax.dynamic_update_slice_in_dim(
            whole, pieces[step], (position ^ step) * width, axis
        )
    return whole


def wide(array):
    return array.astype(jnp.float32)


def hop(array, pairs):
    return lax.ppermute(
        array, "tp", [(2 * i + core, 2 * j + core) for i, j in pairs for core in range(2)]
    )


INWARD = ((0, 1), (3, 2))
ACROSS = ((1, 2), (2, 1))
OUTWARD = ((1, 0), (2, 3))
OWN, NEAR, MIDDLE, FAR = range(4)
IN_MIDDLE = POSITION + 1
CHIPS = ((0, 1, 2, 3), (1, 0, 3, 2), (2, 2, 1, 1), (3, 3, 0, 0))


def plan_kernel(who_ref, plan_ref):
    place = who_ref[1]
    chip, core = place // 2, place % 2
    for number, table in enumerate(CHIPS):
        source = jnp.where(
            chip < 2,
            jnp.where(chip == 0, table[0], table[1]),
            jnp.where(chip == 2, table[2], table[3]),
        )
        plan_ref[2 * number] = 2 * source + core
        plan_ref[2 * number + 1] = 2 * source + 1 - core
    plan_ref[POSITION] = who_ref[0]
    plan_ref[IN_MIDDLE] = ((chip == 1) | (chip == 2)).astype(jnp.int32)


def planned(who):
    return pl.pallas_call(
        plan_kernel,
        out_shape=jax.ShapeDtypeStruct((IN_MIDDLE + 1,), jnp.int32),
        in_specs=[SMEM],
        out_specs=SMEM,
        compiler_params=pltpu.CompilerParams(vmem_limit_bytes=2**20),
        cost_estimate=COST,
        name="plan",
    )(who)


def pass_kernel(*refs):
    del refs


def held_until(values, after):
    return pl.pallas_call(
        pass_kernel,
        out_shape=[jax.ShapeDtypeStruct(value.shape, value.dtype) for value in values],
        in_specs=[ANYWHERE] * (len(values) + len(after)),
        out_specs=[ANYWHERE] * len(values),
        input_output_aliases={number: number for number in range(len(values))},
        compiler_params=pltpu.CompilerParams(vmem_limit_bytes=2**20),
        cost_estimate=COST,
        name="held",
    )(*values, *after)


def add_kernel(*refs):
    refs[-1][...] = sum(wide(ref[...]) for ref in refs[:-1]).astype(jnp.bfloat16)


def added(*arrays):
    rows, width = arrays[0].shape
    part = pl.BlockSpec((rows // 4, width), lambda i: (i, 0))
    return pl.pallas_call(
        add_kernel,
        out_shape=jax.ShapeDtypeStruct((rows, width), jnp.bfloat16),
        grid=(4,),
        in_specs=[part] * len(arrays),
        out_specs=part,
        compiler_params=pltpu.CompilerParams(vmem_limit_bytes=8 * 2**20),
        cost_estimate=COST,
        name="added",
    )(*arrays)


def choice_kernel(plan_ref, middle_ref, end_ref, *refs):
    out_ref = refs[-1]
    in_middle = plan_ref[IN_MIDDLE] == 1

    @pl.when(in_middle)
    def _():
        out_ref[...] = middle_ref[...]

    @pl.when(jnp.logical_not(in_middle))
    def _():
        out_ref[...] = end_ref[...]


def chosen(plan, in_middle, at_end, after=()):
    return pl.pallas_call(
        choice_kernel,
        out_shape=jax.ShapeDtypeStruct(at_end.shape, at_end.dtype),
        in_specs=[SMEM, VMEM, VMEM] + [ANYWHERE] * len(after),
        out_specs=VMEM,
        compiler_params=pltpu.CompilerParams(vmem_limit_bytes=2**20),
        cost_estimate=COST,
        name="chosen",
    )(plan, in_middle, at_end, *after)


def gate_kernel(members, plan_ref, *refs):
    parts = refs[:members]
    query_ref, gated_ref, conv_ref = refs[members], *refs[-2:]
    position = plan_ref[POSITION]
    share = parts[0].shape[1]
    for step in range(members):
        columns = pl.ds(pl.multiple_of((position ^ step) * share, share), share)
        conv = parts[step][...]
        conv_ref[:, columns] = conv
        gated_ref[:, columns] = (wide(conv) * wide(query_ref[:, columns])).astype(jnp.bfloat16)


def gated(plan, parts, query_gate, after):
    array = jax.ShapeDtypeStruct(query_gate.shape, jnp.bfloat16)
    return pl.pallas_call(
        functools.partial(gate_kernel, len(parts)),
        out_shape=[array, array],
        in_specs=[SMEM] + [VMEM] * (len(parts) + 1) + [ANYWHERE] * len(after),
        out_specs=[VMEM] * 2,
        compiler_params=pltpu.CompilerParams(vmem_limit_bytes=8 * 2**20),
        cost_estimate=COST,
        name="gated_output",
    )(plan, *parts, query_gate, *after)


def spans(widths, start, stop):
    found, begin = [], 0
    for number, width in enumerate(widths):
        low, high = max(start, begin), min(stop, begin + width)
        if low < high:
            found.append((number, slice(low - begin, high - begin), slice(low - start, high - start)))
        begin += width
    return found


def product_kernel(steps, more_widths, out_widths, _, data_ref, weight_ref, *refs):
    more, outputs = refs[: len(more_widths)], refs[-len(out_widths) :]
    product = jnp.dot(data_ref[...], weight_ref[...], preferred_element_type=jnp.float32)
    width = product.shape[1]
    for step in range(steps):
        start, stop = step * width, (step + 1) * width

        @pl.when(pl.program_id(0) == step)
        def _(start=start, stop=stop):
            total = product
            if more:
                parts = [wide(more[n][:, there]) for n, there, _ in spans(more_widths, start, stop)]
                total = total + jnp.concatenate(parts, axis=1)
            total = total.astype(jnp.bfloat16)
            for n, there, here in spans(out_widths, start, stop):
                outputs[n][:, there] = total[:, here]


def column_products(
    plan, data, out_weight, first, count, other, more=(), after=(), tiles=1, widths=()
):
    rows, depth = data.shape
    width = data.shape[1]
    tile = width // tiles
    steps = count * tiles
    widths = tuple(widths) or (width,) * count

    def weights(i, at):
        return 0, at[2 * (first - i // tiles) + other] * tiles + i % tiles

    return pl.pallas_call(
        functools.partial(product_kernel, steps, [part.shape[1] for part in more], widths),
        out_shape=[jax.ShapeDtypeStruct((rows, part), jnp.bfloat16) for part in widths],
        grid_spec=pltpu.PrefetchScalarGridSpec(
            num_scalar_prefetch=1,
            grid=(steps,),
            in_specs=[VMEM, pl.BlockSpec((depth, tile), weights)]
            + [VMEM] * len(more)
            + [ANYWHERE] * len(after),
            out_specs=[VMEM] * len(widths),
        ),
        compiler_params=pltpu.CompilerParams(vmem_limit_bytes=16 * 2**20),
        cost_estimate=COST,
        name="projection_blocks",
    )(plan, data, in_hbm(out_weight), *more, *after)


def cotangent_kernel(count, begin, _, weight_ref, *refs):
    blocks, refs = refs[:count], refs[count:]
    step = pl.program_id(0)
    total = refs[-1]

    for number, block in enumerate(blocks):

        @pl.when(step == number)
        def _(number=number, block=block):
            product = lax.dot_general(
                block[...], weight_ref[...], NT, preferred_element_type=jnp.float32
            )
            if number == 0:
                total[...] = product if begin else refs[0][...] + product
            else:
                total[...] += product


def last_cotangent_kernel(
    members, plan_ref, weight_ref, block_ref, start_ref, conv_ref, query_ref, *refs
):
    parts, cot_scr = refs[-1 - members : -1], refs[-1]
    grad_ref = refs[-2 - members]
    product = lax.dot_general(
        block_ref[...], weight_ref[...], NT, preferred_element_type=jnp.float32
    )
    dgated = wide((start_ref[...] + product).astype(jnp.bfloat16))
    grad_ref[...] = (dgated * wide(conv_ref[...])).astype(jnp.bfloat16)
    cot_scr[...] = (dgated * wide(query_ref[...])).astype(jnp.bfloat16)
    share = parts[0].shape[1]
    odd = plan_ref[POSITION] % 2
    for step in range(0, members, 2):

        @pl.when(pl.program_id(0) == step // 2)
        def _(step=step):
            parts[step][...] = cot_scr[:, pl.ds(pl.multiple_of(odd * share, share), share)]
            parts[step + 1][...] = cot_scr[
                :, pl.ds(pl.multiple_of((1 - odd) * share, share), share)
            ]


def last_cotangents(
    plan, first, block, out_weight, start, convolved, query_gate, members, after
):
    rows, width = block.shape
    channels = out_weight.shape[0]
    share = channels // members
    pair = pl.BlockSpec((rows, 2 * share), lambda i, at: (0, at[POSITION] // 2 ^ i))
    return pl.pallas_call(
        functools.partial(last_cotangent_kernel, members),
        out_shape=[jax.ShapeDtypeStruct((rows, channels), jnp.bfloat16)]
        + [jax.ShapeDtypeStruct((rows, share), jnp.bfloat16)] * members,
        grid_spec=pltpu.PrefetchScalarGridSpec(
            num_scalar_prefetch=1,
            grid=(members // 2,),
            in_specs=[
                pl.BlockSpec((2 * share, width), lambda i, at: (at[POSITION] // 2 ^ i, at[first])),
                VMEM,
                pair,
                pair,
                pair,
            ]
            + [ANYWHERE] * len(after),
            out_specs=[pair] + [VMEM] * members,
            scratch_shapes=[pltpu.VMEM((rows, 2 * share), jnp.bfloat16)],
        ),
        compiler_params=pltpu.CompilerParams(vmem_limit_bytes=24 * 2**20),
        cost_estimate=COST,
        name="cotangent_last",
    )(plan, in_hbm(out_weight), block, start, convolved, query_gate, *after)


def both(blocks):
    return [part for block in blocks for part in (block, swapped(block, "tp", 1))]


def cotangent_products(plan, first, parts, out_weight, start=None, after=()):
    rows, width = parts[0].shape
    channels = out_weight.shape[0]
    count = len(parts)
    begin = start is None
    extra = () if begin else (start,)
    return pl.pallas_call(
        functools.partial(cotangent_kernel, count, begin),
        out_shape=jax.ShapeDtypeStruct((rows, channels), jnp.float32),
        grid_spec=pltpu.PrefetchScalarGridSpec(
            num_scalar_prefetch=1,
            grid=(count,),
            in_specs=[pl.BlockSpec((channels, width), lambda i, at: (0, at[first + i]))]
            + [VMEM] * (count + len(extra))
            + [ANYWHERE] * len(after),
            out_specs=VMEM,
        ),
        compiler_params=pltpu.CompilerParams(vmem_limit_bytes=16 * 2**20),
        cost_estimate=COST,
        name="cotangent_blocks",
    )(plan, in_hbm(out_weight), *parts, *extra, *after)


def packed_parts(position, key_gate, value_input, filter_taps, members, scale):
    length, channels = key_gate.shape
    share = channels // members
    product_in = (wide(key_gate) * wide(value_input)).astype(jnp.bfloat16)
    tap_rows = (filter_taps * scale).astype(jnp.bfloat16).T
    owned = filter_taps.shape[1] // members
    chunks = length // share
    packed = []
    pieces = cut(product_in, position, members, 1)
    for piece, taps in zip(pieces, cut(tap_rows, position, members, 0)):
        taps = taps.reshape(owned, chunks, share).transpose(1, 0, 2)
        taps = jnp.pad(taps, ((0, 0), (0, padded(owned) - owned), (0, 0)))
        packed.append(jnp.concatenate([piece, taps.reshape(-1, share)], axis=0))
    return packed


def unpacked_parts(position, parts, key_gate, value_input, groups):
    length, channels = key_gate.shape
    members = len(parts)
    share = channels // members
    owned = groups // members
    chunks = length // share
    input_grad = wide(joined([part[:length] for part in parts], position, 1))
    filter_parts = [
        part[length:]
        .reshape(chunks, padded(owned), share)[:, :owned]
        .transpose(1, 0, 2)
        .reshape(owned, length)
        for part in parts
    ]
    grad_filter = wide(joined(filter_parts, position, 0)).T
    grad_key = (input_grad * wide(value_input)).astype(jnp.bfloat16)
    grad_value = (input_grad * wide(key_gate)).astype(jnp.bfloat16)
    return grad_key, grad_value, grad_filter


def in_line(
    query_gate, key_gate, value_input, filter_taps, out_weight, out_grad, members, scale
):
    length, channels = query_gate.shape
    groups = filter_taps.shape[1]
    per_group = channels // groups
    who = jnp.stack([lax.axis_index("ctx"), lax.axis_index("tp")]).astype(jnp.int32)
    plan = planned(who)
    near, cross = hop(out_grad, INWARD + OUTWARD), hop(out_grad, ACROSS)
    total = cotangent_products(plan, 2 * OWN, both([out_grad]), out_weight)

    packed = prepare(who, key_gate, value_input, filter_taps, members, scale)
    input_parts = traded(packed, "ctx")
    conv_parts, turned, taps = convolve(plan, input_parts, length, per_group, (total,))
    conv_parts = traded(conv_parts, "ctx")
    lags = lag_matrices(taps)
    gated_out, convolved = gated(plan, conv_parts, query_gate, ())
    (near,) = held_until([near], (lags,))
    far = hop(near, ACROSS)
    (cross,) = held_until([cross], (near,))
    skip = hop(cross, OUTWARD)

    def product(first, count, other, more=(), after=(), tiles=1, widths=()):
        return column_products(
            plan, gated_out, out_weight, first, count, other, more, after, tiles, widths
        )

    quarter, half = channels // 4, channels // 2
    given_far = product(FAR, 1, 1, tiles=2, widths=(3 * quarter, quarter))
    received = [swapped(part, "tp", 1) for part in given_far]
    (first,) = product(FAR, 1, 0, received, tiles=2)
    one = hop(first, INWARD)
    far, skip, near = held_until([far, skip, near], (first,))
    last = hop(far, OUTWARD)
    given_middle = product(MIDDLE, 1, 1, (), (far,), tiles=2, widths=(half, half))
    received = [swapped(part, "tp", 1) for part in given_middle]
    (second,) = product(MIDDLE, 1, 0, received, tiles=2)
    middle_block = added(cross, skip)
    given_near, given_own = product(NEAR, 2, 1, (), (second,))
    (one,) = held_until([one], (given_near,))
    through = added(first, one)
    two_a = hop(through, ACROSS)
    (second,) = held_until([second], (one,))
    two_b = hop(second, INWARD)
    blocks = [near, swapped(near, "tp", 1), middle_block]
    total = cotangent_products(plan, 2 * NEAR, blocks, out_weight, total)
    last, middle_block = held_until([last, middle_block], (through, total))
    far_block, far_other = both([added(far, last)])
    blocks = [swapped(middle_block, "tp", 1), far_block]
    total = cotangent_products(plan, 2 * MIDDLE + 1, blocks, out_weight, total)
    received = [swapped(part, "tp", 1) for part in (given_near, given_own)]
    grad_query, *grad_parts = last_cotangents(
        plan, 2 * FAR + 1, far_other, out_weight, total, convolved, query_gate, members, received
    )
    third, own = product(NEAR, 2, 0, received, (grad_parts[0],))
    grad_parts = traded(grad_parts, "ctx")

    two_a, two_b = held_until([two_a, two_b], (own,))
    third, second = added(third, two_a), added(second, two_b)
    back_parts = correlate(plan, turned, lags, grad_parts, per_group, scale, (third, second))
    summands = (own, hop(third, OUTWARD + INWARD), hop(second, ACROSS))
    back_parts = traded(back_parts, "ctx")
    projected, *gradients = finished(
        plan, back_parts, key_gate, value_input, summands, groups
    )
    return projected, grad_query, *gradients


def anywhere(
    query_gate, key_gate, value_input, filter_taps, out_weight, out_grad, members, scale
):
    length, channels = query_gate.shape
    groups = filter_taps.shape[1]
    per_group = channels // groups
    position = lax.axis_index("ctx")
    plan = jnp.full((POSITION + 1,), position, jnp.int32)
    packed = packed_parts(position, key_gate, value_input, filter_taps, members, scale)
    input_parts = traded(packed, "ctx")
    conv_parts, turned, taps = convolve(plan, input_parts, length, per_group)
    conv_parts = traded(conv_parts, "ctx")
    convolved = joined(conv_parts, position, 1)
    gated_out = (wide(query_gate) * wide(convolved)).astype(jnp.bfloat16)
    partial_value = jnp.dot(gated_out, out_weight, preferred_element_type=jnp.float32)
    projected = lax.psum_scatter(
        partial_value.astype(jnp.bfloat16), "tp", scatter_dimension=1, tiled=True
    )
    dgated = jnp.einsum(
        "tk,ck->tc",
        lax.all_gather(out_grad, "tp", axis=1, tiled=True),
        out_weight,
        preferred_element_type=jnp.float32,
    ).astype(jnp.bfloat16)
    grad_query = (wide(dgated) * wide(convolved)).astype(jnp.bfloat16)
    conv_grad = (wide(dgated) * wide(query_gate)).astype(jnp.bfloat16)
    grad_parts = traded(cut(conv_grad, position, members, 1), "ctx")
    back_parts = correlate(plan, turned, lag_matrices(taps), grad_parts, per_group, scale)
    back_parts = traded(back_parts, "ctx")
    return (
        projected,
        grad_query,
        *unpacked_parts(position, back_parts, key_gate, value_input, groups),
    )


def local(query_gate, key_gate, value_input, filter_taps, out_weight, out_grad):
    length, channels = query_gate.shape
    groups = filter_taps.shape[1]
    members = lax.axis_size("ctx")
    scale = 1.0 / math.sqrt(length * members)
    fits = channels // members % 128 == 0 and groups // members % 16 == 0
    body = in_line if lax.axis_size("tp") == 8 and fits else anywhere
    return body(
        query_gate, key_gate, value_input, filter_taps, out_weight, out_grad, members, scale
    )


def solution(mesh):
    both = P("ctx", "tp")
    return jax.shard_map(
        local,
        mesh=mesh,
        in_specs=(both, both, both, both, P("tp", None), both),
        out_specs=(both,) * 5,
        check_vma=False,
    )
```

```python
import functools
import math
import jax
import jax.numpy as jnp
from jax import lax
from jax.experimental import pallas as pl
from jax.experimental.pallas import tpu as pltpu
from jax.sharding import PartitionSpec as P

BLOCK = 128
POSITION = 8
NT = (((1,), (1,)), ((), ()))
COST = pl.CostEstimate(flops=2**20, bytes_accessed=2**12, transcendentals=0)


def lag_matrix(row, length):
    lanes = lax.broadcasted_iota(jnp.int32, (BLOCK, BLOCK), 1)
    rows = lax.broadcasted_iota(jnp.int32, (BLOCK, BLOCK), 0)
    spread = pltpu.roll(
        jnp.broadcast_to(row, (BLOCK, length)), 0, axis=1, stride=1, stride_axis=0
    )
    first = jnp.where(lanes >= rows, spread[:, :BLOCK], 0.0)
    return jnp.concatenate(
        [first.astype(jnp.bfloat16), spread[:, BLOCK:].astype(jnp.bfloat16)], axis=1
    )


def stacked(ref, start, rows, members, width):
    pieces = []
    for member in range(members):
        part = ref[member, pl.ds(start, rows), :]
        for at in range(0, width, BLOCK):
            pieces.append(part[:, at : at + BLOCK])
    return jnp.concatenate(pieces, axis=0)


def spread_out(ref, start, rows, value, members, width):
    per_member = width // BLOCK
    for member in range(members):
        base = member * per_member * rows
        parts = [value[base + i * rows : base + (i + 1) * rows] for i in range(per_member)]
        ref[member, pl.ds(start, rows), :] = jnp.concatenate(parts, axis=1)


def padded(groups):
    return -(-groups // 16) * 16


def load_taps(tap_scr, packed, at, width):
    groups, channels = tap_scr.shape[0], packed.shape[1]
    rows = padded(groups)
    parts = [
        packed[width + chunk * rows : width + (chunk + 1) * rows, :].astype(jnp.float32)
        for chunk in range(width // channels)
    ]
    start = pl.multiple_of(at * width, width)
    tap_scr[:, pl.ds(start, width)] = jnp.concatenate(parts, axis=1)[:groups]


def forward_kernel(members, per_group, width, plan_ref, *refs):
    inputs, outputs = refs[:members], refs[-members - 3 : -3]
    in_scr, tap_scr, out_scr = refs[-3:]
    position = plan_ref[POSITION]
    channels = inputs[0].shape[1]
    groups = channels // per_group
    length = members * width
    blocks = length // BLOCK
    for step in range(members):
        at = position ^ step
        in_scr[at] = inputs[step][:width].T
        load_taps(tap_scr, inputs[step], at, width)

    def one_group(group, carry):
        start = pl.multiple_of(group * per_group, per_group)
        lags = lag_matrix(tap_scr[pl.ds(group, 1), :], length)
        data = stacked(in_scr, start, per_group, members, width)
        total = [jnp.zeros((per_group, BLOCK), jnp.float32) for _ in range(blocks)]
        for offset in range(0, blocks, 2):
            rows = (blocks - offset) * per_group
            result = jnp.dot(
                data[:rows],
                lags[:, offset * BLOCK : (offset + 2) * BLOCK],
                preferred_element_type=jnp.float32,
            )
            for side in range(2):
                for source in range(blocks - offset - side):
                    total[source + offset + side] += result[
                        source * per_group : (source + 1) * per_group,
                        side * BLOCK : (side + 1) * BLOCK,
                    ]
        value = jnp.concatenate(total, axis=0).astype(jnp.bfloat16)
        spread_out(out_scr, start, per_group, value, members, width)
        return carry

    lax.fori_loop(0, groups, one_group, 0, unroll=16)
    for step in range(members):
        outputs[step][...] = out_scr[position ^ step].T


def backward_kernel(members, batch, per_group, scale, width, plan_ref, in_scr, lag_ref, *refs):
    cotangents = refs[:members]
    outputs = refs[-members - 4 : -4]
    cot_scr, out_scr, grad_scr, pad_scr = refs[-4:]
    position = plan_ref[POSITION]
    channels = cotangents[0].shape[1]
    groups = channels // per_group
    length = members * width
    blocks = length // BLOCK
    depth = blocks * per_group
    rows_of = lax.broadcasted_iota(jnp.int32, (BLOCK, BLOCK), 0)
    lanes_of = lax.broadcasted_iota(jnp.int32, (BLOCK, BLOCK), 1)
    mirror = (rows_of + lanes_of == BLOCK - 1).astype(jnp.bfloat16)

    @pl.when(pl.program_id(0) == 0)
    def _():
        for step in range(members):
            cot_scr[position ^ step] = cotangents[step][...].T
        tail = pad_scr.at[:, depth - per_group :, :]
        tail[...] = jnp.zeros(tail.shape, jnp.bfloat16)

    for local_group in range(batch):
        group = pl.program_id(0) * batch + local_group
        start = pl.multiple_of(group * per_group, per_group)
        lags = lag_ref[local_group]
        padded_cot = pad_scr.at[local_group]
        data = stacked(in_scr, start, per_group, members, width)
        cot = stacked(cot_scr, start, per_group, members, width)
        padded_cot[:depth, :BLOCK] = cot
        padded_cot[: depth - per_group, BLOCK:] = cot[per_group:]
        flipped = lax.dot_general(
            mirror, data, NT, preferred_element_type=jnp.float32
        ).astype(jnp.bfloat16)
        total = jnp.zeros((depth, BLOCK), jnp.float32)
        products = []
        for offset in range(0, blocks, 2):
            rows = depth - offset * per_group
            pair = padded_cot[offset * per_group : offset * per_group + depth, :]
            result = lax.dot_general(
                pair[:rows],
                lags[:, offset * BLOCK : (offset + 2) * BLOCK],
                NT,
                preferred_element_type=jnp.float32,
            )
            if rows < depth:
                result = jnp.concatenate(
                    [result, jnp.zeros((depth - rows, BLOCK), jnp.float32)], axis=0
                )
            total = total + result
            products.append(jnp.dot(flipped, pair, preferred_element_type=jnp.float32))
        spread_out(out_scr, start, per_group, total.astype(jnp.bfloat16), members, width)
        kept = jnp.where(rows_of + lanes_of >= BLOCK - 1, products[0][:, :BLOCK], 0.0)
        product = jnp.concatenate([kept, products[0][:, BLOCK:], *products[1:]], axis=1)
        product = pltpu.roll(
            product, length - (BLOCK - 1), axis=1, stride=1, stride_axis=0
        )
        grad_scr[pl.ds(group, 1), :] = jnp.sum(product, axis=0, keepdims=True) * scale

    @pl.when(pl.program_id(0) == pl.num_programs(0) - 1)
    def _():
        for step in range(members):
            at = position ^ step
            outputs[step][:width] = out_scr[at].T
            rows = padded(groups)
            whole = grad_scr[:, pl.ds(pl.multiple_of(at * width, width), width)]
            whole = whole.astype(jnp.bfloat16)
            if rows > groups:
                blank = jnp.zeros((rows - groups, width), jnp.bfloat16)
                whole = jnp.concatenate([whole, blank], axis=0)
            for chunk in range(width // channels):
                outputs[step][width + chunk * rows : width + (chunk + 1) * rows, :] = whole[
                    :, chunk * channels : (chunk + 1) * channels
                ]


def lag_kernel(taps_ref, out_ref):
    row = taps_ref[pl.ds(pl.program_id(0), 1), :]
    out_ref[0] = lag_matrix(row, taps_ref.shape[1])


VMEM = pl.BlockSpec(memory_space=pltpu.VMEM)
ANYWHERE = pl.BlockSpec(memory_space=pl.ANY)
SMEM = pl.BlockSpec(memory_space=pltpu.SMEM)


def convolve(plan, inputs, width, per_group, after=()):
    members = len(inputs)
    channels = inputs[0].shape[1]
    length = members * width
    *parts, turned, taps = pl.pallas_call(
        functools.partial(forward_kernel, members, per_group, width),
        out_shape=[jax.ShapeDtypeStruct((width, channels), jnp.bfloat16)] * members
        + [
            jax.ShapeDtypeStruct((members, channels, width), jnp.bfloat16),
            jax.ShapeDtypeStruct((channels // per_group, length), jnp.float32),
        ],
        in_specs=[SMEM] + [VMEM] * members + [ANYWHERE] * len(after),
        out_specs=[VMEM] * (members + 2),
        scratch_shapes=[pltpu.VMEM((members, channels, width), jnp.bfloat16)],
        compiler_params=pltpu.CompilerParams(vmem_limit_bytes=24 * 2**20),
        cost_estimate=COST,
        name="causal_conv",
    )(plan, *inputs, *after)
    return parts, turned, taps


def lag_matrices(taps):
    groups, length = taps.shape
    return pl.pallas_call(
        lag_kernel,
        out_shape=jax.ShapeDtypeStruct((groups, BLOCK, length), jnp.bfloat16),
        grid=(groups,),
        in_specs=[VMEM],
        out_specs=pl.BlockSpec((1, BLOCK, length), lambda i: (i, 0, 0)),
        compiler_params=pltpu.CompilerParams(vmem_limit_bytes=12 * 2**20),
        cost_estimate=COST,
        name="lag_matrices",
    )(taps)


def correlate(plan, turned, lags, cotangents, per_group, scale, after=()):
    members = len(cotangents)
    width, channels = cotangents[0].shape
    length = members * width
    groups = channels // per_group
    batch = next(size for size in (8, 4, 1) if groups % size == 0)
    rows = width + padded(groups) * width // channels
    return pl.pallas_call(
        functools.partial(backward_kernel, members, batch, per_group, scale, width),
        out_shape=[jax.ShapeDtypeStruct((rows, channels), jnp.bfloat16)] * members,
        grid=(groups // batch,),
        in_specs=[SMEM, VMEM, pl.BlockSpec((batch, BLOCK, length), lambda i: (i, 0, 0))]
        + [VMEM] * members
        + [ANYWHERE] * len(after),
        out_specs=[VMEM] * members,
        scratch_shapes=[
            pltpu.VMEM((members, channels, width), jnp.bfloat16),
            pltpu.VMEM((members, channels, width), jnp.bfloat16),
            pltpu.VMEM((groups, length), jnp.float32),
            pltpu.VMEM((batch, 2 * length // BLOCK * per_group, 2 * BLOCK), jnp.bfloat16),
        ],
        compiler_params=pltpu.CompilerParams(vmem_limit_bytes=32 * 2**20),
        cost_estimate=pl.CostEstimate(flops=10**10, bytes_accessed=2**12, transcendentals=0),
        name="causal_conv_grads",
    )(plan, turned, lags, *cotangents, *after)


def in_hbm(array):
    return pltpu.with_memory_space_constraint(array, pltpu.HBM)


def prepare_kernel(members, scale, who_ref, key_ref, value_ref, taps_ref, *outputs):
    position = who_ref[0]
    step_no = pl.program_id(0)
    rows, channels = key_ref.shape
    share = channels // members
    groups = taps_ref.shape[0] // members
    total_width = taps_ref.shape[1]
    for step in range(members):
        at = position ^ step
        columns = pl.ds(pl.multiple_of(at * share, share), share)
        product = key_ref[:, columns].astype(jnp.float32) * value_ref[:, columns].astype(
            jnp.float32
        )
        here = pl.ds(pl.multiple_of(step_no * rows, rows), rows)
        outputs[step][here, :] = product.astype(jnp.bfloat16)

    @pl.when(step_no == 0)
    def _():
        for step in range(members):
            at = position ^ step
            taps = taps_ref[pl.ds(pl.multiple_of(at * groups, groups), groups), :]
            taps = (taps * scale).astype(jnp.bfloat16)
            for chunk in range(total_width // share):
                start = total_width + chunk * groups
                outputs[step][start : start + groups, :] = taps[
                    :, chunk * share : (chunk + 1) * share
                ]


def prepare(who, key_gate, value_input, filter_taps, members, scale):
    width, channels = key_gate.shape
    share = channels // members
    rows = width + filter_taps.size // members // share
    tile = width // 4
    part = pl.BlockSpec((tile, channels), lambda i: (i, 0))
    return pl.pallas_call(
        functools.partial(prepare_kernel, members, scale),
        out_shape=[jax.ShapeDtypeStruct((rows, share), jnp.bfloat16)] * members,
        grid=(4,),
        in_specs=[SMEM, part, part, pl.BlockSpec(filter_taps.shape[::-1], lambda i: (0, 0))],
        out_specs=[VMEM] * members,
        compiler_params=pltpu.CompilerParams(vmem_limit_bytes=24 * 2**20),
        cost_estimate=COST,
        name="gated_input",
    )(who, in_hbm(key_gate), in_hbm(value_input), in_hbm(filter_taps.T))


def finish_kernel(members, plan_ref, *refs):
    parts = refs[:members]
    key_ref, value_ref = refs[members : members + 2]
    summands = refs[members + 2 : -4]
    key_out, value_out, projected_out, taps_out = refs[-4:]
    position = plan_ref[POSITION]
    width = key_ref.shape[0]
    share = key_out.shape[1]
    groups = taps_out.shape[0] // members
    here = pl.ds(pl.multiple_of(pl.program_id(0) * share, share), share)
    projected = sum(ref[:, here].astype(jnp.float32) for ref in summands)
    projected_out[...] = projected.astype(jnp.bfloat16)
    for step in range(members):

        @pl.when(pl.program_id(0) == step)
        def _(step=step):
            at = position ^ step
            columns = pl.ds(pl.multiple_of(at * share, share), share)
            grad = parts[step][:width].astype(jnp.float32)
            key_out[...] = (grad * value_ref[:, columns].astype(jnp.float32)).astype(jnp.bfloat16)
            value_out[...] = (grad * key_ref[:, columns].astype(jnp.float32)).astype(jnp.bfloat16)
            taps = [
                parts[step][width + chunk * groups : width + (chunk + 1) * groups, :]
                for chunk in range(width // share)
            ]
            taps_out[pl.ds(pl.multiple_of(at * groups, groups), groups), :] = jnp.concatenate(
                taps, axis=1
            ).astype(jnp.float32)


def finished(plan, parts, key_gate, value_input, summands, groups):
    members = len(parts)
    width, channels = key_gate.shape
    share = channels // members
    array = jax.ShapeDtypeStruct((width, channels), jnp.bfloat16)
    swapped_piece = pl.BlockSpec((width, share), lambda i, at: (0, at[POSITION] ^ i))
    piece = pl.BlockSpec((width, share), lambda i, at: (0, i))
    grad_key, grad_value, projected, taps = pl.pallas_call(
        functools.partial(finish_kernel, members),
        out_shape=[array] * 3 + [jax.ShapeDtypeStruct((groups, width), jnp.float32)],
        grid_spec=pltpu.PrefetchScalarGridSpec(
            num_scalar_prefetch=1,
            grid=(members,),
            in_specs=[VMEM] * (members + 2 + len(summands)),
            out_specs=[swapped_piece, swapped_piece, piece, VMEM],
        ),
        compiler_params=pltpu.CompilerParams(vmem_limit_bytes=24 * 2**20),
        cost_estimate=COST,
        name="input_gradients",
    )(plan, *parts, key_gate, value_input, *summands)
    return projected, grad_key, grad_value, taps.T


def swapped(array, axis, step):
    size = lax.axis_size(axis)
    return lax.ppermute(array, axis, [(i, i ^ step) for i in range(size)])


def traded(pieces, axis):
    return [pieces[0]] + [swapped(pieces[step], axis, step) for step in range(1, len(pieces))]


def cut(array, position, members, axis):
    width = array.shape[axis] // members
    return [
        lax.dynamic_slice_in_dim(array, (position ^ step) * width, width, axis)
        for step in range(members)
    ]


def joined(pieces, position, axis):
    members = len(pieces)
    width = pieces[0].shape[axis]
    shape = list(pieces[0].shape)
    shape[axis] = members * width
    whole = jnp.zeros(shape, pieces[0].dtype)
    for step in range(members):
        whole = lax.dynamic_update_slice_in_dim(
            whole, pieces[step], (position ^ step) * width, axis
        )
    return whole


def wide(array):
    return array.astype(jnp.float32)


def hop(array, pairs):
    return lax.ppermute(
        array, "tp", [(2 * i + core, 2 * j + core) for i, j in pairs for core in range(2)]
    )


INWARD = ((0, 1), (3, 2))
ACROSS = ((1, 2), (2, 1))
OUTWARD = ((1, 0), (2, 3))
OWN, NEAR, MIDDLE, FAR = range(4)
IN_MIDDLE = POSITION + 1
CHIPS = ((0, 1, 2, 3), (1, 0, 3, 2), (2, 2, 1, 1), (3, 3, 0, 0))


def plan_kernel(who_ref, plan_ref):
    place = who_ref[1]
    chip, core = place // 2, place % 2
    for number, table in enumerate(CHIPS):
        source = jnp.where(
            chip < 2,
            jnp.where(chip == 0, table[0], table[1]),
            jnp.where(chip == 2, table[2], table[3]),
        )
        plan_ref[2 * number] = 2 * source + core
        plan_ref[2 * number + 1] = 2 * source + 1 - core
    plan_ref[POSITION] = who_ref[0]
    plan_ref[IN_MIDDLE] = ((chip == 1) | (chip == 2)).astype(jnp.int32)


def planned(who):
    return pl.pallas_call(
        plan_kernel,
        out_shape=jax.ShapeDtypeStruct((IN_MIDDLE + 1,), jnp.int32),
        in_specs=[SMEM],
        out_specs=SMEM,
        compiler_params=pltpu.CompilerParams(vmem_limit_bytes=2**20),
        cost_estimate=COST,
        name="plan",
    )(who)


def pass_kernel(*refs):
    del refs


def held_until(values, after):
    return pl.pallas_call(
        pass_kernel,
        out_shape=[jax.ShapeDtypeStruct(value.shape, value.dtype) for value in values],
        in_specs=[ANYWHERE] * (len(values) + len(after)),
        out_specs=[ANYWHERE] * len(values),
        input_output_aliases={number: number for number in range(len(values))},
        compiler_params=pltpu.CompilerParams(vmem_limit_bytes=2**20),
        cost_estimate=COST,
        name="held",
    )(*values, *after)


def add_kernel(*refs):
    refs[-1][...] = sum(wide(ref[...]) for ref in refs[:-1]).astype(jnp.bfloat16)


def added(*arrays):
    rows, width = arrays[0].shape
    part = pl.BlockSpec((rows // 4, width), lambda i: (i, 0))
    return pl.pallas_call(
        add_kernel,
        out_shape=jax.ShapeDtypeStruct((rows, width), jnp.bfloat16),
        grid=(4,),
        in_specs=[part] * len(arrays),
        out_specs=part,
        compiler_params=pltpu.CompilerParams(vmem_limit_bytes=8 * 2**20),
        cost_estimate=COST,
        name="added",
    )(*arrays)


def choice_kernel(plan_ref, middle_ref, end_ref, *refs):
    out_ref = refs[-1]
    in_middle = plan_ref[IN_MIDDLE] == 1

    @pl.when(in_middle)
    def _():
        out_ref[...] = middle_ref[...]

    @pl.when(jnp.logical_not(in_middle))
    def _():
        out_ref[...] = end_ref[...]


def chosen(plan, in_middle, at_end, after=()):
    return pl.pallas_call(
        choice_kernel,
        out_shape=jax.ShapeDtypeStruct(at_end.shape, at_end.dtype),
        in_specs=[SMEM, VMEM, VMEM] + [ANYWHERE] * len(after),
        out_specs=VMEM,
        compiler_params=pltpu.CompilerParams(vmem_limit_bytes=2**20),
        cost_estimate=COST,
        name="chosen",
    )(plan, in_middle, at_end, *after)


def gate_kernel(members, plan_ref, *refs):
    parts = refs[:members]
    query_ref, gated_ref, conv_ref = refs[members], *refs[-2:]
    position = plan_ref[POSITION]
    share = parts[0].shape[1]
    for step in range(members):
        columns = pl.ds(pl.multiple_of((position ^ step) * share, share), share)
        conv = parts[step][...]
        conv_ref[:, columns] = conv
        gated_ref[:, columns] = (wide(conv) * wide(query_ref[:, columns])).astype(jnp.bfloat16)


def gated(plan, parts, query_gate, after):
    array = jax.ShapeDtypeStruct(query_gate.shape, jnp.bfloat16)
    return pl.pallas_call(
        functools.partial(gate_kernel, len(parts)),
        out_shape=[array, array],
        in_specs=[SMEM] + [VMEM] * (len(parts) + 1) + [ANYWHERE] * len(after),
        out_specs=[VMEM] * 2,
        compiler_params=pltpu.CompilerParams(vmem_limit_bytes=8 * 2**20),
        cost_estimate=COST,
        name="gated_output",
    )(plan, *parts, query_gate, *after)


def spans(widths, start, stop):
    found, begin = [], 0
    for number, width in enumerate(widths):
        low, high = max(start, begin), min(stop, begin + width)
        if low < high:
            found.append((number, slice(low - begin, high - begin), slice(low - start, high - start)))
        begin += width
    return found


def product_kernel(steps, more_widths, out_widths, _, data_ref, weight_ref, *refs):
    more, outputs = refs[: len(more_widths)], refs[-len(out_widths) :]
    product = jnp.dot(data_ref[...], weight_ref[...], preferred_element_type=jnp.float32)
    width = product.shape[1]
    for step in range(steps):
        start, stop = step * width, (step + 1) * width

        @pl.when(pl.program_id(0) == step)
        def _(start=start, stop=stop):
            total = product
            if more:
                parts = [wide(more[n][:, there]) for n, there, _ in spans(more_widths, start, stop)]
                total = total + jnp.concatenate(parts, axis=1)
            total = total.astype(jnp.bfloat16)
            for n, there, here in spans(out_widths, start, stop):
                outputs[n][:, there] = total[:, here]


def column_products(
    plan, data, out_weight, first, count, other, more=(), after=(), tiles=1, widths=()
):
    rows, depth = data.shape
    width = data.shape[1]
    tile = width // tiles
    steps = count * tiles
    widths = tuple(widths) or (width,) * count

    def weights(i, at):
        return 0, at[2 * (first - i // tiles) + other] * tiles + i % tiles

    return pl.pallas_call(
        functools.partial(product_kernel, steps, [part.shape[1] for part in more], widths),
        out_shape=[jax.ShapeDtypeStruct((rows, part), jnp.bfloat16) for part in widths],
        grid_spec=pltpu.PrefetchScalarGridSpec(
            num_scalar_prefetch=1,
            grid=(steps,),
            in_specs=[VMEM, pl.BlockSpec((depth, tile), weights)]
            + [VMEM] * len(more)
            + [ANYWHERE] * len(after),
            out_specs=[VMEM] * len(widths),
        ),
        compiler_params=pltpu.CompilerParams(vmem_limit_bytes=16 * 2**20),
        cost_estimate=COST,
        name="projection_blocks",
    )(plan, data, in_hbm(out_weight), *more, *after)


def cotangent_kernel(count, begin, _, weight_ref, *refs):
    blocks, refs = refs[:count], refs[count:]
    step = pl.program_id(0)
    total = refs[-1]

    for number, block in enumerate(blocks):

        @pl.when(step == number)
        def _(number=number, block=block):
            product = lax.dot_general(
                block[...], weight_ref[...], NT, preferred_element_type=jnp.float32
            )
            if number == 0:
                total[...] = product if begin else refs[0][...] + product
            else:
                total[...] += product


def last_cotangent_kernel(
    members, plan_ref, weight_ref, block_ref, start_ref, conv_ref, query_ref, *refs
):
    parts, cot_scr = refs[-1 - members : -1], refs[-1]
    grad_ref = refs[-2 - members]
    product = lax.dot_general(
        block_ref[...], weight_ref[...], NT, preferred_element_type=jnp.float32
    )
    dgated = wide((start_ref[...] + product).astype(jnp.bfloat16))
    grad_ref[...] = (dgated * wide(conv_ref[...])).astype(jnp.bfloat16)
    cot_scr[...] = (dgated * wide(query_ref[...])).astype(jnp.bfloat16)
    share = parts[0].shape[1]
    odd = plan_ref[POSITION] % 2
    for step in range(0, members, 2):

        @pl.when(pl.program_id(0) == step // 2)
        def _(step=step):
            parts[step][...] = cot_scr[:, pl.ds(pl.multiple_of(odd * share, share), share)]
            parts[step + 1][...] = cot_scr[
                :, pl.ds(pl.multiple_of((1 - odd) * share, share), share)
            ]


def last_cotangents(
    plan, first, block, out_weight, start, convolved, query_gate, members, after
):
    rows, width = block.shape
    channels = out_weight.shape[0]
    share = channels // members
    pair = pl.BlockSpec((rows, 2 * share), lambda i, at: (0, at[POSITION] // 2 ^ i))
    return pl.pallas_call(
        functools.partial(last_cotangent_kernel, members),
        out_shape=[jax.ShapeDtypeStruct((rows, channels), jnp.bfloat16)]
        + [jax.ShapeDtypeStruct((rows, share), jnp.bfloat16)] * members,
        grid_spec=pltpu.PrefetchScalarGridSpec(
            num_scalar_prefetch=1,
            grid=(members // 2,),
            in_specs=[
                pl.BlockSpec((2 * share, width), lambda i, at: (at[POSITION] // 2 ^ i, at[first])),
                VMEM,
                pair,
                pair,
                pair,
            ]
            + [ANYWHERE] * len(after),
            out_specs=[pair] + [VMEM] * members,
            scratch_shapes=[pltpu.VMEM((rows, 2 * share), jnp.bfloat16)],
        ),
        compiler_params=pltpu.CompilerParams(vmem_limit_bytes=24 * 2**20),
        cost_estimate=COST,
        name="cotangent_last",
    )(plan, in_hbm(out_weight), block, start, convolved, query_gate, *after)


def both(blocks):
    return [part for block in blocks for part in (block, swapped(block, "tp", 1))]


def cotangent_products(plan, first, parts, out_weight, start=None, after=()):
    rows, width = parts[0].shape
    channels = out_weight.shape[0]
    count = len(parts)
    begin = start is None
    extra = () if begin else (start,)
    return pl.pallas_call(
        functools.partial(cotangent_kernel, count, begin),
        out_shape=jax.ShapeDtypeStruct((rows, channels), jnp.float32),
        grid_spec=pltpu.PrefetchScalarGridSpec(
            num_scalar_prefetch=1,
            grid=(count,),
            in_specs=[pl.BlockSpec((channels, width), lambda i, at: (0, at[first + i]))]
            + [VMEM] * (count + len(extra))
            + [ANYWHERE] * len(after),
            out_specs=VMEM,
        ),
        compiler_params=pltpu.CompilerParams(vmem_limit_bytes=16 * 2**20),
        cost_estimate=COST,
        name="cotangent_blocks",
    )(plan, in_hbm(out_weight), *parts, *extra, *after)


def packed_parts(position, key_gate, value_input, filter_taps, members, scale):
    length, channels = key_gate.shape
    share = channels // members
    product_in = (wide(key_gate) * wide(value_input)).astype(jnp.bfloat16)
    tap_rows = (filter_taps * scale).astype(jnp.bfloat16).T
    owned = filter_taps.shape[1] // members
    chunks = length // share
    packed = []
    pieces = cut(product_in, position, members, 1)
    for piece, taps in zip(pieces, cut(tap_rows, position, members, 0)):
        taps = taps.reshape(owned, chunks, share).transpose(1, 0, 2)
        taps = jnp.pad(taps, ((0, 0), (0, padded(owned) - owned), (0, 0)))
        packed.append(jnp.concatenate([piece, taps.reshape(-1, share)], axis=0))
    return packed


def unpacked_parts(position, parts, key_gate, value_input, groups):
    length, channels = key_gate.shape
    members = len(parts)
    share = channels // members
    owned = groups // members
    chunks = length // share
    input_grad = wide(joined([part[:length] for part in parts], position, 1))
    filter_parts = [
        part[length:]
        .reshape(chunks, padded(owned), share)[:, :owned]
        .transpose(1, 0, 2)
        .reshape(owned, length)
        for part in parts
    ]
    grad_filter = wide(joined(filter_parts, position, 0)).T
    grad_key = (input_grad * wide(value_input)).astype(jnp.bfloat16)
    grad_value = (input_grad * wide(key_gate)).astype(jnp.bfloat16)
    return grad_key, grad_value, grad_filter


def in_line(
    query_gate, key_gate, value_input, filter_taps, out_weight, out_grad, members, scale
):
    length, channels = query_gate.shape
    groups = filter_taps.shape[1]
    per_group = channels // groups
    who = jnp.stack([lax.axis_index("ctx"), lax.axis_index("tp")]).astype(jnp.int32)
    plan = planned(who)
    near, cross = hop(out_grad, INWARD + OUTWARD), hop(out_grad, ACROSS)
    total = cotangent_products(plan, 2 * OWN, both([out_grad]), out_weight)

    packed = prepare(who, key_gate, value_input, filter_taps, members, scale)
    input_parts = traded(packed, "ctx")
    conv_parts, turned, taps = convolve(plan, input_parts, length, per_group, (total,))
    *conv_parts, near, cross = held_until([*conv_parts, near, cross], ())
    far, skip = hop(near, ACROSS), hop(cross, OUTWARD)
    lags = lag_matrices(taps)
    gated_out, convolved = gated(plan, traded(conv_parts, "ctx"), query_gate, (lags,))

    def product(first, count, other, more=(), after=(), tiles=1, widths=()):
        return column_products(
            plan, gated_out, out_weight, first, count, other, more, after, tiles, widths
        )

    quarter, half = channels // 4, channels // 2
    given_far = product(FAR, 1, 1, tiles=2, widths=(3 * quarter, quarter))
    received = [swapped(part, "tp", 1) for part in given_far]
    (first,) = product(FAR, 1, 0, received, tiles=2)
    far, skip = held_until([far, skip], (first,))
    mixed = chosen(plan, far, first)
    arrived = hop(mixed, OUTWARD + INWARD)
    given_middle = product(MIDDLE, 1, 1, (), (mixed,), tiles=2, widths=(half, half))
    received = [swapped(part, "tp", 1) for part in given_middle]
    (second,) = product(MIDDLE, 1, 0, received, tiles=2)
    middle_block = added(cross, skip)
    blocks = [near, swapped(near, "tp", 1), middle_block]
    total = cotangent_products(plan, 2 * NEAR, blocks, out_weight, total, after=(second,))
    given_near, given_own = product(NEAR, 2, 1, (), (second,))
    (arrived,) = held_until([arrived], (total, given_near))
    through = added(first, arrived)
    two_a = hop(through, ACROSS)
    (second,) = held_until([second], (arrived,))
    two_b = hop(second, INWARD)

    far_block, far_other = both([chosen(plan, far, arrived, (through,))])
    blocks = [swapped(middle_block, "tp", 1), far_block]
    total = cotangent_products(
        plan, 2 * MIDDLE + 1, blocks, out_weight, total, after=(through,)
    )
    received = [swapped(part, "tp", 1) for part in (given_near, given_own)]
    grad_query, *grad_parts = last_cotangents(
        plan, 2 * FAR + 1, far_other, out_weight, total, convolved, query_gate, members, received
    )
    third, own = product(NEAR, 2, 0, received, (grad_parts[0],))
    grad_parts = traded(grad_parts, "ctx")

    two_a, two_b = held_until([two_a, two_b], (own,))
    third, second = added(third, two_a), added(second, two_b)
    back_parts = correlate(plan, turned, lags, grad_parts, per_group, scale, (third, second))
    summands = (own, hop(third, OUTWARD + INWARD), hop(second, ACROSS))
    back_parts = traded(back_parts, "ctx")
    projected, *gradients = finished(
        plan, back_parts, key_gate, value_input, summands, groups
    )
    return projected, grad_query, *gradients


def anywhere(
    query_gate, key_gate, value_input, filter_taps, out_weight, out_grad, members, scale
):
    length, channels = query_gate.shape
    groups = filter_taps.shape[1]
    per_group = channels // groups
    position = lax.axis_index("ctx")
    plan = jnp.full((POSITION + 1,), position, jnp.int32)
    packed = packed_parts(position, key_gate, value_input, filter_taps, members, scale)
    input_parts = traded(packed, "ctx")
    conv_parts, turned, taps = convolve(plan, input_parts, length, per_group)
    conv_parts = traded(conv_parts, "ctx")
    convolved = joined(conv_parts, position, 1)
    gated_out = (wide(query_gate) * wide(convolved)).astype(jnp.bfloat16)
    partial_value = jnp.dot(gated_out, out_weight, preferred_element_type=jnp.float32)
    projected = lax.psum_scatter(
        partial_value.astype(jnp.bfloat16), "tp", scatter_dimension=1, tiled=True
    )
    dgated = jnp.einsum(
        "tk,ck->tc",
        lax.all_gather(out_grad, "tp", axis=1, tiled=True),
        out_weight,
        preferred_element_type=jnp.float32,
    ).astype(jnp.bfloat16)
    grad_query = (wide(dgated) * wide(convolved)).astype(jnp.bfloat16)
    conv_grad = (wide(dgated) * wide(query_gate)).astype(jnp.bfloat16)
    grad_parts = traded(cut(conv_grad, position, members, 1), "ctx")
    back_parts = correlate(plan, turned, lag_matrices(taps), grad_parts, per_group, scale)
    back_parts = traded(back_parts, "ctx")
    return (
        projected,
        grad_query,
        *unpacked_parts(position, back_parts, key_gate, value_input, groups),
    )


def local(query_gate, key_gate, value_input, filter_taps, out_weight, out_grad):
    length, channels = query_gate.shape
    groups = filter_taps.shape[1]
    members = lax.axis_size("ctx")
    scale = 1.0 / math.sqrt(length * members)
    fits = channels // members % 128 == 0 and groups // members % 16 == 0
    body = in_line if lax.axis_size("tp") == 8 and fits else anywhere
    return body(
        query_gate, key_gate, value_input, filter_taps, out_weight, out_grad, members, scale
    )


def solution(mesh):
    both = P("ctx", "tp")
    return jax.shard_map(
        local,
        mesh=mesh,
        in_specs=(both, both, both, both, P("tp", None), both),
        out_specs=(both,) * 5,
        check_vma=False,
    )
```
